32 devices in a mesh: fsdp: 2 (over y), seq: 16 (over z, x, core).
Axes of the slice: x: 2, y: 2, z: 4, core: 2. Of those that a mesh axis runs over, the one named last changes fastest.
Arguments:
- inputs: bfloat16 [2, 2, 1024, 2560], P(None, 'fsdp', 'seq'), may hold values from -26 to 26
- cotangent: bfloat16 [2, 2, 1024, 2560], P(None, 'fsdp', 'seq'), may hold values from -6 to 6
- proj_gelu: bfloat16 [2560, 2560], P(('fsdp', 'seq')), may hold values from -0.125 to 0.125
- proj_lru: bfloat16 [2560, 2560], P(('fsdp', 'seq')), may hold values from -0.125 to 0.125
- gate_blocks: bfloat16 [2560, 512], P(('fsdp', 'seq')), may hold values from -0.375 to 0.375
- proj_out: bfloat16 [2560, 2560], P(None, ('fsdp', 'seq')), may hold values from -0.125 to 0.125
- ffw_gate: bfloat16 [2560, 7680], P(('fsdp', 'seq')), may hold values from -0.125 to 0.125
- ffw_up: bfloat16 [2560, 7680], P(('fsdp', 'seq')), may hold values from -0.125 to 0.125
- ffw_down: bfloat16 [7680, 2560], P(None, ('fsdp', 'seq')), may hold values from -0.0625 to 0.0625
- norm_mix: bfloat16 [2560], P(('fsdp', 'seq')), may hold values from 0.099609375 to 1.8984375
- norm_ffw: bfloat16 [2560], P(('fsdp', 'seq')), may hold values from 0.099609375 to 1.8984375
- decay_param: bfloat16 [2560], P(('fsdp', 'seq')), may hold values from 4 to 14
- conv_taps: bfloat16 [2560, 4], P(('fsdp', 'seq')), may hold values from -2.5 to 2.5
Outputs:
- mixed_out: bfloat16 [2, 2, 1024, 2560], P(None, 'fsdp', 'seq')
- grad_inputs: float32 [2, 2, 1024, 2560], P(None, 'fsdp', 'seq')
- grad_proj_gelu: float32 [2560, 2560], P(('fsdp', 'seq'))
- grad_proj_lru: float32 [2560, 2560], P(('fsdp', 'seq'))
- grad_gate_blocks: float32 [2560, 512], P(('fsdp', 'seq'))
- grad_proj_out: float32 [2560, 2560], P(None, ('fsdp', 'seq'))
- grad_ffw_gate: float32 [2560, 7680], P(('fsdp', 'seq'))
- grad_ffw_up: float32 [2560, 7680], P(('fsdp', 'seq'))
- grad_ffw_down: float32 [7680, 2560], P(None, ('fsdp', 'seq'))
- grad_norm_mix: float32 [2560], P(('fsdp', 'seq'))
- grad_norm_ffw: float32 [2560], P(('fsdp', 'seq'))
- grad_decay_param: float32 [2560], P(('fsdp', 'seq'))
- grad_conv_taps: float32 [2560, 4], P(('fsdp', 'seq'))
The draws below stay inside these ranges and needn't reach their ends.
All inputs are finite; a program needn't handle non-finite values.
Results may differ from the reference program's by a relative error of at most 0.009.
Values may be sent and summed in bfloat16 or wider, within the bound.
A program may use at most 1 GiB of HBM per device.

```python
import jax
import jax.numpy as jnp
from jax import lax

D = 2560
R = 2560
FF = 7680
CONV = 4
MICRO = 2
BW = 256
LEN = 1024
SEQS = 2


def draw_inputs(key, part):
    key = jax.random.fold_in(key, 11)
    key_rows, key_cols, key_base = jax.random.split(key, 3)
    row_scale = jnp.exp(jax.random.uniform(key_rows, (MICRO, SEQS, LEN, 1), jnp.float32, jnp.log(0.4), jnp.log(4.0)))
    col_scale = jnp.exp(jax.random.uniform(key_cols, (D,), jnp.float32, jnp.log(0.5), jnp.log(2.0)))
    base = jax.random.truncated_normal(key_base, -3.0, 3.0, (MICRO, SEQS, LEN, D), jnp.float32)
    return (base * row_scale * col_scale).astype(jnp.bfloat16)


def draw_decay_param(key, part):
    key = jax.random.fold_in(key, 12)
    key_pick, key_fast, key_slow = jax.random.split(key, 3)
    fast_share = 0.5
    fast = jax.random.uniform(key_pick, (R,), jnp.float32) < fast_share
    fast_rate = jnp.exp(jax.random.uniform(key_fast, (R,), jnp.float32, jnp.log(0.5), jnp.log(2.0))) / 160.0
    slow_rate = jnp.exp(jax.random.uniform(key_slow, (R,), jnp.float32, jnp.log(0.25), jnp.log(2.0))) / (4.0 * LEN)
    soft_vals = jnp.where(fast, fast_rate, slow_rate)
    return (-jnp.log(jnp.expm1(soft_vals))).astype(jnp.bfloat16)


def levels(own_key, dims, pieces, low, top_value):
    loudness = 1.0
    for position, shards_of in pieces:
        heights = jax.random.uniform(jax.random.fold_in(jax.random.fold_in(own_key, 6), position), (shards_of,), jnp.float32, low / len(pieces), top_value / len(pieces))
        loudness = loudness * jnp.repeat(jnp.exp(heights), dims[position] // shards_of).reshape((-1,) + (1,) * (len(dims) - 1 - position))
    return loudness


def normal_values(key, extent, width, limit, cuts=(), kind=jnp.bfloat16):
    entries = jax.random.normal(key, extent, jnp.float32) * width
    if len(cuts) > 0:
        entries = levels(key, extent, cuts, -0.22, 0.18) * entries
    return jnp.clip(entries, min=-limit, max=limit).astype(kind)


def setup_inputs(seed: int = 0) -> dict:
    keys = jax.random.split(jax.random.key(seed), 14)
    return {
        "inputs": draw_inputs(jax.random.fold_in(keys[13], 71), 0),
        "cotangent": normal_values(keys[1], (MICRO, SEQS, LEN, D), 1.0, 6.0, ((1, 2), (2, 16))),
        "proj_gelu": normal_values(keys[2], (D, R), D ** -0.5, 0.125, ((0, 32),)),
        "proj_lru": normal_values(keys[3], (D, R), D ** -0.5, 0.125, ((0, 32),)),
        "gate_blocks": normal_values(keys[4], (R, 2 * BW), BW ** -0.5, 0.375, ((0, 32),)),
        "proj_out": normal_values(keys[5], (R, D), R ** -0.5, 0.125, ((1, 32),)),
        "ffw_gate": normal_values(keys[6], (D, FF), D ** -0.5, 0.125, ((0, 32),)),
        "ffw_up": normal_values(keys[7], (D, FF), D ** -0.5, 0.125, ((0, 32),)),
        "ffw_down": normal_values(keys[8], (FF, D), FF ** -0.5, 0.0625, ((1, 32),)),
        "norm_mix": jnp.clip(1.0 + 0.18 * jax.random.normal(keys[9], (D,), jnp.float32), 0.099609375, 1.8984375).astype(jnp.bfloat16),
        "norm_ffw": jnp.clip(1.0 + 0.18 * jax.random.normal(keys[10], (D,), jnp.float32), 0.099609375, 1.8984375).astype(jnp.bfloat16),
        "decay_param": draw_decay_param(jax.random.fold_in(keys[13], 71), 0),
        "conv_taps": normal_values(keys[12], (R, CONV), 0.5, 2.5, ((0, 32),)),
    }


EPS = 1e-06
GUARD = 0.001
RATE = 8.0

@jax.custom_vjp
def low(v):
    return lax.optimization_barrier(v.astype(jnp.bfloat16)).astype(jnp.float32)

@jax.custom_vjp
def low_back(v):
    return v

def low_keep(v):
    return (low(v), None)

def low_pass(kept, grad):
    return (grad,)

def back_keep(v):
    return (v, None)

def back_low(kept, grad):
    return (low(grad),)
low.defvjp(low_keep, low_pass)
low_back.defvjp(back_keep, back_low)

def exact_dot(left_mat, right_mat):
    return jnp.dot(left_mat, right_mat, precision=lax.Precision.HIGHEST, preferred_element_type=jnp.float32)

def normed(values, gain_vec):
    return values * lax.rsqrt(lax.optimization_barrier(jnp.mean(values * values, axis=-1, keepdims=True)) + EPS) * gain_vec

def linked(earlier, latter):
    return (earlier[0] * latter[0], latter[0] * earlier[1] + latter[1])

def gate_math(gate_pre, conv_vals, decay_param):
    row_count = conv_vals.shape[0]
    lru_width = conv_vals.shape[1]
    half_width = gate_pre.shape[-1] // 2
    rec_gate = jax.nn.sigmoid(gate_pre[..., :half_width].reshape(row_count, lru_width))
    in_gate = jax.nn.sigmoid(gate_pre[..., half_width:].reshape(row_count, lru_width))
    log_decay = -RATE * rec_gate * jax.nn.softplus(-decay_param)
    root_vals = jnp.sqrt(1.0 - jnp.exp(2.0 * log_decay) + GUARD)
    return (log_decay, root_vals * in_gate * conv_vals)

def geglu(gate_vals, up_vals):
    return jax.nn.gelu(gate_vals) * up_vals

def block_forward(params, x_seq):
    proj_gelu, proj_lru, gate_blocks, proj_out, ffw_gate, ffw_up, ffw_down, norm_mix, norm_ffw, decay_param, conv_taps = params
    seq_len = x_seq.shape[0]
    tap_count = conv_taps.shape[1]
    block_width = gate_blocks.shape[1] // 2
    head_count = gate_blocks.shape[0] // block_width
    mixed = low(normed(x_seq, norm_mix))
    gelu_pre = low_back(exact_dot(mixed, proj_gelu))
    gelu_act = jax.nn.gelu(gelu_pre)
    lru_in = low(low_back(exact_dot(mixed, proj_lru)))
    padded = jnp.concatenate([jnp.zeros((tap_count - 1, lru_in.shape[1]), jnp.float32), lru_in], axis=0)
    conv_sum = conv_taps[:, 0] * padded[tap_count - 1:tap_count - 1 + seq_len]
    for tap_index in range(1, tap_count):
        start_row = tap_count - 1 - tap_index
        conv_sum = conv_sum + conv_taps[:, tap_index] * padded[start_row:start_row + seq_len]
    conv_out = low(conv_sum)
    gate_pre = low_back(jnp.einsum('shi,hij->shj', conv_out.reshape(seq_len, head_count, block_width), gate_blocks.reshape(head_count, block_width, 2 * block_width), precision=lax.Precision.HIGHEST))
    log_decay, drive_in = gate_math(gate_pre, conv_out, decay_param)
    _, states = lax.associative_scan(linked, (jnp.exp(log_decay), drive_in), axis=0)
    mix_vals = low(states * gelu_act)
    x_one = x_seq + low_back(exact_dot(mix_vals, proj_out))
    ffw_in = low(normed(x_one, norm_ffw))
    gate_vals = low_back(exact_dot(ffw_in, ffw_gate))
    up_vals = low_back(exact_dot(ffw_in, ffw_up))
    hidden = low(geglu(gate_vals, up_vals))
    return x_one + exact_dot(hidden, ffw_down)

def reference(inputs, cotangent, proj_gelu, proj_lru, gate_blocks, proj_out, ffw_gate, ffw_up, ffw_down, norm_mix, norm_ffw, decay_param, conv_taps):
    params = tuple((weight.astype(jnp.float32) for weight in (proj_gelu, proj_lru, gate_blocks, proj_out, ffw_gate, ffw_up, ffw_down, norm_mix, norm_ffw, decay_param, conv_taps)))
    seq_count = inputs.shape[0] * inputs.shape[1]
    x_all = inputs.reshape(seq_count, inputs.shape[2], inputs.shape[3]).astype(jnp.float32)
    cot_all = cotangent.reshape(seq_count, inputs.shape[2], inputs.shape[3]).astype(jnp.float32)

    def sequence_step(totals, pair_in):
        x_seq, cot_seq = pair_in
        result, pull_back = jax.vjp(block_forward, params, x_seq)
        grad_params, grad_x = pull_back(cot_seq)
        totals = tuple((total_g + new_g for total_g, new_g in zip(totals, grad_params)))
        return (totals, (result.astype(jnp.bfloat16), grad_x))
    start_totals = tuple((jnp.zeros_like(weight) for weight in params))
    totals, (results, grads_x) = lax.scan(sequence_step, start_totals, (x_all, cot_all))
    return (results.reshape(inputs.shape), grads_x.reshape(inputs.shape), totals[0], totals[1], totals[2], totals[3], totals[4], totals[5], totals[6], totals[7], totals[8], totals[9], totals[10])
```

```python
import jax
import jax.numpy as jnp
from jax import lax
from jax.sharding import PartitionSpec as P

EPS = 1e-06
GUARD = 0.001
RATE = 8.0
TP = 4
NQ = 4
HALO = 8
BF = jnp.bfloat16
F32 = jnp.float32


def move(value, step):
    pairs = []
    for here in range(lax.axis_size("seq")):
        there = step(here // (TP * NQ), here // NQ % TP, here % NQ)
        if there is not None:
            pairs.append((here, (there[0] * TP + there[1]) * NQ + there[2]))
    return lax.ppermute(value, "seq", pairs)


def swap_core(value):
    return move(value, lambda r, z, q: (r, z, q ^ 1))


def swap_x(value):
    return move(value, lambda r, z, q: (r, z, q ^ 2))


def swap_f(value):
    return lax.ppermute(value, "fsdp", [(0, 1), (1, 0)])


def shift_z(value, d):
    return move(value, lambda r, z, q: (r, (z + d) % TP, q))


def shift_q(value, d):
    return move(value, lambda r, z, q: (r, z, (q + d) % NQ))


def shift_r(value, d):
    count = lax.axis_size("seq") // (TP * NQ)
    return move(value, lambda r, z, q: ((r + d) % count, z, q))


def hop(value, d, low, high):
    return move(value, lambda r, z, q: (r, z + d, q) if low <= z <= high else None)


class Place:
    def __init__(self):
        seq = lax.axis_index("seq")
        self.f = lax.axis_index("fsdp")
        self.r, self.z, self.q = seq // (TP * NQ), seq // NQ % TP, seq % NQ
        self.x, self.c = self.q // 2, self.q % 2
        self.rests = lax.axis_size("seq") // (TP * NQ)
        self.fs = lax.axis_size("fsdp")
        self.index = self.f * lax.axis_size("seq") + seq


def at(value, index):
    return lax.dynamic_index_in_dim(value, index, 0, keepdims=False)


def put(base, value, *index):
    starts = [jnp.int32(0) if i is None else jnp.int32(i) for i in index]
    starts += [jnp.int32(0)] * (base.ndim - len(index))
    for dim, i in enumerate(index):
        if i is not None:
            value = jnp.expand_dims(value, dim)
    return lax.dynamic_update_slice(base, value, starts)


def everywhere(value, shifter, mine, count):
    out = put(jnp.zeros((count,) + value.shape, value.dtype), value, mine)
    for d in range(1, count):
        out = put(out, shifter(value, d), (mine - d) % count)
    return out


def gather_z(value, p):
    ups, downs = [], []
    up = down = value
    for k in range(1, TP):
        up = hop(up, 1, k - 1, TP - 2)
        down = hop(down, -1, 1, TP - k)
        ups.append(up)
        downs.append(down)
    out = put(jnp.zeros((TP,) + value.shape, value.dtype), value, p.z)
    for k in range(1, TP):
        out = put(out, downs[k - 1] + ups[TP - 1 - k], (p.z + k) % TP)
    return out


def scatter_z(parts, p):
    right = left = None
    for k in range(TP - 1, 0, -1):
        send = at(parts, (p.z + k) % TP)
        if right is not None:
            send = (send.astype(F32) + right.astype(F32)).astype(BF)
        right = hop(send, 1, 0, TP - 1 - k)
        send = at(parts, (p.z - k) % TP)
        if left is not None:
            send = (send.astype(F32) + left.astype(F32)).astype(BF)
        left = hop(send, -1, k, TP - 1)
    return at(parts, p.z).astype(F32) + right.astype(F32) + left.astype(F32)


def weights_in(pieces, p):
    rows, cols = pieces.shape[1:]
    mine = put(jnp.zeros(pieces.shape, BF), at(pieces, p.z), p.z)
    for d in range(1, TP):
        mine = put(mine, shift_z(at(pieces, (p.z + d) % TP), d), (p.z - d) % TP)
    mine = everywhere(mine, shift_r, p.r, p.rests)
    half = TP // 2
    by_x, by_f = swap_x(mine), swap_f(mine)
    corner = (swap_f(by_x[:, :half]), swap_x(by_f[:, half:]))
    whole = jnp.zeros((p.fs, p.rests, TP, 2, 2, rows, cols), BF)
    for block, f, x, z in (
        (mine, p.f, p.x, 0),
        (by_x, p.f, 1 - p.x, 0),
        (by_f, 1 - p.f, p.x, 0),
        (corner[0], 1 - p.f, 1 - p.x, 0),
        (corner[1], 1 - p.f, 1 - p.x, half),
    ):
        other = swap_core(block)
        for part, c in ((block, p.c), (other, 1 - p.c)):
            part = part[None, :, :, None, None]
            whole = lax.dynamic_update_slice(
                whole, part, [jnp.int32(i) for i in (f, 0, z, x, c, 0, 0)]
            )
    return whole.reshape(-1, cols)


def row_blocks(acts, p):
    tokens = acts.shape[0]
    rows = acts.shape[1] // (p.fs * p.rests * TP * 4)
    turned = acts.T.reshape(p.fs, p.rests, TP, 2, 2, rows, tokens)

    def block(f_rel, x_rel, c_rel, low):
        f, x, c = (p.f + f_rel) % 2, (p.x + x_rel) % 2, (p.c + c_rel) % 2
        got = lax.dynamic_slice(
            turned,
            [jnp.int32(i) for i in (f, 0, low, x, c, 0, 0)],
            (1, p.rests, TP // 2, 1, 1, rows, tokens),
        )
        return got.reshape(-1, tokens)

    def core(c_rel):
        half = TP // 2
        return [
            jnp.concatenate([block(0, 1, c_rel, 0), block(1, 1, c_rel, 0)], axis=0),
            jnp.concatenate([block(0, 0, c_rel, 0), block(1, 0, c_rel, 0)], axis=0),
            jnp.concatenate([block(1, 0, c_rel, half), block(1, 1, c_rel, half)], axis=0),
            jnp.concatenate([block(0, 0, c_rel, half), block(0, 1, c_rel, half)], axis=0),
        ]

    return (jnp.concatenate(core(1), axis=0), core(0))


def grads_out(far, near, p):
    got = swap_core(far)
    size, cols = got.shape[0] // 4, got.shape[1]
    halves = [near(i, got[i * size : (i + 1) * size]) for i in range(4)]
    plus = lambda a, b: (a.astype(F32) + b.astype(F32)).astype(BF)
    from_x = swap_x(halves[0])
    from_f = swap_f(halves[2])
    one = plus(halves[1], from_x)
    two = plus(halves[3], from_f)
    cut = size // 2
    one_f = swap_f(one[cut:])
    two_x = swap_x(two[cut:])
    low = plus(one[:cut], one_f).reshape(p.rests, TP // 2, -1, cols)
    high = plus(two[:cut], two_x).reshape(p.rests, TP // 2, -1, cols)
    total = jnp.concatenate([low, high], axis=1)
    mine = at(total, p.r)
    for d in range(1, p.rests):
        mine = plus(mine, shift_r(at(total, (p.r + d) % p.rests), d))
    out = put(jnp.zeros(mine.shape, BF), at(mine, p.z), p.z)
    for d in range(1, TP):
        out = put(out, shift_z(at(mine, (p.z + d) % TP), d), (p.z - d) % TP)
    return out


def dot_plain(left_mat, right_mat):
    return jnp.dot(left_mat, right_mat, preferred_element_type=F32)


def dot_right_t(left_mat, right_mat):
    return lax.dot_general(
        left_mat, right_mat, (((1,), (1,)), ((), ())), preferred_element_type=F32
    )


def normed(values, gain_vec):
    return values * lax.rsqrt(jnp.mean(values * values, axis=-1, keepdims=True) + EPS) * gain_vec


def linked(earlier, latter):
    return (earlier[0] * latter[0], latter[0] * earlier[1] + latter[1])


def gate_math(gate_pre, conv_vals, decay_param):
    half_width = gate_pre.shape[-1] // 2
    rec_gate = jax.nn.sigmoid(gate_pre[..., :half_width].reshape(conv_vals.shape))
    in_gate = jax.nn.sigmoid(gate_pre[..., half_width:].reshape(conv_vals.shape))
    log_decay = -RATE * rec_gate * jax.nn.softplus(-decay_param)
    root_vals = jnp.sqrt(1.0 - jnp.exp(2.0 * log_decay) + GUARD)
    return (log_decay, root_vals * in_gate * conv_vals)


def geglu(gate_vals, up_vals):
    return jax.nn.gelu(gate_vals) * up_vals


def all_spans(value, p):
    by_q = everywhere(value, shift_q, p.q, NQ)
    by_r = everywhere(by_q, shift_r, p.r, p.rests)
    return jnp.swapaxes(by_r, 1, 2).reshape((-1,) + value.shape[1:])


def own_spans(spans, p):
    split = spans.reshape((p.rests, TP, NQ) + spans.shape[1:])
    return lax.dynamic_index_in_dim(at(split, p.r), p.q, 1, keepdims=False)


def on_device(
    inputs,
    cotangent,
    proj_gelu,
    proj_lru,
    gate_blocks,
    proj_out,
    ffw_gate,
    ffw_up,
    ffw_down,
    norm_mix,
    norm_ffw,
    decay_param,
    conv_taps,
):
    p = Place()
    micro, span, width = inputs.shape[0], inputs.shape[2], inputs.shape[3]
    lru_width = proj_gelu.shape[1]
    tap_count = conv_taps.shape[1]
    block_width = gate_blocks.shape[1] // 2
    heads = lru_width // block_width
    ffw_part = ffw_gate.shape[1] // TP
    rows = proj_gelu.shape[0]
    held = -(-heads // TP)
    first = [k * heads // TP for k in range(TP)]
    owned = [range(first[k], first[k + 1] if k + 1 < TP else heads) for k in range(TP)]
    part = held * block_width

    out_t, down_t = proj_out.T, ffw_down.T
    small = jnp.concatenate(
        [norm_mix[:, None], norm_ffw[:, None], decay_param[:, None], conv_taps], axis=1
    )
    small = jnp.pad(small, ((0, 0), (0, 128 - small.shape[1])))
    mix_pieces, ffw_pieces = [], []
    for k in range(TP):
        cols = slice(first[k] * block_width, first[k] * block_width + part)
        mix_pieces.append(
            jnp.concatenate(
                [proj_gelu[:, cols], proj_lru[:, cols], out_t[:, cols], gate_blocks, small], axis=1
            )
        )
        cols = slice(k * ffw_part, (k + 1) * ffw_part)
        ffw_pieces.append(
            jnp.concatenate([ffw_gate[:, cols], ffw_up[:, cols], down_t[:, cols]], axis=1)
        )
    mix_w = weights_in(jnp.stack(mix_pieces), p)

    x_rows = inputs[:, 0]
    edge = lax.ppermute(
        x_rows[:, span - (tap_count - 1) :],
        "seq",
        [(i, i + 1) for i in range(lax.axis_size("seq") - 1)],
    )
    pad = jnp.zeros((micro, HALO - (tap_count - 1), width), BF)
    x_all = gather_z(jnp.concatenate([pad, edge, x_rows], axis=1), p)
    ffw_w = weights_in(jnp.stack(ffw_pieces), p)
    cot_all = gather_z(cotangent[:, 0], p).reshape(-1, width)

    gelu_lru_w = mix_w[:, : 2 * part]
    out_w = mix_w[:, 2 * part : 3 * part]
    blocks_w = mix_w[:, 3 * part : 3 * part + 2 * block_width]
    small_w = mix_w[:, 3 * part + 2 * block_width :].astype(F32).T
    mix_gain, ffw_gain = small_w[0], small_w[1]
    start = sum(jnp.where(p.z == k, first[k] * block_width, 0) for k in range(TP))
    feature = jnp.arange(part) + start
    low = sum(jnp.where(p.z == k, owned[k][0] * block_width, 0) for k in range(TP))
    high = sum(jnp.where(p.z == k, (owned[k][-1] + 1) * block_width, 0) for k in range(TP))
    is_own = ((feature >= low) & (feature < high)).astype(F32)
    decay_f = lax.dynamic_slice_in_dim(small_w[2], start, part, 0)
    taps_f = lax.dynamic_slice_in_dim(small_w[3 : 3 + tap_count], start, part, 1)
    block_mats = lax.dynamic_slice_in_dim(blocks_w, start, part, 0).reshape(
        held, block_width, 2 * block_width
    )

    x_all_f = x_all.astype(F32)
    mixed_all = normed(x_all_f, mix_gain).astype(BF)
    pre = dot_plain(mixed_all.reshape(-1, width), gelu_lru_w)
    pre = pre.reshape(TP, micro, HALO + span, 2 * part)
    gelu_pre = pre[:, :, HALO:, :part]
    lru_in = pre[:, :, :, part:].astype(BF).astype(F32)
    mixed = mixed_all[:, :, HALO:].reshape(-1, width)
    gelu_act = jax.nn.gelu(gelu_pre)
    back = lambda k: lru_in[:, :, HALO - k : HALO - k + span]
    conv_sum = taps_f[0] * back(0)
    for k in range(1, tap_count):
        conv_sum = conv_sum + taps_f[k] * back(k)
    conv_bf = conv_sum.astype(BF)
    conv_vals = conv_bf.astype(F32)
    conv_heads = conv_bf.reshape(-1, held, block_width)
    gate_pre = jnp.einsum("shi,hij->shj", conv_heads, block_mats, preferred_element_type=F32)
    gate_pre = gate_pre.reshape(TP, micro, span, held, 2 * block_width)
    log_decay, drive_in = gate_math(gate_pre, conv_vals, decay_f)
    decay_rate = jnp.exp(log_decay)
    log_total = jnp.cumsum(log_decay, axis=2)
    _, local_state = lax.associative_scan(linked, (decay_rate, drive_in), axis=2)
    span_decay = jnp.exp(log_total[:, :, -1])
    sums = all_spans(jnp.stack([span_decay, local_state[:, :, -1]], axis=1), p)
    carry, carries = jnp.zeros_like(sums[0, 0]), []
    for k in range(sums.shape[0]):
        carries.append(carry)
        carry = sums[k, 0] * carry + sums[k, 1]
    state_in = own_spans(jnp.stack(carries), p)
    states = local_state + jnp.exp(log_total) * state_in[:, :, None]
    mix_bf = (states * gelu_act * is_own).astype(BF).reshape(-1, part)
    out_parts = dot_right_t(mix_bf, out_w).astype(BF).reshape(TP, -1, width)
    x_zero = x_rows.reshape(-1, width).astype(F32)
    x_one = x_zero + scatter_z(out_parts, p)

    ffw_bf = gather_z(normed(x_one, ffw_gain).astype(BF), p).reshape(-1, width)
    gate_up_w, down_w = ffw_w[:, : 2 * ffw_part], ffw_w[:, 2 * ffw_part :]
    gate_up = dot_plain(ffw_bf, gate_up_w)
    gate_vals, up_vals = gate_up[:, :ffw_part], gate_up[:, ffw_part:]
    hidden_bf = geglu(gate_vals, up_vals).astype(BF)
    grad_hidden = dot_plain(cot_all, down_w)
    _, pull_back = jax.vjp(geglu, gate_vals, up_vals)
    grad_gate_up = jnp.concatenate(pull_back(grad_hidden), axis=1).astype(BF)
    grad_in_parts = dot_right_t(grad_gate_up, gate_up_w).astype(BF).reshape(TP, -1, width)
    grad_ffw_in = scatter_z(grad_in_parts, p)
    ffw_parts = dot_right_t(hidden_bf, down_w).astype(BF).reshape(TP, -1, width)
    mixed_out = (x_one + scatter_z(ffw_parts, p)).astype(BF)
    _, pull_back = jax.vjp(normed, x_one, ffw_gain)
    grad_x_part, grad_ffw_gain = pull_back(grad_ffw_in)
    grad_x_one = cotangent[:, 0].reshape(-1, width).astype(F32) + grad_x_part
    grad_mix = gather_z(grad_x_one.astype(BF), p).reshape(-1, width)

    ffw_far, ffw_near = row_blocks(ffw_bf, p)
    cot_far, cot_near = row_blocks(cot_all, p)

    def ffw_term(ffw_rows, cot_rows):
        return jnp.concatenate(
            [dot_plain(ffw_rows, grad_gate_up), dot_plain(cot_rows, hidden_bf)], axis=1
        )

    ffw_grads = grads_out(
        ffw_term(ffw_far, cot_far).astype(BF),
        lambda i, got: (ffw_term(ffw_near[i], cot_near[i]) + got.astype(F32)).astype(BF),
        p,
    )

    back_mix = dot_plain(grad_mix, out_w).reshape(TP, micro, span, part)
    grad_states = back_mix * gelu_act
    _, pull_back = jax.vjp(jax.nn.gelu, gelu_pre)
    (grad_gelu_pre,) = pull_back(back_mix * states)
    grad_gelu_bf = (grad_gelu_pre * is_own).astype(BF).reshape(-1, part)
    next_decay = jnp.concatenate([decay_rate[:, :, 1:], jnp.zeros_like(decay_rate[:, :, :1])], 2)
    _, local_back = lax.associative_scan(
        linked, (next_decay, grad_states), axis=2, reverse=True
    )
    back_sums = all_spans((decay_rate[:, :, 0] * local_back[:, :, 0])[:, None], p)
    carry, carries = jnp.zeros_like(sums[0, 0]), []
    for k in range(sums.shape[0] - 1, -1, -1):
        carries.append(carry)
        carry = sums[k, 0] * carry + back_sums[k, 0]
    carried = own_spans(jnp.stack(carries[::-1]), p)
    adjoint = local_back + jnp.exp(log_total[:, :, -1:] - log_total) * carried[:, :, None]
    prev_states = jnp.concatenate([state_in[:, :, None], states[:, :, :-1]], axis=2)
    grad_log = adjoint * prev_states * decay_rate
    _, pull_back = jax.vjp(gate_math, gate_pre, conv_vals, decay_f)
    grad_gate_pre, grad_conv_direct, grad_decay = pull_back((grad_log, adjoint))
    grad_pre_bf = grad_gate_pre.astype(BF).reshape(-1, held, 2 * block_width)
    grad_blocks = jnp.einsum("shi,shj->hij", conv_heads, grad_pre_bf, preferred_element_type=F32)
    grad_conv = grad_conv_direct + jnp.einsum(
        "shj,hij->shi", grad_pre_bf, block_mats, preferred_element_type=F32
    ).reshape(conv_vals.shape)
    grad_taps = jnp.stack([jnp.sum(grad_conv * back(k), axis=(0, 1, 2)) for k in range(tap_count)])
    rim = tap_count - 1
    grad_padded = jnp.zeros((TP, micro, rim + span, part), F32)
    for k in range(tap_count):
        grad_padded = grad_padded + jnp.pad(
            taps_f[k] * grad_conv, ((0, 0), (0, 0), (rim - k, k), (0, 0))
        )
    head_rows = grad_padded[:, :, :rim]
    from_next = shift_q(head_rows, -1)
    last = jnp.zeros_like(head_rows[:1])
    if p.rests > 1:
        last = move(
            head_rows[:1], lambda r, z, q: (r - 1, z, NQ - 1) if q == 0 and r > 0 else None
        )
    from_next = jnp.where(
        p.q == NQ - 1, jnp.concatenate([from_next[1:], last], axis=0), from_next
    )
    grad_lru = grad_padded[:, :, rim:] + jnp.pad(
        from_next, ((0, 0), (0, 0), (span - rim, 0), (0, 0))
    )
    grad_lru_bf = (grad_lru * is_own).astype(BF).reshape(-1, part)
    grad_pair = jnp.concatenate([grad_gelu_bf, grad_lru_bf], axis=1)
    grad_mixed = dot_right_t(grad_pair, gelu_lru_w)
    x_rows_f = x_all_f[:, :, HALO:].reshape(-1, width)
    _, pull_back = jax.vjp(lambda gain: normed(x_rows_f, gain), mix_gain)
    (grad_mix_gain,) = pull_back(grad_mixed)
    grad_mixed_own = scatter_z(grad_mixed.astype(BF).reshape(TP, -1, width), p)
    _, pull_back = jax.vjp(lambda value: normed(value, mix_gain), x_zero)
    grad_inputs = grad_x_one + pull_back(grad_mixed_own)[0]

    blocks_all = lax.dynamic_update_slice_in_dim(
        jnp.zeros((lru_width, 2 * block_width), BF),
        (grad_blocks.reshape(part, -1) * is_own[:, None]).astype(BF),
        start,
        0,
    )
    blocks_far, blocks_near = row_blocks(blocks_all.T, p)
    mixed_far, mixed_near = row_blocks(mixed, p)
    back_far, back_near = row_blocks(grad_mix, p)

    def mixer_term(mixed_rows, back_rows, block_rows):
        return jnp.concatenate(
            [dot_plain(mixed_rows, grad_pair), dot_plain(back_rows, mix_bf), block_rows], axis=1
        )

    mix_grads = grads_out(
        mixer_term(mixed_far, back_far, blocks_far).astype(BF),
        lambda i, got: (
            mixer_term(mixed_near[i], back_near[i], blocks_near[i]) + got.astype(F32)
        ).astype(BF),
        p,
    )
    vectors = jnp.concatenate([grad_decay[None], grad_taps], axis=0) * is_own
    vectors = lax.dynamic_update_slice_in_dim(
        jnp.zeros((vectors.shape[0], lru_width), F32), vectors, start, 1
    )
    vectors = jnp.concatenate([grad_mix_gain[None], grad_ffw_gain[None], vectors], axis=0)
    vectors = jnp.pad(vectors, ((0, -vectors.shape[0] % 8), (0, 0)))
    for exchange in (swap_core, swap_x, swap_f):
        vectors = vectors + exchange(vectors)
    for bit in (1, 2):
        vectors = vectors + move(vectors, lambda r, z, q, bit=bit: (r, z ^ bit, q))
    total = vectors
    for d in range(1, p.rests):
        total = total + shift_r(vectors, d)
    vectors = lax.dynamic_slice_in_dim(total, p.index * rows, rows, 1)

    def mix_columns(offset):
        picked = [
            mix_grads[k][
                :,
                offset + (owned[k][0] - first[k]) * block_width : offset
                + (owned[k][-1] + 1 - first[k]) * block_width,
            ]
            for k in range(TP)
        ]
        return jnp.concatenate(picked, axis=1).astype(F32)

    def ffw_columns(offset):
        picked = [ffw_grads[k][:, offset : offset + ffw_part] for k in range(TP)]
        return jnp.concatenate(picked, axis=1).astype(F32)

    shape = (micro, 1, span, width)
    return (
        mixed_out.reshape(shape),
        grad_inputs.reshape(shape),
        mix_columns(0),
        mix_columns(part),
        jnp.sum(mix_grads[:, :, 3 * part :].astype(F32), axis=0),
        mix_columns(2 * part).T,
        ffw_columns(0),
        ffw_columns(ffw_part),
        ffw_columns(2 * ffw_part).T,
        vectors[0],
        vectors[1],
        vectors[2],
        vectors[3 : 3 + tap_count].T,
    )


def solution(mesh):
    in_specs = (
        P(None, "fsdp", "seq", None),
        P(None, "fsdp", "seq", None),
        P(("fsdp", "seq"), None),
        P(("fsdp", "seq"), None),
        P(("fsdp", "seq"), None),
        P(None, ("fsdp", "seq")),
        P(("fsdp", "seq"), None),
        P(("fsdp", "seq"), None),
        P(None, ("fsdp", "seq")),
        P(("fsdp", "seq")),
        P(("fsdp", "seq")),
        P(("fsdp", "seq")),
        P(("fsdp", "seq"), None),
    )
    out_specs = (
        P(None, "fsdp", "seq", None),
        P(None, "fsdp", "seq", None),
        P(("fsdp", "seq"), None),
        P(("fsdp", "seq"), None),
        P(("fsdp", "seq"), None),
        P(None, ("fsdp", "seq")),
        P(("fsdp", "seq"), None),
        P(("fsdp", "seq"), None),
        P(None, ("fsdp", "seq")),
        P(("fsdp", "seq")),
        P(("fsdp", "seq")),
        P(("fsdp", "seq")),
        P(("fsdp", "seq"), None),
    )
    return jax.shard_map(
        on_device, mesh=mesh, in_specs=in_specs, out_specs=out_specs, check_vma=False
    )
```

```python
import functools

import jax
import jax.numpy as jnp
from jax import lax
from jax.experimental import pallas as pl
from jax.experimental.pallas import tpu as pltpu
from jax.sharding import PartitionSpec as P

EPS = 1e-06
GUARD = 0.001
RATE = 8.0
TP = 4
NQ = 4
HALO = 8
BF = jnp.bfloat16
F32 = jnp.float32
MESH = pl.DeviceIdType.MESH
ANY = pl.BlockSpec(memory_space=pl.ANY)
VMEM = pl.BlockSpec(memory_space=pltpu.VMEM)
GRANT = 60 * 1024 * 1024


def move(value, step):
    pairs = []
    for here in range(lax.axis_size("seq")):
        there = step(here // (TP * NQ), here // NQ % TP, here % NQ)
        if there is not None:
            pairs.append((here, (there[0] * TP + there[1]) * NQ + there[2]))
    return lax.ppermute(value, "seq", pairs)


def swap_core(value):
    return move(value, lambda r, z, q: (r, z, q ^ 1))


def swap_x(value):
    return move(value, lambda r, z, q: (r, z, q ^ 2))


def swap_f(value):
    return lax.ppermute(value, "fsdp", [(0, 1), (1, 0)])


def shift_z(value, d):
    return move(value, lambda r, z, q: (r, (z + d) % TP, q))


def shift_q(value, d):
    return move(value, lambda r, z, q: (r, z, (q + d) % NQ))


def shift_r(value, d):
    count = lax.axis_size("seq") // (TP * NQ)
    return move(value, lambda r, z, q: ((r + d) % count, z, q))


def hop(value, d, low, high):
    return move(value, lambda r, z, q: (r, z + d, q) if low <= z <= high else None)


class Place:
    def __init__(self):
        seq = lax.axis_index("seq")
        self.f = lax.axis_index("fsdp")
        self.r, self.z, self.q = seq // (TP * NQ), seq // NQ % TP, seq % NQ
        self.x, self.c = self.q // 2, self.q % 2
        self.rests = lax.axis_size("seq") // (TP * NQ)
        self.fs = lax.axis_size("fsdp")
        self.index = self.f * lax.axis_size("seq") + seq


def at(value, index):
    return lax.dynamic_index_in_dim(value, index, 0, keepdims=False)


def put(base, value, *index):
    starts = [jnp.int32(0) if i is None else jnp.int32(i) for i in index]
    starts += [jnp.int32(0)] * (base.ndim - len(index))
    for dim, i in enumerate(index):
        if i is not None:
            value = jnp.expand_dims(value, dim)
    return lax.dynamic_update_slice(base, value, starts)


def everywhere(value, shifter, mine, count):
    out = put(jnp.zeros((count,) + value.shape, value.dtype), value, mine)
    for d in range(1, count):
        out = put(out, shifter(value, d), (mine - d) % count)
    return out


def gather_z(value, p):
    ups, downs = [], []
    up = down = value
    for k in range(1, TP):
        up = hop(up, 1, k - 1, TP - 2)
        down = hop(down, -1, 1, TP - k)
        ups.append(up)
        downs.append(down)
    out = put(jnp.zeros((TP,) + value.shape, value.dtype), value, p.z)
    for k in range(1, TP):
        out = put(out, downs[k - 1] + ups[TP - 1 - k], (p.z + k) % TP)
    return out


def scatter_z(parts, p):
    right = left = None
    for k in range(TP - 1, 0, -1):
        send = at(parts, (p.z + k) % TP)
        if right is not None:
            send = (send.astype(F32) + right.astype(F32)).astype(BF)
        right = hop(send, 1, 0, TP - 1 - k)
        send = at(parts, (p.z - k) % TP)
        if left is not None:
            send = (send.astype(F32) + left.astype(F32)).astype(BF)
        left = hop(send, -1, k, TP - 1)
    return at(parts, p.z).astype(F32) + right.astype(F32) + left.astype(F32)


def weights_in(pieces, p):
    rows, cols = pieces.shape[1:]
    mine = put(jnp.zeros(pieces.shape, BF), at(pieces, p.z), p.z)
    for d in range(1, TP):
        mine = put(mine, shift_z(at(pieces, (p.z + d) % TP), d), (p.z - d) % TP)
    mine = everywhere(mine, shift_r, p.r, p.rests)
    half = TP // 2
    by_x, by_f = swap_x(mine), swap_f(mine)
    corner = (swap_f(by_x[:, :half]), swap_x(by_f[:, half:]))
    whole = jnp.zeros((p.fs, p.rests, TP, 2, 2, rows, cols), BF)
    for block, f, x, z in (
        (mine, p.f, p.x, 0),
        (by_x, p.f, 1 - p.x, 0),
        (by_f, 1 - p.f, p.x, 0),
        (corner[0], 1 - p.f, 1 - p.x, 0),
        (corner[1], 1 - p.f, 1 - p.x, half),
    ):
        other = swap_core(block)
        for part, c in ((block, p.c), (other, 1 - p.c)):
            part = part[None, :, :, None, None]
            whole = lax.dynamic_update_slice(
                whole, part, [jnp.int32(i) for i in (f, 0, z, x, c, 0, 0)]
            )
    return whole.reshape(-1, cols)


def row_blocks(acts, p):
    tokens = acts.shape[0]
    rows = acts.shape[1] // (p.fs * p.rests * TP * 4)
    turned = acts.T.reshape(p.fs, p.rests, TP, 2, 2, rows, tokens)

    def block(f_rel, x_rel, c_rel, low):
        f, x, c = (p.f + f_rel) % 2, (p.x + x_rel) % 2, (p.c + c_rel) % 2
        got = lax.dynamic_slice(
            turned,
            [jnp.int32(i) for i in (f, 0, low, x, c, 0, 0)],
            (1, p.rests, TP // 2, 1, 1, rows, tokens),
        )
        return got.reshape(-1, tokens)

    def core(c_rel):
        half = TP // 2
        return [
            jnp.concatenate([block(0, 1, c_rel, 0), block(1, 1, c_rel, 0)], axis=0),
            jnp.concatenate([block(0, 0, c_rel, 0), block(1, 0, c_rel, 0)], axis=0),
            jnp.concatenate([block(1, 0, c_rel, half), block(1, 1, c_rel, half)], axis=0),
            jnp.concatenate([block(0, 0, c_rel, half), block(0, 1, c_rel, half)], axis=0),
        ]

    return (jnp.concatenate(core(1), axis=0), core(0))


def near_groups(far, near):
    got = swap_core(far)
    size = got.shape[0] // 4
    groups = [near(i, got[i * size : (i + 1) * size]) for i in range(4)]
    return [group.reshape(2, size // 2, -1) for group in groups]


def grads_out(far, near, p):
    got = swap_core(far)
    size, cols = got.shape[0] // 4, got.shape[1]
    halves = [near(i, got[i * size : (i + 1) * size]) for i in range(4)]
    plus = lambda a, b: (a.astype(F32) + b.astype(F32)).astype(BF)
    from_x = swap_x(halves[0])
    from_f = swap_f(halves[2])
    one = plus(halves[1], from_x)
    two = plus(halves[3], from_f)
    cut = size // 2
    one_f = swap_f(one[cut:])
    two_x = swap_x(two[cut:])
    low = plus(one[:cut], one_f).reshape(p.rests, TP // 2, -1, cols)
    high = plus(two[:cut], two_x).reshape(p.rests, TP // 2, -1, cols)
    total = jnp.concatenate([low, high], axis=1)
    mine = at(total, p.r)
    for d in range(1, p.rests):
        mine = plus(mine, shift_r(at(total, (p.r + d) % p.rests), d))
    out = put(jnp.zeros(mine.shape, BF), at(mine, p.z), p.z)
    for d in range(1, TP):
        out = put(out, shift_z(at(mine, (p.z + d) % TP), d), (p.z - d) % TP)
    return out


def dot_plain(left_mat, right_mat):
    return jnp.dot(left_mat, right_mat, preferred_element_type=F32)


def dot_right_t(left_mat, right_mat):
    return lax.dot_general(
        left_mat, right_mat, (((1,), (1,)), ((), ())), preferred_element_type=F32
    )


def normed(values, gain_vec):
    return values * lax.rsqrt(jnp.mean(values * values, axis=-1, keepdims=True) + EPS) * gain_vec


def gelu_pair(v):
    scale = 0.7978845608028654
    inner = jnp.tanh(scale * (v + 0.044715 * v * v * v))
    slope = 0.5 * v * (1.0 - inner * inner) * scale * (1.0 + 0.134145 * v * v)
    return 0.5 * v * (1.0 + inner), 0.5 * (1.0 + inner) + slope


def span_scan(decay, drive, backward):
    count = decay.shape[0]
    row = lax.broadcasted_iota(jnp.int32, decay.shape, 0)
    step = 1
    while step < count:
        inside = row < count - step if backward else row >= step
        turn = count - step if backward else step
        drive = drive + jnp.where(inside, decay * pltpu.roll(drive, turn, 0), 0.0)
        decay = decay * jnp.where(inside, pltpu.roll(decay, turn, 0), 1.0)
        step *= 2
    return decay, drive


def gate_values(gate, soft):
    half = gate.shape[1] // 2
    rec_gate = jax.nn.sigmoid(gate[:, :half])
    in_gate = jax.nn.sigmoid(gate[:, half:])
    log_decay = -RATE * rec_gate * soft
    square = jnp.exp(2.0 * log_decay)
    return rec_gate, in_gate, jnp.exp(log_decay), square, jnp.sqrt(1.0 - square + GUARD)


def recur_kernel(span, pre, rows, block, conv, gate, state, prod, sums):
    count = conv.shape[0] // span
    soft, taps = rows[0:1], [rows[k + 2 : k + 3] for k in range(4)]

    def convolve(i, _):
        start = pl.multiple_of(i * (span + HALO), 8)
        vals = pre[pl.ds(start, span + HALO)].astype(BF).astype(F32)
        total = taps[0] * vals
        for k in range(1, 4):
            total = total + taps[k] * pltpu.roll(vals, k, 0)
        conv[pl.ds(pl.multiple_of(i * span, 16), span)] = total[HALO:].astype(BF)
        return 0

    lax.fori_loop(0, count, convolve, 0)
    gate[...] = dot_plain(conv[...], block[0])
    for i in range(count):
        here = pl.ds(i * span, span)
        _, in_gate, decay, _, root = gate_values(gate[here], soft)
        decay, local = span_scan(decay, root * in_gate * conv[here].astype(F32), False)
        state[here] = local
        prod[here] = decay
        sums[0, i : i + 1] = decay[span - 1 :]
        sums[1, i : i + 1] = local[span - 1 :]


def recur(pre, rows, block_mats, span):
    held, bw = block_mats.shape[:2]
    spans, part = pre.shape[0] // (span + HALO), held * bw
    tokens = spans * span
    column = lambda h: (0, h)
    shapes = [((tokens, part), BF), ((tokens, 2 * part), F32), ((tokens, part), F32)]
    shapes += [((tokens, part), F32), ((2, spans, part), F32)]
    return pl.pallas_call(
        functools.partial(recur_kernel, span),
        grid=(held,),
        in_specs=[
            pl.BlockSpec((pre.shape[0], bw), lambda h: (0, held + h)),
            pl.BlockSpec((8, bw), column),
            pl.BlockSpec((1, bw, 2 * bw), lambda h: (h, 0, 0)),
        ],
        out_specs=[
            pl.BlockSpec((tokens, bw), column),
            pl.BlockSpec((tokens, 2 * bw), column),
            pl.BlockSpec((tokens, bw), column),
            pl.BlockSpec((tokens, bw), column),
            pl.BlockSpec((2, spans, bw), lambda h: (0, 0, h)),
        ],
        out_shape=[jax.ShapeDtypeStruct(*shape) for shape in shapes],
        compiler_params=pltpu.CompilerParams(vmem_limit_bytes=GRANT),
    )(pre, rows, block_mats)


def recur_mix_kernel(span, pre, rows, state, prod, start, mix):
    for i in range(state.shape[0] // span):
        here = pl.ds(i * span, span)
        act, _ = gelu_pair(pre[pl.ds(i * (span + HALO) + HALO, span)])
        states = state[here] + prod[here] * start[i : i + 1]
        mix[here] = (states * act * rows[6:7]).astype(BF)


def recur_mix(pre, rows, state, prod, start, bw, span):
    tokens, part = state.shape
    column = lambda h: (0, h)
    return pl.pallas_call(
        functools.partial(recur_mix_kernel, span),
        grid=(part // bw,),
        in_specs=[
            pl.BlockSpec((pre.shape[0], bw), column),
            pl.BlockSpec((8, bw), column),
            pl.BlockSpec((tokens, bw), column),
            pl.BlockSpec((tokens, bw), column),
            pl.BlockSpec((start.shape[0], bw), column),
        ],
        out_specs=pl.BlockSpec((tokens, bw), column),
        out_shape=jax.ShapeDtypeStruct((tokens, part), BF),
        compiler_params=pltpu.CompilerParams(vmem_limit_bytes=GRANT),
    )(pre, rows, state, prod, start)


def recur_back_kernel(span, back, pre, rows, state, prod, start, gate, gelu, local, prods, sums):
    soft = rows[0:1]
    for i in range(back.shape[0] // span):
        here = pl.ds(i * span, span)
        act, slope = gelu_pair(pre[pl.ds(i * (span + HALO) + HALO, span)])
        states = state[here] + prod[here] * start[i : i + 1]
        gelu[here] = (back[here] * states * slope * rows[6:7]).astype(BF)
        _, _, decay, _, _ = gate_values(gate[here], soft)
        row = lax.broadcasted_iota(jnp.int32, decay.shape, 0)
        later = jnp.where(row < span - 1, pltpu.roll(decay, span - 1, 0), 1.0)
        later, adjoint = span_scan(later, back[here] * act, True)
        local[here] = adjoint
        prods[here] = later
        sums[i : i + 1] = decay[:1] * adjoint[:1]


def recur_back(back, pre, rows, state, prod, start, gate, bw, span):
    tokens, part = state.shape
    column = lambda h: (0, h)
    whole = pl.BlockSpec((tokens, bw), column)
    ends = pl.BlockSpec((start.shape[0], bw), column)
    return pl.pallas_call(
        functools.partial(recur_back_kernel, span),
        grid=(part // bw,),
        in_specs=[
            whole,
            pl.BlockSpec((pre.shape[0], bw), column),
            pl.BlockSpec((8, bw), column),
            whole,
            whole,
            ends,
            pl.BlockSpec((tokens, 2 * bw), column),
        ],
        out_specs=[whole, whole, whole, ends],
        out_shape=[
            jax.ShapeDtypeStruct((tokens, part), BF),
            jax.ShapeDtypeStruct((tokens, part), F32),
            jax.ShapeDtypeStruct((tokens, part), F32),
            jax.ShapeDtypeStruct(start.shape, F32),
        ],
        compiler_params=pltpu.CompilerParams(vmem_limit_bytes=GRANT),
    )(back, pre, rows, state, prod, start, gate)


def recur_grad_kernel(
    span, local, prods, carried, state, prod, start, gate, conv, pre, rows, block,
    blocks_out, lru_out, spill_out, rows_out, gate_grad, conv_grad,
):
    count = local.shape[0] // span
    soft, sig, own = rows[0:1], rows[1:2], rows[6:7]
    taps = [rows[k + 2 : k + 3] for k in range(4)]
    width = local.shape[1]
    add_up = lambda v: jnp.sum(v, axis=0, keepdims=True)
    decay_sum = jnp.zeros((1, width), F32)
    for i in range(count):
        here = pl.ds(i * span, span)
        adjoint = local[here] + prods[here] * carried[i : i + 1]
        states = state[here] + prod[here] * start[i : i + 1]
        row = lax.broadcasted_iota(jnp.int32, states.shape, 0)
        earlier = jnp.where(row >= 1, pltpu.roll(states, 1, 0), start[i : i + 1])
        rec_gate, in_gate, decay, square, root = gate_values(gate[here], soft)
        conv_vals = conv[here].astype(F32)
        drive = adjoint * conv_vals
        grad_log = adjoint * earlier * decay - drive * in_gate * square / root
        decay_sum = decay_sum + add_up(grad_log * rec_gate)
        gate_grad[here, :width] = (-RATE * soft * grad_log * rec_gate * (1.0 - rec_gate)).astype(BF)
        gate_grad[here, width:] = (drive * root * in_gate * (1.0 - in_gate)).astype(BF)
        conv_grad[here] = adjoint * root * in_gate
    blocks_out[...] = lax.dot_general(
        conv[...], gate_grad[...], (((0,), (0,)), ((), ())), preferred_element_type=F32
    )
    conv_grad[...] += dot_right_t(gate_grad[...], block[0])
    tap_sums = [jnp.zeros((1, width), F32) for _ in range(4)]
    for i in range(count):
        here = pl.ds(i * span, span)
        grad = conv_grad[here]
        vals = pre[pl.ds(i * (span + HALO), span + HALO)].astype(BF).astype(F32)
        wide = jnp.concatenate([jnp.zeros((HALO, width), F32), grad], axis=0)
        total = taps[0] * wide
        tap_sums[0] = tap_sums[0] + add_up(grad * vals[HALO:])
        for k in range(1, 4):
            total = total + taps[k] * pltpu.roll(wide, span + HALO - k, 0)
            tap_sums[k] = tap_sums[k] + add_up(grad * pltpu.roll(vals, k, 0)[HALO:])
        lru_out[here] = total[HALO:]
        spill_out[pl.ds(i * HALO, HALO)] = total[:HALO]
    rows_out[...] = jnp.zeros(rows_out.shape, F32)
    rows_out[0:1] = decay_sum * sig * own * RATE
    for k in range(4):
        rows_out[k + 1 : k + 2] = tap_sums[k] * own


def recur_grad(local, prods, carried, state, prod, start, gate, conv, pre, rows, block_mats, span):
    tokens, part = state.shape
    held, bw = block_mats.shape[:2]
    column = lambda h: (0, h)
    whole = pl.BlockSpec((tokens, bw), column)
    ends = pl.BlockSpec((start.shape[0], bw), column)
    return pl.pallas_call(
        functools.partial(recur_grad_kernel, span),
        grid=(held,),
        in_specs=[
            whole,
            whole,
            ends,
            whole,
            whole,
            ends,
            pl.BlockSpec((tokens, 2 * bw), column),
            whole,
            pl.BlockSpec((pre.shape[0], bw), lambda h: (0, held + h)),
            pl.BlockSpec((8, bw), column),
            pl.BlockSpec((1, bw, 2 * bw), lambda h: (h, 0, 0)),
        ],
        out_specs=[
            pl.BlockSpec((bw, 2 * bw), lambda h: (h, 0)),
            whole,
            pl.BlockSpec((start.shape[0] * HALO, bw), column),
            pl.BlockSpec((8, bw), column),
        ],
        out_shape=[
            jax.ShapeDtypeStruct((part, 2 * bw), F32),
            jax.ShapeDtypeStruct((tokens, part), F32),
            jax.ShapeDtypeStruct((start.shape[0] * HALO, part), F32),
            jax.ShapeDtypeStruct((8, part), F32),
        ],
        scratch_shapes=[pltpu.VMEM((tokens, 2 * bw), BF), pltpu.VMEM((tokens, bw), F32)],
        compiler_params=pltpu.CompilerParams(vmem_limit_bytes=GRANT),
    )(local, prods, carried, state, prod, start, gate, conv, pre, rows, block_mats)


def device(p, f=None, z=None, x=None, c=None):
    f, z = p.f if f is None else f, p.z if z is None else z
    x, c = p.x if x is None else x, p.c if c is None else c
    return (f, ((p.r * TP + z) * 2 + x) * 2 + c)


def copy_to(src, dst, sems, index, dev):
    return pltpu.make_async_remote_copy(
        src_ref=src,
        dst_ref=dst,
        send_sem=sems[0].at[index],
        recv_sem=sems[1].at[index],
        device_id=dev,
        device_id_type=MESH,
    )


def pairs(*shape):
    return [pltpu.SemaphoreType.DMA(shape), pltpu.SemaphoreType.DMA(shape)]


def greet(devices):
    barrier = pltpu.get_barrier_semaphore()
    for dev in devices:
        pl.semaphore_signal(barrier, inc=1, device_id=dev, device_id_type=MESH)
    pl.semaphore_wait(barrier, len(devices))


def by_rows(count, body, step=16):
    def turn(i, _):
        body(pl.ds(pl.multiple_of(i * step, step), step))
        return 0

    lax.fori_loop(0, count // step, turn, 0)


class Gather:
    def __init__(self, p, out, ups, downs):
        self.p, self.out, self.ups, self.downs = p, out, ups, downs
        self.up = device(p, z=jnp.minimum(p.z + 1, TP - 1))
        self.down = device(p, z=jnp.maximum(p.z - 1, 0))

    def begin(self, h, src):
        z = self.p.z

        @pl.when(z < TP - 1)
        def _():
            copy_to(src, self.out.at[z, h], self.ups, (0, h), self.up).start()

        @pl.when(z > 0)
        def _():
            copy_to(src, self.out.at[z, h], self.downs, (0, h), self.down).start()

    def step(self, k, h):
        z, out = self.p.z, self.out

        @pl.when(z >= k)
        def _():
            block = out.at[z - k, h]
            copy_to(block, block, self.ups, (k - 1, h), self.up).wait_recv()
            if k < TP - 1:

                @pl.when(z < TP - 1)
                def _():
                    copy_to(block, block, self.ups, (k, h), self.up).start()

        @pl.when(z <= TP - 1 - k)
        def _():
            block = out.at[z + k, h]
            copy_to(block, block, self.downs, (k - 1, h), self.down).wait_recv()
            if k < TP - 1:

                @pl.when(z > 0)
                def _():
                    copy_to(block, block, self.downs, (k, h), self.down).start()

    def close(self, halves):
        z, block = self.p.z, self.out.at[0, 0]
        for h in range(halves):
            for k in range(TP - 1):

                @pl.when((z >= k) & (z < TP - 1))
                def _():
                    copy_to(block, block, self.ups, (k, h), self.up).wait_send()

                @pl.when((z <= TP - 1 - k) & (z > 0))
                def _():
                    copy_to(block, block, self.downs, (k, h), self.down).wait_send()


class LineSum:
    def __init__(self, p, parts, scratch):
        self.p, self.parts = p, parts
        self.got_up, self.got_down, self.out_up, self.out_down = scratch[:4]
        self.ups, self.downs = scratch[4:6], scratch[6:8]
        self.halves, self.rows = parts.shape[1:3]
        self.up = device(p, z=jnp.minimum(p.z + 1, TP - 1))
        self.down = device(p, z=jnp.maximum(p.z - 1, 0))

    @staticmethod
    def scratch(parts):
        block = parts[1:]
        return [
            pltpu.VMEM((TP - 1,) + block, BF),
            pltpu.VMEM((TP - 1,) + block, BF),
            pltpu.VMEM((TP - 2,) + block, BF),
            pltpu.VMEM((TP - 2,) + block, BF),
            *pairs(TP - 1, parts[1]),
            *pairs(TP - 1, parts[1]),
        ]

    def clear(self):
        z = self.p.z

        @pl.when(z == 0)
        def _():
            for h in range(self.halves):
                by_rows(self.rows, lambda at: self.fill(self.got_up, h, at))

        @pl.when(z == TP - 1)
        def _():
            for h in range(self.halves):
                by_rows(self.rows, lambda at: self.fill(self.got_down, h, at))

    def fill(self, ref, h, at):
        ref[0, h, at] = jnp.zeros((at.size, ref.shape[-1]), BF)

    def one_way(self, k, h, place, block, got, out, sems, dev):
        @pl.when(place == 0)
        def _():
            copy_to(self.parts.at[block, h], got.at[k - 1, h], sems, (k - 1, h), dev).start()

        if k < TP - 1:

            @pl.when((place >= 1) & (place + k <= TP - 1))
            def _():
                copy_to(got.at[k, h], got.at[k, h], sems, (k, h), dev).wait_recv()

                def add(at):
                    total = self.parts[block, h, at].astype(F32) + got[k, h, at].astype(F32)
                    out[k - 1, h, at] = total.astype(BF)

                by_rows(self.rows, add)
                copy_to(out.at[k - 1, h], got.at[k - 1, h], sems, (k - 1, h), dev).start()

    def step(self, k, h):
        z = self.p.z
        block = jnp.minimum(z + k, TP - 1)
        self.one_way(k, h, z, block, self.got_up, self.out_up, self.ups, self.up)
        block = jnp.maximum(z - k, 0)
        self.one_way(k, h, TP - 1 - z, block, self.got_down, self.out_down, self.downs, self.down)

    def arrive(self, h):
        z = self.p.z

        @pl.when(z >= 1)
        def _():
            got = self.got_up.at[0, h]
            copy_to(got, got, self.ups, (0, h), self.up).wait_recv()

        @pl.when(z <= TP - 2)
        def _():
            got = self.got_down.at[0, h]
            copy_to(got, got, self.downs, (0, h), self.down).wait_recv()

    def total(self, h, at):
        total = self.parts[self.p.z, h, at].astype(F32) + self.got_up[0, h, at].astype(F32)
        return total + self.got_down[0, h, at].astype(F32)

    def close(self):
        z, got = self.p.z, self.got_up.at[0, 0]
        for h in range(self.halves):
            for k in range(1, TP):

                @pl.when(z + k <= TP - 1)
                def _():
                    copy_to(got, got, self.ups, (k - 1, h), self.up).wait_send()

                @pl.when(z - k >= 0)
                def _():
                    copy_to(got, got, self.downs, (k - 1, h), self.down).wait_send()


def greet_line(p, others=()):
    barrier = pltpu.get_barrier_semaphore()
    for dev in others:
        pl.semaphore_signal(barrier, inc=1, device_id=dev, device_id_type=MESH)

    @pl.when(p.z > 0)
    def _():
        pl.semaphore_signal(barrier, inc=1, device_id=device(p, z=p.z - 1), device_id_type=MESH)

    @pl.when(p.z < TP - 1)
    def _():
        pl.semaphore_signal(barrier, inc=1, device_id=device(p, z=p.z + 1), device_id_type=MESH)

    inner = (p.z > 0) & (p.z < TP - 1)

    @pl.when(inner)
    def _():
        pl.semaphore_wait(barrier, len(others) + 2)

    @pl.when(jnp.logical_not(inner))
    def _():
        pl.semaphore_wait(barrier, len(others) + 1)


def intake_kernel(
    mix_p, ffw_p, x_p, cot_p, mix_w, ffw_w, x_all, cot_all, zs, zr, xs, xr, fs, fr, gs, gr, cs, cr,
    us, ur, vs, vr, local,
):
    p = Place()
    pieces, wholes = (mix_p, ffw_p), (mix_w, ffw_w)
    zsem, xsem, fsem, gsem, csem = (zs, zr), (xs, xr), (fs, fr), (gs, gr), (cs, cr)
    to_x, to_f, to_c = device(p, x=1 - p.x), device(p, f=1 - p.f), device(p, c=1 - p.c)
    to_z = [device(p, z=(p.z + d) % TP) for d in range(TP)]
    greet(to_z[1:] + [to_x, to_f, to_c])
    started = []
    kinds = ((0, 0), (0, 1), (1, 0), (1, 1))

    def slot(m, kind, d, c=None):
        f, x = (p.f + kinds[kind][0]) % 2, (p.x + kinds[kind][1]) % 2
        return wholes[m].at[f, 0, (p.z - d) % TP, x, p.c if c is None else c]

    def send(src, dst, sems, index, dev):
        copy = copy_to(src, dst, sems, index, dev)
        copy.start()
        started.append(copy)

    def wait(ref, sems, index):
        copy_to(ref, ref, sems, index, to_x).wait_recv()

    def along_z(m, d):
        send(pieces[m].at[(p.z + d) % TP], slot(m, 0, 0), zsem, (m, d - 1), to_z[d])

    def spread(m, d):
        dst = slot(m, 0, d)
        src = dst if d > 0 else pieces[m].at[p.z]
        send(src, dst, xsem, (m, d), to_x)
        send(src, dst, fsem, (m, d), to_f)
        send(src, dst, csem, (m, 0, d), to_c)

    def take(m, d):
        wait(slot(m, 0, d), zsem, (m, d - 1))
        spread(m, d)

    def sides(m, d):
        ref = slot(m, 1, d)
        wait(ref, xsem, (m, d))
        if d % 2 == 0:
            send(ref, ref, gsem, (m, d), to_f)
        send(ref, ref, csem, (m, 1, d), to_c)
        ref = slot(m, 2, d)
        wait(ref, fsem, (m, d))
        if d % 2 == 1:
            send(ref, ref, gsem, (m, d), to_x)
        send(ref, ref, csem, (m, 2, d), to_c)

    def corner(m, d):
        ref = slot(m, 3, d)
        wait(ref, gsem, (m, d))
        send(ref, ref, csem, (m, 3, d), to_c)

    for d in (1, 3, 2):
        along_z(0, d)
    along_z(1, 1)
    stays = [
        pltpu.make_async_copy(pieces[m].at[p.z], slot(m, 0, 0), local.at[m]) for m in range(2)
    ]
    stays.append(pltpu.make_async_copy(x_p, x_all.at[p.z, 0], local.at[2]))
    stays.append(pltpu.make_async_copy(cot_p, cot_all.at[p.z, 0], local.at[3]))
    for copy in stays:
        copy.start()
    spread(0, 0)
    spread(1, 0)
    for d in (1, 3, 2):
        take(0, d)
    along_z(1, 3)
    sides(0, 0)
    take(1, 1)
    along_z(1, 2)
    sides(1, 0)
    for d in (1, 3, 2):
        sides(0, d)
    take(1, 3)
    lines = [Gather(p, x_all, (us.at[0], ur.at[0]), (vs.at[0], vr.at[0]))]
    lines.append(Gather(p, cot_all, (us.at[1], ur.at[1]), (vs.at[1], vr.at[1])))
    lines[0].begin(0, x_p)
    lines[1].begin(0, cot_p)
    for d in (0, 1, 3, 2):
        corner(0, d)
    corner(1, 0)
    take(1, 2)
    for line in lines:
        line.step(1, 0)
    sides(1, 1)
    for line in lines:
        line.step(2, 0)
    sides(1, 3)
    corner(1, 1)
    sides(1, 2)
    corner(1, 3)
    for line in lines:
        line.step(3, 0)
    corner(1, 2)
    for m in range(2):
        for kind in range(4):
            for d in range(TP):
                wait(slot(m, kind, d, 1 - p.c), csem, (m, kind, d))
    for copy in started:
        copy.wait_send()
    for line in lines:
        line.close(1)
    for copy in stays:
        copy.wait()


def intake(mix_p, ffw_p, x_p, cot_p, p):
    whole = lambda v: jax.ShapeDtypeStruct((p.fs, 1, TP, 2, 2) + v.shape[1:], BF)
    line = lambda v: jax.ShapeDtypeStruct((TP, 1) + v.shape, BF)
    mix_w, ffw_w, x_all, cot_all = pl.pallas_call(
        intake_kernel,
        in_specs=[ANY] * 4,
        out_specs=[ANY] * 4,
        out_shape=[whole(mix_p), whole(ffw_p), line(x_p), line(cot_p)],
        scratch_shapes=[
            *pairs(2, TP - 1),
            *pairs(2, TP),
            *pairs(2, TP),
            *pairs(2, TP),
            *pairs(2, 4, TP),
            *pairs(2, TP - 1, 1),
            *pairs(2, TP - 1, 1),
            pltpu.SemaphoreType.DMA((4,)),
        ],
        compiler_params=pltpu.CompilerParams(collective_id=0, has_side_effects=True),
    )(mix_p, ffw_p, x_p, cot_p)
    columns = lambda v: v.reshape(-1, v.shape[-1])
    return columns(mix_w), columns(ffw_w), x_all[:, 0], cot_all[:, 0]


def middle_kernel(parts, x_zero, gain, x_one, ffw_all, own, local, gu0, gu1, gd0, gd1, *scratch):
    p = Place()
    line = LineSum(p, parts, scratch)
    out = Gather(p, ffw_all, (gu0, gu1), (gd0, gd1))
    halves, rows = parts.shape[1:3]
    line.clear()
    greet_line(p)
    for k in range(TP - 1, 0, -1):
        for h in range(halves):
            line.step(k, h)
    stays = []
    for h in range(halves):
        line.arrive(h)

        def finish(at, h=h):
            value = x_zero[h, at].astype(F32) + line.total(h, at)
            x_one[h, at] = value
            own[h, at] = normed(value, gain[...]).astype(BF)

        by_rows(rows, finish)
        out.begin(h, own.at[h])
        stays.append(pltpu.make_async_copy(own.at[h], ffw_all.at[p.z, h], local.at[h]))
        stays[-1].start()
    for k in range(1, TP):
        for h in range(halves):
            out.step(k, h)
    line.close()
    out.close(halves)
    for copy in stays:
        copy.wait()


def middle(parts, x_zero, gain):
    shape = parts.shape
    return pl.pallas_call(
        middle_kernel,
        in_specs=[VMEM] * 3,
        out_specs=[VMEM, ANY],
        out_shape=[jax.ShapeDtypeStruct(shape[1:], F32), jax.ShapeDtypeStruct(shape, BF)],
        scratch_shapes=[
            pltpu.VMEM(shape[1:], BF),
            pltpu.SemaphoreType.DMA((shape[1],)),
            *pairs(TP - 1, shape[1]),
            *pairs(TP - 1, shape[1]),
            *LineSum.scratch(shape),
        ],
        compiler_params=pltpu.CompilerParams(
            collective_id=1, has_side_effects=True, vmem_limit_bytes=GRANT
        ),
    )(parts, x_zero, gain)


def norm_back(values, gain, grad):
    inv = lax.rsqrt(jnp.mean(values * values, axis=-1, keepdims=True) + EPS)
    unit = values * inv
    through = grad * gain
    inner = jnp.mean(through * unit, axis=-1, keepdims=True)
    return inv * (through - unit * inner), grad * unit


class Fold:
    def __init__(self, p, groups, total, scratch):
        self.groups, self.total = groups, total
        self.got, self.got_late, self.out = scratch[:3]
        self.early, self.late = scratch[3:5], scratch[5:7]
        self.to = (device(p, x=1 - p.x), device(p, f=1 - p.f))
        self.rows = groups[0].shape[1]

    @staticmethod
    def scratch(group):
        return [
            pltpu.VMEM((2,) + group, BF),
            pltpu.VMEM((2,) + group[1:], BF),
            pltpu.VMEM((2,) + group[1:], BF),
            *pairs(2, 2),
            *pairs(2),
        ]

    def first(self, way, block):
        src = self.groups[2 * way].at[block]
        return copy_to(src, self.got.at[way, block], self.early, (way, block), self.to[way])

    def second(self, way):
        return copy_to(
            self.out.at[way], self.got_late.at[way], self.late, (way,), self.to[1 - way]
        )

    def begin(self):
        for block in (1, 0):
            for way in range(2):
                self.first(way, block).start()

    def middle(self):
        for way in range(2):
            self.first(way, 1).wait_recv()

            def add(at, way=way):
                total = self.groups[2 * way + 1][1, at].astype(F32)
                self.out[way, at] = (total + self.got[way, 1, at].astype(F32)).astype(BF)

            by_rows(self.rows, add)
            self.second(way).start()

    def finish(self):
        for way in range(2):
            self.first(way, 0).wait_recv()
            self.second(way).wait_recv()

            def add(at, way=way):
                total = self.groups[2 * way + 1][0, at].astype(F32)
                total = total + self.got[way, 0, at].astype(F32)
                self.total[way, at] = (total + self.got_late[way, at].astype(F32)).astype(BF)

            by_rows(self.rows, add)
        for way in range(2):
            self.second(way).wait_send()
            for block in range(2):
                self.first(way, block).wait_send()


def turn_kernel(
    with_fold, parts, out_parts, x_one, cot, gain, h0, h1, h2, h3,
    mixed_out, grad_x_one, grad_gain, mix_all, total, own, local, gu0, gu1, gd0, gd1, *scratch
):
    p = Place()
    line, late = LineSum(p, parts, scratch[:8]), LineSum(p, out_parts, scratch[8:16])
    out = Gather(p, mix_all, (gu0, gu1), (gd0, gd1))
    halves, rows = parts.shape[1:3]
    line.clear()
    late.clear()
    fold = Fold(p, (h0, h1, h2, h3), total, scratch[16:])
    greet_line(p, fold.to if with_fold else ())
    if with_fold:
        fold.begin()
    for k in range(TP - 1, 0, -1):
        for h in range(halves):
            line.step(k, h)
    stays = []
    grad_gain[...] = jnp.zeros(grad_gain.shape, F32)
    for h in range(halves):
        line.arrive(h)

        def finish(at, h=h):
            grad, gains = norm_back(x_one[h, at], gain[...], line.total(h, at))
            grad = grad + cot[h, at].astype(F32)
            grad_x_one[h, at] = grad
            own[h, at] = grad.astype(BF)
            grad_gain[0:1] += jnp.sum(gains, axis=0, keepdims=True)

        by_rows(rows, finish)
        out.begin(h, own.at[h])
        stays.append(pltpu.make_async_copy(own.at[h], mix_all.at[p.z, h], local.at[h]))
        stays[-1].start()
    if with_fold:
        fold.middle()
    for k in range(1, TP):
        for h in range(halves):
            out.step(k, h)
        for h in range(halves):
            late.step(TP - k, h)
    for h in range(halves):
        late.arrive(h)

        def store(at, h=h):
            mixed_out[h, at] = (x_one[h, at] + late.total(h, at)).astype(BF)

        by_rows(rows, store)
    if with_fold:
        fold.finish()
    line.close()
    late.close()
    out.close(halves)
    for copy in stays:
        copy.wait()


def turn(parts, out_parts, x_one, cot, gain, groups):
    shape = parts.shape
    with_fold = groups is not None
    if groups is None:
        groups = [jnp.zeros((2, 16, 128), BF)] * 4
    group = groups[0].shape
    width = shape[-1]
    return pl.pallas_call(
        functools.partial(turn_kernel, with_fold),
        in_specs=[VMEM] * 5 + [ANY, VMEM, ANY, VMEM],
        out_specs=[VMEM, VMEM, VMEM, ANY, VMEM],
        out_shape=[
            jax.ShapeDtypeStruct(shape[1:], BF),
            jax.ShapeDtypeStruct(shape[1:], F32),
            jax.ShapeDtypeStruct((8, width), F32),
            jax.ShapeDtypeStruct(shape, BF),
            jax.ShapeDtypeStruct((2,) + group[1:], BF),
        ],
        scratch_shapes=[
            pltpu.VMEM(shape[1:], BF),
            pltpu.SemaphoreType.DMA((shape[1],)),
            *pairs(TP - 1, shape[1]),
            *pairs(TP - 1, shape[1]),
            *LineSum.scratch(shape),
            *LineSum.scratch(shape),
            *Fold.scratch(group),
        ],
        compiler_params=pltpu.CompilerParams(
            collective_id=2, has_side_effects=True, vmem_limit_bytes=GRANT
        ),
    )(parts, out_parts, x_one, cot, gain, *groups)


def final_kernel(
    parts, x_zero, gain, grad_x_one, vectors, ffw_total, h0, h1, h2, h3,
    grad_in, sums, ffw_out, mix_out, total, acc, got, vs, vr, zs, zr, local, *scratch
):
    p = Place()
    line = LineSum(p, parts, scratch[:8])
    fold = Fold(p, (h0, h1, h2, h3), total, scratch[8:])
    halves, rows = parts.shape[1:3]
    outs, half = (ffw_out, mix_out), TP // 2
    line.clear()
    to_z = [device(p, z=(p.z + d) % TP) for d in range(TP)]
    to_c = device(p, c=1 - p.c)
    greet(to_z[1:] + list(fold.to) + [to_c])
    partners = [to_c, fold.to[0], fold.to[1]] + [
        device(p, z=p.z + bit * (1 - 2 * (p.z // bit % 2))) for bit in (1, 2)
    ]
    started = []

    def block_of(z):
        count = ffw_out.shape[1]
        return pl.ds(pl.multiple_of(z % half * count, 16), count)

    def along_z(m, src, d):
        target = (p.z + d) % TP
        src = src.at[target // half, block_of(target)]
        copy = copy_to(src, outs[m].at[p.z], (zs, zr), (m, d - 1), to_z[d])
        copy.start()
        started.append(copy)

    def arrived(m, d):
        ref = outs[m].at[(p.z - d) % TP]
        copy_to(ref, ref, (zs, zr), (m, d - 1), to_z[1]).wait_recv()

    def vector(i):
        return copy_to(acc.at[i], got.at[i], (vs, vr), (i,), partners[i])

    acc[0] = vectors[...]
    vector(0).start()
    fold.begin()
    for d in (1, 3):
        along_z(0, ffw_total, d)
    stays = [
        pltpu.make_async_copy(
            ffw_total.at[p.z // half, block_of(p.z)], ffw_out.at[p.z], local.at[0]
        )
    ]
    stays[0].start()
    for k in range(TP - 1, 0, -1):
        for h in range(halves):
            line.step(k, h)
    along_z(0, ffw_total, 2)
    for i in range(5):
        vector(i).wait_recv()
        if i < 4:
            acc[i + 1] = acc[i] + got[i]
            vector(i + 1).start()
        else:
            sums[...] = acc[i] + got[i]
    fold.middle()
    for h in range(halves):
        line.arrive(h)

        def finish(at, h=h):
            grad, _ = norm_back(x_zero[h, at].astype(F32), gain[...], line.total(h, at))
            grad_in[h, at] = grad_x_one[h, at] + grad

        by_rows(rows, finish)
    fold.finish()
    for d in (1, 3, 2):
        along_z(1, total, d)
    stays.append(
        pltpu.make_async_copy(total.at[p.z // half, block_of(p.z)], mix_out.at[p.z], local.at[1])
    )
    stays[1].start()
    for m in range(2):
        for d in range(1, TP):
            arrived(m, d)
    for copy in started:
        copy.wait_send()
    for i in range(5):
        vector(i).wait_send()
    line.close()
    for copy in stays:
        copy.wait()


def final(parts, x_zero, gain, grad_x_one, vectors, ffw_total, groups):
    shape, group = parts.shape, groups[0].shape
    rows = group[1] // 2
    return pl.pallas_call(
        final_kernel,
        in_specs=[VMEM] * 5 + [ANY, ANY, VMEM, ANY, VMEM],
        out_specs=[VMEM, VMEM, ANY, ANY],
        out_shape=[
            jax.ShapeDtypeStruct(shape[1:], F32),
            jax.ShapeDtypeStruct(vectors.shape, F32),
            jax.ShapeDtypeStruct((TP, rows, ffw_total.shape[2]), BF),
            jax.ShapeDtypeStruct((TP, rows, group[2]), BF),
        ],
        scratch_shapes=[
            pltpu.VMEM(group, BF),
            pltpu.VMEM((5,) + vectors.shape, F32),
            pltpu.VMEM((5,) + vectors.shape, F32),
            *pairs(5),
            *pairs(2, TP - 1),
            pltpu.SemaphoreType.DMA((2,)),
            *LineSum.scratch(shape),
            *Fold.scratch(group),
        ],
        compiler_params=pltpu.CompilerParams(
            collective_id=3, has_side_effects=True, vmem_limit_bytes=GRANT
        ),
    )(parts, x_zero, gain, grad_x_one, vectors, ffw_total, *groups)


def geglu(gate_vals, up_vals):
    return jax.nn.gelu(gate_vals) * up_vals


def all_spans(value, p):
    by_q = everywhere(value, shift_q, p.q, NQ)
    by_r = everywhere(by_q, shift_r, p.r, p.rests)
    return jnp.swapaxes(by_r, 1, 2).reshape((-1,) + value.shape[1:])


def own_spans(spans, p):
    split = spans.reshape((p.rests, TP, NQ) + spans.shape[1:])
    return lax.dynamic_index_in_dim(at(split, p.r), p.q, 1, keepdims=False)


def on_device(
    inputs,
    cotangent,
    proj_gelu,
    proj_lru,
    gate_blocks,
    proj_out,
    ffw_gate,
    ffw_up,
    ffw_down,
    norm_mix,
    norm_ffw,
    decay_param,
    conv_taps,
):
    p = Place()
    micro, span, width = inputs.shape[0], inputs.shape[2], inputs.shape[3]
    lru_width = proj_gelu.shape[1]
    tap_count = conv_taps.shape[1]
    block_width = gate_blocks.shape[1] // 2
    heads = lru_width // block_width
    ffw_part = ffw_gate.shape[1] // TP
    rows = proj_gelu.shape[0]
    held = -(-heads // TP)
    first = [k * heads // TP for k in range(TP)]
    owned = [range(first[k], first[k + 1] if k + 1 < TP else heads) for k in range(TP)]
    part = held * block_width

    out_t, down_t = proj_out.T, ffw_down.T
    small = jnp.concatenate(
        [norm_mix[:, None], norm_ffw[:, None], decay_param[:, None], conv_taps], axis=1
    )
    small = jnp.pad(small, ((0, 0), (0, 128 - small.shape[1])))
    mix_pieces, ffw_pieces = [], []
    for k in range(TP):
        cols = slice(first[k] * block_width, first[k] * block_width + part)
        mix_pieces.append(
            jnp.concatenate(
                [proj_gelu[:, cols], proj_lru[:, cols], out_t[:, cols], gate_blocks, small], axis=1
            )
        )
        cols = slice(k * ffw_part, (k + 1) * ffw_part)
        ffw_pieces.append(
            jnp.concatenate([ffw_gate[:, cols], ffw_up[:, cols], down_t[:, cols]], axis=1)
        )
    mix_pieces, ffw_pieces = jnp.stack(mix_pieces), jnp.stack(ffw_pieces)
    x_rows, cot = inputs[:, 0], cotangent[:, 0]
    edge = lax.ppermute(
        x_rows[:, span - (tap_count - 1) :],
        "seq",
        [(i, i + 1) for i in range(lax.axis_size("seq") - 1)],
    )
    pad = jnp.zeros((micro, HALO - (tap_count - 1), width), BF)
    x_wide = jnp.concatenate([pad, edge, x_rows], axis=1)
    if p.rests == 1:
        mix_w, ffw_w, x_all, cot_all = intake(
            mix_pieces, ffw_pieces, x_wide.reshape(-1, width), cot.reshape(-1, width), p
        )
    else:
        mix_w, ffw_w = weights_in(mix_pieces, p), weights_in(ffw_pieces, p)
        x_all, cot_all = gather_z(x_wide, p), gather_z(cot, p)
    x_all = x_all.reshape(TP, micro, HALO + span, width)
    cot_all = cot_all.reshape(-1, width)

    gelu_lru_w = mix_w[:, : 2 * part]
    out_w = mix_w[:, 2 * part : 3 * part]
    blocks_w = mix_w[:, 3 * part : 3 * part + 2 * block_width]
    small_w = mix_w[:, 3 * part + 2 * block_width :].astype(F32).T
    mix_gain, ffw_gain = small_w[0:1], small_w[1:2]
    start = sum(jnp.where(p.z == k, first[k] * block_width, 0) for k in range(TP))
    feature = jnp.arange(part) + start
    low = sum(jnp.where(p.z == k, owned[k][0] * block_width, 0) for k in range(TP))
    high = sum(jnp.where(p.z == k, (owned[k][-1] + 1) * block_width, 0) for k in range(TP))
    is_own = ((feature >= low) & (feature < high)).astype(F32)[None]
    own_part = lax.dynamic_slice_in_dim(small_w[2 : 3 + tap_count], start, part, 1)
    decay_f = own_part[:1]
    rows_w = jnp.concatenate(
        [jax.nn.softplus(-decay_f), jax.nn.sigmoid(-decay_f), own_part[1:], is_own, 0 * is_own]
    )
    block_mats = lax.dynamic_slice_in_dim(blocks_w, start, part, 0).reshape(
        held, block_width, 2 * block_width
    )

    x_all_f = x_all.astype(F32)
    mixed_all = normed(x_all_f, mix_gain[0]).astype(BF)
    pre = dot_plain(mixed_all.reshape(-1, width), gelu_lru_w)
    mixed = mixed_all[:, :, HALO:].reshape(-1, width)
    conv, gate, state, prod, sums = recur(pre, rows_w, block_mats, span)
    ends = (TP, micro, part)
    sums = all_spans(jnp.stack([sums[0].reshape(ends), sums[1].reshape(ends)], axis=1), p)
    carry, carries = jnp.zeros_like(sums[0, 0]), []
    for k in range(sums.shape[0]):
        carries.append(carry)
        carry = sums[k, 0] * carry + sums[k, 1]
    state_in = own_spans(jnp.stack(carries), p).reshape(-1, part)
    mix_bf = recur_mix(pre, rows_w, state, prod, state_in, block_width, span)
    blocked = (TP, micro, span, width)
    out_parts = dot_right_t(mix_bf, out_w).astype(BF).reshape(blocked)
    x_one, ffw_bf = middle(out_parts, x_rows, ffw_gain)

    ffw_bf = ffw_bf.reshape(-1, width)
    gate_up_w, down_w = ffw_w[:, : 2 * ffw_part], ffw_w[:, 2 * ffw_part :]
    gate_up = dot_plain(ffw_bf, gate_up_w)
    gate_vals, up_vals = gate_up[:, :ffw_part], gate_up[:, ffw_part:]
    hidden_bf = geglu(gate_vals, up_vals).astype(BF)
    grad_hidden = dot_plain(cot_all, down_w)
    _, pull_back = jax.vjp(geglu, gate_vals, up_vals)
    grad_gate_up = jnp.concatenate(pull_back(grad_hidden), axis=1).astype(BF)
    ffw_parts = dot_right_t(hidden_bf, down_w).astype(BF).reshape(blocked)
    grad_in_parts = dot_right_t(grad_gate_up, gate_up_w).astype(BF).reshape(blocked)
    ffw_far, ffw_near = row_blocks(ffw_bf, p)
    cot_far, cot_near = row_blocks(cot_all, p)

    def ffw_term(ffw_rows, cot_rows):
        return jnp.concatenate(
            [dot_plain(ffw_rows, grad_gate_up), dot_plain(cot_rows, hidden_bf)], axis=1
        )

    def ffw_close(i, got):
        return (ffw_term(ffw_near[i], cot_near[i]) + got.astype(F32)).astype(BF)

    far = ffw_term(ffw_far, cot_far).astype(BF)
    if p.rests == 1:
        groups, ffw_grads = near_groups(far, ffw_close), None
    else:
        groups, ffw_grads = None, grads_out(far, ffw_close, p)
    mixed_out, grad_x_one, gain_rows, grad_mix, ffw_total = turn(
        grad_in_parts, ffw_parts, x_one, cot, ffw_gain, groups
    )
    grad_mix = grad_mix.reshape(-1, width)

    back_mix = dot_plain(grad_mix, out_w)
    grad_gelu_bf, local_back, prod_back, back_sums = recur_back(
        back_mix, pre, rows_w, state, prod, state_in, gate, block_width, span
    )
    back_sums = all_spans(back_sums.reshape(ends), p)
    carry, carries = jnp.zeros_like(sums[0, 0]), []
    for k in range(sums.shape[0] - 1, -1, -1):
        carries.append(carry)
        carry = sums[k, 0] * carry + back_sums[k]
    carried = own_spans(jnp.stack(carries[::-1]), p).reshape(-1, part)
    grad_blocks, grad_lru, spill, row_grads = recur_grad(
        local_back, prod_back, carried, state, prod, state_in, gate, conv, pre, rows_w, block_mats,
        span,
    )
    spill = spill.reshape(TP, micro, HALO, part)
    from_next = shift_q(spill, -1)
    last = jnp.zeros_like(spill[:1])
    if p.rests > 1:
        last = move(spill[:1], lambda r, z, q: (r - 1, z, NQ - 1) if q == 0 and r > 0 else None)
    from_next = jnp.where(
        p.q == NQ - 1, jnp.concatenate([from_next[1:], last], axis=0), from_next
    )
    grad_lru = grad_lru.reshape(TP, micro, span, part) + jnp.pad(
        from_next, ((0, 0), (0, 0), (span - HALO, 0), (0, 0))
    )
    grad_lru_bf = (grad_lru * is_own[0]).astype(BF).reshape(-1, part)
    grad_pair = jnp.concatenate([grad_gelu_bf, grad_lru_bf], axis=1)
    grad_mixed = dot_right_t(grad_pair, gelu_lru_w)
    x_rows_f = x_all_f[:, :, HALO:].reshape(-1, width)
    unit = x_rows_f * lax.rsqrt(jnp.mean(x_rows_f * x_rows_f, axis=-1, keepdims=True) + EPS)
    grad_mix_gain = jnp.sum(grad_mixed * unit, axis=0, keepdims=True)
    grad_mixed_parts = grad_mixed.astype(BF).reshape(blocked)

    blocks_all = lax.dynamic_update_slice_in_dim(
        jnp.zeros((lru_width, 2 * block_width), BF),
        (grad_blocks * is_own[0][:, None]).astype(BF),
        start,
        0,
    )
    blocks_far, blocks_near = row_blocks(blocks_all.T, p)
    mixed_far, mixed_near = row_blocks(mixed, p)
    back_far, back_near = row_blocks(grad_mix, p)

    def mixer_term(mixed_rows, back_rows, block_rows):
        return jnp.concatenate(
            [dot_plain(mixed_rows, grad_pair), dot_plain(back_rows, mix_bf), block_rows], axis=1
        )

    def mixer_close(i, got):
        own = mixer_term(mixed_near[i], back_near[i], blocks_near[i])
        return (own + got.astype(F32)).astype(BF)

    far = mixer_term(mixed_far, back_far, blocks_far).astype(BF)
    vectors = lax.dynamic_update_slice_in_dim(
        jnp.zeros((1 + tap_count, lru_width), F32), row_grads[: 1 + tap_count], start, 1
    )
    vectors = jnp.concatenate([grad_mix_gain, gain_rows[:1], vectors], axis=0)
    vectors = jnp.pad(vectors, ((0, -vectors.shape[0] % 8), (0, 0)))
    if p.rests == 1:
        grad_inputs, vectors, ffw_grads, mix_grads = final(
            grad_mixed_parts, x_rows, mix_gain, grad_x_one, vectors, ffw_total,
            near_groups(far, mixer_close),
        )
    else:
        mix_grads = grads_out(far, mixer_close, p)
        grad_mixed_own = scatter_z(grad_mixed_parts, p)
        grad_inputs = grad_x_one + norm_back(x_rows.astype(F32), mix_gain, grad_mixed_own)[0]
        for exchange in (swap_core, swap_x, swap_f):
            vectors = vectors + exchange(vectors)
        for bit in (1, 2):
            vectors = vectors + move(vectors, lambda r, z, q, bit=bit: (r, z ^ bit, q))
        total = vectors
        for d in range(1, p.rests):
            total = total + shift_r(vectors, d)
        vectors = total
    vectors = lax.dynamic_slice_in_dim(vectors, p.index * rows, rows, 1)

    def mix_columns(offset):
        picked = [
            mix_grads[k][
                :,
                offset + (owned[k][0] - first[k]) * block_width : offset
                + (owned[k][-1] + 1 - first[k]) * block_width,
            ]
            for k in range(TP)
        ]
        return jnp.concatenate(picked, axis=1).astype(F32)

    def ffw_columns(offset):
        picked = [ffw_grads[k][:, offset : offset + ffw_part] for k in range(TP)]
        return jnp.concatenate(picked, axis=1).astype(F32)

    shape = (micro, 1, span, width)
    return (
        mixed_out.reshape(shape),
        grad_inputs.reshape(shape),
        mix_columns(0),
        mix_columns(part),
        jnp.sum(mix_grads[:, :, 3 * part :].astype(F32), axis=0),
        mix_columns(2 * part).T,
        ffw_columns(0),
        ffw_columns(ffw_part),
        ffw_columns(2 * ffw_part).T,
        vectors[0],
        vectors[1],
        vectors[2],
        vectors[3 : 3 + tap_count].T,
    )


def solution(mesh):
    in_specs = (
        P(None, "fsdp", "seq", None),
        P(None, "fsdp", "seq", None),
        P(("fsdp", "seq"), None),
        P(("fsdp", "seq"), None),
        P(("fsdp", "seq"), None),
        P(None, ("fsdp", "seq")),
        P(("fsdp", "seq"), None),
        P(("fsdp", "seq"), None),
        P(None, ("fsdp", "seq")),
        P(("fsdp", "seq")),
        P(("fsdp", "seq")),
        P(("fsdp", "seq")),
        P(("fsdp", "seq"), None),
    )
    out_specs = (
        P(None, "fsdp", "seq", None),
        P(None, "fsdp", "seq", None),
        P(("fsdp", "seq"), None),
        P(("fsdp", "seq"), None),
        P(("fsdp", "seq"), None),
        P(None, ("fsdp", "seq")),
        P(("fsdp", "seq"), None),
        P(("fsdp", "seq"), None),
        P(None, ("fsdp", "seq")),
        P(("fsdp", "seq")),
        P(("fsdp", "seq")),
        P(("fsdp", "seq")),
        P(("fsdp", "seq"), None),
    )
    return jax.shard_map(
        on_device, mesh=mesh, in_specs=in_specs, out_specs=out_specs, check_vma=False
    )
```

```python
import functools

import jax
import jax.numpy as jnp
from jax import lax
from jax.experimental import pallas as pl
from jax.experimental.pallas import tpu as pltpu
from jax.sharding import PartitionSpec as P

EPS = 1e-06
GUARD = 0.001
RATE = 8.0
TP = 4
NQ = 4
HALO = 8
BF = jnp.bfloat16
F32 = jnp.float32
MESH = pl.DeviceIdType.MESH
ANY = pl.BlockSpec(memory_space=pl.ANY)
VMEM = pl.BlockSpec(memory_space=pltpu.VMEM)
GRANT = 60 * 1024 * 1024


def move(value, step):
    pairs = []
    for here in range(lax.axis_size("seq")):
        there = step(here // (TP * NQ), here // NQ % TP, here % NQ)
        if there is not None:
            pairs.append((here, (there[0] * TP + there[1]) * NQ + there[2]))
    return lax.ppermute(value, "seq", pairs)


def swap_core(value):
    return move(value, lambda r, z, q: (r, z, q ^ 1))


def swap_x(value):
    return move(value, lambda r, z, q: (r, z, q ^ 2))


def swap_f(value):
    return lax.ppermute(value, "fsdp", [(0, 1), (1, 0)])


def shift_z(value, d):
    return move(value, lambda r, z, q: (r, (z + d) % TP, q))


def shift_q(value, d):
    return move(value, lambda r, z, q: (r, z, (q + d) % NQ))


def shift_r(value, d):
    count = lax.axis_size("seq") // (TP * NQ)
    return move(value, lambda r, z, q: ((r + d) % count, z, q))


def hop(value, d, low, high):
    return move(value, lambda r, z, q: (r, z + d, q) if low <= z <= high else None)


class Place:
    def __init__(self):
        seq = lax.axis_index("seq")
        self.f = lax.axis_index("fsdp")
        self.r, self.z, self.q = seq // (TP * NQ), seq // NQ % TP, seq % NQ
        self.x, self.c = self.q // 2, self.q % 2
        self.rests = lax.axis_size("seq") // (TP * NQ)
        self.fs = lax.axis_size("fsdp")
        self.index = self.f * lax.axis_size("seq") + seq


def at(value, index):
    return lax.dynamic_index_in_dim(value, index, 0, keepdims=False)


def put(base, value, *index):
    starts = [jnp.int32(0) if i is None else jnp.int32(i) for i in index]
    starts += [jnp.int32(0)] * (base.ndim - len(index))
    for dim, i in enumerate(index):
        if i is not None:
            value = jnp.expand_dims(value, dim)
    return lax.dynamic_update_slice(base, value, starts)


def everywhere(value, shifter, mine, count):
    out = put(jnp.zeros((count,) + value.shape, value.dtype), value, mine)
    for d in range(1, count):
        out = put(out, shifter(value, d), (mine - d) % count)
    return out


def gather_z(value, p):
    ups, downs = [], []
    up = down = value
    for k in range(1, TP):
        up = hop(up, 1, k - 1, TP - 2)
        down = hop(down, -1, 1, TP - k)
        ups.append(up)
        downs.append(down)
    out = put(jnp.zeros((TP,) + value.shape, value.dtype), value, p.z)
    for k in range(1, TP):
        out = put(out, downs[k - 1] + ups[TP - 1 - k], (p.z + k) % TP)
    return out


def scatter_z(parts, p):
    right = left = None
    for k in range(TP - 1, 0, -1):
        send = at(parts, (p.z + k) % TP)
        if right is not None:
            send = (send.astype(F32) + right.astype(F32)).astype(BF)
        right = hop(send, 1, 0, TP - 1 - k)
        send = at(parts, (p.z - k) % TP)
        if left is not None:
            send = (send.astype(F32) + left.astype(F32)).astype(BF)
        left = hop(send, -1, k, TP - 1)
    return at(parts, p.z).astype(F32) + right.astype(F32) + left.astype(F32)


def weights_in(pieces, p):
    rows, cols = pieces.shape[1:]
    mine = put(jnp.zeros(pieces.shape, BF), at(pieces, p.z), p.z)
    for d in range(1, TP):
        mine = put(mine, shift_z(at(pieces, (p.z + d) % TP), d), (p.z - d) % TP)
    mine = everywhere(mine, shift_r, p.r, p.rests)
    half = TP // 2
    by_x, by_f = swap_x(mine), swap_f(mine)
    corner = (swap_f(by_x[:, :half]), swap_x(by_f[:, half:]))
    whole = jnp.zeros((p.fs, p.rests, TP, 2, 2, rows, cols), BF)
    for block, f, x, z in (
        (mine, p.f, p.x, 0),
        (by_x, p.f, 1 - p.x, 0),
        (by_f, 1 - p.f, p.x, 0),
        (corner[0], 1 - p.f, 1 - p.x, 0),
        (corner[1], 1 - p.f, 1 - p.x, half),
    ):
        other = swap_core(block)
        for part, c in ((block, p.c), (other, 1 - p.c)):
            part = part[None, :, :, None, None]
            whole = lax.dynamic_update_slice(
                whole, part, [jnp.int32(i) for i in (f, 0, z, x, c, 0, 0)]
            )
    return whole.reshape(-1, cols)


def by_owner(grad, p):
    return grad.reshape(p.fs, p.rests, TP, 2, 2, -1, grad.shape[1])


def to_owner_z(total, p):
    out = put(jnp.zeros(total.shape, BF), at(total, p.z), p.z)
    for d in (1, 3, 2):
        out = put(out, shift_z(at(total, (p.z + d) % TP), d), (p.z - d) % TP)
    return out


def grads_out(grad, p):
    plus = lambda a, b: (a.astype(F32) + b.astype(F32)).astype(BF)
    pick = lambda v, dim, i: lax.dynamic_index_in_dim(v, i, dim, keepdims=False)
    total = by_owner(grad, p)
    total = plus(pick(total, 4, p.c), swap_core(pick(total, 4, 1 - p.c)))
    total = plus(pick(total, 3, p.x), swap_x(pick(total, 3, 1 - p.x)))
    total = plus(at(total, p.f), swap_f(at(total, 1 - p.f)))
    mine = at(total, p.r)
    for d in range(1, p.rests):
        mine = plus(mine, shift_r(at(total, (p.r + d) % p.rests), d))
    return to_owner_z(mine, p)


def dot_left_t(left_mat, right_mat):
    return lax.dot_general(
        left_mat, right_mat, (((0,), (0,)), ((), ())), preferred_element_type=F32
    )


def dot_plain(left_mat, right_mat):
    return jnp.dot(left_mat, right_mat, preferred_element_type=F32)


def dot_right_t(left_mat, right_mat):
    return lax.dot_general(
        left_mat, right_mat, (((1,), (1,)), ((), ())), preferred_element_type=F32
    )


def normed(values, gain_vec):
    return values * lax.rsqrt(jnp.mean(values * values, axis=-1, keepdims=True) + EPS) * gain_vec


def gelu_pair(v):
    scale = 0.7978845608028654
    inner = jnp.tanh(scale * (v + 0.044715 * v * v * v))
    slope = 0.5 * v * (1.0 - inner * inner) * scale * (1.0 + 0.134145 * v * v)
    return 0.5 * v * (1.0 + inner), 0.5 * (1.0 + inner) + slope


def span_scan(decay, drive, backward):
    count = decay.shape[0]
    row = lax.broadcasted_iota(jnp.int32, decay.shape, 0)
    step = 1
    while step < count:
        inside = row < count - step if backward else row >= step
        turn = count - step if backward else step
        drive = drive + jnp.where(inside, decay * pltpu.roll(drive, turn, 0), 0.0)
        decay = decay * jnp.where(inside, pltpu.roll(decay, turn, 0), 1.0)
        step *= 2
    return decay, drive


def gate_values(gate, soft):
    half = gate.shape[1] // 2
    rec_gate = jax.nn.sigmoid(gate[:, :half])
    in_gate = jax.nn.sigmoid(gate[:, half:])
    log_decay = -RATE * rec_gate * soft
    square = jnp.exp(2.0 * log_decay)
    return rec_gate, in_gate, jnp.exp(log_decay), square, jnp.sqrt(1.0 - square + GUARD)


def recur_kernel(span, pre, rows, block, conv, gate, state, prod, sums):
    count = conv.shape[0] // span
    soft, taps = rows[0:1], [rows[k + 2 : k + 3] for k in range(4)]

    def convolve(i, _):
        start = pl.multiple_of(i * (span + HALO), 8)
        vals = pre[pl.ds(start, span + HALO)].astype(BF).astype(F32)
        total = taps[0] * vals
        for k in range(1, 4):
            total = total + taps[k] * pltpu.roll(vals, k, 0)
        conv[pl.ds(pl.multiple_of(i * span, 16), span)] = total[HALO:].astype(BF)
        return 0

    lax.fori_loop(0, count, convolve, 0)
    gate[...] = dot_plain(conv[...], block[0])
    for i in range(count):
        here = pl.ds(i * span, span)
        _, in_gate, decay, _, root = gate_values(gate[here], soft)
        decay, local = span_scan(decay, root * in_gate * conv[here].astype(F32), False)
        state[here] = local
        prod[here] = decay
        sums[0, i : i + 1] = decay[span - 1 :]
        sums[1, i : i + 1] = local[span - 1 :]


def recur(pre, rows, block_mats, span):
    held, bw = block_mats.shape[:2]
    spans, part = pre.shape[0] // (span + HALO), held * bw
    tokens = spans * span
    column = lambda h: (0, h)
    shapes = [((tokens, part), BF), ((tokens, 2 * part), F32), ((tokens, part), F32)]
    shapes += [((tokens, part), F32), ((2, spans, part), F32)]
    return pl.pallas_call(
        functools.partial(recur_kernel, span),
        grid=(held,),
        in_specs=[
            pl.BlockSpec((pre.shape[0], bw), lambda h: (0, held + h)),
            pl.BlockSpec((8, bw), column),
            pl.BlockSpec((1, bw, 2 * bw), lambda h: (h, 0, 0)),
        ],
        out_specs=[
            pl.BlockSpec((tokens, bw), column),
            pl.BlockSpec((tokens, 2 * bw), column),
            pl.BlockSpec((tokens, bw), column),
            pl.BlockSpec((tokens, bw), column),
            pl.BlockSpec((2, spans, bw), lambda h: (0, 0, h)),
        ],
        out_shape=[jax.ShapeDtypeStruct(*shape) for shape in shapes],
        compiler_params=pltpu.CompilerParams(vmem_limit_bytes=GRANT),
    )(pre, rows, block_mats)


def recur_mix_kernel(span, pre, rows, state, prod, start, mix):
    for i in range(state.shape[0] // span):
        here = pl.ds(i * span, span)
        act, _ = gelu_pair(pre[pl.ds(i * (span + HALO) + HALO, span)])
        states = state[here] + prod[here] * start[i : i + 1]
        mix[here] = (states * act * rows[6:7]).astype(BF)


def recur_mix(pre, rows, state, prod, start, bw, span):
    tokens, part = state.shape
    column = lambda h: (0, h)
    return pl.pallas_call(
        functools.partial(recur_mix_kernel, span),
        grid=(part // bw,),
        in_specs=[
            pl.BlockSpec((pre.shape[0], bw), column),
            pl.BlockSpec((8, bw), column),
            pl.BlockSpec((tokens, bw), column),
            pl.BlockSpec((tokens, bw), column),
            pl.BlockSpec((start.shape[0], bw), column),
        ],
        out_specs=pl.BlockSpec((tokens, bw), column),
        out_shape=jax.ShapeDtypeStruct((tokens, part), BF),
        compiler_params=pltpu.CompilerParams(vmem_limit_bytes=GRANT),
    )(pre, rows, state, prod, start)


def recur_back_kernel(span, back, pre, rows, state, prod, start, gate, gelu, local, prods, sums):
    soft = rows[0:1]
    for i in range(back.shape[0] // span):
        here = pl.ds(i * span, span)
        act, slope = gelu_pair(pre[pl.ds(i * (span + HALO) + HALO, span)])
        states = state[here] + prod[here] * start[i : i + 1]
        gelu[here] = (back[here] * states * slope * rows[6:7]).astype(BF)
        _, _, decay, _, _ = gate_values(gate[here], soft)
        row = lax.broadcasted_iota(jnp.int32, decay.shape, 0)
        later = jnp.where(row < span - 1, pltpu.roll(decay, span - 1, 0), 1.0)
        later, adjoint = span_scan(later, back[here] * act, True)
        local[here] = adjoint
        prods[here] = later
        sums[i : i + 1] = decay[:1] * adjoint[:1]


def recur_back(back, pre, rows, state, prod, start, gate, bw, span):
    tokens, part = state.shape
    column = lambda h: (0, h)
    whole = pl.BlockSpec((tokens, bw), column)
    ends = pl.BlockSpec((start.shape[0], bw), column)
    return pl.pallas_call(
        functools.partial(recur_back_kernel, span),
        grid=(part // bw,),
        in_specs=[
            whole,
            pl.BlockSpec((pre.shape[0], bw), column),
            pl.BlockSpec((8, bw), column),
            whole,
            whole,
            ends,
            pl.BlockSpec((tokens, 2 * bw), column),
        ],
        out_specs=[whole, whole, whole, ends],
        out_shape=[
            jax.ShapeDtypeStruct((tokens, part), BF),
            jax.ShapeDtypeStruct((tokens, part), F32),
            jax.ShapeDtypeStruct((tokens, part), F32),
            jax.ShapeDtypeStruct(start.shape, F32),
        ],
        compiler_params=pltpu.CompilerParams(vmem_limit_bytes=GRANT),
    )(back, pre, rows, state, prod, start, gate)


def recur_grad_kernel(
    span, local, prods, carried, state, prod, start, gate, conv, pre, rows, block,
    blocks_out, lru_out, spill_out, rows_out, gate_grad, conv_grad,
):
    count = local.shape[0] // span
    soft, sig, own = rows[0:1], rows[1:2], rows[6:7]
    taps = [rows[k + 2 : k + 3] for k in range(4)]
    width = local.shape[1]
    add_up = lambda v: jnp.sum(v, axis=0, keepdims=True)
    decay_sum = jnp.zeros((1, width), F32)
    for i in range(count):
        here = pl.ds(i * span, span)
        adjoint = local[here] + prods[here] * carried[i : i + 1]
        states = state[here] + prod[here] * start[i : i + 1]
        row = lax.broadcasted_iota(jnp.int32, states.shape, 0)
        earlier = jnp.where(row >= 1, pltpu.roll(states, 1, 0), start[i : i + 1])
        rec_gate, in_gate, decay, square, root = gate_values(gate[here], soft)
        conv_vals = conv[here].astype(F32)
        drive = adjoint * conv_vals
        grad_log = adjoint * earlier * decay - drive * in_gate * square / root
        decay_sum = decay_sum + add_up(grad_log * rec_gate)
        gate_grad[here, :width] = (-RATE * soft * grad_log * rec_gate * (1.0 - rec_gate)).astype(BF)
        gate_grad[here, width:] = (drive * root * in_gate * (1.0 - in_gate)).astype(BF)
        conv_grad[here] = adjoint * root * in_gate
    blocks_out[...] = lax.dot_general(
        conv[...], gate_grad[...], (((0,), (0,)), ((), ())), preferred_element_type=F32
    )
    conv_grad[...] += dot_right_t(gate_grad[...], block[0])
    tap_sums = [jnp.zeros((1, width), F32) for _ in range(4)]
    for i in range(count):
        here = pl.ds(i * span, span)
        grad = conv_grad[here]
        vals = pre[pl.ds(i * (span + HALO), span + HALO)].astype(BF).astype(F32)
        wide = jnp.concatenate([jnp.zeros((HALO, width), F32), grad], axis=0)
        total = taps[0] * wide
        tap_sums[0] = tap_sums[0] + add_up(grad * vals[HALO:])
        for k in range(1, 4):
            total = total + taps[k] * pltpu.roll(wide, span + HALO - k, 0)
            tap_sums[k] = tap_sums[k] + add_up(grad * pltpu.roll(vals, k, 0)[HALO:])
        lru_out[here] = total[HALO:]
        spill_out[pl.ds(i * HALO, HALO)] = total[:HALO]
    rows_out[...] = jnp.zeros(rows_out.shape, F32)
    rows_out[0:1] = decay_sum * sig * own * RATE
    for k in range(4):
        rows_out[k + 1 : k + 2] = tap_sums[k] * own


def recur_grad(local, prods, carried, state, prod, start, gate, conv, pre, rows, block_mats, span):
    tokens, part = state.shape
    held, bw = block_mats.shape[:2]
    column = lambda h: (0, h)
    whole = pl.BlockSpec((tokens, bw), column)
    ends = pl.BlockSpec((start.shape[0], bw), column)
    return pl.pallas_call(
        functools.partial(recur_grad_kernel, span),
        grid=(held,),
        in_specs=[
            whole,
            whole,
            ends,
            whole,
            whole,
            ends,
            pl.BlockSpec((tokens, 2 * bw), column),
            whole,
            pl.BlockSpec((pre.shape[0], bw), lambda h: (0, held + h)),
            pl.BlockSpec((8, bw), column),
            pl.BlockSpec((1, bw, 2 * bw), lambda h: (h, 0, 0)),
        ],
        out_specs=[
            pl.BlockSpec((bw, 2 * bw), lambda h: (h, 0)),
            whole,
            pl.BlockSpec((start.shape[0] * HALO, bw), column),
            pl.BlockSpec((8, bw), column),
        ],
        out_shape=[
            jax.ShapeDtypeStruct((part, 2 * bw), F32),
            jax.ShapeDtypeStruct((tokens, part), F32),
            jax.ShapeDtypeStruct((start.shape[0] * HALO, part), F32),
            jax.ShapeDtypeStruct((8, part), F32),
        ],
        scratch_shapes=[pltpu.VMEM((tokens, 2 * bw), BF), pltpu.VMEM((tokens, bw), F32)],
        compiler_params=pltpu.CompilerParams(vmem_limit_bytes=GRANT),
    )(local, prods, carried, state, prod, start, gate, conv, pre, rows, block_mats)


def device(p, f=None, z=None, x=None, c=None):
    f, z = p.f if f is None else f, p.z if z is None else z
    x, c = p.x if x is None else x, p.c if c is None else c
    return (f, ((p.r * TP + z) * 2 + x) * 2 + c)


def copy_to(src, dst, sems, index, dev):
    return pltpu.make_async_remote_copy(
        src_ref=src,
        dst_ref=dst,
        send_sem=sems[0].at[index],
        recv_sem=sems[1].at[index],
        device_id=dev,
        device_id_type=MESH,
    )


def pairs(*shape):
    return [pltpu.SemaphoreType.DMA(shape), pltpu.SemaphoreType.DMA(shape)]


def greet(devices):
    barrier = pltpu.get_barrier_semaphore()
    for dev in devices:
        pl.semaphore_signal(barrier, inc=1, device_id=dev, device_id_type=MESH)
    pl.semaphore_wait(barrier, len(devices))


def by_rows(count, body, step=16):
    def turn(i, _):
        body(pl.ds(pl.multiple_of(i * step, step), step))
        return 0

    assert count % step == 0
    lax.fori_loop(0, count // step, turn, 0)


class Gather:
    def __init__(self, p, out, ups, downs):
        self.p, self.out, self.ups, self.downs = p, out, ups, downs
        self.up = device(p, z=jnp.minimum(p.z + 1, TP - 1))
        self.down = device(p, z=jnp.maximum(p.z - 1, 0))

    def begin(self, h, src):
        z = self.p.z

        @pl.when(z < TP - 1)
        def _():
            copy_to(src, self.out.at[z, h], self.ups, (0, h), self.up).start()

        @pl.when(z > 0)
        def _():
            copy_to(src, self.out.at[z, h], self.downs, (0, h), self.down).start()

    def step(self, k, h):
        z, out = self.p.z, self.out

        @pl.when(z >= k)
        def _():
            block = out.at[z - k, h]
            copy_to(block, block, self.ups, (k - 1, h), self.up).wait_recv()
            if k < TP - 1:

                @pl.when(z < TP - 1)
                def _():
                    copy_to(block, block, self.ups, (k, h), self.up).start()

        @pl.when(z <= TP - 1 - k)
        def _():
            block = out.at[z + k, h]
            copy_to(block, block, self.downs, (k - 1, h), self.down).wait_recv()
            if k < TP - 1:

                @pl.when(z > 0)
                def _():
                    copy_to(block, block, self.downs, (k, h), self.down).start()

    def close(self, halves):
        z, block = self.p.z, self.out.at[0, 0]
        for h in range(halves):
            for k in range(TP - 1):

                @pl.when((z >= k) & (z < TP - 1))
                def _():
                    copy_to(block, block, self.ups, (k, h), self.up).wait_send()

                @pl.when((z <= TP - 1 - k) & (z > 0))
                def _():
                    copy_to(block, block, self.downs, (k, h), self.down).wait_send()


class LineSum:
    def __init__(self, p, parts, scratch):
        self.p, self.parts = p, parts
        self.got_up, self.got_down, self.out_up, self.out_down = scratch[:4]
        self.ups, self.downs = scratch[4:6], scratch[6:8]
        self.halves, self.rows = parts.shape[1:3]
        self.up = device(p, z=jnp.minimum(p.z + 1, TP - 1))
        self.down = device(p, z=jnp.maximum(p.z - 1, 0))

    @staticmethod
    def scratch(parts):
        block = parts[1:]
        return [
            pltpu.VMEM((TP - 1,) + block, BF),
            pltpu.VMEM((TP - 1,) + block, BF),
            pltpu.VMEM((TP - 2,) + block, BF),
            pltpu.VMEM((TP - 2,) + block, BF),
            *pairs(TP - 1, parts[1]),
            *pairs(TP - 1, parts[1]),
        ]

    def clear(self):
        z = self.p.z

        @pl.when(z == 0)
        def _():
            for h in range(self.halves):
                by_rows(self.rows, lambda at: self.fill(self.got_up, h, at))

        @pl.when(z == TP - 1)
        def _():
            for h in range(self.halves):
                by_rows(self.rows, lambda at: self.fill(self.got_down, h, at))

    def fill(self, ref, h, at):
        ref[0, h, at] = jnp.zeros((at.size, ref.shape[-1]), BF)

    def one_way(self, k, h, place, block, got, out, sems, dev):
        @pl.when(place == 0)
        def _():
            copy_to(self.parts.at[block, h], got.at[k - 1, h], sems, (k - 1, h), dev).start()

        if k < TP - 1:

            @pl.when((place >= 1) & (place + k <= TP - 1))
            def _():
                copy_to(got.at[k, h], got.at[k, h], sems, (k, h), dev).wait_recv()

                def add(at):
                    total = self.parts[block, h, at].astype(F32) + got[k, h, at].astype(F32)
                    out[k - 1, h, at] = total.astype(BF)

                by_rows(self.rows, add)
                copy_to(out.at[k - 1, h], got.at[k - 1, h], sems, (k - 1, h), dev).start()

    def step(self, k, h):
        z = self.p.z
        block = jnp.minimum(z + k, TP - 1)
        self.one_way(k, h, z, block, self.got_up, self.out_up, self.ups, self.up)
        block = jnp.maximum(z - k, 0)
        self.one_way(k, h, TP - 1 - z, block, self.got_down, self.out_down, self.downs, self.down)

    def arrive(self, h):
        z = self.p.z

        @pl.when(z >= 1)
        def _():
            got = self.got_up.at[0, h]
            copy_to(got, got, self.ups, (0, h), self.up).wait_recv()

        @pl.when(z <= TP - 2)
        def _():
            got = self.got_down.at[0, h]
            copy_to(got, got, self.downs, (0, h), self.down).wait_recv()

    def total(self, h, at):
        total = self.parts[self.p.z, h, at].astype(F32) + self.got_up[0, h, at].astype(F32)
        return total + self.got_down[0, h, at].astype(F32)

    def close(self):
        z, got = self.p.z, self.got_up.at[0, 0]
        for h in range(self.halves):
            for k in range(1, TP):

                @pl.when(z + k <= TP - 1)
                def _():
                    copy_to(got, got, self.ups, (k - 1, h), self.up).wait_send()

                @pl.when(z - k >= 0)
                def _():
                    copy_to(got, got, self.downs, (k - 1, h), self.down).wait_send()


def greet_line(p, others=()):
    barrier = pltpu.get_barrier_semaphore()
    for dev in others:
        pl.semaphore_signal(barrier, inc=1, device_id=dev, device_id_type=MESH)

    @pl.when(p.z > 0)
    def _():
        pl.semaphore_signal(barrier, inc=1, device_id=device(p, z=p.z - 1), device_id_type=MESH)

    @pl.when(p.z < TP - 1)
    def _():
        pl.semaphore_signal(barrier, inc=1, device_id=device(p, z=p.z + 1), device_id_type=MESH)

    inner = (p.z > 0) & (p.z < TP - 1)

    @pl.when(inner)
    def _():
        pl.semaphore_wait(barrier, len(others) + 2)

    @pl.when(jnp.logical_not(inner))
    def _():
        pl.semaphore_wait(barrier, len(others) + 1)


class Spread:
    KINDS = ((0, 0), (0, 1), (1, 0), (1, 1))

    def __init__(self, p, whole, sems):
        self.p, self.whole, self.started = p, whole, []
        self.xs, self.fs, self.gs, self.cs = sems[0:2], sems[2:4], sems[4:6], sems[6:8]
        self.to_x, self.to_f = device(p, x=1 - p.x), device(p, f=1 - p.f)
        self.to_c = device(p, c=1 - p.c)

    @staticmethod
    def scratch():
        return [*pairs(TP), *pairs(TP), *pairs(TP), *pairs(4, TP)]

    def slot(self, kind, d, other_core=False):
        p, (f, x) = self.p, self.KINDS[kind]
        c = 1 - p.c if other_core else p.c
        return self.whole.at[(p.f + f) % 2, 0, (p.z - d) % TP, (p.x + x) % 2, c]

    def send(self, src, dst, sems, index, dev):
        copy = copy_to(src, dst, sems, index, dev)
        copy.start()
        self.started.append(copy)

    def wait(self, ref, sems, index):
        copy_to(ref, ref, sems, index, self.to_x).wait_recv()

    def spread(self, d, src=None):
        dst = self.slot(0, d)
        src = dst if src is None else src
        self.send(src, dst, self.xs, (d,), self.to_x)
        self.send(src, dst, self.fs, (d,), self.to_f)
        self.send(src, dst, self.cs, (0, d), self.to_c)

    def sides(self, d):
        ref = self.slot(1, d)
        self.wait(ref, self.xs, (d,))
        if d % 2 == 0:
            self.send(ref, ref, self.gs, (d,), self.to_f)
        self.send(ref, ref, self.cs, (1, d), self.to_c)
        ref = self.slot(2, d)
        self.wait(ref, self.fs, (d,))
        if d % 2 == 1:
            self.send(ref, ref, self.gs, (d,), self.to_x)
        self.send(ref, ref, self.cs, (2, d), self.to_c)

    def corner(self, d):
        ref = self.slot(3, d)
        self.wait(ref, self.gs, (d,))
        self.send(ref, ref, self.cs, (3, d), self.to_c)

    def close(self, pieces):
        for kind in range(4):
            for d in pieces:
                self.wait(self.slot(kind, d, True), self.cs, (kind, d))
        for copy in self.started:
            copy.wait_send()


def intake_kernel(mix_p, ffw_p, x_p, mix_w, ffw_w, x_all, zs, zr, us, ur, vs, vr, local, *sems):
    p = Place()
    pieces, wholes = (mix_p, ffw_p), (mix_w, ffw_w)
    mix, ffw = Spread(p, mix_w, sems[:8]), Spread(p, ffw_w, sems[8:])
    to_z = [device(p, z=(p.z + d) % TP) for d in range(TP)]
    greet(to_z[1:] + [mix.to_x, mix.to_f, mix.to_c])
    started = []

    def along_z(m, d):
        src, dst = pieces[m].at[(p.z + d) % TP], (mix, ffw)[m].slot(0, 0)
        copy = copy_to(src, dst, (zs, zr), (m, d - 1), to_z[d])
        copy.start()
        started.append(copy)

    def from_z(m, d):
        ref = (mix, ffw)[m].slot(0, d)
        copy_to(ref, ref, (zs, zr), (m, d - 1), to_z[1]).wait_recv()

    for d in (1, 3, 2):
        along_z(0, d)
    mix.spread(0, mix_p.at[p.z])
    ffw.spread(0, ffw_p.at[p.z])
    stays = [
        pltpu.make_async_copy(mix_p.at[p.z], mix.slot(0, 0), local.at[0]),
        pltpu.make_async_copy(ffw_p.at[p.z], ffw.slot(0, 0), local.at[1]),
        pltpu.make_async_copy(x_p, x_all.at[p.z, 0], local.at[2]),
    ]
    for copy in stays:
        copy.start()
    line = Gather(p, x_all, (us, ur), (vs, vr))
    line.begin(0, x_p)
    for d in (1, 3):
        from_z(0, d)
        mix.spread(d)
    mix.sides(0)
    line.step(1, 0)
    from_z(0, 2)
    mix.spread(2)
    along_z(1, 1)
    line.step(2, 0)
    for d in (1, 3):
        mix.sides(d)
    mix.corner(0)
    line.step(3, 0)
    mix.sides(2)
    for d in (1, 3):
        mix.corner(d)
    ffw.sides(0)
    mix.corner(2)
    ffw.corner(0)
    from_z(1, 1)
    mix.close(range(TP))
    ffw.close((0,))
    for copy in started:
        copy.wait_send()
    line.close(1)
    for copy in stays:
        copy.wait()


def intake(mix_p, ffw_p, x_p, p):
    whole = lambda v: jax.ShapeDtypeStruct((p.fs, 1, TP, 2, 2) + v.shape[1:], BF)
    mix_w, ffw_w, x_all = pl.pallas_call(
        intake_kernel,
        in_specs=[ANY] * 3,
        out_specs=[ANY] * 3,
        out_shape=[whole(mix_p), whole(ffw_p), jax.ShapeDtypeStruct((TP, 1) + x_p.shape, BF)],
        scratch_shapes=[
            *pairs(2, TP - 1),
            *pairs(TP - 1, 1),
            *pairs(TP - 1, 1),
            pltpu.SemaphoreType.DMA((3,)),
            *Spread.scratch(),
            *Spread.scratch(),
        ],
        compiler_params=pltpu.CompilerParams(collective_id=0, has_side_effects=True),
    )(mix_p, ffw_p, x_p)
    return mix_w.reshape(-1, mix_p.shape[-1]), ffw_w, x_all[:, 0]


def middle_kernel(with_ffw, *refs):
    parts, x_zero, gain, cot_p, piece_2, piece_3, _ = refs[:7]
    x_one, ffw_all, cot_all, ffw_w, own, local, gu0, gu1, gd0, gd1, cu0, cu1, cd0, cd1 = refs[7:21]
    p = Place()
    line = LineSum(p, parts, refs[21:29])
    out = Gather(p, ffw_all, (gu0, gu1), (gd0, gd1))
    cot = Gather(p, cot_all, (cu0, cu1), (cd0, cd1))
    halves, rows = parts.shape[1:3]
    line.clear()
    stays = []

    def stay(src, dst):
        copy = pltpu.make_async_copy(src, dst, local.at[len(stays)])
        copy.start()
        stays.append(copy)

    if with_ffw:
        ffw = Spread(p, ffw_w, refs[29:])
        greet_line(p, (ffw.to_x, ffw.to_f, ffw.to_c))
        stay(piece_3, ffw.slot(0, 3))
        stay(piece_2, ffw.slot(0, 2))
    else:
        greet_line(p)
    side = lambda name, *args: getattr(ffw, name)(*args) if with_ffw else None
    for h in range(halves):
        line.step(TP - 1, h)
    side("spread", 1)
    side("spread", 3, piece_3)
    side("spread", 2, piece_2)
    for k in range(TP - 2, 0, -1):
        for h in range(halves):
            line.step(k, h)
    for h in range(halves):
        line.arrive(h)

        def finish(at, h=h):
            value = x_zero[h, at].astype(F32) + line.total(h, at)
            x_one[h, at] = value
            own[h, at] = normed(value, gain[...]).astype(BF)

        by_rows(rows, finish)
        out.begin(h, own.at[h])
        stay(own.at[h], ffw_all.at[p.z, h])
    cot.begin(0, cot_p)
    stay(cot_p, cot_all.at[p.z, 0])
    side("sides", 1)
    for h in range(halves):
        out.step(1, h)
    cot.step(1, 0)
    side("sides", 3)
    for h in range(halves):
        out.step(2, h)
    side("corner", 1)
    cot.step(2, 0)
    side("sides", 2)
    for h in range(halves):
        out.step(3, h)
    side("corner", 3)
    cot.step(3, 0)
    side("corner", 2)
    side("close", (1, 2, 3))
    line.close()
    out.close(halves)
    cot.close(1)
    for copy in stays:
        copy.wait()


def middle(parts, x_zero, gain, cot_p, piece_2, piece_3, ffw_w):
    shape = parts.shape
    with_ffw = ffw_w is not None
    if not with_ffw:
        piece_2 = piece_3 = ffw_w = jnp.zeros((16, 128), BF)
    return pl.pallas_call(
        functools.partial(middle_kernel, with_ffw),
        in_specs=[VMEM] * 3 + [ANY] * 4,
        out_specs=[VMEM, ANY, ANY, ANY],
        out_shape=[
            jax.ShapeDtypeStruct(shape[1:], F32),
            jax.ShapeDtypeStruct(shape, BF),
            jax.ShapeDtypeStruct((TP, 1) + cot_p.shape, BF),
            jax.ShapeDtypeStruct(ffw_w.shape, BF),
        ],
        input_output_aliases={6: 3},
        scratch_shapes=[
            pltpu.VMEM(shape[1:], BF),
            pltpu.SemaphoreType.DMA((shape[1] + 3,)),
            *pairs(TP - 1, shape[1]),
            *pairs(TP - 1, shape[1]),
            *pairs(TP - 1, 1),
            *pairs(TP - 1, 1),
            *LineSum.scratch(shape),
            *(Spread.scratch() if with_ffw else []),
        ],
        compiler_params=pltpu.CompilerParams(
            collective_id=1, has_side_effects=True, vmem_limit_bytes=GRANT
        ),
    )(parts, x_zero, gain, cot_p, piece_2, piece_3, ffw_w)


def norm_back(values, gain, grad):
    inv = lax.rsqrt(jnp.mean(values * values, axis=-1, keepdims=True) + EPS)
    unit = values * inv
    through = grad * gain
    inner = jnp.mean(through * unit, axis=-1, keepdims=True)
    return inv * (through - unit * inner), grad * unit


class Fold:
    ORDER = ((0, 1, 1), (1, 1, 1), (0, 0, 1), (1, 1, 0), (0, 1, 0), (1, 0, 1), (0, 0, 0), (1, 0, 0))

    def __init__(self, p, grad, cores, scratch):
        self.p, self.grad, self.cores = p, grad, cores
        self.sums, self.stage, self.got, self.got_late = scratch[:4]
        self.near, self.staged = scratch[4:6]
        self.core_sems, self.early, self.late = scratch[6:8], scratch[8:10], scratch[10:12]
        self.to = (device(p, x=1 - p.x), device(p, f=1 - p.f))
        self.to_c = device(p, c=1 - p.c)

    @staticmethod
    def shapes(grad):
        block = (TP // 2,) + grad.shape[-2:]
        return jax.ShapeDtypeStruct((2, 2, 2) + block, BF), [
            pltpu.VMEM((2, 2, 2) + block, BF),
            pltpu.VMEM((2,) + block, BF),
            pltpu.VMEM((2, 2) + block, BF),
            pltpu.VMEM((2,) + block, BF),
            pltpu.SemaphoreType.DMA((8,)),
            pltpu.SemaphoreType.DMA((2,)),
            *pairs(8),
            *pairs(2, 2),
            *pairs(2),
        ]

    def block(self, way, f_rel, x_rel, c):
        p, half = self.p, TP // 2
        f, x = (p.f + f_rel) % 2, (p.x + x_rel) % 2
        return self.grad.at[f, 0, pl.ds(way * half, half), x, c]

    def cross(self, i):
        name = self.ORDER[i]
        src = self.block(*name, 1 - self.p.c)
        return copy_to(src, self.cores.at[name], self.core_sems, (i,), self.to_c)

    def load(self, i):
        name = self.ORDER[i]
        return pltpu.make_async_copy(
            self.block(*name, self.p.c), self.sums.at[name], self.near.at[i]
        )

    def fetch(self, i):
        src = self.cores.at[self.ORDER[i]]
        return pltpu.make_async_copy(src, self.stage.at[i % 2], self.staged.at[i % 2])

    def first(self, way, block):
        src = self.sums.at[(0, block, 1) if way == 0 else (1, 1, block)]
        return copy_to(src, self.got.at[way, block], self.early, (way, block), self.to[way])

    def second(self, way):
        src = self.sums.at[(0, 1, 0) if way == 0 else (1, 0, 1)]
        return copy_to(src, self.got_late.at[way], self.late, (way,), self.to[1 - way])

    def add(self, name, *others):
        rows = self.sums.shape[-2]

        def turn(at):
            for k in range(TP // 2):
                total = self.sums[(*name, k, at)].astype(F32)
                for other in others:
                    total = total + other[k, at].astype(F32)
                self.sums[(*name, k, at)] = total.astype(BF)

        by_rows(rows, turn)

    def begin(self):
        for i in range(8):
            self.cross(i).start()
            self.load(i).start()

    def issue(self, i):
        self.cross(i).wait_recv()
        self.fetch(i).start()

    def join(self, i):
        if i == 0:
            self.issue(0)
        if i + 1 < 8:
            self.issue(i + 1)
        self.fetch(i).wait()
        self.load(i).wait()
        self.add(self.ORDER[i], self.stage.at[i % 2])
        if i < 4:
            way = self.ORDER[i][0]
            self.first(way, self.ORDER[i][1 + way]).start()

    def middle(self):
        for way in range(2):
            self.first(way, 1).wait_recv()
            self.add((0, 1, 0) if way == 0 else (1, 0, 1), self.got.at[way, 1])
            self.second(way).start()

    def finish(self):
        for way in range(2):
            self.first(way, 0).wait_recv()
            self.second(way).wait_recv()
            self.add((way, 0, 0), self.got.at[way, 0], self.got_late.at[way])

    def result(self, z):
        return self.sums.at[z // (TP // 2), 0, 0, z % (TP // 2)]

    def close(self):
        for i in range(8):
            self.cross(i).wait_send()
        for way in range(2):
            self.second(way).wait_send()
            for block in range(2):
                self.first(way, block).wait_send()


def folds_of(p, grads, cores, scratch):
    return [Fold(p, g, c, scratch[12 * i : 12 * i + 12]) for i, (g, c) in enumerate(zip(grads, cores))]


def turn_kernel(count, *refs):
    parts, out_parts, x_one, cot, gain = refs[:5]
    grads, refs = refs[5 : 5 + count], refs[5 + count :]
    mixed_out, grad_x_one, grad_gain, mix_all = refs[:4]
    totals, cores, refs = refs[4 : 4 + count], refs[4 + count : 4 + 2 * count], refs[4 + 2 * count :]
    own, local, gu0, gu1, gd0, gd1 = refs[:6]
    p = Place()
    line, late = LineSum(p, parts, refs[6:14]), LineSum(p, out_parts, refs[14:22])
    folds = folds_of(p, grads, cores, refs[22:])
    out = Gather(p, mix_all, (gu0, gu1), (gd0, gd1))
    halves, rows = parts.shape[1:3]
    line.clear()
    late.clear()
    greet_line(p, (*folds[0].to, folds[0].to_c) if folds else ())
    for fold in folds:
        fold.begin()
    for h in range(halves):
        line.step(TP - 1, h)
    for h in range(halves):
        late.step(TP - 1, h)
    for fold in folds:
        fold.join(0)
        fold.join(1)
    for k in range(TP - 2, 0, -1):
        for h in range(halves):
            line.step(k, h)
        for fold in folds:
            fold.join(4 - k)
    stays = []

    def stay(src, dst):
        copy = pltpu.make_async_copy(src, dst, local.at[len(stays)])
        copy.start()
        stays.append(copy)

    grad_gain[...] = jnp.zeros(grad_gain.shape, F32)
    for h in range(halves):
        line.arrive(h)

        def finish(at, h=h):
            grad, gains = norm_back(x_one[h, at], gain[...], line.total(h, at))
            grad = grad + cot[h, at].astype(F32)
            grad_x_one[h, at] = grad
            own[h, at] = grad.astype(BF)
            grad_gain[0:1] += jnp.sum(gains, axis=0, keepdims=True)

        by_rows(rows, finish)
        out.begin(h, own.at[h])
        stay(own.at[h], mix_all.at[p.z, h])
    for fold in folds:
        for i in range(4, 8):
            fold.join(i)
    for h in range(halves):
        out.step(1, h)
        late.step(2, h)
    for fold in folds:
        fold.middle()
    for h in range(halves):
        out.step(2, h)
        late.step(1, h)
    for h in range(halves):
        out.step(3, h)
    for h in range(halves):
        late.arrive(h)

        def store(at, h=h):
            mixed_out[h, at] = (x_one[h, at] + late.total(h, at)).astype(BF)

        by_rows(rows, store)
    for fold, total in zip(folds, totals):
        fold.finish()
        for z in range(TP):
            stay(fold.result(z), total.at[z])
    for fold in folds:
        fold.close()
    line.close()
    late.close()
    out.close(halves)
    for copy in stays:
        copy.wait()


def turn(parts, out_parts, x_one, cot, gain, grads):
    shape, count = parts.shape, len(grads)
    folded = [Fold.shapes(grad) for grad in grads]
    results = pl.pallas_call(
        functools.partial(turn_kernel, count),
        in_specs=[VMEM] * 5 + [ANY] * count,
        out_specs=[VMEM, VMEM, VMEM, ANY] + [ANY] * (2 * count),
        out_shape=[
            jax.ShapeDtypeStruct(shape[1:], BF),
            jax.ShapeDtypeStruct(shape[1:], F32),
            jax.ShapeDtypeStruct((8, shape[-1]), F32),
            jax.ShapeDtypeStruct(shape, BF),
            *(jax.ShapeDtypeStruct((TP,) + grad.shape[-2:], BF) for grad in grads),
            *(cores for cores, _ in folded),
        ],
        scratch_shapes=[
            pltpu.VMEM(shape[1:], BF),
            pltpu.SemaphoreType.DMA((shape[1] + TP * count,)),
            *pairs(TP - 1, shape[1]),
            *pairs(TP - 1, shape[1]),
            *LineSum.scratch(shape),
            *LineSum.scratch(shape),
            *(item for _, scratch in folded for item in scratch),
        ],
        compiler_params=pltpu.CompilerParams(
            collective_id=2, has_side_effects=True, vmem_limit_bytes=GRANT
        ),
    )(parts, out_parts, x_one, cot, gain, *grads)
    return results[: 4 + count]


def final_kernel(count, *refs):
    parts, x_zero, gain, grad_x_one, vectors = refs[:5]
    grads, refs = refs[5 : 5 + count], refs[5 + count :]
    grad_in, sums = refs[:2]
    outs, cores, refs = refs[2 : 2 + count], refs[2 + count : 2 + 2 * count], refs[2 + 2 * count :]
    acc, got, vs, vr, zs, zr, local = refs[:7]
    p = Place()
    line = LineSum(p, parts, refs[7:15])
    folds = folds_of(p, grads, cores, refs[15:])
    halves, rows = parts.shape[1:3]
    line.clear()
    to_z = [device(p, z=(p.z + d) % TP) for d in range(TP)]
    (to_x, to_f), to_c = folds[0].to, folds[0].to_c
    greet(to_z[1:] + [to_x, to_f, to_c])
    partners = [to_c, to_x, to_f] + [
        device(p, z=p.z + bit * (1 - 2 * (p.z // bit % 2))) for bit in (1, 2)
    ]

    def vector(i):
        return copy_to(acc.at[i], got.at[i], (vs, vr), (i,), partners[i])

    def next_vector(i):
        vector(i).wait_recv()
        if i < 4:
            acc[i + 1] = acc[i] + got[i]
            vector(i + 1).start()
        else:
            sums[...] = acc[i] + got[i]

    acc[0] = vectors[...]
    vector(0).start()
    for fold in folds:
        fold.begin()
    for h in range(halves):
        line.step(TP - 1, h)
    for i in range(4):
        for fold in folds:
            fold.join(i)
    next_vector(0)
    for h in range(halves):
        line.step(2, h)
    next_vector(1)
    for i in range(4, 8):
        for fold in folds:
            fold.join(i)
    next_vector(2)
    for h in range(halves):
        line.step(1, h)
    next_vector(3)
    for fold in folds:
        fold.middle()
    for h in range(halves):
        line.arrive(h)

        def finish(at, h=h):
            grad, _ = norm_back(x_zero[h, at].astype(F32), gain[...], line.total(h, at))
            grad_in[h, at] = grad_x_one[h, at] + grad

        by_rows(rows, finish)
    next_vector(4)
    started, stays = [], []
    for m, fold in enumerate(folds):
        fold.finish()
        for d in (1, 3, 2):
            src = fold.result((p.z + d) % TP)
            copy = copy_to(src, outs[m].at[p.z], (zs, zr), (m, d - 1), to_z[d])
            copy.start()
            started.append(copy)
        stays.append(pltpu.make_async_copy(fold.result(p.z), outs[m].at[p.z], local.at[m]))
        stays[-1].start()
    for m in range(count):
        for d in range(1, TP):
            ref = outs[m].at[(p.z - d) % TP]
            copy_to(ref, ref, (zs, zr), (m, d - 1), to_z[1]).wait_recv()
    for copy in started:
        copy.wait_send()
    for i in range(5):
        vector(i).wait_send()
    for fold in folds:
        fold.close()
    line.close()
    for copy in stays:
        copy.wait()


def final(parts, x_zero, gain, grad_x_one, vectors, grads):
    shape, count = parts.shape, len(grads)
    folded = [Fold.shapes(grad) for grad in grads]
    results = pl.pallas_call(
        functools.partial(final_kernel, count),
        in_specs=[VMEM] * 5 + [ANY] * count,
        out_specs=[VMEM, VMEM] + [ANY] * (2 * count),
        out_shape=[
            jax.ShapeDtypeStruct(shape[1:], F32),
            jax.ShapeDtypeStruct(vectors.shape, F32),
            *(jax.ShapeDtypeStruct((TP,) + grad.shape[-2:], BF) for grad in grads),
            *(cores for cores, _ in folded),
        ],
        scratch_shapes=[
            pltpu.VMEM((5,) + vectors.shape, F32),
            pltpu.VMEM((5,) + vectors.shape, F32),
            *pairs(5),
            *pairs(count, TP - 1),
            pltpu.SemaphoreType.DMA((count,)),
            *LineSum.scratch(shape),
            *(item for _, scratch in folded for item in scratch),
        ],
        compiler_params=pltpu.CompilerParams(
            collective_id=3, has_side_effects=True, vmem_limit_bytes=GRANT
        ),
    )(parts, x_zero, gain, grad_x_one, vectors, *grads)
    return results[0], results[1], results[2 : 2 + count]


def chain_kernel(backward, sums, *refs):
    if backward:
        known, start, spans, send, recv = refs
    else:
        start, spans, send, recv = refs
    p = Place()
    peers = [device_q(p, (p.q + d) % NQ) for d in range(NQ)]
    greet(peers[1:])
    spans[p.q] = sums[...]
    copies = []
    for d in range(1, NQ):
        copies.append(copy_to(spans.at[p.q], spans.at[p.q], (send, recv), (d,), peers[d]))
        copies[-1].start()
    for d in range(1, NQ):
        ref = spans.at[(p.q - d) % NQ]
        copy_to(ref, ref, (send, recv), (d,), peers[d]).wait_recv()
    micro = sums.shape[1] // TP
    carry = jnp.zeros((micro, sums.shape[2]), F32)
    order = [(z, q) for z in range(TP) for q in range(NQ)]
    for z, q in reversed(order) if backward else order:
        here = slice(z * micro, (z + 1) * micro)

        @pl.when(p.q == q)
        def _(carry=carry, here=here):
            start[here] = carry

        decay = known[q, 0, here] if backward else spans[q, 0, here]
        carry = decay * carry + spans[q, 0 if backward else 1, here]
    for copy in copies:
        copy.wait_send()


def device_q(p, q):
    return device(p, x=q // 2, c=q % 2)


def chain(sums, known=None):
    backward = known is not None
    every = (NQ,) + sums.shape
    return pl.pallas_call(
        functools.partial(chain_kernel, backward),
        in_specs=[VMEM] * (2 if backward else 1),
        out_specs=[VMEM, VMEM],
        out_shape=[
            jax.ShapeDtypeStruct(sums.shape[1:], F32),
            jax.ShapeDtypeStruct(every, F32),
        ],
        scratch_shapes=pairs(NQ),
        compiler_params=pltpu.CompilerParams(
            collective_id=5 if backward else 4, has_side_effects=True
        ),
    )(*((sums, known) if backward else (sums,)))


def geglu(gate_vals, up_vals):
    return jax.nn.gelu(gate_vals) * up_vals


def all_spans(value, p):
    by_q = everywhere(value, shift_q, p.q, NQ)
    by_r = everywhere(by_q, shift_r, p.r, p.rests)
    return jnp.swapaxes(by_r, 1, 2).reshape((-1,) + value.shape[1:])


def own_spans(spans, p):
    split = spans.reshape((p.rests, TP, NQ) + spans.shape[1:])
    return lax.dynamic_index_in_dim(at(split, p.r), p.q, 1, keepdims=False)


def on_device(
    inputs,
    cotangent,
    proj_gelu,
    proj_lru,
    gate_blocks,
    proj_out,
    ffw_gate,
    ffw_up,
    ffw_down,
    norm_mix,
    norm_ffw,
    decay_param,
    conv_taps,
):
    p = Place()
    micro, span, width = inputs.shape[0], inputs.shape[2], inputs.shape[3]
    lru_width = proj_gelu.shape[1]
    tap_count = conv_taps.shape[1]
    block_width = gate_blocks.shape[1] // 2
    heads = lru_width // block_width
    ffw_part = ffw_gate.shape[1] // TP
    rows = proj_gelu.shape[0]
    held = -(-heads // TP)
    first = [k * heads // TP for k in range(TP)]
    owned = [range(first[k], first[k + 1] if k + 1 < TP else heads) for k in range(TP)]
    part = held * block_width

    out_t, down_t = proj_out.T, ffw_down.T
    small = jnp.concatenate(
        [norm_mix[:, None], norm_ffw[:, None], decay_param[:, None], conv_taps], axis=1
    )
    small = jnp.pad(small, ((0, 0), (0, 128 - small.shape[1])))
    mix_pieces, ffw_pieces = [], []
    for k in range(TP):
        cols = slice(first[k] * block_width, first[k] * block_width + part)
        mix_pieces.append(
            jnp.concatenate(
                [proj_gelu[:, cols], proj_lru[:, cols], out_t[:, cols], gate_blocks, small], axis=1
            )
        )
        cols = slice(k * ffw_part, (k + 1) * ffw_part)
        ffw_pieces.append(
            jnp.concatenate([ffw_gate[:, cols], ffw_up[:, cols], down_t[:, cols]], axis=1)
        )
    mix_pieces, ffw_pieces = jnp.stack(mix_pieces), jnp.stack(ffw_pieces)
    x_rows, cot = inputs[:, 0], cotangent[:, 0]
    one = 1 if p.rests == 1 else 0
    edge = lax.ppermute(
        x_rows[:, span - (tap_count - 1) :],
        "seq",
        [(i, i + 1) for i in range(lax.axis_size("seq") - 1)],
    )
    pad = jnp.zeros((micro, HALO - (tap_count - 1), width), BF)
    x_wide = jnp.concatenate([pad, edge, x_rows], axis=1)
    if p.rests == 1:
        mix_w, ffw_w, x_all = intake(mix_pieces, ffw_pieces, x_wide.reshape(-1, width), p)
        ffw_pieces, x_all = lax.optimization_barrier((ffw_pieces, x_all))
        piece_3, piece_2 = (shift_z(at(ffw_pieces, (p.z + d) % TP), d) for d in (3, 2))
    else:
        mix_w, whole_ffw = weights_in(mix_pieces, p), weights_in(ffw_pieces, p)
        x_all, piece_2, piece_3, ffw_w = gather_z(x_wide, p), None, None, None
    x_all = x_all.reshape(TP, micro, HALO + span, width)

    gelu_lru_w = mix_w[:, : 2 * part]
    out_w = mix_w[:, 2 * part : 3 * part]
    blocks_w = mix_w[:, 3 * part : 3 * part + 2 * block_width]
    small_w = mix_w[:, 3 * part + 2 * block_width :].astype(F32).T
    mix_gain, ffw_gain = small_w[0:1], small_w[1:2]
    start = sum(jnp.where(p.z == k, first[k] * block_width, 0) for k in range(TP))
    feature = jnp.arange(part) + start
    low = sum(jnp.where(p.z == k, owned[k][0] * block_width, 0) for k in range(TP))
    high = sum(jnp.where(p.z == k, (owned[k][-1] + 1) * block_width, 0) for k in range(TP))
    is_own = ((feature >= low) & (feature < high)).astype(F32)[None]
    own_part = lax.dynamic_slice_in_dim(small_w[2 : 3 + tap_count], start, part, 1)
    decay_f = own_part[:1]
    rows_w = jnp.concatenate(
        [jax.nn.softplus(-decay_f), jax.nn.sigmoid(-decay_f), own_part[1:], is_own, 0 * is_own]
    )
    block_mats = lax.dynamic_slice_in_dim(blocks_w, start, part, 0).reshape(
        held, block_width, 2 * block_width
    )

    x_all_f = x_all.astype(F32)
    mixed_all = normed(x_all_f, mix_gain[0]).astype(BF)
    pre = dot_plain(mixed_all.reshape(-1, width), gelu_lru_w)
    mixed = mixed_all[:, :, HALO:].reshape(-1, width)
    conv, gate, state, prod, sums = recur(pre, rows_w, block_mats, span)
    ends = (TP, micro, part)
    if p.rests == 1:
        state_in, every_sum = chain(sums)
    else:
        sums = all_spans(jnp.stack([sums[0].reshape(ends), sums[1].reshape(ends)], axis=1), p)
        carry, carries = jnp.zeros_like(sums[0, 0]), []
        for k in range(sums.shape[0]):
            carries.append(carry)
            carry = sums[k, 0] * carry + sums[k, 1]
        state_in = own_spans(jnp.stack(carries), p).reshape(-1, part)
    mix_bf = recur_mix(pre, rows_w, state, prod, state_in, block_width, span)
    blocked = (TP, micro, span, width)
    out_parts = dot_right_t(mix_bf, out_w).astype(BF).reshape(blocked)
    x_one, ffw_bf, cot_all, ffw_w = middle(
        out_parts, x_rows, ffw_gain, cot.reshape(-1, width), piece_2, piece_3, ffw_w
    )
    cot_all = cot_all.reshape(-1, width)
    ffw_w = ffw_w.reshape(width, -1) if p.rests == 1 else whole_ffw

    ffw_bf = ffw_bf.reshape(-1, width)
    gate_up_w, down_w = ffw_w[:, : 2 * ffw_part], ffw_w[:, 2 * ffw_part :]
    gate_up = dot_plain(ffw_bf, gate_up_w)
    gate_vals, up_vals = gate_up[:, :ffw_part], gate_up[:, ffw_part:]
    hidden_bf = geglu(gate_vals, up_vals).astype(BF)
    grad_hidden = dot_plain(cot_all, down_w)
    _, pull_back = jax.vjp(geglu, gate_vals, up_vals)
    grad_gate_up = jnp.concatenate(pull_back(grad_hidden), axis=1).astype(BF)
    ffw_parts = dot_right_t(hidden_bf, down_w).astype(BF).reshape(blocked)
    grad_in_parts = dot_right_t(grad_gate_up, gate_up_w).astype(BF).reshape(blocked)
    ffw_grads = [dot_left_t(ffw_bf, grad_gate_up), dot_left_t(cot_all, hidden_bf)]
    ffw_grads = [grad.astype(BF) for grad in ffw_grads]
    mixed_out, grad_x_one, gain_rows, grad_mix, *ffw_totals = turn(
        grad_in_parts, ffw_parts, x_one, cot, ffw_gain, [by_owner(g, p) for g in ffw_grads] * one
    )
    if p.rests == 1:
        ffw_grads = [to_owner_z(total, p) for total in ffw_totals]
    else:
        ffw_grads = [grads_out(grad, p) for grad in ffw_grads]
    grad_mix = grad_mix.reshape(-1, width)

    back_mix = dot_plain(grad_mix, out_w)
    grad_gelu_bf, local_back, prod_back, back_sums = recur_back(
        back_mix, pre, rows_w, state, prod, state_in, gate, block_width, span
    )
    if p.rests == 1:
        carried, _ = chain(back_sums[None], every_sum)
    else:
        back_sums = all_spans(back_sums.reshape(ends), p)
        carry, carries = jnp.zeros_like(sums[0, 0]), []
        for k in range(sums.shape[0] - 1, -1, -1):
            carries.append(carry)
            carry = sums[k, 0] * carry + back_sums[k]
        carried = own_spans(jnp.stack(carries[::-1]), p).reshape(-1, part)
    grad_blocks, grad_lru, spill, row_grads = recur_grad(
        local_back, prod_back, carried, state, prod, state_in, gate, conv, pre, rows_w, block_mats,
        span,
    )
    spill = spill.reshape(TP, micro, HALO, part)
    from_next = shift_q(spill, -1)
    last = jnp.zeros_like(spill[:1])
    if p.rests > 1:
        last = move(spill[:1], lambda r, z, q: (r - 1, z, NQ - 1) if q == 0 and r > 0 else None)
    from_next = jnp.where(
        p.q == NQ - 1, jnp.concatenate([from_next[1:], last], axis=0), from_next
    )
    grad_lru = grad_lru.reshape(TP, micro, span, part) + jnp.pad(
        from_next, ((0, 0), (0, 0), (span - HALO, 0), (0, 0))
    )
    grad_lru_bf = (grad_lru * is_own[0]).astype(BF).reshape(-1, part)
    grad_pair = jnp.concatenate([grad_gelu_bf, grad_lru_bf], axis=1)
    grad_mixed = dot_right_t(grad_pair, gelu_lru_w)
    x_rows_f = x_all_f[:, :, HALO:].reshape(-1, width)
    unit = x_rows_f * lax.rsqrt(jnp.mean(x_rows_f * x_rows_f, axis=-1, keepdims=True) + EPS)
    grad_mix_gain = jnp.sum(grad_mixed * unit, axis=0, keepdims=True)
    grad_mixed_parts = grad_mixed.astype(BF).reshape(blocked)

    blocks_all = lax.dynamic_update_slice_in_dim(
        jnp.zeros((lru_width, 2 * block_width), BF),
        (grad_blocks * is_own[0][:, None]).astype(BF),
        start,
        0,
    )
    mix_grads = [dot_left_t(mixed, grad_pair), dot_left_t(grad_mix, mix_bf), blocks_all]
    mix_grads = [grad.astype(BF) for grad in mix_grads]
    vectors = lax.dynamic_update_slice_in_dim(
        jnp.zeros((1 + tap_count, lru_width), F32), row_grads[: 1 + tap_count], start, 1
    )
    vectors = jnp.concatenate([grad_mix_gain, gain_rows[:1], vectors], axis=0)
    vectors = jnp.pad(vectors, ((0, -vectors.shape[0] % 8), (0, 0)))
    if p.rests == 1:
        grad_inputs, vectors, mix_grads = final(
            grad_mixed_parts, x_rows, mix_gain, grad_x_one, vectors,
            [by_owner(grad, p) for grad in mix_grads],
        )
    else:
        mix_grads = [grads_out(grad, p) for grad in mix_grads]
        grad_mixed_own = scatter_z(grad_mixed_parts, p)
        grad_inputs = grad_x_one + norm_back(x_rows.astype(F32), mix_gain, grad_mixed_own)[0]
        for exchange in (swap_core, swap_x, swap_f):
            vectors = vectors + exchange(vectors)
        for bit in (1, 2):
            vectors = vectors + move(vectors, lambda r, z, q, bit=bit: (r, z ^ bit, q))
        total = vectors
        for d in range(1, p.rests):
            total = total + shift_r(vectors, d)
        vectors = total
    vectors = lax.dynamic_slice_in_dim(vectors, p.index * rows, rows, 1)

    def mix_columns(grad, offset):
        picked = [
            grad[k][
                :,
                offset + (owned[k][0] - first[k]) * block_width : offset
                + (owned[k][-1] + 1 - first[k]) * block_width,
            ]
            for k in range(TP)
        ]
        return jnp.concatenate(picked, axis=1).astype(F32)

    def ffw_columns(grad, offset):
        picked = [grad[k][:, offset : offset + ffw_part] for k in range(TP)]
        return jnp.concatenate(picked, axis=1).astype(F32)

    shape = (micro, 1, span, width)
    return (
        mixed_out.reshape(shape),
        grad_inputs.reshape(shape),
        mix_columns(mix_grads[0], 0),
        mix_columns(mix_grads[0], part),
        jnp.sum(mix_grads[2].astype(F32), axis=0),
        mix_columns(mix_grads[1], 0).T,
        ffw_columns(ffw_grads[0], 0),
        ffw_columns(ffw_grads[0], ffw_part),
        ffw_columns(ffw_grads[1], 0).T,
        vectors[0],
        vectors[1],
        vectors[2],
        vectors[3 : 3 + tap_count].T,
    )


def solution(mesh):
    in_specs = (
        P(None, "fsdp", "seq", None),
        P(None, "fsdp", "seq", None),
        P(("fsdp", "seq"), None),
        P(("fsdp", "seq"), None),
        P(("fsdp", "seq"), None),
        P(None, ("fsdp", "seq")),
        P(("fsdp", "seq"), None),
        P(("fsdp", "seq"), None),
        P(None, ("fsdp", "seq")),
        P(("fsdp", "seq")),
        P(("fsdp", "seq")),
        P(("fsdp", "seq")),
        P(("fsdp", "seq"), None),
    )
    out_specs = (
        P(None, "fsdp", "seq", None),
        P(None, "fsdp", "seq", None),
        P(("fsdp", "seq"), None),
        P(("fsdp", "seq"), None),
        P(("fsdp", "seq"), None),
        P(None, ("fsdp", "seq")),
        P(("fsdp", "seq"), None),
        P(("fsdp", "seq"), None),
        P(None, ("fsdp", "seq")),
        P(("fsdp", "seq")),
        P(("fsdp", "seq")),
        P(("fsdp", "seq")),
        P(("fsdp", "seq"), None),
    )
    return jax.shard_map(
        on_device, mesh=mesh, in_specs=in_specs, out_specs=out_specs, check_vma=False
    )
```

```python
import functools

import jax
import jax.numpy as jnp
from jax import lax
from jax.experimental import pallas as pl
from jax.experimental.pallas import tpu as pltpu
from jax.sharding import PartitionSpec as P

EPS = 1e-06
GUARD = 0.001
RATE = 8.0
TP = 4
NQ = 4
HALO = 8
BF = jnp.bfloat16
F32 = jnp.float32
MESH = pl.DeviceIdType.MESH
ANY = pl.BlockSpec(memory_space=pl.ANY)
VMEM = pl.BlockSpec(memory_space=pltpu.VMEM)
GRANT = 60 * 1024 * 1024


def move(value, step):
    pairs = []
    for here in range(lax.axis_size("seq")):
        there = step(here // (TP * NQ), here // NQ % TP, here % NQ)
        if there is not None:
            pairs.append((here, (there[0] * TP + there[1]) * NQ + there[2]))
    return lax.ppermute(value, "seq", pairs)


def swap_core(value):
    return move(value, lambda r, z, q: (r, z, q ^ 1))


def swap_x(value):
    return move(value, lambda r, z, q: (r, z, q ^ 2))


def swap_f(value):
    return lax.ppermute(value, "fsdp", [(0, 1), (1, 0)])


def shift_z(value, d):
    return move(value, lambda r, z, q: (r, (z + d) % TP, q))


def shift_q(value, d):
    return move(value, lambda r, z, q: (r, z, (q + d) % NQ))


def shift_r(value, d):
    count = lax.axis_size("seq") // (TP * NQ)
    return move(value, lambda r, z, q: ((r + d) % count, z, q))


def hop(value, d, low, high):
    return move(value, lambda r, z, q: (r, z + d, q) if low <= z <= high else None)


class Place:
    def __init__(self):
        seq = lax.axis_index("seq")
        self.f = lax.axis_index("fsdp")
        self.r, self.z, self.q = seq // (TP * NQ), seq // NQ % TP, seq % NQ
        self.x, self.c = self.q // 2, self.q % 2
        self.rests = lax.axis_size("seq") // (TP * NQ)
        self.fs = lax.axis_size("fsdp")
        self.index = self.f * lax.axis_size("seq") + seq


def at(value, index):
    return lax.dynamic_index_in_dim(value, index, 0, keepdims=False)


def put(base, value, *index):
    starts = [jnp.int32(0) if i is None else jnp.int32(i) for i in index]
    starts += [jnp.int32(0)] * (base.ndim - len(index))
    for dim, i in enumerate(index):
        if i is not None:
            value = jnp.expand_dims(value, dim)
    return lax.dynamic_update_slice(base, value, starts)


def everywhere(value, shifter, mine, count):
    out = put(jnp.zeros((count,) + value.shape, value.dtype), value, mine)
    for d in range(1, count):
        out = put(out, shifter(value, d), (mine - d) % count)
    return out


def gather_z(value, p):
    ups, downs = [], []
    up = down = value
    for k in range(1, TP):
        up = hop(up, 1, k - 1, TP - 2)
        down = hop(down, -1, 1, TP - k)
        ups.append(up)
        downs.append(down)
    out = put(jnp.zeros((TP,) + value.shape, value.dtype), value, p.z)
    for k in range(1, TP):
        out = put(out, downs[k - 1] + ups[TP - 1 - k], (p.z + k) % TP)
    return out


def scatter_z(parts, p):
    right = left = None
    for k in range(TP - 1, 0, -1):
        send = at(parts, (p.z + k) % TP)
        if right is not None:
            send = (send.astype(F32) + right.astype(F32)).astype(BF)
        right = hop(send, 1, 0, TP - 1 - k)
        send = at(parts, (p.z - k) % TP)
        if left is not None:
            send = (send.astype(F32) + left.astype(F32)).astype(BF)
        left = hop(send, -1, k, TP - 1)
    return at(parts, p.z).astype(F32) + right.astype(F32) + left.astype(F32)


def weights_in(pieces, p):
    rows, cols = pieces.shape[1:]
    mine = put(jnp.zeros(pieces.shape, BF), at(pieces, p.z), p.z)
    for d in range(1, TP):
        mine = put(mine, shift_z(at(pieces, (p.z + d) % TP), d), (p.z - d) % TP)
    mine = everywhere(mine, shift_r, p.r, p.rests)
    half = TP // 2
    by_x, by_f = swap_x(mine), swap_f(mine)
    corner = (swap_f(by_x[:, :half]), swap_x(by_f[:, half:]))
    whole = jnp.zeros((p.fs, p.rests, TP, 2, 2, rows, cols), BF)
    for block, f, x, z in (
        (mine, p.f, p.x, 0),
        (by_x, p.f, 1 - p.x, 0),
        (by_f, 1 - p.f, p.x, 0),
        (corner[0], 1 - p.f, 1 - p.x, 0),
        (corner[1], 1 - p.f, 1 - p.x, half),
    ):
        other = swap_core(block)
        for part, c in ((block, p.c), (other, 1 - p.c)):
            part = part[None, :, :, None, None]
            whole = lax.dynamic_update_slice(
                whole, part, [jnp.int32(i) for i in (f, 0, z, x, c, 0, 0)]
            )
    return whole.reshape(-1, cols)


def by_owner(grad, p):
    return grad.reshape(p.fs, p.rests, TP, 2, 2, -1, grad.shape[1])


def to_owner_z(total, p):
    out = put(jnp.zeros(total.shape, BF), at(total, p.z), p.z)
    for d in (1, 3, 2):
        out = put(out, shift_z(at(total, (p.z + d) % TP), d), (p.z - d) % TP)
    return out


def grads_out(grad, p):
    plus = lambda a, b: (a.astype(F32) + b.astype(F32)).astype(BF)
    pick = lambda v, dim, i: lax.dynamic_index_in_dim(v, i, dim, keepdims=False)
    total = by_owner(grad, p)
    total = plus(pick(total, 4, p.c), swap_core(pick(total, 4, 1 - p.c)))
    total = plus(pick(total, 3, p.x), swap_x(pick(total, 3, 1 - p.x)))
    total = plus(at(total, p.f), swap_f(at(total, 1 - p.f)))
    mine = at(total, p.r)
    for d in range(1, p.rests):
        mine = plus(mine, shift_r(at(total, (p.r + d) % p.rests), d))
    return to_owner_z(mine, p)


def dot_left_t(left_mat, right_mat):
    return lax.dot_general(
        left_mat, right_mat, (((0,), (0,)), ((), ())), preferred_element_type=F32
    )


def dot_plain(left_mat, right_mat):
    return jnp.dot(left_mat, right_mat, preferred_element_type=F32)


def dot_right_t(left_mat, right_mat):
    return lax.dot_general(
        left_mat, right_mat, (((1,), (1,)), ((), ())), preferred_element_type=F32
    )


def normed(values, gain_vec):
    return values * lax.rsqrt(jnp.mean(values * values, axis=-1, keepdims=True) + EPS) * gain_vec


def gelu_pair(v):
    scale = 0.7978845608028654
    inner = jnp.tanh(scale * (v + 0.044715 * v * v * v))
    slope = 0.5 * v * (1.0 - inner * inner) * scale * (1.0 + 0.134145 * v * v)
    return 0.5 * v * (1.0 + inner), 0.5 * (1.0 + inner) + slope


def span_scan(decay, drive, backward):
    count = decay.shape[0]
    row = lax.broadcasted_iota(jnp.int32, decay.shape, 0)
    step = 1
    while step < count:
        inside = row < count - step if backward else row >= step
        turn = count - step if backward else step
        drive = drive + jnp.where(inside, decay * pltpu.roll(drive, turn, 0), 0.0)
        decay = decay * jnp.where(inside, pltpu.roll(decay, turn, 0), 1.0)
        step *= 2
    return decay, drive


def gate_values(gate, soft):
    half = gate.shape[1] // 2
    rec_gate = jax.nn.sigmoid(gate[:, :half])
    in_gate = jax.nn.sigmoid(gate[:, half:])
    log_decay = -RATE * rec_gate * soft
    square = jnp.exp(2.0 * log_decay)
    return rec_gate, in_gate, jnp.exp(log_decay), square, jnp.sqrt(1.0 - square + GUARD)


def recur_kernel(span, pre, rows, block, conv, gate, state, prod, sums):
    count = conv.shape[0] // span
    soft, taps = rows[0:1], [rows[k + 2 : k + 3] for k in range(4)]

    def convolve(i, _):
        start = pl.multiple_of(i * (span + HALO), 8)
        vals = pre[pl.ds(start, span + HALO)].astype(BF).astype(F32)
        total = taps[0] * vals
        for k in range(1, 4):
            total = total + taps[k] * pltpu.roll(vals, k, 0)
        conv[pl.ds(pl.multiple_of(i * span, 16), span)] = total[HALO:].astype(BF)
        return 0

    lax.fori_loop(0, count, convolve, 0)
    gate[...] = dot_plain(conv[...], block[0])
    for i in range(count):
        here = pl.ds(i * span, span)
        _, in_gate, decay, _, root = gate_values(gate[here], soft)
        decay, local = span_scan(decay, root * in_gate * conv[here].astype(F32), False)
        state[here] = local
        prod[here] = decay
        sums[0, i : i + 1] = decay[span - 1 :]
        sums[1, i : i + 1] = local[span - 1 :]


def recur(pre, rows, block_mats, span):
    held, bw = block_mats.shape[:2]
    spans, part = pre.shape[0] // (span + HALO), held * bw
    tokens = spans * span
    column = lambda h: (0, h)
    shapes = [((tokens, part), BF), ((tokens, 2 * part), F32), ((tokens, part), F32)]
    shapes += [((tokens, part), F32), ((2, spans, part), F32)]
    return pl.pallas_call(
        functools.partial(recur_kernel, span),
        grid=(held,),
        in_specs=[
            pl.BlockSpec((pre.shape[0], bw), lambda h: (0, held + h)),
            pl.BlockSpec((8, bw), column),
            pl.BlockSpec((1, bw, 2 * bw), lambda h: (h, 0, 0)),
        ],
        out_specs=[
            pl.BlockSpec((tokens, bw), column),
            pl.BlockSpec((tokens, 2 * bw), column),
            pl.BlockSpec((tokens, bw), column),
            pl.BlockSpec((tokens, bw), column),
            pl.BlockSpec((2, spans, bw), lambda h: (0, 0, h)),
        ],
        out_shape=[jax.ShapeDtypeStruct(*shape) for shape in shapes],
        compiler_params=pltpu.CompilerParams(vmem_limit_bytes=GRANT),
    )(pre, rows, block_mats)


def recur_mix_kernel(span, pre, rows, state, prod, start, mix):
    for i in range(state.shape[0] // span):
        here = pl.ds(i * span, span)
        act, _ = gelu_pair(pre[pl.ds(i * (span + HALO) + HALO, span)])
        states = state[here] + prod[here] * start[i : i + 1]
        mix[here] = (states * act * rows[6:7]).astype(BF)


def recur_mix(pre, rows, state, prod, start, bw, span):
    tokens, part = state.shape
    column = lambda h: (0, h)
    return pl.pallas_call(
        functools.partial(recur_mix_kernel, span),
        grid=(part // bw,),
        in_specs=[
            pl.BlockSpec((pre.shape[0], bw), column),
            pl.BlockSpec((8, bw), column),
            pl.BlockSpec((tokens, bw), column),
            pl.BlockSpec((tokens, bw), column),
            pl.BlockSpec((start.shape[0], bw), column),
        ],
        out_specs=pl.BlockSpec((tokens, bw), column),
        out_shape=jax.ShapeDtypeStruct((tokens, part), BF),
        compiler_params=pltpu.CompilerParams(vmem_limit_bytes=GRANT),
    )(pre, rows, state, prod, start)


def recur_back_kernel(span, back, pre, rows, state, prod, start, gate, gelu, local, prods, sums):
    soft = rows[0:1]
    for i in range(back.shape[0] // span):
        here = pl.ds(i * span, span)
        act, slope = gelu_pair(pre[pl.ds(i * (span + HALO) + HALO, span)])
        states = state[here] + prod[here] * start[i : i + 1]
        gelu[here] = (back[here] * states * slope * rows[6:7]).astype(BF)
        _, _, decay, _, _ = gate_values(gate[here], soft)
        row = lax.broadcasted_iota(jnp.int32, decay.shape, 0)
        later = jnp.where(row < span - 1, pltpu.roll(decay, span - 1, 0), 1.0)
        later, adjoint = span_scan(later, back[here] * act, True)
        local[here] = adjoint
        prods[here] = later
        sums[i : i + 1] = decay[:1] * adjoint[:1]


def recur_back(back, pre, rows, state, prod, start, gate, bw, span):
    tokens, part = state.shape
    column = lambda h: (0, h)
    whole = pl.BlockSpec((tokens, bw), column)
    ends = pl.BlockSpec((start.shape[0], bw), column)
    return pl.pallas_call(
        functools.partial(recur_back_kernel, span),
        grid=(part // bw,),
        in_specs=[
            whole,
            pl.BlockSpec((pre.shape[0], bw), column),
            pl.BlockSpec((8, bw), column),
            whole,
            whole,
            ends,
            pl.BlockSpec((tokens, 2 * bw), column),
        ],
        out_specs=[whole, whole, whole, ends],
        out_shape=[
            jax.ShapeDtypeStruct((tokens, part), BF),
            jax.ShapeDtypeStruct((tokens, part), F32),
            jax.ShapeDtypeStruct((tokens, part), F32),
            jax.ShapeDtypeStruct(start.shape, F32),
        ],
        compiler_params=pltpu.CompilerParams(vmem_limit_bytes=GRANT),
    )(back, pre, rows, state, prod, start, gate)


def recur_grad_kernel(
    span, local, prods, carried, state, prod, start, gate, conv, pre, rows, block,
    blocks_out, lru_out, spill_out, rows_out, gate_grad, conv_grad,
):
    count = local.shape[0] // span
    soft, sig, own = rows[0:1], rows[1:2], rows[6:7]
    taps = [rows[k + 2 : k + 3] for k in range(4)]
    width = local.shape[1]
    add_up = lambda v: jnp.sum(v, axis=0, keepdims=True)
    decay_sum = jnp.zeros((1, width), F32)
    for i in range(count):
        here = pl.ds(i * span, span)
        adjoint = local[here] + prods[here] * carried[i : i + 1]
        states = state[here] + prod[here] * start[i : i + 1]
        row = lax.broadcasted_iota(jnp.int32, states.shape, 0)
        earlier = jnp.where(row >= 1, pltpu.roll(states, 1, 0), start[i : i + 1])
        rec_gate, in_gate, decay, square, root = gate_values(gate[here], soft)
        conv_vals = conv[here].astype(F32)
        drive = adjoint * conv_vals
        grad_log = adjoint * earlier * decay - drive * in_gate * square / root
        decay_sum = decay_sum + add_up(grad_log * rec_gate)
        gate_grad[here, :width] = (-RATE * soft * grad_log * rec_gate * (1.0 - rec_gate)).astype(BF)
        gate_grad[here, width:] = (drive * root * in_gate * (1.0 - in_gate)).astype(BF)
        conv_grad[here] = adjoint * root * in_gate
    blocks_out[...] = lax.dot_general(
        conv[...], gate_grad[...], (((0,), (0,)), ((), ())), preferred_element_type=F32
    )
    conv_grad[...] += dot_right_t(gate_grad[...], block[0])
    tap_sums = [jnp.zeros((1, width), F32) for _ in range(4)]
    for i in range(count):
        here = pl.ds(i * span, span)
        grad = conv_grad[here]
        vals = pre[pl.ds(i * (span + HALO), span + HALO)].astype(BF).astype(F32)
        wide = jnp.concatenate([jnp.zeros((HALO, width), F32), grad], axis=0)
        total = taps[0] * wide
        tap_sums[0] = tap_sums[0] + add_up(grad * vals[HALO:])
        for k in range(1, 4):
            total = total + taps[k] * pltpu.roll(wide, span + HALO - k, 0)
            tap_sums[k] = tap_sums[k] + add_up(grad * pltpu.roll(vals, k, 0)[HALO:])
        lru_out[here] = total[HALO:]
        spill_out[pl.ds(i * HALO, HALO)] = total[:HALO]
    rows_out[...] = jnp.zeros(rows_out.shape, F32)
    rows_out[0:1] = decay_sum * sig * own * RATE
    for k in range(4):
        rows_out[k + 1 : k + 2] = tap_sums[k] * own


def recur_grad(local, prods, carried, state, prod, start, gate, conv, pre, rows, block_mats, span):
    tokens, part = state.shape
    held, bw = block_mats.shape[:2]
    column = lambda h: (0, h)
    whole = pl.BlockSpec((tokens, bw), column)
    ends = pl.BlockSpec((start.shape[0], bw), column)
    return pl.pallas_call(
        functools.partial(recur_grad_kernel, span),
        grid=(held,),
        in_specs=[
            whole,
            whole,
            ends,
            whole,
            whole,
            ends,
            pl.BlockSpec((tokens, 2 * bw), column),
            whole,
            pl.BlockSpec((pre.shape[0], bw), lambda h: (0, held + h)),
            pl.BlockSpec((8, bw), column),
            pl.BlockSpec((1, bw, 2 * bw), lambda h: (h, 0, 0)),
        ],
        out_specs=[
            pl.BlockSpec((bw, 2 * bw), lambda h: (h, 0)),
            whole,
            pl.BlockSpec((start.shape[0] * HALO, bw), column),
            pl.BlockSpec((8, bw), column),
        ],
        out_shape=[
            jax.ShapeDtypeStruct((part, 2 * bw), F32),
            jax.ShapeDtypeStruct((tokens, part), F32),
            jax.ShapeDtypeStruct((start.shape[0] * HALO, part), F32),
            jax.ShapeDtypeStruct((8, part), F32),
        ],
        scratch_shapes=[pltpu.VMEM((tokens, 2 * bw), BF), pltpu.VMEM((tokens, bw), F32)],
        compiler_params=pltpu.CompilerParams(vmem_limit_bytes=GRANT),
    )(local, prods, carried, state, prod, start, gate, conv, pre, rows, block_mats)


def device(p, f=None, z=None, x=None, c=None):
    f, z = p.f if f is None else f, p.z if z is None else z
    x, c = p.x if x is None else x, p.c if c is None else c
    return (f, ((p.r * TP + z) * 2 + x) * 2 + c)


def copy_to(src, dst, sems, index, dev):
    return pltpu.make_async_remote_copy(
        src_ref=src,
        dst_ref=dst,
        send_sem=sems[0].at[index],
        recv_sem=sems[1].at[index],
        device_id=dev,
        device_id_type=MESH,
    )


def pairs(*shape):
    return [pltpu.SemaphoreType.DMA(shape), pltpu.SemaphoreType.DMA(shape)]


def greet(devices):
    barrier = pltpu.get_barrier_semaphore()
    for dev in devices:
        pl.semaphore_signal(barrier, inc=1, device_id=dev, device_id_type=MESH)
    pl.semaphore_wait(barrier, len(devices))


def by_rows(count, body, step=16):
    def turn(i, _):
        body(pl.ds(pl.multiple_of(i * step, step), step))
        return 0

    assert count % step == 0
    lax.fori_loop(0, count // step, turn, 0)


class Gather:
    def __init__(self, p, out, ups, downs):
        self.p, self.out, self.ups, self.downs = p, out, ups, downs
        self.up = device(p, z=jnp.minimum(p.z + 1, TP - 1))
        self.down = device(p, z=jnp.maximum(p.z - 1, 0))

    def begin(self, h, src):
        z = self.p.z

        @pl.when(z < TP - 1)
        def _():
            copy_to(src, self.out.at[z, h], self.ups, (0, h), self.up).start()

        @pl.when(z > 0)
        def _():
            copy_to(src, self.out.at[z, h], self.downs, (0, h), self.down).start()

    def step(self, k, h):
        z, out = self.p.z, self.out

        @pl.when(z >= k)
        def _():
            block = out.at[z - k, h]
            copy_to(block, block, self.ups, (k - 1, h), self.up).wait_recv()
            if k < TP - 1:

                @pl.when(z < TP - 1)
                def _():
                    copy_to(block, block, self.ups, (k, h), self.up).start()

        @pl.when(z <= TP - 1 - k)
        def _():
            block = out.at[z + k, h]
            copy_to(block, block, self.downs, (k - 1, h), self.down).wait_recv()
            if k < TP - 1:

                @pl.when(z > 0)
                def _():
                    copy_to(block, block, self.downs, (k, h), self.down).start()

    def close(self, halves):
        z, block = self.p.z, self.out.at[0, 0]
        for h in range(halves):
            for k in range(TP - 1):

                @pl.when((z >= k) & (z < TP - 1))
                def _():
                    copy_to(block, block, self.ups, (k, h), self.up).wait_send()

                @pl.when((z <= TP - 1 - k) & (z > 0))
                def _():
                    copy_to(block, block, self.downs, (k, h), self.down).wait_send()


class LineSum:
    def __init__(self, p, parts, scratch):
        self.p, self.parts = p, parts
        self.got_up, self.got_down, self.out_up, self.out_down = scratch[:4]
        self.ups, self.downs = scratch[4:6], scratch[6:8]
        self.halves, self.rows = parts.shape[1:3]
        self.up = device(p, z=jnp.minimum(p.z + 1, TP - 1))
        self.down = device(p, z=jnp.maximum(p.z - 1, 0))

    @staticmethod
    def scratch(parts):
        block = parts[1:]
        return [
            pltpu.VMEM((TP - 1,) + block, BF),
            pltpu.VMEM((TP - 1,) + block, BF),
            pltpu.VMEM((TP - 2,) + block, BF),
            pltpu.VMEM((TP - 2,) + block, BF),
            *pairs(TP - 1, parts[1]),
            *pairs(TP - 1, parts[1]),
        ]

    def clear(self):
        z = self.p.z

        @pl.when(z == 0)
        def _():
            for h in range(self.halves):
                by_rows(self.rows, lambda at: self.fill(self.got_up, h, at))

        @pl.when(z == TP - 1)
        def _():
            for h in range(self.halves):
                by_rows(self.rows, lambda at: self.fill(self.got_down, h, at))

    def fill(self, ref, h, at):
        ref[0, h, at] = jnp.zeros((at.size, ref.shape[-1]), BF)

    def one_way(self, k, h, place, block, got, out, sems, dev):
        @pl.when(place == 0)
        def _():
            copy_to(self.parts.at[block, h], got.at[k - 1, h], sems, (k - 1, h), dev).start()

        if k < TP - 1:

            @pl.when((place >= 1) & (place + k <= TP - 1))
            def _():
                copy_to(got.at[k, h], got.at[k, h], sems, (k, h), dev).wait_recv()

                def add(at):
                    total = self.parts[block, h, at].astype(F32) + got[k, h, at].astype(F32)
                    out[k - 1, h, at] = total.astype(BF)

                by_rows(self.rows, add)
                copy_to(out.at[k - 1, h], got.at[k - 1, h], sems, (k - 1, h), dev).start()

    def step(self, k, h):
        z = self.p.z
        block = jnp.minimum(z + k, TP - 1)
        self.one_way(k, h, z, block, self.got_up, self.out_up, self.ups, self.up)
        block = jnp.maximum(z - k, 0)
        self.one_way(k, h, TP - 1 - z, block, self.got_down, self.out_down, self.downs, self.down)

    def arrive(self, h):
        z = self.p.z

        @pl.when(z >= 1)
        def _():
            got = self.got_up.at[0, h]
            copy_to(got, got, self.ups, (0, h), self.up).wait_recv()

        @pl.when(z <= TP - 2)
        def _():
            got = self.got_down.at[0, h]
            copy_to(got, got, self.downs, (0, h), self.down).wait_recv()

    def total(self, h, at):
        total = self.parts[self.p.z, h, at].astype(F32) + self.got_up[0, h, at].astype(F32)
        return total + self.got_down[0, h, at].astype(F32)

    def close(self):
        z, got = self.p.z, self.got_up.at[0, 0]
        for h in range(self.halves):
            for k in range(1, TP):

                @pl.when(z + k <= TP - 1)
                def _():
                    copy_to(got, got, self.ups, (k - 1, h), self.up).wait_send()

                @pl.when(z - k >= 0)
                def _():
                    copy_to(got, got, self.downs, (k - 1, h), self.down).wait_send()


def greet_line(p, others=()):
    barrier = pltpu.get_barrier_semaphore()
    for dev in others:
        pl.semaphore_signal(barrier, inc=1, device_id=dev, device_id_type=MESH)

    @pl.when(p.z > 0)
    def _():
        pl.semaphore_signal(barrier, inc=1, device_id=device(p, z=p.z - 1), device_id_type=MESH)

    @pl.when(p.z < TP - 1)
    def _():
        pl.semaphore_signal(barrier, inc=1, device_id=device(p, z=p.z + 1), device_id_type=MESH)

    inner = (p.z > 0) & (p.z < TP - 1)

    @pl.when(inner)
    def _():
        pl.semaphore_wait(barrier, len(others) + 2)

    @pl.when(jnp.logical_not(inner))
    def _():
        pl.semaphore_wait(barrier, len(others) + 1)


class Spread:
    KINDS = ((0, 0), (0, 1), (1, 0), (1, 1))

    def __init__(self, p, whole, sems):
        self.p, self.whole, self.started = p, whole, []
        self.xs, self.fs, self.gs, self.cs = sems[0:2], sems[2:4], sems[4:6], sems[6:8]
        self.to_x, self.to_f = device(p, x=1 - p.x), device(p, f=1 - p.f)
        self.to_c = device(p, c=1 - p.c)

    @staticmethod
    def scratch():
        return [*pairs(TP), *pairs(TP), *pairs(TP), *pairs(4, TP)]

    def slot(self, kind, d, other_core=False):
        p, (f, x) = self.p, self.KINDS[kind]
        c = 1 - p.c if other_core else p.c
        return self.whole.at[(p.f + f) % 2, 0, (p.z - d) % TP, (p.x + x) % 2, c]

    def send(self, src, dst, sems, index, dev):
        copy = copy_to(src, dst, sems, index, dev)
        copy.start()
        self.started.append(copy)

    def wait(self, ref, sems, index):
        copy_to(ref, ref, sems, index, self.to_x).wait_recv()

    def spread(self, d, src=None):
        dst = self.slot(0, d)
        src = dst if src is None else src
        self.send(src, dst, self.xs, (d,), self.to_x)
        self.send(src, dst, self.fs, (d,), self.to_f)
        self.send(src, dst, self.cs, (0, d), self.to_c)

    def sides(self, d):
        ref = self.slot(1, d)
        self.wait(ref, self.xs, (d,))
        if d % 2 == 0:
            self.send(ref, ref, self.gs, (d,), self.to_f)
        self.send(ref, ref, self.cs, (1, d), self.to_c)
        ref = self.slot(2, d)
        self.wait(ref, self.fs, (d,))
        if d % 2 == 1:
            self.send(ref, ref, self.gs, (d,), self.to_x)
        self.send(ref, ref, self.cs, (2, d), self.to_c)

    def corner(self, d):
        ref = self.slot(3, d)
        self.wait(ref, self.gs, (d,))
        self.send(ref, ref, self.cs, (3, d), self.to_c)

    def close(self, pieces):
        for kind in range(4):
            for d in pieces:
                self.wait(self.slot(kind, d, True), self.cs, (kind, d))
        for copy in self.started:
            copy.wait_send()


def intake_kernel(sizes, *refs):
    heads, bw, part, ffw_part = sizes
    gelu, lru, out_t, blocks, small, gate, up, down_t, x_p = refs[:9]
    mix_w, ffw_w, x_all, piece_2, piece_3 = refs[9:14]
    zs, zr, us, ur, vs, vr, local = refs[14:21]
    p = Place()
    mix, ffw = Spread(p, mix_w, refs[21:29]), Spread(p, ffw_w, refs[29:])
    to_z = [device(p, z=(p.z + d) % TP) for d in range(TP)]
    greet(to_z[1:] + [mix.to_x, mix.to_f, mix.to_c])
    started, stays = [], []

    def mix_sources(z):
        cols = pl.ds(pl.multiple_of(z * heads // TP * bw, 128), part)
        return [gelu.at[:, cols], lru.at[:, cols], out_t.at[:, cols], blocks, small]

    def ffw_sources(z):
        cols = pl.ds(pl.multiple_of(z * ffw_part, 128), ffw_part)
        return [gate.at[:, cols], up.at[:, cols], down_t.at[:, cols]]

    def targets(spread, sources):
        place = (p.f, 0, p.z, p.x, p.c, slice(None))
        found, offset = [], 0
        for source in sources:
            found.append(spread.whole.at[(*place, pl.ds(offset, source.shape[1]))])
            offset += source.shape[1]
        return found

    def along_z(m, d):
        sources = (mix_sources, ffw_sources)[m]((p.z + d) % TP)
        for i, (src, dst) in enumerate(zip(sources, targets((mix, ffw)[m], sources))):
            copy = copy_to(src, dst, (zs, zr), (m, d - 1, i), to_z[d])
            copy.start()
            started.append(copy)

    def from_z(m, d):
        sources = (mix_sources, ffw_sources)[m](p.z)
        offset = 0
        for i, source in enumerate(sources):
            place = (p.f, 0, (p.z - d) % TP, p.x, p.c, slice(None))
            ref = (mix, ffw)[m].whole.at[(*place, pl.ds(offset, source.shape[1]))]
            copy_to(ref, ref, (zs, zr), (m, d - 1, i), to_z[1]).wait_recv()
            offset += source.shape[1]

    def stay(src, dst):
        copy = pltpu.make_async_copy(src, dst, local.at[len(stays)])
        copy.start()
        stays.append(copy)

    for d in (1, 3, 2):
        along_z(0, d)
    for m, sources in enumerate((mix_sources(p.z), ffw_sources(p.z))):
        for src, dst in zip(sources, targets((mix, ffw)[m], sources)):
            stay(src, dst)
    first = len(stays)
    for copy in stays:
        copy.wait()
    mix.spread(0)
    ffw.spread(0)
    stay(x_p, x_all.at[p.z, 0])
    for d, piece in ((2, piece_2), (3, piece_3)):
        for i, src in enumerate(ffw_sources((p.z + d) % TP)):
            stay(src, piece.at[:, pl.ds(i * ffw_part, ffw_part)])
    line = Gather(p, x_all, (us, ur), (vs, vr))
    for d in (1, 3, 2):
        from_z(0, d)
        mix.spread(d)
    line.begin(0, x_p)
    along_z(1, 1)
    mix.sides(0)
    ffw.sides(0)
    mix.corner(0)
    line.step(1, 0)
    for d in (1, 3):
        mix.sides(d)
    ffw.corner(0)
    line.step(2, 0)
    for d in (1, 3):
        mix.corner(d)
    mix.sides(2)
    line.step(3, 0)
    mix.corner(2)
    from_z(1, 1)
    mix.close(range(TP))
    ffw.close((0,))
    for copy in started:
        copy.wait_send()
    line.close(1)
    for copy in stays[first:]:
        copy.wait()


def intake(weights, x_p, bw, p):
    rows, lru_width = weights[0].shape
    heads = lru_width // bw
    part, ffw_part = -(-heads // TP) * bw, weights[5].shape[1] // TP
    mix_cols = 3 * part + weights[3].shape[1] + weights[4].shape[1]
    whole = lambda cols: jax.ShapeDtypeStruct((p.fs, 1, TP, 2, 2, rows, cols), BF)
    piece = jax.ShapeDtypeStruct((rows, 3 * ffw_part), BF)
    mix_w, ffw_w, x_all, piece_2, piece_3 = pl.pallas_call(
        functools.partial(intake_kernel, (heads, bw, part, ffw_part)),
        in_specs=[ANY] * 9,
        out_specs=[ANY] * 5,
        out_shape=[
            whole(mix_cols),
            whole(3 * ffw_part),
            jax.ShapeDtypeStruct((TP, 1) + x_p.shape, BF),
            piece,
            piece,
        ],
        scratch_shapes=[
            *pairs(2, TP - 1, 5),
            *pairs(TP - 1, 1),
            *pairs(TP - 1, 1),
            pltpu.SemaphoreType.DMA((15,)),
            *Spread.scratch(),
            *Spread.scratch(),
        ],
        compiler_params=pltpu.CompilerParams(collective_id=0, has_side_effects=True),
    )(*weights, x_p)
    return mix_w.reshape(-1, mix_cols), ffw_w, x_all[:, 0], piece_2, piece_3


def middle_kernel(with_ffw, *refs):
    parts, x_zero, gain, cot_p, piece_2, piece_3, _ = refs[:7]
    x_one, ffw_all, cot_all, ffw_w, own, local, gu0, gu1, gd0, gd1, cu0, cu1, cd0, cd1 = refs[7:21]
    p = Place()
    line = LineSum(p, parts, refs[21:29])
    out = Gather(p, ffw_all, (gu0, gu1), (gd0, gd1))
    cot = Gather(p, cot_all, (cu0, cu1), (cd0, cd1))
    halves, rows = parts.shape[1:3]
    line.clear()
    stays = []

    def stay(src, dst):
        copy = pltpu.make_async_copy(src, dst, local.at[len(stays)])
        copy.start()
        stays.append(copy)

    if with_ffw:
        ffw = Spread(p, ffw_w, refs[29:])
        greet_line(p, (ffw.to_x, ffw.to_f, ffw.to_c))
        stay(piece_3, ffw.slot(0, 3))
        stay(piece_2, ffw.slot(0, 2))
    else:
        greet_line(p)
    side = lambda name, *args: getattr(ffw, name)(*args) if with_ffw else None
    for h in range(halves):
        line.step(TP - 1, h)
    side("spread", 1)
    side("spread", 3, piece_3)
    side("spread", 2, piece_2)
    for k in range(TP - 2, 0, -1):
        for h in range(halves):
            line.step(k, h)
    for h in range(halves):
        line.arrive(h)

        def finish(at, h=h):
            value = x_zero[h, at].astype(F32) + line.total(h, at)
            x_one[h, at] = value
            own[h, at] = normed(value, gain[...]).astype(BF)

        by_rows(rows, finish)
        out.begin(h, own.at[h])
        stay(own.at[h], ffw_all.at[p.z, h])
    cot.begin(0, cot_p)
    stay(cot_p, cot_all.at[p.z, 0])
    for h in range(halves):
        out.step(1, h)
    for d in (1, 3, 2):
        side("sides", d)
    for h in range(halves):
        out.step(2, h)
    cot.step(1, 0)
    for h in range(halves):
        out.step(3, h)
    cot.step(2, 0)
    for d in (1, 3, 2):
        side("corner", d)
    cot.step(3, 0)
    side("close", (1, 2, 3))
    line.close()
    out.close(halves)
    cot.close(1)
    for copy in stays:
        copy.wait()


def middle(parts, x_zero, gain, cot_p, piece_2, piece_3, ffw_w):
    shape = parts.shape
    with_ffw = ffw_w is not None
    if not with_ffw:
        piece_2 = piece_3 = ffw_w = jnp.zeros((16, 128), BF)
    return pl.pallas_call(
        functools.partial(middle_kernel, with_ffw),
        in_specs=[VMEM] * 3 + [ANY] * 4,
        out_specs=[VMEM, ANY, ANY, ANY],
        out_shape=[
            jax.ShapeDtypeStruct(shape[1:], F32),
            jax.ShapeDtypeStruct(shape, BF),
            jax.ShapeDtypeStruct((TP, 1) + cot_p.shape, BF),
            jax.ShapeDtypeStruct(ffw_w.shape, BF),
        ],
        input_output_aliases={6: 3},
        scratch_shapes=[
            pltpu.VMEM(shape[1:], BF),
            pltpu.SemaphoreType.DMA((shape[1] + 3,)),
            *pairs(TP - 1, shape[1]),
            *pairs(TP - 1, shape[1]),
            *pairs(TP - 1, 1),
            *pairs(TP - 1, 1),
            *LineSum.scratch(shape),
            *(Spread.scratch() if with_ffw else []),
        ],
        compiler_params=pltpu.CompilerParams(
            collective_id=1, has_side_effects=True, vmem_limit_bytes=GRANT
        ),
    )(parts, x_zero, gain, cot_p, piece_2, piece_3, ffw_w)


def norm_back(values, gain, grad):
    inv = lax.rsqrt(jnp.mean(values * values, axis=-1, keepdims=True) + EPS)
    unit = values * inv
    through = grad * gain
    inner = jnp.mean(through * unit, axis=-1, keepdims=True)
    return inv * (through - unit * inner), grad * unit


class Fold:
    ORDER = ((0, 1, 1), (1, 1, 1), (0, 0, 1), (1, 1, 0), (0, 1, 0), (1, 0, 1), (0, 0, 0), (1, 0, 0))

    def __init__(self, p, grad, cores, scratch):
        self.p, self.grad, self.cores = p, grad, cores
        self.sums, self.stage, self.got, self.got_late = scratch[:4]
        self.near, self.staged = scratch[4:6]
        self.core_sems, self.early, self.late = scratch[6:8], scratch[8:10], scratch[10:12]
        self.to = (device(p, x=1 - p.x), device(p, f=1 - p.f))
        self.to_c = device(p, c=1 - p.c)

    @staticmethod
    def shapes(grad, staged):
        block = (TP // 2,) + grad.shape[-2:]
        waiting = (2,) if staged else (2, 2, 2)
        return jax.ShapeDtypeStruct((2, 2, 2) + block, BF), [
            pltpu.VMEM((2, 2, 2) + block, BF),
            pltpu.VMEM(waiting + block, BF),
            pltpu.VMEM((2, 2) + block, BF),
            pltpu.VMEM((2,) + block, BF),
            pltpu.SemaphoreType.DMA((8,)),
            pltpu.SemaphoreType.DMA((2,)),
            *pairs(8),
            *pairs(2, 2),
            *pairs(2),
        ]

    def block(self, way, f_rel, x_rel, c):
        p, half = self.p, TP // 2
        f, x = (p.f + f_rel) % 2, (p.x + x_rel) % 2
        return self.grad.at[f, 0, pl.ds(way * half, half), x, c]

    def cross(self, i):
        name = self.ORDER[i]
        src = self.block(*name, 1 - self.p.c)
        dst = self.stage if self.cores is None else self.cores
        return copy_to(src, dst.at[name], self.core_sems, (i,), self.to_c)

    def load(self, i):
        name = self.ORDER[i]
        return pltpu.make_async_copy(
            self.block(*name, self.p.c), self.sums.at[name], self.near.at[i]
        )

    def fetch(self, i):
        src = self.cores.at[self.ORDER[i]]
        return pltpu.make_async_copy(src, self.stage.at[i % 2], self.staged.at[i % 2])

    def first(self, way, block):
        src = self.sums.at[(0, block, 1) if way == 0 else (1, 1, block)]
        return copy_to(src, self.got.at[way, block], self.early, (way, block), self.to[way])

    def second(self, way):
        src = self.sums.at[(0, 1, 0) if way == 0 else (1, 0, 1)]
        return copy_to(src, self.got_late.at[way], self.late, (way,), self.to[1 - way])

    def add(self, name, *others):
        rows = self.sums.shape[-2]

        def turn(at):
            for k in range(TP // 2):
                total = self.sums[(*name, k, at)].astype(F32)
                for other in others:
                    total = total + other[k, at].astype(F32)
                self.sums[(*name, k, at)] = total.astype(BF)

        by_rows(rows, turn)

    def begin(self):
        for i in range(8):
            self.cross(i).start()
            self.load(i).start()

    def issue(self, i):
        self.cross(i).wait_recv()
        self.fetch(i).start()

    def join(self, i):
        if self.cores is None:
            self.cross(i).wait_recv()
            self.load(i).wait()
            self.add(self.ORDER[i], self.stage.at[self.ORDER[i]])
        else:
            if i == 0:
                self.issue(0)
            if i + 1 < 8:
                self.issue(i + 1)
            self.fetch(i).wait()
            self.load(i).wait()
            self.add(self.ORDER[i], self.stage.at[i % 2])
        if i < 4:
            way = self.ORDER[i][0]
            self.first(way, self.ORDER[i][1 + way]).start()

    def middle(self):
        for way in range(2):
            self.first(way, 1).wait_recv()
            self.add((0, 1, 0) if way == 0 else (1, 0, 1), self.got.at[way, 1])
            self.second(way).start()

    def finish(self):
        for way in range(2):
            self.first(way, 0).wait_recv()
            self.second(way).wait_recv()
            self.add((way, 0, 0), self.got.at[way, 0], self.got_late.at[way])

    def result(self, z):
        return self.sums.at[z // (TP // 2), 0, 0, z % (TP // 2)]

    def close(self):
        for i in range(8):
            self.cross(i).wait_send()
        for way in range(2):
            self.second(way).wait_send()
            for block in range(2):
                self.first(way, block).wait_send()


def folds_of(p, grads, cores, scratch):
    return [Fold(p, g, c, scratch[12 * i : 12 * i + 12]) for i, (g, c) in enumerate(zip(grads, cores))]


def turn_kernel(count, *refs):
    parts, out_parts, x_one, cot, gain = refs[:5]
    grads, refs = refs[5 : 5 + count], refs[5 + count :]
    mixed_out, grad_x_one, grad_gain, mix_all = refs[:4]
    pieces, cores, refs = refs[4 : 4 + TP], refs[4 + TP : 4 + TP + count], refs[4 + TP + count :]
    own, local, gu0, gu1, gd0, gd1 = refs[:6]
    p = Place()
    line, late = LineSum(p, parts, refs[6:14]), LineSum(p, out_parts, refs[14:22])
    folds = folds_of(p, grads, cores, refs[22:])
    out = Gather(p, mix_all, (gu0, gu1), (gd0, gd1))
    halves, rows = parts.shape[1:3]
    line.clear()
    late.clear()
    greet_line(p, (*folds[0].to, folds[0].to_c) if folds else ())
    for fold in folds:
        fold.begin()
    for h in range(halves):
        line.step(TP - 1, h)
    for h in range(halves):
        late.step(TP - 1, h)
    for fold in folds:
        fold.join(0)
        fold.join(1)
    for k in range(TP - 2, 0, -1):
        for h in range(halves):
            line.step(k, h)
        for fold in folds:
            fold.join(4 - k)
    stays = []

    def stay(src, dst):
        copy = pltpu.make_async_copy(src, dst, local.at[len(stays)])
        copy.start()
        stays.append(copy)

    grad_gain[...] = jnp.zeros(grad_gain.shape, F32)
    for h in range(halves):
        line.arrive(h)

        def finish(at, h=h):
            grad, gains = norm_back(x_one[h, at], gain[...], line.total(h, at))
            grad = grad + cot[h, at].astype(F32)
            grad_x_one[h, at] = grad
            own[h, at] = grad.astype(BF)
            grad_gain[0:1] += jnp.sum(gains, axis=0, keepdims=True)

        by_rows(rows, finish)
        out.begin(h, own.at[h])
        stay(own.at[h], mix_all.at[p.z, h])
    for fold in folds:
        for i in range(4, 8):
            fold.join(i)
    for h in range(halves):
        out.step(1, h)
        late.step(2, h)
    for fold in folds:
        fold.middle()
    for h in range(halves):
        out.step(2, h)
        late.step(1, h)
    for h in range(halves):
        out.step(3, h)
    for h in range(halves):
        late.arrive(h)

        def store(at, h=h):
            mixed_out[h, at] = (x_one[h, at] + late.total(h, at)).astype(BF)

        by_rows(rows, store)
    offset = 0
    for fold in folds:
        fold.finish()
        cols = fold.grad.shape[-1]
        for d in range(TP):
            stay(fold.result((p.z + d) % TP), pieces[d].at[:, pl.ds(offset, cols)])
        offset += cols
    for fold in folds:
        fold.close()
    line.close()
    late.close()
    out.close(halves)
    for copy in stays:
        copy.wait()


def turn(parts, out_parts, x_one, cot, gain, grads):
    shape, count = parts.shape, len(grads)
    folded = [Fold.shapes(grad, True) for grad in grads]
    rows = grads[0].shape[-2] if grads else 16
    piece = jax.ShapeDtypeStruct((rows, sum(g.shape[-1] for g in grads) if grads else 128), BF)
    results = pl.pallas_call(
        functools.partial(turn_kernel, count),
        in_specs=[VMEM] * 5 + [ANY] * count,
        out_specs=[VMEM, VMEM, VMEM, ANY] + [ANY] * (TP + count),
        out_shape=[
            jax.ShapeDtypeStruct(shape[1:], BF),
            jax.ShapeDtypeStruct(shape[1:], F32),
            jax.ShapeDtypeStruct((8, shape[-1]), F32),
            jax.ShapeDtypeStruct(shape, BF),
            *[piece] * TP,
            *(cores for cores, _ in folded),
        ],
        scratch_shapes=[
            pltpu.VMEM(shape[1:], BF),
            pltpu.SemaphoreType.DMA((shape[1] + TP * count,)),
            *pairs(TP - 1, shape[1]),
            *pairs(TP - 1, shape[1]),
            *LineSum.scratch(shape),
            *LineSum.scratch(shape),
            *(item for _, scratch in folded for item in scratch),
        ],
        compiler_params=pltpu.CompilerParams(
            collective_id=2, has_side_effects=True, vmem_limit_bytes=GRANT
        ),
    )(parts, out_parts, x_one, cot, gain, *grads)
    return results[: 4 + TP]


def final_kernel(count, *refs):
    parts, x_zero, gain, grad_x_one, vectors = refs[:5]
    grads, refs = refs[5 : 5 + count], refs[5 + count :]
    grad_in, sums = refs[:2]
    outs, cores, refs = refs[2 : 2 + count], [None] * count, refs[2 + count :]
    acc, got, vs, vr, zs, zr, local = refs[:7]
    p = Place()
    line = LineSum(p, parts, refs[7:15])
    folds = folds_of(p, grads, cores, refs[15:])
    halves, rows = parts.shape[1:3]
    line.clear()
    to_z = [device(p, z=(p.z + d) % TP) for d in range(TP)]
    (to_x, to_f), to_c = folds[0].to, folds[0].to_c
    greet(to_z[1:] + [to_x, to_f, to_c])
    partners = [to_c, to_x, to_f] + [
        device(p, z=p.z + bit * (1 - 2 * (p.z // bit % 2))) for bit in (1, 2)
    ]

    def vector(i):
        return copy_to(acc.at[i], got.at[i], (vs, vr), (i,), partners[i])

    def next_vector(i):
        vector(i).wait_recv()
        if i < 4:
            acc[i + 1] = acc[i] + got[i]
            vector(i + 1).start()
        else:
            sums[...] = acc[i] + got[i]

    acc[0] = vectors[...]
    vector(0).start()
    for fold in folds:
        fold.begin()
    for h in range(halves):
        line.step(TP - 1, h)
    started, stays = [], []

    def send_on(m):
        folds[m].finish()
        for d in (1, 3, 2):
            src = folds[m].result((p.z + d) % TP)
            copy = copy_to(src, outs[m].at[p.z], (zs, zr), (m, d - 1), to_z[d])
            copy.start()
            started.append(copy)
        stays.append(pltpu.make_async_copy(folds[m].result(p.z), outs[m].at[p.z], local.at[m]))
        stays[-1].start()

    for i in range(4):
        folds[0].join(i)
    for m, fold in enumerate(folds):
        fold.join(4)
        fold.join(5)
        if m + 1 < count:
            folds[m + 1].join(0)
            folds[m + 1].join(1)
        fold.middle()
        if m + 1 < count:
            folds[m + 1].join(2)
            folds[m + 1].join(3)
        fold.join(6)
        fold.join(7)
        if m < TP - 2:
            for h in range(halves):
                line.step(TP - 2 - m, h)
        next_vector(m)
        if m > 0:
            send_on(m - 1)
    next_vector(3)
    for h in range(halves):
        line.arrive(h)

        def finish(at, h=h):
            grad, _ = norm_back(x_zero[h, at].astype(F32), gain[...], line.total(h, at))
            grad_in[h, at] = grad_x_one[h, at] + grad

        by_rows(rows, finish)
    next_vector(4)
    send_on(count - 1)
    for m in range(count):
        for d in range(1, TP):
            ref = outs[m].at[(p.z - d) % TP]
            copy_to(ref, ref, (zs, zr), (m, d - 1), to_z[1]).wait_recv()
    for copy in started:
        copy.wait_send()
    for i in range(5):
        vector(i).wait_send()
    for fold in folds:
        fold.close()
    line.close()
    for copy in stays:
        copy.wait()


def final(parts, x_zero, gain, grad_x_one, vectors, grads):
    shape, count = parts.shape, len(grads)
    folded = [Fold.shapes(grad, False) for grad in grads]
    results = pl.pallas_call(
        functools.partial(final_kernel, count),
        in_specs=[VMEM] * 5 + [ANY] * count,
        out_specs=[VMEM, VMEM] + [ANY] * count,
        out_shape=[
            jax.ShapeDtypeStruct(shape[1:], F32),
            jax.ShapeDtypeStruct(vectors.shape, F32),
            *(jax.ShapeDtypeStruct((TP,) + grad.shape[-2:], BF) for grad in grads),
        ],
        scratch_shapes=[
            pltpu.VMEM((5,) + vectors.shape, F32),
            pltpu.VMEM((5,) + vectors.shape, F32),
            *pairs(5),
            *pairs(count, TP - 1),
            pltpu.SemaphoreType.DMA((count,)),
            *LineSum.scratch(shape),
            *(item for _, scratch in folded for item in scratch),
        ],
        compiler_params=pltpu.CompilerParams(
            collective_id=3, has_side_effects=True, vmem_limit_bytes=GRANT
        ),
    )(parts, x_zero, gain, grad_x_one, vectors, *grads)
    return results[0], results[1], results[2 : 2 + count]


def chain_kernel(backward, sums, *refs):
    if backward:
        known, start, spans, send, recv = refs
    else:
        start, spans, send, recv = refs
    p = Place()
    peers = [device_q(p, (p.q + d) % NQ) for d in range(NQ)]
    greet(peers[1:])
    spans[p.q] = sums[...]
    copies = []
    for d in range(1, NQ):
        copies.append(copy_to(spans.at[p.q], spans.at[p.q], (send, recv), (d,), peers[d]))
        copies[-1].start()
    for d in range(1, NQ):
        ref = spans.at[(p.q - d) % NQ]
        copy_to(ref, ref, (send, recv), (d,), peers[d]).wait_recv()
    micro = sums.shape[1] // TP
    carry = jnp.zeros((micro, sums.shape[2]), F32)
    order = [(z, q) for z in range(TP) for q in range(NQ)]
    for z, q in reversed(order) if backward else order:
        here = slice(z * micro, (z + 1) * micro)

        @pl.when(p.q == q)
        def _(carry=carry, here=here):
            start[here] = carry

        decay = known[q, 0, here] if backward else spans[q, 0, here]
        carry = decay * carry + spans[q, 0 if backward else 1, here]
    for copy in copies:
        copy.wait_send()


def device_q(p, q):
    return device(p, x=q // 2, c=q % 2)


def chain(sums, known=None):
    backward = known is not None
    every = (NQ,) + sums.shape
    return pl.pallas_call(
        functools.partial(chain_kernel, backward),
        in_specs=[VMEM] * (2 if backward else 1),
        out_specs=[VMEM, VMEM],
        out_shape=[
            jax.ShapeDtypeStruct(sums.shape[1:], F32),
            jax.ShapeDtypeStruct(every, F32),
        ],
        scratch_shapes=pairs(NQ),
        compiler_params=pltpu.CompilerParams(
            collective_id=5 if backward else 4, has_side_effects=True
        ),
    )(*((sums, known) if backward else (sums,)))


def unpack_kernel(own, one, two, three, *outs):
    p = Place()
    part = own.shape[1] // len(outs)
    for d, piece in enumerate((own, one, two, three)):
        cols = pl.ds(pl.multiple_of((p.z - d) % TP * part, 128), part)
        for i, out in enumerate(outs):
            out[:, cols] = piece[:, i * part : (i + 1) * part].astype(F32)


def unpack(pieces, count):
    rows, cols = pieces[0].shape
    return pl.pallas_call(
        unpack_kernel,
        in_specs=[VMEM] * TP,
        out_specs=[VMEM] * count,
        out_shape=[jax.ShapeDtypeStruct((rows, cols // count * TP), F32)] * count,
        compiler_params=pltpu.CompilerParams(vmem_limit_bytes=GRANT),
    )(*pieces)


def geglu(gate_vals, up_vals):
    return jax.nn.gelu(gate_vals) * up_vals


def all_spans(value, p):
    by_q = everywhere(value, shift_q, p.q, NQ)
    by_r = everywhere(by_q, shift_r, p.r, p.rests)
    return jnp.swapaxes(by_r, 1, 2).reshape((-1,) + value.shape[1:])


def own_spans(spans, p):
    split = spans.reshape((p.rests, TP, NQ) + spans.shape[1:])
    return lax.dynamic_index_in_dim(at(split, p.r), p.q, 1, keepdims=False)


def on_device(
    inputs,
    cotangent,
    proj_gelu,
    proj_lru,
    gate_blocks,
    proj_out,
    ffw_gate,
    ffw_up,
    ffw_down,
    norm_mix,
    norm_ffw,
    decay_param,
    conv_taps,
):
    p = Place()
    micro, span, width = inputs.shape[0], inputs.shape[2], inputs.shape[3]
    lru_width = proj_gelu.shape[1]
    tap_count = conv_taps.shape[1]
    block_width = gate_blocks.shape[1] // 2
    heads = lru_width // block_width
    ffw_part = ffw_gate.shape[1] // TP
    rows = proj_gelu.shape[0]
    held = -(-heads // TP)
    first = [k * heads // TP for k in range(TP)]
    owned = [range(first[k], first[k + 1] if k + 1 < TP else heads) for k in range(TP)]
    part = held * block_width

    out_t, down_t = proj_out.T, ffw_down.T
    small = jnp.concatenate([norm_mix[None], norm_ffw[None], decay_param[None], conv_taps.T])
    small = jnp.pad(small, ((0, 128 - small.shape[0]), (0, 0))).T
    x_rows, cot = inputs[:, 0], cotangent[:, 0]
    one = 1 if p.rests == 1 else 0
    edge = lax.ppermute(
        x_rows[:, span - (tap_count - 1) :],
        "seq",
        [(i, i + 1) for i in range(lax.axis_size("seq") - 1)],
    )
    pad = jnp.zeros((micro, HALO - (tap_count - 1), width), BF)
    x_wide = jnp.concatenate([pad, edge, x_rows], axis=1)
    if p.rests == 1:
        weights = (proj_gelu, proj_lru, out_t, gate_blocks, small, ffw_gate, ffw_up, down_t)
        mix_w, ffw_w, x_all, piece_2, piece_3 = intake(
            weights, x_wide.reshape(-1, width), block_width, p
        )
        piece_3, piece_2 = shift_z(piece_3, 3), shift_z(piece_2, 2)
    else:
        mix_pieces, ffw_pieces = [], []
        for k in range(TP):
            cols = slice(first[k] * block_width, first[k] * block_width + part)
            pieces = [proj_gelu[:, cols], proj_lru[:, cols], out_t[:, cols], gate_blocks, small]
            mix_pieces.append(jnp.concatenate(pieces, axis=1))
            cols = slice(k * ffw_part, (k + 1) * ffw_part)
            pieces = [ffw_gate[:, cols], ffw_up[:, cols], down_t[:, cols]]
            ffw_pieces.append(jnp.concatenate(pieces, axis=1))
        mix_w = weights_in(jnp.stack(mix_pieces), p)
        whole_ffw = weights_in(jnp.stack(ffw_pieces), p)
        x_all, piece_2, piece_3, ffw_w = gather_z(x_wide, p), None, None, None
    x_all = x_all.reshape(TP, micro, HALO + span, width)

    gelu_lru_w = mix_w[:, : 2 * part]
    out_w = mix_w[:, 2 * part : 3 * part]
    small_w = dot_right_t(jnp.eye(8, 128, dtype=BF), mix_w[:, 3 * part + 2 * block_width :])
    mix_gain, ffw_gain = small_w[0:1], small_w[1:2]
    start = sum(jnp.where(p.z == k, first[k] * block_width, 0) for k in range(TP))
    feature = jnp.arange(part) + start
    low = sum(jnp.where(p.z == k, owned[k][0] * block_width, 0) for k in range(TP))
    high = sum(jnp.where(p.z == k, (owned[k][-1] + 1) * block_width, 0) for k in range(TP))
    is_own = ((feature >= low) & (feature < high)).astype(F32)[None]
    own_part = lax.dynamic_slice_in_dim(small_w[2 : 3 + tap_count], start, part, 1)
    decay_f = own_part[:1]
    rows_w = jnp.concatenate(
        [jax.nn.softplus(-decay_f), jax.nn.sigmoid(-decay_f), own_part[1:], is_own, 0 * is_own]
    )
    block_mats = lax.dynamic_slice(mix_w, (start, 3 * part), (part, 2 * block_width))
    block_mats = block_mats.reshape(held, block_width, 2 * block_width)

    x_all_f = x_all.astype(F32)
    mixed_all = normed(x_all_f, mix_gain[0]).astype(BF)
    pre = dot_plain(mixed_all.reshape(-1, width), gelu_lru_w)
    mixed = mixed_all[:, :, HALO:].reshape(-1, width)
    conv, gate, state, prod, sums = recur(pre, rows_w, block_mats, span)
    ends = (TP, micro, part)
    if p.rests == 1:
        state_in, every_sum = chain(sums)
    else:
        sums = all_spans(jnp.stack([sums[0].reshape(ends), sums[1].reshape(ends)], axis=1), p)
        carry, carries = jnp.zeros_like(sums[0, 0]), []
        for k in range(sums.shape[0]):
            carries.append(carry)
            carry = sums[k, 0] * carry + sums[k, 1]
        state_in = own_spans(jnp.stack(carries), p).reshape(-1, part)
    mix_bf = recur_mix(pre, rows_w, state, prod, state_in, block_width, span)
    blocked = (TP, micro, span, width)
    out_parts = dot_right_t(mix_bf, out_w).astype(BF).reshape(blocked)
    x_one, ffw_bf, cot_all, ffw_w = middle(
        out_parts, x_rows, ffw_gain, cot.reshape(-1, width), piece_2, piece_3, ffw_w
    )
    cot_all = cot_all.reshape(-1, width)
    ffw_w = ffw_w.reshape(width, -1) if p.rests == 1 else whole_ffw

    ffw_bf = ffw_bf.reshape(-1, width)
    gate_up_w, down_w = ffw_w[:, : 2 * ffw_part], ffw_w[:, 2 * ffw_part :]
    gate_up = dot_plain(ffw_bf, gate_up_w)
    gate_vals, up_vals = gate_up[:, :ffw_part], gate_up[:, ffw_part:]
    hidden_bf = geglu(gate_vals, up_vals).astype(BF)
    grad_hidden = dot_plain(cot_all, down_w)
    _, pull_back = jax.vjp(geglu, gate_vals, up_vals)
    grad_gate_up = jnp.concatenate(pull_back(grad_hidden), axis=1).astype(BF)
    ffw_parts = dot_right_t(hidden_bf, down_w).astype(BF).reshape(blocked)
    grad_in_parts = dot_right_t(grad_gate_up, gate_up_w).astype(BF).reshape(blocked)
    ffw_grads = [dot_left_t(ffw_bf, grad_gate_up), dot_left_t(cot_all, hidden_bf)]
    ffw_grads = [grad.astype(BF) for grad in ffw_grads]
    mixed_out, grad_x_one, gain_rows, grad_mix, *ffw_pieces = turn(
        grad_in_parts, ffw_parts, x_one, cot, ffw_gain, [by_owner(g, p) for g in ffw_grads] * one
    )
    if p.rests == 1:
        for d in (1, 3, 2):
            ffw_pieces[d] = shift_z(ffw_pieces[d], d)
    grad_mix = grad_mix.reshape(-1, width)

    back_mix = dot_plain(grad_mix, out_w)
    grad_gelu_bf, local_back, prod_back, back_sums = recur_back(
        back_mix, pre, rows_w, state, prod, state_in, gate, block_width, span
    )
    if p.rests == 1:
        carried, _ = chain(back_sums[None], every_sum)
    else:
        back_sums = all_spans(back_sums.reshape(ends), p)
        carry, carries = jnp.zeros_like(sums[0, 0]), []
        for k in range(sums.shape[0] - 1, -1, -1):
            carries.append(carry)
            carry = sums[k, 0] * carry + back_sums[k]
        carried = own_spans(jnp.stack(carries[::-1]), p).reshape(-1, part)
    grad_blocks, grad_lru, spill, row_grads = recur_grad(
        local_back, prod_back, carried, state, prod, state_in, gate, conv, pre, rows_w, block_mats,
        span,
    )
    spill = spill.reshape(TP, micro, HALO, part)
    from_next = shift_q(spill, -1)
    last = jnp.zeros_like(spill[:1])
    if p.rests > 1:
        last = move(spill[:1], lambda r, z, q: (r - 1, z, NQ - 1) if q == 0 and r > 0 else None)
    from_next = jnp.where(
        p.q == NQ - 1, jnp.concatenate([from_next[1:], last], axis=0), from_next
    )
    grad_lru = grad_lru.reshape(TP, micro, span, part) + jnp.pad(
        from_next, ((0, 0), (0, 0), (span - HALO, 0), (0, 0))
    )
    grad_lru_bf = (grad_lru * is_own[0]).astype(BF).reshape(-1, part)
    grad_pair = jnp.concatenate([grad_gelu_bf, grad_lru_bf], axis=1)
    grad_mixed = dot_right_t(grad_pair, gelu_lru_w)
    x_back, grad_pair = lax.optimization_barrier((x_all, grad_pair))
    x_rows_f = x_back[:, :, HALO:].reshape(-1, width).astype(F32)
    unit = x_rows_f * lax.rsqrt(jnp.mean(x_rows_f * x_rows_f, axis=-1, keepdims=True) + EPS)
    grad_mix_gain = jnp.sum(grad_mixed * unit, axis=0, keepdims=True)
    grad_mixed_parts = grad_mixed.astype(BF).reshape(blocked)

    blocks_all = lax.dynamic_update_slice_in_dim(
        jnp.zeros((lru_width, 2 * block_width), BF),
        (grad_blocks * is_own[0][:, None]).astype(BF),
        start,
        0,
    )
    mix_grads = [dot_left_t(mixed, grad_pair), dot_left_t(grad_mix, mix_bf), blocks_all]
    mix_grads = [grad.astype(BF) for grad in mix_grads]
    vectors = lax.dynamic_update_slice_in_dim(
        jnp.zeros((1 + tap_count, lru_width), F32), row_grads[: 1 + tap_count], start, 1
    )
    vectors = jnp.concatenate([grad_mix_gain, gain_rows[:1], vectors], axis=0)
    vectors = jnp.pad(vectors, ((0, -vectors.shape[0] % 8), (0, 0)))
    if p.rests == 1:
        grad_inputs, vectors, mix_grads = final(
            grad_mixed_parts, x_rows, mix_gain, grad_x_one, vectors,
            [by_owner(grad, p) for grad in mix_grads],
        )
    else:
        mix_grads = [grads_out(grad, p) for grad in mix_grads]
        grad_mixed_own = scatter_z(grad_mixed_parts, p)
        grad_inputs = grad_x_one + norm_back(x_rows.astype(F32), mix_gain, grad_mixed_own)[0]
        for exchange in (swap_core, swap_x, swap_f):
            vectors = vectors + exchange(vectors)
        for bit in (1, 2):
            vectors = vectors + move(vectors, lambda r, z, q, bit=bit: (r, z ^ bit, q))
        total = vectors
        for d in range(1, p.rests):
            total = total + shift_r(vectors, d)
        vectors = total
    vectors = lax.dynamic_slice_in_dim(vectors, p.index * rows, rows, 1)

    def mix_columns(grad, offset):
        picked = [
            grad[k][
                :,
                offset + (owned[k][0] - first[k]) * block_width : offset
                + (owned[k][-1] + 1 - first[k]) * block_width,
            ]
            for k in range(TP)
        ]
        return jnp.concatenate(picked, axis=1).astype(F32)

    if p.rests == 1:
        share_gate, share_up, share_down = unpack(ffw_pieces, 3)
    else:
        ffw_grads = [grads_out(grad, p) for grad in ffw_grads]
        beside = lambda v: jnp.swapaxes(v, 0, 1).reshape(rows, -1).astype(F32)
        share_gate = beside(ffw_grads[0][:, :, :ffw_part])
        share_up = beside(ffw_grads[0][:, :, ffw_part:])
        share_down = beside(ffw_grads[1])
    shape = (micro, 1, span, width)
    return (
        mixed_out.reshape(shape),
        grad_inputs.reshape(shape),
        mix_columns(mix_grads[0], 0),
        mix_columns(mix_grads[0], part),
        jnp.sum(mix_grads[2].astype(F32), axis=0),
        mix_columns(mix_grads[1], 0).T,
        share_gate,
        share_up,
        share_down.T,
        vectors[0],
        vectors[1],
        vectors[2],
        vectors[3 : 3 + tap_count].T,
    )


def solution(mesh):
    in_specs = (
        P(None, "fsdp", "seq", None),
        P(None, "fsdp", "seq", None),
        P(("fsdp", "seq"), None),
        P(("fsdp", "seq"), None),
        P(("fsdp", "seq"), None),
        P(None, ("fsdp", "seq")),
        P(("fsdp", "seq"), None),
        P(("fsdp", "seq"), None),
        P(None, ("fsdp", "seq")),
        P(("fsdp", "seq")),
        P(("fsdp", "seq")),
        P(("fsdp", "seq")),
        P(("fsdp", "seq"), None),
    )
    out_specs = (
        P(None, "fsdp", "seq", None),
        P(None, "fsdp", "seq", None),
        P(("fsdp", "seq"), None),
        P(("fsdp", "seq"), None),
        P(("fsdp", "seq"), None),
        P(None, ("fsdp", "seq")),
        P(("fsdp", "seq"), None),
        P(("fsdp", "seq"), None),
        P(None, ("fsdp", "seq")),
        P(("fsdp", "seq")),
        P(("fsdp", "seq")),
        P(("fsdp", "seq")),
        P(("fsdp", "seq"), None),
    )
    return jax.shard_map(
        on_device, mesh=mesh, in_specs=in_specs, out_specs=out_specs, check_vma=False
    )
```

```python
import functools

import jax
import jax.numpy as jnp
from jax import lax
from jax.experimental import pallas as pl
from jax.experimental.pallas import tpu as pltpu
from jax.sharding import PartitionSpec as P

EPS = 1e-06
GUARD = 0.001
RATE = 8.0
TP = 4
NQ = 4
HALO = 8
BF = jnp.bfloat16
F32 = jnp.float32
MESH = pl.DeviceIdType.MESH
ANY = pl.BlockSpec(memory_space=pl.ANY)
VMEM = pl.BlockSpec(memory_space=pltpu.VMEM)
GRANT = 60 * 1024 * 1024
FREE = pl.CostEstimate(flops=0, bytes_accessed=0, transcendentals=0)


def move(value, step):
    pairs = []
    for here in range(lax.axis_size("seq")):
        there = step(here // (TP * NQ), here // NQ % TP, here % NQ)
        if there is not None:
            pairs.append((here, (there[0] * TP + there[1]) * NQ + there[2]))
    return lax.ppermute(value, "seq", pairs)


def swap_core(value):
    return move(value, lambda r, z, q: (r, z, q ^ 1))


def swap_x(value):
    return move(value, lambda r, z, q: (r, z, q ^ 2))


def swap_f(value):
    return lax.ppermute(value, "fsdp", [(0, 1), (1, 0)])


def shift_z(value, d):
    return move(value, lambda r, z, q: (r, (z + d) % TP, q))


def shift_q(value, d):
    return move(value, lambda r, z, q: (r, z, (q + d) % NQ))


def shift_r(value, d):
    count = lax.axis_size("seq") // (TP * NQ)
    return move(value, lambda r, z, q: ((r + d) % count, z, q))


def hop(value, d, low, high):
    return move(value, lambda r, z, q: (r, z + d, q) if low <= z <= high else None)


class Place:
    def __init__(self):
        seq = lax.axis_index("seq")
        self.f = lax.axis_index("fsdp")
        self.r, self.z, self.q = seq // (TP * NQ), seq // NQ % TP, seq % NQ
        self.x, self.c = self.q // 2, self.q % 2
        self.rests = lax.axis_size("seq") // (TP * NQ)
        self.fs = lax.axis_size("fsdp")
        self.index = self.f * lax.axis_size("seq") + seq


def at(value, index):
    return lax.dynamic_index_in_dim(value, index, 0, keepdims=False)


def put(base, value, *index):
    starts = [jnp.int32(0) if i is None else jnp.int32(i) for i in index]
    starts += [jnp.int32(0)] * (base.ndim - len(index))
    for dim, i in enumerate(index):
        if i is not None:
            value = jnp.expand_dims(value, dim)
    return lax.dynamic_update_slice(base, value, starts)


def everywhere(value, shifter, mine, count):
    out = put(jnp.zeros((count,) + value.shape, value.dtype), value, mine)
    for d in range(1, count):
        out = put(out, shifter(value, d), (mine - d) % count)
    return out


def gather_z(value, p):
    ups, downs = [], []
    up = down = value
    for k in range(1, TP):
        up = hop(up, 1, k - 1, TP - 2)
        down = hop(down, -1, 1, TP - k)
        ups.append(up)
        downs.append(down)
    out = put(jnp.zeros((TP,) + value.shape, value.dtype), value, p.z)
    for k in range(1, TP):
        out = put(out, downs[k - 1] + ups[TP - 1 - k], (p.z + k) % TP)
    return out


def scatter_z(parts, p):
    right = left = None
    for k in range(TP - 1, 0, -1):
        send = at(parts, (p.z + k) % TP)
        if right is not None:
            send = (send.astype(F32) + right.astype(F32)).astype(BF)
        right = hop(send, 1, 0, TP - 1 - k)
        send = at(parts, (p.z - k) % TP)
        if left is not None:
            send = (send.astype(F32) + left.astype(F32)).astype(BF)
        left = hop(send, -1, k, TP - 1)
    return at(parts, p.z).astype(F32) + right.astype(F32) + left.astype(F32)


def weights_in(pieces, p):
    rows, cols = pieces.shape[1:]
    mine = put(jnp.zeros(pieces.shape, BF), at(pieces, p.z), p.z)
    for d in range(1, TP):
        mine = put(mine, shift_z(at(pieces, (p.z + d) % TP), d), (p.z - d) % TP)
    mine = everywhere(mine, shift_r, p.r, p.rests)
    half = TP // 2
    by_x, by_f = swap_x(mine), swap_f(mine)
    corner = (swap_f(by_x[:, :half]), swap_x(by_f[:, half:]))
    whole = jnp.zeros((p.fs, p.rests, TP, 2, 2, rows, cols), BF)
    for block, f, x, z in (
        (mine, p.f, p.x, 0),
        (by_x, p.f, 1 - p.x, 0),
        (by_f, 1 - p.f, p.x, 0),
        (corner[0], 1 - p.f, 1 - p.x, 0),
        (corner[1], 1 - p.f, 1 - p.x, half),
    ):
        other = swap_core(block)
        for part, c in ((block, p.c), (other, 1 - p.c)):
            part = part[None, :, :, None, None]
            whole = lax.dynamic_update_slice(
                whole, part, [jnp.int32(i) for i in (f, 0, z, x, c, 0, 0)]
            )
    return whole.reshape(-1, cols)


def by_owner(grad, p):
    return grad.reshape(p.fs, p.rests, TP, 2, 2, -1, grad.shape[1])


def to_owner_z(total, p):
    out = put(jnp.zeros(total.shape, BF), at(total, p.z), p.z)
    for d in (1, 3, 2):
        out = put(out, shift_z(at(total, (p.z + d) % TP), d), (p.z - d) % TP)
    return out


def grads_out(grad, p):
    plus = lambda a, b: (a.astype(F32) + b.astype(F32)).astype(BF)
    pick = lambda v, dim, i: lax.dynamic_index_in_dim(v, i, dim, keepdims=False)
    total = by_owner(grad, p)
    total = plus(pick(total, 4, p.c), swap_core(pick(total, 4, 1 - p.c)))
    total = plus(pick(total, 3, p.x), swap_x(pick(total, 3, 1 - p.x)))
    total = plus(at(total, p.f), swap_f(at(total, 1 - p.f)))
    mine = at(total, p.r)
    for d in range(1, p.rests):
        mine = plus(mine, shift_r(at(total, (p.r + d) % p.rests), d))
    return to_owner_z(mine, p)


def dot_left_t(left_mat, right_mat):
    return lax.dot_general(
        left_mat, right_mat, (((0,), (0,)), ((), ())), preferred_element_type=F32
    )


def dot_plain(left_mat, right_mat):
    return jnp.dot(left_mat, right_mat, preferred_element_type=F32)


def dot_right_t(left_mat, right_mat):
    return lax.dot_general(
        left_mat, right_mat, (((1,), (1,)), ((), ())), preferred_element_type=F32
    )


def normed(values, gain_vec):
    return values * lax.rsqrt(jnp.mean(values * values, axis=-1, keepdims=True) + EPS) * gain_vec


def gelu_pair(v):
    scale = 0.7978845608028654
    inner = jnp.tanh(scale * (v + 0.044715 * v * v * v))
    slope = 0.5 * v * (1.0 - inner * inner) * scale * (1.0 + 0.134145 * v * v)
    return 0.5 * v * (1.0 + inner), 0.5 * (1.0 + inner) + slope


def span_scan(decay, drive, backward):
    count = decay.shape[0]
    row = lax.broadcasted_iota(jnp.int32, decay.shape, 0)
    step = 1
    while step < count:
        inside = row < count - step if backward else row >= step
        turn = count - step if backward else step
        drive = drive + jnp.where(inside, decay * pltpu.roll(drive, turn, 0), 0.0)
        decay = decay * jnp.where(inside, pltpu.roll(decay, turn, 0), 1.0)
        step *= 2
    return decay, drive


def gate_values(gate, soft):
    half = gate.shape[1] // 2
    rec_gate = jax.nn.sigmoid(gate[:, :half])
    in_gate = jax.nn.sigmoid(gate[:, half:])
    log_decay = -RATE * rec_gate * soft
    square = jnp.exp(2.0 * log_decay)
    return rec_gate, in_gate, jnp.exp(log_decay), square, jnp.sqrt(1.0 - square + GUARD)


def main_rows(i, span, micro):
    return pl.ds(i // micro * micro * (span + HALO) + i % micro * span, span)


def with_halo(pre, i, span, micro):
    start = i // micro * micro * (span + HALO) + micro * span + i % micro * HALO
    both = [pre[pl.ds(start, HALO)], pre[main_rows(i, span, micro)]]
    return jnp.concatenate(both, axis=0)


def recur_head(span, micro, pre, rows, block, conv, gate, state, prod, sums):
    count = conv.shape[0] // span
    soft, taps = rows[0:1], [rows[k + 2 : k + 3] for k in range(4)]
    for i in range(count):
        vals = with_halo(pre, i, span, micro).astype(BF).astype(F32)
        total = taps[0] * vals
        for k in range(1, 4):
            total = total + taps[k] * pltpu.roll(vals, k, 0)
        conv[pl.ds(i * span, span)] = total[HALO:].astype(BF)
    gate[...] = dot_plain(conv[...], block[...])
    for i in range(count):
        here = pl.ds(i * span, span)
        _, in_gate, decay, _, root = gate_values(gate[here], soft)
        decay, local = span_scan(decay, root * in_gate * conv[here].astype(F32), False)
        state[here] = local
        prod[here] = decay
        sums[0, i : i + 1] = decay[span - 1 :]
        sums[1, i : i + 1] = local[span - 1 :]


def columns(ref, h, width):
    return ref.at[:, pl.ds(pl.multiple_of(h * width, 128), width)]


def by_heads(count, body):
    def turn(h, _):
        body(h)
        return 0

    lax.fori_loop(0, count, turn, 0)


def recur_kernel(
    dims, x_all, mix_w, small, rows, mixed, pre, conv, gate, state, prod, sums,
    small_w, gl_w, block_w, mixed_all, sems,
):
    span, micro, heads, held, bw, taps = dims
    part = held * bw
    p = Place()
    start = pl.multiple_of(p.z * heads // TP * bw, 128)
    pieces = (
        (mix_w.at[:, pl.ds(3 * part + 2 * bw, 128)], small_w),
        (mix_w.at[:, pl.ds(0, 2 * part)], gl_w),
        (mix_w.at[pl.ds(start, part), pl.ds(3 * part, 2 * bw)], block_w),
    )
    loads = [pltpu.make_async_copy(src, dst, sems.at[i]) for i, (src, dst) in enumerate(pieces)]
    for load in loads:
        load.start()
    loads[0].wait()
    row = lax.broadcasted_iota(jnp.int32, (8, 128), 0)
    lane = lax.broadcasted_iota(jnp.int32, (8, 128), 1)
    small[...] = dot_right_t(jnp.where(row == lane, 1.0, 0.0).astype(BF), small_w[...])
    own = small[:, pl.ds(start, part)]
    decay = -own[2:3]
    feature = lax.broadcasted_iota(jnp.int32, (1, part), 1)
    count = ((p.z + 1) * heads // TP - p.z * heads // TP) * bw
    rows[0:1] = jnp.maximum(decay, 0.0) + jnp.log1p(jnp.exp(-jnp.abs(decay)))
    rows[1:2] = jax.nn.sigmoid(decay)
    rows[2 : 2 + taps] = own[3 : 3 + taps]
    rows[6:7] = jnp.where(feature < count, 1.0, 0.0)
    rows[7:8] = jnp.zeros((1, part), F32)
    gain, wide, step = small[0:1], micro * (span + HALO), 16

    def norm(z, _):
        for k in range(0, wide, step):
            vals = x_all[pl.ds(pl.multiple_of(z * wide + k, step), step)].astype(F32)
            vals = normed(vals, gain).astype(BF)
            mixed_all[pl.ds(pl.multiple_of(z * wide + k, step), step)] = vals
            if k < micro * span:
                mixed[pl.ds(pl.multiple_of(z * micro * span + k, step), step)] = vals
        return 0

    lax.fori_loop(0, TP, norm, 0)
    loads[1].wait()

    def project(h):
        cols = pl.ds(pl.multiple_of(h * bw, 128), bw)
        pre[:, cols] = dot_plain(mixed_all[...], gl_w[:, cols])

    by_heads(2 * held, project)
    loads[2].wait()

    def one_head(h):
        block = block_w.at[pl.ds(pl.multiple_of(h * bw, 128), bw)]
        sums_h = sums.at[:, :, pl.ds(pl.multiple_of(h * bw, 128), bw)]
        recur_head(
            span, micro, columns(pre, held + h, bw), columns(rows, h, bw), block,
            columns(conv, h, bw), columns(gate, h, 2 * bw), columns(state, h, bw),
            columns(prod, h, bw), sums_h,
        )

    by_heads(held, one_head)


def recur(x_all, mix_w, dims):
    span, micro, _, held, bw, _ = dims
    part, width = held * bw, x_all.shape[1]
    tokens = x_all.shape[0] // (span + HALO) * span
    shapes = [((8, width), F32), ((8, part), F32), ((tokens, width), BF)]
    shapes += [((x_all.shape[0], 2 * part), F32), ((tokens, part), BF), ((tokens, 2 * part), F32)]
    shapes += [((tokens, part), F32), ((tokens, part), F32), ((2, tokens // span, part), F32)]
    return pl.pallas_call(
        functools.partial(recur_kernel, dims),
        in_specs=[VMEM, ANY],
        out_specs=[VMEM] * len(shapes),
        out_shape=[jax.ShapeDtypeStruct(*shape) for shape in shapes],
        scratch_shapes=[
            pltpu.VMEM((width, 128), BF),
            pltpu.VMEM((width, 2 * part), BF),
            pltpu.VMEM((part, 2 * bw), BF),
            pltpu.VMEM(x_all.shape, BF),
            pltpu.SemaphoreType.DMA((3,)),
        ],
        cost_estimate=FREE,
        compiler_params=pltpu.CompilerParams(vmem_limit_bytes=GRANT),
    )(x_all, mix_w)


def recur_mix_kernel(dims, pre, rows, state, prod, start, mix_w, mix, parts, out_w, sem):
    span, micro, _, held, bw, _ = dims
    part = held * bw
    load = pltpu.make_async_copy(mix_w.at[:, pl.ds(2 * part, part)], out_w, sem.at[0])
    load.start()

    def one_head(h):
        pre_h, state_h, prod_h = columns(pre, h, bw), columns(state, h, bw), columns(prod, h, bw)
        rows_h, start_h, mix_h = columns(rows, h, bw), columns(start, h, bw), columns(mix, h, bw)
        for i in range(state.shape[0] // span):
            here = pl.ds(i * span, span)
            act, _ = gelu_pair(pre_h[main_rows(i, span, micro)])
            states = state_h[here] + prod_h[here] * start_h[i : i + 1]
            mix_h[here] = (states * act * rows_h[6:7]).astype(BF)

    by_heads(held, one_head)
    load.wait()

    def project(j):
        cols = pl.ds(pl.multiple_of(j * 256, 256), 256)
        parts[:, cols] = dot_right_t(mix[...], out_w[cols]).astype(BF)

    by_heads(out_w.shape[0] // 256, project)


def recur_mix(pre, rows, state, prod, start, mix_w, dims):
    tokens, part = state.shape
    width = mix_w.shape[0]
    return pl.pallas_call(
        functools.partial(recur_mix_kernel, dims),
        in_specs=[VMEM] * 5 + [ANY],
        out_specs=[VMEM, VMEM],
        out_shape=[
            jax.ShapeDtypeStruct((tokens, part), BF),
            jax.ShapeDtypeStruct((tokens, width), BF),
        ],
        scratch_shapes=[pltpu.VMEM((width, part), BF), pltpu.SemaphoreType.DMA((1,))],
        cost_estimate=FREE,
        compiler_params=pltpu.CompilerParams(vmem_limit_bytes=GRANT),
    )(pre, rows, state, prod, start, mix_w)


def recur_back_kernel(
    dims, grad, pre, rows, state, prod, start, gate, mix_w, gelu, local, prods, sums, back, out_w, sem
):
    span, micro, _, held, bw, _ = dims
    part = held * bw
    load = pltpu.make_async_copy(mix_w.at[:, pl.ds(2 * part, part)], out_w, sem.at[0])
    load.start()
    load.wait()

    def one_head(h):
        back[...] = dot_plain(grad[...], out_w[:, pl.ds(pl.multiple_of(h * bw, 128), bw)])
        pre_h, state_h, prod_h = columns(pre, h, bw), columns(state, h, bw), columns(prod, h, bw)
        rows_h, start_h, gate_h = columns(rows, h, bw), columns(start, h, bw), columns(gate, h, 2 * bw)
        gelu_h, local_h = columns(gelu, h, bw), columns(local, h, bw)
        prods_h, sums_h = columns(prods, h, bw), columns(sums, h, bw)
        soft = rows_h[0:1]
        for i in range(back.shape[0] // span):
            here = pl.ds(i * span, span)
            act, slope = gelu_pair(pre_h[main_rows(i, span, micro)])
            states = state_h[here] + prod_h[here] * start_h[i : i + 1]
            gelu_h[here] = (back[here] * states * slope * rows_h[6:7]).astype(BF)
            _, _, decay, _, _ = gate_values(gate_h[here], soft)
            row = lax.broadcasted_iota(jnp.int32, decay.shape, 0)
            later = jnp.where(row < span - 1, pltpu.roll(decay, span - 1, 0), 1.0)
            later, adjoint = span_scan(later, back[here] * act, True)
            local_h[here] = adjoint
            prods_h[here] = later
            sums_h[i : i + 1] = decay[:1] * adjoint[:1]

    by_heads(held, one_head)


def recur_back(grad, pre, rows, state, prod, start, gate, mix_w, dims):
    tokens, part = state.shape
    shapes = [((tokens, part), BF), ((tokens, part), F32), ((tokens, part), F32), (start.shape, F32)]
    return pl.pallas_call(
        functools.partial(recur_back_kernel, dims),
        in_specs=[VMEM] * 7 + [ANY],
        out_specs=[VMEM] * 4,
        out_shape=[jax.ShapeDtypeStruct(*shape) for shape in shapes],
        scratch_shapes=[
            pltpu.VMEM((tokens, dims[4]), F32),
            pltpu.VMEM((mix_w.shape[0], part), BF),
            pltpu.SemaphoreType.DMA((1,)),
        ],
        cost_estimate=FREE,
        compiler_params=pltpu.CompilerParams(vmem_limit_bytes=GRANT),
    )(grad, pre, rows, state, prod, start, gate, mix_w)


def recur_grad_kernel(
    span, micro, local, prods, carried, state, prod, start, gate, conv, pre, rows, block,
    blocks_out, lru_out, spill_out, rows_out, gate_grad, conv_grad,
):
    count = local.shape[0] // span
    soft, sig, own = rows[0:1], rows[1:2], rows[6:7]
    taps = [rows[k + 2 : k + 3] for k in range(4)]
    width = local.shape[1]
    add_up = lambda v: jnp.sum(v, axis=0, keepdims=True)
    decay_sum = jnp.zeros((1, width), F32)
    for i in range(count):
        here = pl.ds(i * span, span)
        adjoint = local[here] + prods[here] * carried[i : i + 1]
        states = state[here] + prod[here] * start[i : i + 1]
        row = lax.broadcasted_iota(jnp.int32, states.shape, 0)
        earlier = jnp.where(row >= 1, pltpu.roll(states, 1, 0), start[i : i + 1])
        rec_gate, in_gate, decay, square, root = gate_values(gate[here], soft)
        conv_vals = conv[here].astype(F32)
        drive = adjoint * conv_vals
        grad_log = adjoint * earlier * decay - drive * in_gate * square / root
        decay_sum = decay_sum + add_up(grad_log * rec_gate)
        gate_grad[here, :width] = (-RATE * soft * grad_log * rec_gate * (1.0 - rec_gate)).astype(BF)
        gate_grad[here, width:] = (drive * root * in_gate * (1.0 - in_gate)).astype(BF)
        conv_grad[here] = adjoint * root * in_gate
    blocks_out[...] = lax.dot_general(
        conv[...], gate_grad[...], (((0,), (0,)), ((), ())), preferred_element_type=F32
    )
    conv_grad[...] += dot_right_t(gate_grad[...], block[0])
    tap_sums = [jnp.zeros((1, width), F32) for _ in range(4)]
    for i in range(count):
        here = pl.ds(i * span, span)
        grad = conv_grad[here]
        vals = with_halo(pre, i, span, micro).astype(BF).astype(F32)
        wide = jnp.concatenate([jnp.zeros((HALO, width), F32), grad], axis=0)
        total = taps[0] * wide
        tap_sums[0] = tap_sums[0] + add_up(grad * vals[HALO:])
        for k in range(1, 4):
            total = total + taps[k] * pltpu.roll(wide, span + HALO - k, 0)
            tap_sums[k] = tap_sums[k] + add_up(grad * pltpu.roll(vals, k, 0)[HALO:])
        lru_out[here] = total[HALO:]
        spill_out[pl.ds(i * HALO, HALO)] = total[:HALO]
    rows_out[...] = jnp.zeros(rows_out.shape, F32)
    rows_out[0:1] = decay_sum * sig * own * RATE
    for k in range(4):
        rows_out[k + 1 : k + 2] = tap_sums[k] * own


def recur_grad(local, prods, carried, state, prod, start, gate, conv, pre, rows, blocks, dims):
    tokens, part = state.shape
    span, micro, _, held, bw, _ = dims
    column = lambda h: (0, h)
    whole = pl.BlockSpec((tokens, bw), column)
    ends = pl.BlockSpec((start.shape[0], bw), column)
    return pl.pallas_call(
        functools.partial(recur_grad_kernel, span, micro),
        grid=(held,),
        in_specs=[
            whole,
            whole,
            ends,
            whole,
            whole,
            ends,
            pl.BlockSpec((tokens, 2 * bw), column),
            whole,
            pl.BlockSpec((pre.shape[0], bw), lambda h: (0, held + h)),
            pl.BlockSpec((8, bw), column),
            pl.BlockSpec((1, bw, 2 * bw), lambda h: (h, 0, 0)),
        ],
        out_specs=[
            pl.BlockSpec((bw, 2 * bw), lambda h: (h, 0)),
            whole,
            pl.BlockSpec((start.shape[0] * HALO, bw), column),
            pl.BlockSpec((8, bw), column),
        ],
        out_shape=[
            jax.ShapeDtypeStruct((part, 2 * bw), F32),
            jax.ShapeDtypeStruct((tokens, part), F32),
            jax.ShapeDtypeStruct((start.shape[0] * HALO, part), F32),
            jax.ShapeDtypeStruct((8, part), F32),
        ],
        scratch_shapes=[pltpu.VMEM((tokens, 2 * bw), BF), pltpu.VMEM((tokens, bw), F32)],
        cost_estimate=FREE,
        compiler_params=pltpu.CompilerParams(vmem_limit_bytes=GRANT),
    )(local, prods, carried, state, prod, start, gate, conv, pre, rows, blocks)


def recur_in_kernel(
    dims, gelu, lru, spill, rows, small, mixed, mix_w, pair, parts, gains, gl_w, sem
):
    span, _, _, held, bw, _ = dims
    part = held * bw
    load = pltpu.make_async_copy(mix_w.at[:, pl.ds(0, 2 * part)], gl_w, sem.at[0])
    load.start()
    pair[:, :part] = gelu[...]

    def one_head(h):
        lru_h, spill_h, own = columns(lru, h, bw), columns(spill, h, bw), columns(rows, h, bw)[6:7]
        for i in range(lru.shape[0] // span):
            vals = lru_h[pl.ds(i * span, span)]
            late = vals[span - HALO :] + spill_h[pl.ds(i * HALO, HALO)]
            vals = jnp.concatenate([vals[: span - HALO], late], axis=0) * own
            pair[pl.ds(i * span, span), pl.ds(pl.multiple_of((held + h) * bw, 128), bw)] = vals.astype(BF)

    by_heads(held, one_head)
    load.wait()

    def project(j):
        cols = pl.ds(pl.multiple_of(j * 256, 256), 256)
        grad = dot_right_t(pair[...], gl_w[cols])
        parts[:, cols] = grad.astype(BF)
        gain = jnp.sum(grad * mixed[:, cols].astype(F32), axis=0, keepdims=True)
        gains[0:1, cols] = gain / small[0:1, cols]

    by_heads(gl_w.shape[0] // 256, project)


def recur_in(gelu, lru, spill, rows, small, mixed, mix_w, dims):
    tokens, part = gelu.shape
    width = mix_w.shape[0]
    return pl.pallas_call(
        functools.partial(recur_in_kernel, dims),
        in_specs=[VMEM] * 6 + [ANY],
        out_specs=[VMEM] * 3,
        out_shape=[
            jax.ShapeDtypeStruct((tokens, 2 * part), BF),
            jax.ShapeDtypeStruct((tokens, width), BF),
            jax.ShapeDtypeStruct((8, width), F32),
        ],
        scratch_shapes=[pltpu.VMEM((width, 2 * part), BF), pltpu.SemaphoreType.DMA((1,))],
        cost_estimate=FREE,
        compiler_params=pltpu.CompilerParams(vmem_limit_bytes=GRANT),
    )(gelu, lru, spill, rows, small, mixed, mix_w)


def device(p, f=None, z=None, x=None, c=None):
    f, z = p.f if f is None else f, p.z if z is None else z
    x, c = p.x if x is None else x, p.c if c is None else c
    return (f, ((p.r * TP + z) * 2 + x) * 2 + c)


def copy_to(src, dst, sems, index, dev):
    return pltpu.make_async_remote_copy(
        src_ref=src,
        dst_ref=dst,
        send_sem=sems[0].at[index],
        recv_sem=sems[1].at[index],
        device_id=dev,
        device_id_type=MESH,
    )


def pairs(*shape):
    return [pltpu.SemaphoreType.DMA(shape), pltpu.SemaphoreType.DMA(shape)]


def greet(devices):
    barrier = pltpu.get_barrier_semaphore()
    for dev in devices:
        pl.semaphore_signal(barrier, inc=1, device_id=dev, device_id_type=MESH)
    pl.semaphore_wait(barrier, len(devices))


def by_rows(count, body, step=16):
    def turn(i, _):
        body(pl.ds(pl.multiple_of(i * step, step), step))
        return 0

    assert count % step == 0
    lax.fori_loop(0, count // step, turn, 0)


class Gather:
    def __init__(self, p, out, ups, downs):
        self.p, self.out, self.ups, self.downs = p, out, ups, downs
        self.up = device(p, z=jnp.minimum(p.z + 1, TP - 1))
        self.down = device(p, z=jnp.maximum(p.z - 1, 0))

    def begin(self, h, src):
        z = self.p.z

        @pl.when(z < TP - 1)
        def _():
            copy_to(src, self.out.at[z, h], self.ups, (0, h), self.up).start()

        @pl.when(z > 0)
        def _():
            copy_to(src, self.out.at[z, h], self.downs, (0, h), self.down).start()

    def step(self, k, h):
        z, out = self.p.z, self.out

        @pl.when(z >= k)
        def _():
            block = out.at[z - k, h]
            copy_to(block, block, self.ups, (k - 1, h), self.up).wait_recv()
            if k < TP - 1:

                @pl.when(z < TP - 1)
                def _():
                    copy_to(block, block, self.ups, (k, h), self.up).start()

        @pl.when(z <= TP - 1 - k)
        def _():
            block = out.at[z + k, h]
            copy_to(block, block, self.downs, (k - 1, h), self.down).wait_recv()
            if k < TP - 1:

                @pl.when(z > 0)
                def _():
                    copy_to(block, block, self.downs, (k, h), self.down).start()

    def close(self, halves):
        z, block = self.p.z, self.out.at[0, 0]
        for h in range(halves):
            for k in range(TP - 1):

                @pl.when((z >= k) & (z < TP - 1))
                def _():
                    copy_to(block, block, self.ups, (k, h), self.up).wait_send()

                @pl.when((z <= TP - 1 - k) & (z > 0))
                def _():
                    copy_to(block, block, self.downs, (k, h), self.down).wait_send()


class LineSum:
    def __init__(self, p, parts, scratch):
        self.p, self.parts = p, parts
        self.got_up, self.got_down, self.out_up, self.out_down = scratch[:4]
        self.ups, self.downs = scratch[4:6], scratch[6:8]
        self.halves, self.rows = parts.shape[1:3]
        self.up = device(p, z=jnp.minimum(p.z + 1, TP - 1))
        self.down = device(p, z=jnp.maximum(p.z - 1, 0))

    @staticmethod
    def scratch(parts):
        block = parts[1:]
        return [
            pltpu.VMEM((TP - 1,) + block, BF),
            pltpu.VMEM((TP - 1,) + block, BF),
            pltpu.VMEM((TP - 2,) + block, BF),
            pltpu.VMEM((TP - 2,) + block, BF),
            *pairs(TP - 1, parts[1]),
            *pairs(TP - 1, parts[1]),
        ]

    def clear(self):
        z = self.p.z

        @pl.when(z == 0)
        def _():
            for h in range(self.halves):
                by_rows(self.rows, lambda at: self.fill(self.got_up, h, at))

        @pl.when(z == TP - 1)
        def _():
            for h in range(self.halves):
                by_rows(self.rows, lambda at: self.fill(self.got_down, h, at))

    def fill(self, ref, h, at):
        ref[0, h, at] = jnp.zeros((at.size, ref.shape[-1]), BF)

    def one_way(self, k, h, place, block, got, out, sems, dev):
        @pl.when(place == 0)
        def _():
            copy_to(self.parts.at[block, h], got.at[k - 1, h], sems, (k - 1, h), dev).start()

        if k < TP - 1:

            @pl.when((place >= 1) & (place + k <= TP - 1))
            def _():
                copy_to(got.at[k, h], got.at[k, h], sems, (k, h), dev).wait_recv()

                def add(at):
                    total = self.parts[block, h, at].astype(F32) + got[k, h, at].astype(F32)
                    out[k - 1, h, at] = total.astype(BF)

                by_rows(self.rows, add)
                copy_to(out.at[k - 1, h], got.at[k - 1, h], sems, (k - 1, h), dev).start()

    def step(self, k, h):
        z = self.p.z
        block = jnp.minimum(z + k, TP - 1)
        self.one_way(k, h, z, block, self.got_up, self.out_up, self.ups, self.up)
        block = jnp.maximum(z - k, 0)
        self.one_way(k, h, TP - 1 - z, block, self.got_down, self.out_down, self.downs, self.down)

    def arrive(self, h):
        z = self.p.z

        @pl.when(z >= 1)
        def _():
            got = self.got_up.at[0, h]
            copy_to(got, got, self.ups, (0, h), self.up).wait_recv()

        @pl.when(z <= TP - 2)
        def _():
            got = self.got_down.at[0, h]
            copy_to(got, got, self.downs, (0, h), self.down).wait_recv()

    def total(self, h, at):
        total = self.parts[self.p.z, h, at].astype(F32) + self.got_up[0, h, at].astype(F32)
        return total + self.got_down[0, h, at].astype(F32)

    def close(self):
        z, got = self.p.z, self.got_up.at[0, 0]
        for h in range(self.halves):
            for k in range(1, TP):

                @pl.when(z + k <= TP - 1)
                def _():
                    copy_to(got, got, self.ups, (k - 1, h), self.up).wait_send()

                @pl.when(z - k >= 0)
                def _():
                    copy_to(got, got, self.downs, (k - 1, h), self.down).wait_send()


def greet_line(p, others=()):
    barrier = pltpu.get_barrier_semaphore()
    for dev in others:
        pl.semaphore_signal(barrier, inc=1, device_id=dev, device_id_type=MESH)

    @pl.when(p.z > 0)
    def _():
        pl.semaphore_signal(barrier, inc=1, device_id=device(p, z=p.z - 1), device_id_type=MESH)

    @pl.when(p.z < TP - 1)
    def _():
        pl.semaphore_signal(barrier, inc=1, device_id=device(p, z=p.z + 1), device_id_type=MESH)

    inner = (p.z > 0) & (p.z < TP - 1)

    @pl.when(inner)
    def _():
        pl.semaphore_wait(barrier, len(others) + 2)

    @pl.when(jnp.logical_not(inner))
    def _():
        pl.semaphore_wait(barrier, len(others) + 1)


class Spread:
    KINDS = ((0, 0), (0, 1), (1, 0), (1, 1))

    def __init__(self, p, whole, sems):
        self.p, self.whole, self.started = p, whole, []
        self.xs, self.fs, self.gs, self.cs = sems[0:2], sems[2:4], sems[4:6], sems[6:8]
        self.to_x, self.to_f = device(p, x=1 - p.x), device(p, f=1 - p.f)
        self.to_c = device(p, c=1 - p.c)

    @staticmethod
    def scratch():
        return [*pairs(TP), *pairs(TP), *pairs(TP), *pairs(4, TP)]

    def slot(self, kind, d, other_core=False):
        p, (f, x) = self.p, self.KINDS[kind]
        c = 1 - p.c if other_core else p.c
        return self.whole.at[(p.f + f) % 2, 0, (p.z - d) % TP, (p.x + x) % 2, c]

    def send(self, src, dst, sems, index, dev):
        copy = copy_to(src, dst, sems, index, dev)
        copy.start()
        self.started.append(copy)

    def wait(self, ref, sems, index):
        copy_to(ref, ref, sems, index, self.to_x).wait_recv()

    def spread(self, d, src=None):
        dst = self.slot(0, d)
        src = dst if src is None else src
        self.send(src, dst, self.xs, (d,), self.to_x)
        self.send(src, dst, self.fs, (d,), self.to_f)
        self.send(src, dst, self.cs, (0, d), self.to_c)

    def sides(self, d):
        ref = self.slot(1, d)
        self.wait(ref, self.xs, (d,))
        if d % 2 == 0:
            self.send(ref, ref, self.gs, (d,), self.to_f)
        self.send(ref, ref, self.cs, (1, d), self.to_c)
        ref = self.slot(2, d)
        self.wait(ref, self.fs, (d,))
        if d % 2 == 1:
            self.send(ref, ref, self.gs, (d,), self.to_x)
        self.send(ref, ref, self.cs, (2, d), self.to_c)

    def corner(self, d):
        ref = self.slot(3, d)
        self.wait(ref, self.gs, (d,))
        self.send(ref, ref, self.cs, (3, d), self.to_c)

    def close(self, pieces):
        for kind in range(4):
            for d in pieces:
                self.wait(self.slot(kind, d, True), self.cs, (kind, d))
        for copy in self.started:
            copy.wait_send()


def pack_kernel(bw, gelu, lru, out_t, blocks, small, gate, up, down_t, mix, *ffw):
    p = Place()
    heads = gelu.shape[1] // bw
    part, ffw_part = -(-heads // TP) * bw, gate.shape[1] // TP
    for d in range(TP):
        z = (p.z + d) % TP
        cols = pl.ds(pl.multiple_of(z * heads // TP * bw, 128), part)
        sources = [gelu[:, cols], lru[:, cols], out_t[:, cols], blocks[...], small[...]]
        offset = 0
        for source in sources:
            mix[d, :, offset : offset + source.shape[1]] = source
            offset += source.shape[1]
        cols = pl.ds(pl.multiple_of(z * ffw_part, 128), ffw_part)
        for i, source in enumerate((gate, up, down_t)):
            ffw[d][:, i * ffw_part : (i + 1) * ffw_part] = source[:, cols]


def pack(weights, bw):
    rows, lru_width = weights[0].shape
    part = -(-lru_width // bw // TP) * bw
    mix_cols = 3 * part + weights[3].shape[1] + weights[4].shape[1]
    piece = jax.ShapeDtypeStruct((rows, 3 * weights[5].shape[1] // TP), BF)
    mix, *ffw = pl.pallas_call(
        functools.partial(pack_kernel, bw),
        in_specs=[VMEM] * 8,
        out_specs=[VMEM] * (1 + TP),
        out_shape=[jax.ShapeDtypeStruct((TP, rows, mix_cols), BF), *[piece] * TP],
        compiler_params=pltpu.CompilerParams(vmem_limit_bytes=GRANT),
    )(*weights)
    return mix, ffw


def intake_kernel(mix_p, ffw_0, ffw_1, x_p, mix_w, ffw_w, x_all, zs, zr, us, ur, vs, vr, local, *sems):
    p = Place()
    mix, ffw = Spread(p, mix_w, sems[:8]), Spread(p, ffw_w, sems[8:])
    to_z = [device(p, z=(p.z + d) % TP) for d in range(TP)]
    greet(to_z[1:] + [mix.to_x, mix.to_f, mix.to_c])
    started = []

    def along_z(i, spread, src, d):
        copy = copy_to(src, spread.slot(0, 0), (zs, zr), (i,), to_z[d])
        copy.start()
        started.append(copy)

    def from_z(i, spread, d):
        ref = spread.slot(0, d)
        copy_to(ref, ref, (zs, zr), (i,), to_z[1]).wait_recv()

    for d in (1, 3, 2):
        along_z(d, mix, mix_p.at[d], d)
    mix.spread(0, mix_p.at[0])
    ffw.spread(0, ffw_0)
    stays = [
        pltpu.make_async_copy(mix_p.at[0], mix.slot(0, 0), local.at[0]),
        pltpu.make_async_copy(ffw_0, ffw.slot(0, 0), local.at[1]),
        pltpu.make_async_copy(x_p, x_all.at[p.z, 0], local.at[2]),
    ]
    for copy in stays:
        copy.start()
    line = Gather(p, x_all, (us, ur), (vs, vr))
    for d in (1, 3, 2):
        from_z(d, mix, d)
        mix.spread(d)
    line.begin(0, x_p)
    along_z(0, ffw, ffw_1, 1)
    mix.sides(0)
    ffw.sides(0)
    mix.corner(0)
    line.step(1, 0)
    for d in (1, 3):
        mix.sides(d)
    ffw.corner(0)
    line.step(2, 0)
    for d in (1, 3):
        mix.corner(d)
    mix.sides(2)
    line.step(3, 0)
    mix.corner(2)
    from_z(0, ffw, 1)
    mix.close(range(TP))
    ffw.close((0,))
    for copy in started:
        copy.wait_send()
    line.close(1)
    for copy in stays:
        copy.wait()


def intake(mix_p, ffw_0, ffw_1, x_p, p):
    whole = lambda v: jax.ShapeDtypeStruct((p.fs, 1, TP, 2, 2) + v.shape[-2:], BF)
    mix_w, ffw_w, x_all = pl.pallas_call(
        intake_kernel,
        in_specs=[ANY] * 4,
        out_specs=[ANY] * 3,
        out_shape=[whole(mix_p), whole(ffw_0), jax.ShapeDtypeStruct((TP, 1) + x_p.shape, BF)],
        scratch_shapes=[
            *pairs(TP),
            *pairs(TP - 1, 1),
            *pairs(TP - 1, 1),
            pltpu.SemaphoreType.DMA((3,)),
            *Spread.scratch(),
            *Spread.scratch(),
        ],
        compiler_params=pltpu.CompilerParams(collective_id=0, has_side_effects=True),
    )(mix_p, ffw_0, ffw_1, x_p)
    return mix_w.reshape(-1, mix_p.shape[-1]), ffw_w, x_all[:, 0]


def middle_kernel(with_ffw, *refs):
    parts, x_zero, gain, cot_p, piece_2, piece_3, _ = refs[:7]
    x_one, ffw_all, cot_all, ffw_w, own, local, gu0, gu1, gd0, gd1, cu0, cu1, cd0, cd1 = refs[7:21]
    p = Place()
    line = LineSum(p, parts, refs[21:29])
    out = Gather(p, ffw_all, (gu0, gu1), (gd0, gd1))
    cot = Gather(p, cot_all, (cu0, cu1), (cd0, cd1))
    halves, rows = parts.shape[1:3]
    line.clear()
    stays = []

    def stay(src, dst):
        copy = pltpu.make_async_copy(src, dst, local.at[len(stays)])
        copy.start()
        stays.append(copy)

    if with_ffw:
        ffw = Spread(p, ffw_w, refs[29:])
        greet_line(p, (ffw.to_x, ffw.to_f, ffw.to_c))
        stay(piece_3, ffw.slot(0, 3))
        stay(piece_2, ffw.slot(0, 2))
    else:
        greet_line(p)
    side = lambda name, *args: getattr(ffw, name)(*args) if with_ffw else None
    for h in range(halves):
        line.step(TP - 1, h)
    side("spread", 1)
    side("spread", 3, piece_3)
    side("spread", 2, piece_2)
    for k in range(TP - 2, 0, -1):
        for h in range(halves):
            line.step(k, h)
    for h in range(halves):
        line.arrive(h)

        def finish(at, h=h):
            value = x_zero[h, at].astype(F32) + line.total(h, at)
            x_one[h, at] = value
            own[h, at] = normed(value, gain[...]).astype(BF)

        by_rows(rows, finish)
        out.begin(h, own.at[h])
        stay(own.at[h], ffw_all.at[p.z, h])
    cot.begin(0, cot_p)
    stay(cot_p, cot_all.at[p.z, 0])
    for h in range(halves):
        out.step(1, h)
    for d in (1, 3, 2):
        side("sides", d)
    for h in range(halves):
        out.step(2, h)
    cot.step(1, 0)
    for h in range(halves):
        out.step(3, h)
    cot.step(2, 0)
    for d in (1, 3, 2):
        side("corner", d)
    cot.step(3, 0)
    side("close", (1, 2, 3))
    line.close()
    out.close(halves)
    cot.close(1)
    for copy in stays:
        copy.wait()


def middle(parts, x_zero, gain, cot_p, piece_2, piece_3, ffw_w):
    shape = parts.shape
    with_ffw = ffw_w is not None
    if not with_ffw:
        piece_2 = piece_3 = ffw_w = jnp.zeros((16, 128), BF)
    return pl.pallas_call(
        functools.partial(middle_kernel, with_ffw),
        in_specs=[VMEM] * 3 + [ANY] * 4,
        out_specs=[VMEM, ANY, ANY, ANY],
        out_shape=[
            jax.ShapeDtypeStruct(shape[1:], F32),
            jax.ShapeDtypeStruct(shape, BF),
            jax.ShapeDtypeStruct((TP, 1) + cot_p.shape, BF),
            jax.ShapeDtypeStruct(ffw_w.shape, BF),
        ],
        input_output_aliases={6: 3},
        scratch_shapes=[
            pltpu.VMEM(shape[1:], BF),
            pltpu.SemaphoreType.DMA((shape[1] + 3,)),
            *pairs(TP - 1, shape[1]),
            *pairs(TP - 1, shape[1]),
            *pairs(TP - 1, 1),
            *pairs(TP - 1, 1),
            *LineSum.scratch(shape),
            *(Spread.scratch() if with_ffw else []),
        ],
        compiler_params=pltpu.CompilerParams(
            collective_id=1, has_side_effects=True, vmem_limit_bytes=GRANT
        ),
    )(parts, x_zero, gain, cot_p, piece_2, piece_3, ffw_w)


def norm_back(values, gain, grad):
    inv = lax.rsqrt(jnp.mean(values * values, axis=-1, keepdims=True) + EPS)
    unit = values * inv
    through = grad * gain
    inner = jnp.mean(through * unit, axis=-1, keepdims=True)
    return inv * (through - unit * inner), grad * unit


class Fold:
    ORDER = ((0, 1, 1), (1, 1, 1), (0, 0, 1), (1, 1, 0), (0, 1, 0), (1, 0, 1), (0, 0, 0), (1, 0, 0))

    def __init__(self, p, grad, cores, scratch):
        self.p, self.grad, self.cores = p, grad, cores
        self.sums, self.stage, self.got, self.got_late = scratch[:4]
        self.near, self.staged = scratch[4:6]
        self.core_sems, self.early, self.late = scratch[6:8], scratch[8:10], scratch[10:12]
        self.to = (device(p, x=1 - p.x), device(p, f=1 - p.f))
        self.to_c = device(p, c=1 - p.c)

    @staticmethod
    def shapes(grad, staged):
        block = (TP // 2,) + grad.shape[-2:]
        waiting = (2,) if staged else (2, 2, 2)
        return jax.ShapeDtypeStruct((2, 2, 2) + block, BF), [
            pltpu.VMEM((2, 2, 2) + block, BF),
            pltpu.VMEM(waiting + block, BF),
            pltpu.VMEM((2, 2) + block, BF),
            pltpu.VMEM((2,) + block, BF),
            pltpu.SemaphoreType.DMA((8,)),
            pltpu.SemaphoreType.DMA((2,)),
            *pairs(8),
            *pairs(2, 2),
            *pairs(2),
        ]

    def block(self, way, f_rel, x_rel, c):
        p, half = self.p, TP // 2
        f, x = (p.f + f_rel) % 2, (p.x + x_rel) % 2
        return self.grad.at[f, 0, pl.ds(way * half, half), x, c]

    def cross(self, i):
        name = self.ORDER[i]
        src = self.block(*name, 1 - self.p.c)
        dst = self.stage if self.cores is None else self.cores
        return copy_to(src, dst.at[name], self.core_sems, (i,), self.to_c)

    def load(self, i):
        name = self.ORDER[i]
        return pltpu.make_async_copy(
            self.block(*name, self.p.c), self.sums.at[name], self.near.at[i]
        )

    def fetch(self, i):
        src = self.cores.at[self.ORDER[i]]
        return pltpu.make_async_copy(src, self.stage.at[i % 2], self.staged.at[i % 2])

    def first(self, way, block):
        src = self.sums.at[(0, block, 1) if way == 0 else (1, 1, block)]
        return copy_to(src, self.got.at[way, block], self.early, (way, block), self.to[way])

    def second(self, way):
        src = self.sums.at[(0, 1, 0) if way == 0 else (1, 0, 1)]
        return copy_to(src, self.got_late.at[way], self.late, (way,), self.to[1 - way])

    def add(self, name, *others):
        rows = self.sums.shape[-2]

        def turn(at):
            for k in range(TP // 2):
                total = self.sums[(*name, k, at)].astype(F32)
                for other in others:
                    total = total + other[k, at].astype(F32)
                self.sums[(*name, k, at)] = total.astype(BF)

        by_rows(rows, turn)

    def begin(self):
        for i in range(8):
            self.cross(i).start()
            self.load(i).start()

    def issue(self, i):
        self.cross(i).wait_recv()
        self.fetch(i).start()

    def join(self, i):
        if self.cores is None:
            self.cross(i).wait_recv()
            self.load(i).wait()
            self.add(self.ORDER[i], self.stage.at[self.ORDER[i]])
        else:
            if i == 0:
                self.issue(0)
            if i + 1 < 8:
                self.issue(i + 1)
            self.fetch(i).wait()
            self.load(i).wait()
            self.add(self.ORDER[i], self.stage.at[i % 2])
        if i < 4:
            way = self.ORDER[i][0]
            self.first(way, self.ORDER[i][1 + way]).start()

    def middle(self):
        for way in range(2):
            self.first(way, 1).wait_recv()
            self.add((0, 1, 0) if way == 0 else (1, 0, 1), self.got.at[way, 1])
            self.second(way).start()

    def finish(self):
        for way in range(2):
            self.first(way, 0).wait_recv()
            self.second(way).wait_recv()
            self.add((way, 0, 0), self.got.at[way, 0], self.got_late.at[way])

    def result(self, z):
        return self.sums.at[z // (TP // 2), 0, 0, z % (TP // 2)]

    def close(self):
        for i in range(8):
            self.cross(i).wait_send()
        for way in range(2):
            self.second(way).wait_send()
            for block in range(2):
                self.first(way, block).wait_send()


def folds_of(p, grads, cores, scratch):
    return [Fold(p, g, c, scratch[12 * i : 12 * i + 12]) for i, (g, c) in enumerate(zip(grads, cores))]


def turn_kernel(count, *refs):
    parts, out_parts, x_one, cot, gain = refs[:5]
    grads, refs = refs[5 : 5 + count], refs[5 + count :]
    mixed_out, grad_x_one, grad_gain, mix_all = refs[:4]
    pieces, cores, refs = refs[4 : 4 + TP], refs[4 + TP : 4 + TP + count], refs[4 + TP + count :]
    own, local, gu0, gu1, gd0, gd1 = refs[:6]
    p = Place()
    line, late = LineSum(p, parts, refs[6:14]), LineSum(p, out_parts, refs[14:22])
    folds = folds_of(p, grads, cores, refs[22:])
    out = Gather(p, mix_all, (gu0, gu1), (gd0, gd1))
    halves, rows = parts.shape[1:3]
    line.clear()
    late.clear()
    greet_line(p, (*folds[0].to, folds[0].to_c) if folds else ())
    for fold in folds:
        fold.begin()
    for h in range(halves):
        line.step(TP - 1, h)
    for h in range(halves):
        late.step(TP - 1, h)
    for fold in folds:
        fold.join(0)
        fold.join(1)
    for k in range(TP - 2, 0, -1):
        for h in range(halves):
            line.step(k, h)
        for fold in folds:
            fold.join(4 - k)
    stays = []

    def stay(src, dst):
        copy = pltpu.make_async_copy(src, dst, local.at[len(stays)])
        copy.start()
        stays.append(copy)

    grad_gain[...] = jnp.zeros(grad_gain.shape, F32)
    for h in range(halves):
        line.arrive(h)

        def finish(at, h=h):
            grad, gains = norm_back(x_one[h, at], gain[...], line.total(h, at))
            grad = grad + cot[h, at].astype(F32)
            grad_x_one[h, at] = grad
            own[h, at] = grad.astype(BF)
            grad_gain[0:1] += jnp.sum(gains, axis=0, keepdims=True)

        by_rows(rows, finish)
        out.begin(h, own.at[h])
        stay(own.at[h], mix_all.at[p.z, h])
    for fold in folds:
        for i in range(4, 8):
            fold.join(i)
    for h in range(halves):
        out.step(1, h)
        late.step(2, h)
    for fold in folds:
        fold.middle()
    for h in range(halves):
        out.step(2, h)
        late.step(1, h)
    for h in range(halves):
        out.step(3, h)
    for h in range(halves):
        late.arrive(h)

        def store(at, h=h):
            mixed_out[h, at] = (x_one[h, at] + late.total(h, at)).astype(BF)

        by_rows(rows, store)
    offset = 0
    for fold in folds:
        fold.finish()
        cols = fold.grad.shape[-1]
        for d in range(TP):
            stay(fold.result((p.z + d) % TP), pieces[d].at[:, pl.ds(offset, cols)])
        offset += cols
    for fold in folds:
        fold.close()
    line.close()
    late.close()
    out.close(halves)
    for copy in stays:
        copy.wait()


def turn(parts, out_parts, x_one, cot, gain, grads):
    shape, count = parts.shape, len(grads)
    folded = [Fold.shapes(grad, True) for grad in grads]
    rows = grads[0].shape[-2] if grads else 16
    piece = jax.ShapeDtypeStruct((rows, sum(g.shape[-1] for g in grads) if grads else 128), BF)
    results = pl.pallas_call(
        functools.partial(turn_kernel, count),
        in_specs=[VMEM] * 5 + [ANY] * count,
        out_specs=[VMEM, VMEM, VMEM, ANY] + [ANY] * (TP + count),
        out_shape=[
            jax.ShapeDtypeStruct(shape[1:], BF),
            jax.ShapeDtypeStruct(shape[1:], F32),
            jax.ShapeDtypeStruct((8, shape[-1]), F32),
            jax.ShapeDtypeStruct(shape, BF),
            *[piece] * TP,
            *(cores for cores, _ in folded),
        ],
        scratch_shapes=[
            pltpu.VMEM(shape[1:], BF),
            pltpu.SemaphoreType.DMA((shape[1] + TP * count,)),
            *pairs(TP - 1, shape[1]),
            *pairs(TP - 1, shape[1]),
            *LineSum.scratch(shape),
            *LineSum.scratch(shape),
            *(item for _, scratch in folded for item in scratch),
        ],
        compiler_params=pltpu.CompilerParams(
            collective_id=2, has_side_effects=True, vmem_limit_bytes=GRANT
        ),
    )(parts, out_parts, x_one, cot, gain, *grads)
    return results[: 4 + TP]


def final_kernel(count, *refs):
    parts, x_zero, gain, grad_x_one, vectors = refs[:5]
    grads, refs = refs[5 : 5 + count], refs[5 + count :]
    grad_in, sums = refs[:2]
    outs, cores, refs = refs[2 : 2 + count], [None] * count, refs[2 + count :]
    acc, got, vs, vr, zs, zr, local = refs[:7]
    p = Place()
    line = LineSum(p, parts, refs[7:15])
    folds = folds_of(p, grads, cores, refs[15:])
    halves, rows = parts.shape[1:3]
    line.clear()
    to_z = [device(p, z=(p.z + d) % TP) for d in range(TP)]
    (to_x, to_f), to_c = folds[0].to, folds[0].to_c
    greet(to_z[1:] + [to_x, to_f, to_c])
    partners = [to_c, to_x, to_f] + [
        device(p, z=p.z + bit * (1 - 2 * (p.z // bit % 2))) for bit in (1, 2)
    ]

    def vector(i):
        return copy_to(acc.at[i], got.at[i], (vs, vr), (i,), partners[i])

    def next_vector(i):
        vector(i).wait_recv()
        if i < 4:
            acc[i + 1] = acc[i] + got[i]
            vector(i + 1).start()
        else:
            sums[...] = acc[i] + got[i]

    acc[0] = vectors[...]
    vector(0).start()
    for fold in folds:
        fold.begin()
    for h in range(halves):
        line.step(TP - 1, h)
    started, stays = [], []

    def send_on(m):
        folds[m].finish()
        for d in (1, 3, 2):
            src = folds[m].result((p.z + d) % TP)
            copy = copy_to(src, outs[m].at[p.z], (zs, zr), (m, d - 1), to_z[d])
            copy.start()
            started.append(copy)
        stays.append(pltpu.make_async_copy(folds[m].result(p.z), outs[m].at[p.z], local.at[m]))
        stays[-1].start()

    for i in range(4):
        folds[0].join(i)
    for m, fold in enumerate(folds):
        fold.join(4)
        fold.join(5)
        if m + 1 < count:
            folds[m + 1].join(0)
            folds[m + 1].join(1)
        fold.middle()
        if m + 1 < count:
            folds[m + 1].join(2)
            folds[m + 1].join(3)
        fold.join(6)
        fold.join(7)
        if m < TP - 2:
            for h in range(halves):
                line.step(TP - 2 - m, h)
        next_vector(m)
        if m > 0:
            send_on(m - 1)
    next_vector(3)
    for h in range(halves):
        line.arrive(h)

        def finish(at, h=h):
            grad, _ = norm_back(x_zero[h, at].astype(F32), gain[...], line.total(h, at))
            grad_in[h, at] = grad_x_one[h, at] + grad

        by_rows(rows, finish)
    next_vector(4)
    send_on(count - 1)
    for m in range(count):
        for d in range(1, TP):
            ref = outs[m].at[(p.z - d) % TP]
            copy_to(ref, ref, (zs, zr), (m, d - 1), to_z[1]).wait_recv()
    for copy in started:
        copy.wait_send()
    for i in range(5):
        vector(i).wait_send()
    for fold in folds:
        fold.close()
    line.close()
    for copy in stays:
        copy.wait()


def final(parts, x_zero, gain, grad_x_one, vectors, grads):
    shape, count = parts.shape, len(grads)
    folded = [Fold.shapes(grad, False) for grad in grads]
    results = pl.pallas_call(
        functools.partial(final_kernel, count),
        in_specs=[VMEM] * 5 + [ANY] * count,
        out_specs=[VMEM, VMEM] + [ANY] * count,
        out_shape=[
            jax.ShapeDtypeStruct(shape[1:], F32),
            jax.ShapeDtypeStruct(vectors.shape, F32),
            *(jax.ShapeDtypeStruct((TP,) + grad.shape[-2:], BF) for grad in grads),
        ],
        scratch_shapes=[
            pltpu.VMEM((5,) + vectors.shape, F32),
            pltpu.VMEM((5,) + vectors.shape, F32),
            *pairs(5),
            *pairs(count, TP - 1),
            pltpu.SemaphoreType.DMA((count,)),
            *LineSum.scratch(shape),
            *(item for _, scratch in folded for item in scratch),
        ],
        compiler_params=pltpu.CompilerParams(
            collective_id=3, has_side_effects=True, vmem_limit_bytes=GRANT
        ),
    )(parts, x_zero, gain, grad_x_one, vectors, *grads)
    return results[0], results[1], results[2 : 2 + count]


def chain_kernel(backward, sums, *refs):
    if backward:
        known, start, spans, send, recv = refs
    else:
        start, spans, send, recv = refs
    p = Place()
    peers = [device_q(p, (p.q + d) % NQ) for d in range(NQ)]
    greet(peers[1:])
    spans[p.q] = sums[...]
    copies = []
    for d in range(1, NQ):
        copies.append(copy_to(spans.at[p.q], spans.at[p.q], (send, recv), (d,), peers[d]))
        copies[-1].start()
    for d in range(1, NQ):
        ref = spans.at[(p.q - d) % NQ]
        copy_to(ref, ref, (send, recv), (d,), peers[d]).wait_recv()
    micro = sums.shape[1] // TP
    carry = jnp.zeros((micro, sums.shape[2]), F32)
    order = [(z, q) for z in range(TP) for q in range(NQ)]
    for z, q in reversed(order) if backward else order:
        here = slice(z * micro, (z + 1) * micro)

        @pl.when(p.q == q)
        def _(carry=carry, here=here):
            start[here] = carry

        decay = known[q, 0, here] if backward else spans[q, 0, here]
        carry = decay * carry + spans[q, 0 if backward else 1, here]
    for copy in copies:
        copy.wait_send()


def device_q(p, q):
    return device(p, x=q // 2, c=q % 2)


def chain(sums, known=None):
    backward = known is not None
    every = (NQ,) + sums.shape
    return pl.pallas_call(
        functools.partial(chain_kernel, backward),
        in_specs=[VMEM] * (2 if backward else 1),
        out_specs=[VMEM, VMEM],
        out_shape=[
            jax.ShapeDtypeStruct(sums.shape[1:], F32),
            jax.ShapeDtypeStruct(every, F32),
        ],
        scratch_shapes=pairs(NQ),
        cost_estimate=FREE,
        compiler_params=pltpu.CompilerParams(
            collective_id=5 if backward else 4, has_side_effects=True
        ),
    )(*((sums, known) if backward else (sums,)))


def unpack_kernel(own, one, two, three, *outs):
    p = Place()
    part = own.shape[1] // len(outs)
    for d, piece in enumerate((own, one, two, three)):
        cols = pl.ds(pl.multiple_of((p.z - d) % TP * part, 128), part)
        for i, out in enumerate(outs):
            out[:, cols] = piece[:, i * part : (i + 1) * part].astype(F32)


def unpack(pieces, count):
    rows, cols = pieces[0].shape
    return pl.pallas_call(
        unpack_kernel,
        in_specs=[VMEM] * TP,
        out_specs=[VMEM] * count,
        out_shape=[jax.ShapeDtypeStruct((rows, cols // count * TP), F32)] * count,
        compiler_params=pltpu.CompilerParams(vmem_limit_bytes=GRANT),
    )(*pieces)


def geglu(gate_vals, up_vals):
    return jax.nn.gelu(gate_vals) * up_vals


def all_spans(value, p):
    by_q = everywhere(value, shift_q, p.q, NQ)
    by_r = everywhere(by_q, shift_r, p.r, p.rests)
    return jnp.swapaxes(by_r, 1, 2).reshape((-1,) + value.shape[1:])


def own_spans(spans, p):
    split = spans.reshape((p.rests, TP, NQ) + spans.shape[1:])
    return lax.dynamic_index_in_dim(at(split, p.r), p.q, 1, keepdims=False)


def on_device(
    inputs,
    cotangent,
    proj_gelu,
    proj_lru,
    gate_blocks,
    proj_out,
    ffw_gate,
    ffw_up,
    ffw_down,
    norm_mix,
    norm_ffw,
    decay_param,
    conv_taps,
):
    p = Place()
    micro, span, width = inputs.shape[0], inputs.shape[2], inputs.shape[3]
    lru_width = proj_gelu.shape[1]
    tap_count = conv_taps.shape[1]
    block_width = gate_blocks.shape[1] // 2
    heads = lru_width // block_width
    ffw_part = ffw_gate.shape[1] // TP
    rows = proj_gelu.shape[0]
    held = -(-heads // TP)
    first = [k * heads // TP for k in range(TP)]
    owned = [range(first[k], first[k + 1] if k + 1 < TP else heads) for k in range(TP)]
    part = held * block_width

    out_t, down_t = proj_out.T, ffw_down.T
    small = jnp.concatenate([norm_mix[None], norm_ffw[None], decay_param[None], conv_taps.T])
    small = jnp.pad(small, ((0, 128 - small.shape[0]), (0, 0))).T
    x_rows, cot = inputs[:, 0], cotangent[:, 0]
    one = 1 if p.rests == 1 else 0
    edge = lax.ppermute(
        x_rows[:, span - (tap_count - 1) :],
        "seq",
        [(i, i + 1) for i in range(lax.axis_size("seq") - 1)],
    )
    edge = jnp.pad(edge, ((0, 0), (HALO - (tap_count - 1), 0), (0, 0)))
    x_wide = jnp.concatenate([x_rows.reshape(-1, width), edge.reshape(-1, width)])
    if p.rests == 1:
        weights = (proj_gelu, proj_lru, out_t, gate_blocks, small, ffw_gate, ffw_up, down_t)
        mix_pieces, ffw_pieces = pack(weights, block_width)
        mix_w, ffw_w, x_all = intake(
            mix_pieces, ffw_pieces[0], ffw_pieces[1], x_wide, p
        )
        piece_2, piece_3, x_all = lax.optimization_barrier((*ffw_pieces[2:], x_all))
        piece_3, piece_2 = shift_z(piece_3, 3), shift_z(piece_2, 2)
    else:
        mix_pieces, ffw_pieces = [], []
        for k in range(TP):
            cols = slice(first[k] * block_width, first[k] * block_width + part)
            pieces = [proj_gelu[:, cols], proj_lru[:, cols], out_t[:, cols], gate_blocks, small]
            mix_pieces.append(jnp.concatenate(pieces, axis=1))
            cols = slice(k * ffw_part, (k + 1) * ffw_part)
            pieces = [ffw_gate[:, cols], ffw_up[:, cols], down_t[:, cols]]
            ffw_pieces.append(jnp.concatenate(pieces, axis=1))
        mix_w = weights_in(jnp.stack(mix_pieces), p)
        whole_ffw = weights_in(jnp.stack(ffw_pieces), p)
        x_all, piece_2, piece_3, ffw_w = gather_z(x_wide, p), None, None, None
    dims = (span, micro, heads, held, block_width, tap_count)
    small_w, rows_w, mixed, pre, conv, gate, state, prod, sums = recur(
        x_all.reshape(-1, width), mix_w, dims
    )
    mix_gain, ffw_gain = small_w[0:1], small_w[1:2]
    start = sum(jnp.where(p.z == k, first[k] * block_width, 0) for k in range(TP))

    ends = (TP, micro, part)
    if p.rests == 1:
        state_in, every_sum = chain(sums)
    else:
        sums = all_spans(jnp.stack([sums[0].reshape(ends), sums[1].reshape(ends)], axis=1), p)
        carry, carries = jnp.zeros_like(sums[0, 0]), []
        for k in range(sums.shape[0]):
            carries.append(carry)
            carry = sums[k, 0] * carry + sums[k, 1]
        state_in = own_spans(jnp.stack(carries), p).reshape(-1, part)
    mix_bf, out_parts = recur_mix(pre, rows_w, state, prod, state_in, mix_w, dims)
    blocked = (TP, micro, span, width)
    out_parts = out_parts.reshape(blocked)
    x_one, ffw_bf, cot_all, ffw_w = middle(
        out_parts, x_rows, ffw_gain, cot.reshape(-1, width), piece_2, piece_3, ffw_w
    )
    cot_all = cot_all.reshape(-1, width)
    ffw_w = ffw_w.reshape(width, -1) if p.rests == 1 else whole_ffw

    ffw_bf = ffw_bf.reshape(-1, width)
    gate_up_w, down_w = ffw_w[:, : 2 * ffw_part], ffw_w[:, 2 * ffw_part :]
    gate_up = dot_plain(ffw_bf, gate_up_w)
    gate_vals, up_vals = gate_up[:, :ffw_part], gate_up[:, ffw_part:]
    hidden_bf = geglu(gate_vals, up_vals).astype(BF)
    grad_hidden = dot_plain(cot_all, down_w)
    _, pull_back = jax.vjp(geglu, gate_vals, up_vals)
    grad_gate_up = jnp.concatenate(pull_back(grad_hidden), axis=1).astype(BF)
    ffw_parts = dot_right_t(hidden_bf, down_w).astype(BF).reshape(blocked)
    grad_in_parts = dot_right_t(grad_gate_up, gate_up_w).astype(BF).reshape(blocked)
    ffw_grads = [dot_left_t(ffw_bf, grad_gate_up), dot_left_t(cot_all, hidden_bf)]
    ffw_grads = [grad.astype(BF) for grad in ffw_grads]
    mixed_out, grad_x_one, gain_rows, grad_mix, *ffw_pieces = turn(
        grad_in_parts, ffw_parts, x_one, cot, ffw_gain, [by_owner(g, p) for g in ffw_grads] * one
    )
    if p.rests == 1:
        for d in (1, 3, 2):
            ffw_pieces[d] = shift_z(ffw_pieces[d], d)
    grad_mix = grad_mix.reshape(-1, width)

    grad_gelu_bf, local_back, prod_back, back_sums = recur_back(
        grad_mix, pre, rows_w, state, prod, state_in, gate, mix_w, dims
    )
    if p.rests == 1:
        carried, _ = chain(back_sums[None], every_sum)
    else:
        back_sums = all_spans(back_sums.reshape(ends), p)
        carry, carries = jnp.zeros_like(sums[0, 0]), []
        for k in range(sums.shape[0] - 1, -1, -1):
            carries.append(carry)
            carry = sums[k, 0] * carry + back_sums[k]
        carried = own_spans(jnp.stack(carries[::-1]), p).reshape(-1, part)
    block_mats = lax.dynamic_slice(mix_w, (start, 3 * part), (part, 2 * block_width))
    grad_blocks, grad_lru, spill, row_grads = recur_grad(
        local_back, prod_back, carried, state, prod, state_in, gate, conv, pre, rows_w,
        block_mats.reshape(held, block_width, 2 * block_width), dims,
    )
    spill = spill.reshape(TP, micro, HALO, part)
    from_next = shift_q(spill, -1)
    last = jnp.zeros_like(spill[:1])
    if p.rests > 1:
        last = move(spill[:1], lambda r, z, q: (r - 1, z, NQ - 1) if q == 0 and r > 0 else None)
    from_next = jnp.where(
        p.q == NQ - 1, jnp.concatenate([from_next[1:], last], axis=0), from_next
    )
    grad_pair, grad_mixed_parts, mix_gain_rows = recur_in(
        grad_gelu_bf, grad_lru, from_next.reshape(-1, part), rows_w, small_w, mixed, mix_w, dims
    )
    grad_mixed_parts = grad_mixed_parts.reshape(blocked)

    blocks_all = lax.dynamic_update_slice_in_dim(
        jnp.zeros((lru_width, 2 * block_width), BF),
        (grad_blocks * rows_w[6][:, None]).astype(BF),
        start,
        0,
    )
    mix_grads = [dot_left_t(mixed, grad_pair), dot_left_t(grad_mix, mix_bf), blocks_all]
    mix_grads = [grad.astype(BF) for grad in mix_grads]
    vectors = lax.dynamic_update_slice_in_dim(
        jnp.zeros((1 + tap_count, lru_width), F32), row_grads[: 1 + tap_count], start, 1
    )
    vectors = jnp.concatenate([mix_gain_rows[:1], gain_rows[:1], vectors], axis=0)
    vectors = jnp.pad(vectors, ((0, -vectors.shape[0] % 8), (0, 0)))
    if p.rests == 1:
        grad_inputs, vectors, mix_grads = final(
            grad_mixed_parts, x_rows, mix_gain, grad_x_one, vectors,
            [by_owner(grad, p) for grad in mix_grads],
        )
    else:
        mix_grads = [grads_out(grad, p) for grad in mix_grads]
        grad_mixed_own = scatter_z(grad_mixed_parts, p)
        grad_inputs = grad_x_one + norm_back(x_rows.astype(F32), mix_gain, grad_mixed_own)[0]
        for exchange in (swap_core, swap_x, swap_f):
            vectors = vectors + exchange(vectors)
        for bit in (1, 2):
            vectors = vectors + move(vectors, lambda r, z, q, bit=bit: (r, z ^ bit, q))
        total = vectors
        for d in range(1, p.rests):
            total = total + shift_r(vectors, d)
        vectors = total
    vectors = lax.dynamic_slice_in_dim(vectors, p.index * rows, rows, 1)

    def mix_columns(grad, offset):
        picked = [
            grad[k][
                :,
                offset + (owned[k][0] - first[k]) * block_width : offset
                + (owned[k][-1] + 1 - first[k]) * block_width,
            ]
            for k in range(TP)
        ]
        return jnp.concatenate(picked, axis=1).astype(F32)

    if p.rests == 1:
        share_gate, share_up, share_down = unpack(ffw_pieces, 3)
    else:
        ffw_grads = [grads_out(grad, p) for grad in ffw_grads]
        beside = lambda v: jnp.swapaxes(v, 0, 1).reshape(rows, -1).astype(F32)
        share_gate = beside(ffw_grads[0][:, :, :ffw_part])
        share_up = beside(ffw_grads[0][:, :, ffw_part:])
        share_down = beside(ffw_grads[1])
    shape = (micro, 1, span, width)
    return (
        mixed_out.reshape(shape),
        grad_inputs.reshape(shape),
        mix_columns(mix_grads[0], 0),
        mix_columns(mix_grads[0], part),
        jnp.sum(mix_grads[2].astype(F32), axis=0),
        mix_columns(mix_grads[1], 0).T,
        share_gate,
        share_up,
        share_down.T,
        vectors[0],
        vectors[1],
        vectors[2],
        vectors[3 : 3 + tap_count].T,
    )


def solution(mesh):
    in_specs = (
        P(None, "fsdp", "seq", None),
        P(None, "fsdp", "seq", None),
        P(("fsdp", "seq"), None),
        P(("fsdp", "seq"), None),
        P(("fsdp", "seq"), None),
        P(None, ("fsdp", "seq")),
        P(("fsdp", "seq"), None),
        P(("fsdp", "seq"), None),
        P(None, ("fsdp", "seq")),
        P(("fsdp", "seq")),
        P(("fsdp", "seq")),
        P(("fsdp", "seq")),
        P(("fsdp", "seq"), None),
    )
    out_specs = (
        P(None, "fsdp", "seq", None),
        P(None, "fsdp", "seq", None),
        P(("fsdp", "seq"), None),
        P(("fsdp", "seq"), None),
        P(("fsdp", "seq"), None),
        P(None, ("fsdp", "seq")),
        P(("fsdp", "seq"), None),
        P(("fsdp", "seq"), None),
        P(None, ("fsdp", "seq")),
        P(("fsdp", "seq")),
        P(("fsdp", "seq")),
        P(("fsdp", "seq")),
        P(("fsdp", "seq"), None),
    )
    return jax.shard_map(
        on_device, mesh=mesh, in_specs=in_specs, out_specs=out_specs, check_vma=False
    )
```

```python
import functools

import jax
import jax.numpy as jnp
from jax import lax
from jax.experimental import pallas as pl
from jax.experimental.pallas import tpu as pltpu
from jax.sharding import PartitionSpec as P

EPS = 1e-06
GUARD = 0.001
RATE = 8.0
TP = 4
NQ = 4
HALO = 8
BF = jnp.bfloat16
F32 = jnp.float32
MESH = pl.DeviceIdType.MESH
ANY = pl.BlockSpec(memory_space=pl.ANY)
VMEM = pl.BlockSpec(memory_space=pltpu.VMEM)
GRANT = 60 * 1024 * 1024
FREE = pl.CostEstimate(flops=0, bytes_accessed=0, transcendentals=0)


def move(value, step):
    pairs = []
    for here in range(lax.axis_size("seq")):
        there = step(here // (TP * NQ), here // NQ % TP, here % NQ)
        if there is not None:
            pairs.append((here, (there[0] * TP + there[1]) * NQ + there[2]))
    return lax.ppermute(value, "seq", pairs)


def swap_core(value):
    return move(value, lambda r, z, q: (r, z, q ^ 1))


def swap_x(value):
    return move(value, lambda r, z, q: (r, z, q ^ 2))


def swap_f(value):
    return lax.ppermute(value, "fsdp", [(0, 1), (1, 0)])


def shift_z(value, d):
    return move(value, lambda r, z, q: (r, (z + d) % TP, q))


def shift_q(value, d):
    return move(value, lambda r, z, q: (r, z, (q + d) % NQ))


def shift_r(value, d):
    count = lax.axis_size("seq") // (TP * NQ)
    return move(value, lambda r, z, q: ((r + d) % count, z, q))


def hop(value, d, low, high):
    return move(value, lambda r, z, q: (r, z + d, q) if low <= z <= high else None)


class Place:
    def __init__(self):
        seq = lax.axis_index("seq")
        self.f = lax.axis_index("fsdp")
        self.r, self.z, self.q = seq // (TP * NQ), seq // NQ % TP, seq % NQ
        self.x, self.c = self.q // 2, self.q % 2
        self.rests = lax.axis_size("seq") // (TP * NQ)
        self.fs = lax.axis_size("fsdp")
        self.index = self.f * lax.axis_size("seq") + seq


def at(value, index):
    return lax.dynamic_index_in_dim(value, index, 0, keepdims=False)


def put(base, value, *index):
    starts = [jnp.int32(0) if i is None else jnp.int32(i) for i in index]
    starts += [jnp.int32(0)] * (base.ndim - len(index))
    for dim, i in enumerate(index):
        if i is not None:
            value = jnp.expand_dims(value, dim)
    return lax.dynamic_update_slice(base, value, starts)


def everywhere(value, shifter, mine, count):
    out = put(jnp.zeros((count,) + value.shape, value.dtype), value, mine)
    for d in range(1, count):
        out = put(out, shifter(value, d), (mine - d) % count)
    return out


def gather_z(value, p):
    ups, downs = [], []
    up = down = value
    for k in range(1, TP):
        up = hop(up, 1, k - 1, TP - 2)
        down = hop(down, -1, 1, TP - k)
        ups.append(up)
        downs.append(down)
    out = put(jnp.zeros((TP,) + value.shape, value.dtype), value, p.z)
    for k in range(1, TP):
        out = put(out, downs[k - 1] + ups[TP - 1 - k], (p.z + k) % TP)
    return out


def scatter_z(parts, p):
    right = left = None
    for k in range(TP - 1, 0, -1):
        send = at(parts, (p.z + k) % TP)
        if right is not None:
            send = (send.astype(F32) + right.astype(F32)).astype(BF)
        right = hop(send, 1, 0, TP - 1 - k)
        send = at(parts, (p.z - k) % TP)
        if left is not None:
            send = (send.astype(F32) + left.astype(F32)).astype(BF)
        left = hop(send, -1, k, TP - 1)
    return at(parts, p.z).astype(F32) + right.astype(F32) + left.astype(F32)


def weights_in(pieces, p):
    rows, cols = pieces.shape[1:]
    mine = put(jnp.zeros(pieces.shape, BF), at(pieces, p.z), p.z)
    for d in range(1, TP):
        mine = put(mine, shift_z(at(pieces, (p.z + d) % TP), d), (p.z - d) % TP)
    mine = everywhere(mine, shift_r, p.r, p.rests)
    half = TP // 2
    by_x, by_f = swap_x(mine), swap_f(mine)
    corner = (swap_f(by_x[:, :half]), swap_x(by_f[:, half:]))
    whole = jnp.zeros((p.fs, p.rests, TP, 2, 2, rows, cols), BF)
    for block, f, x, z in (
        (mine, p.f, p.x, 0),
        (by_x, p.f, 1 - p.x, 0),
        (by_f, 1 - p.f, p.x, 0),
        (corner[0], 1 - p.f, 1 - p.x, 0),
        (corner[1], 1 - p.f, 1 - p.x, half),
    ):
        other = swap_core(block)
        for part, c in ((block, p.c), (other, 1 - p.c)):
            part = part[None, :, :, None, None]
            whole = lax.dynamic_update_slice(
                whole, part, [jnp.int32(i) for i in (f, 0, z, x, c, 0, 0)]
            )
    return whole.reshape(-1, cols)


def by_owner(grad, p):
    return grad.reshape(p.fs, p.rests, TP, 2, 2, -1, grad.shape[1])


def to_owner_z(total, p):
    out = put(jnp.zeros(total.shape, BF), at(total, p.z), p.z)
    for d in (1, 3, 2):
        out = put(out, shift_z(at(total, (p.z + d) % TP), d), (p.z - d) % TP)
    return out


def grads_out(grad, p):
    plus = lambda a, b: (a.astype(F32) + b.astype(F32)).astype(BF)
    pick = lambda v, dim, i: lax.dynamic_index_in_dim(v, i, dim, keepdims=False)
    total = by_owner(grad, p)
    total = plus(pick(total, 4, p.c), swap_core(pick(total, 4, 1 - p.c)))
    total = plus(pick(total, 3, p.x), swap_x(pick(total, 3, 1 - p.x)))
    total = plus(at(total, p.f), swap_f(at(total, 1 - p.f)))
    mine = at(total, p.r)
    for d in range(1, p.rests):
        mine = plus(mine, shift_r(at(total, (p.r + d) % p.rests), d))
    return to_owner_z(mine, p)


def dot_left_t(left_mat, right_mat):
    return lax.dot_general(
        left_mat, right_mat, (((0,), (0,)), ((), ())), preferred_element_type=F32
    )


def dot_plain(left_mat, right_mat):
    return jnp.dot(left_mat, right_mat, preferred_element_type=F32)


def dot_right_t(left_mat, right_mat):
    return lax.dot_general(
        left_mat, right_mat, (((1,), (1,)), ((), ())), preferred_element_type=F32
    )


def normed(values, gain_vec):
    return values * lax.rsqrt(jnp.mean(values * values, axis=-1, keepdims=True) + EPS) * gain_vec


def gelu_pair(v):
    scale = 0.7978845608028654
    inner = jnp.tanh(scale * (v + 0.044715 * v * v * v))
    slope = 0.5 * v * (1.0 - inner * inner) * scale * (1.0 + 0.134145 * v * v)
    return 0.5 * v * (1.0 + inner), 0.5 * (1.0 + inner) + slope


def span_scan(decay, drive, backward):
    count = decay.shape[0]
    row = lax.broadcasted_iota(jnp.int32, decay.shape, 0)
    step = 1
    while step < count:
        inside = row < count - step if backward else row >= step
        turn = count - step if backward else step
        drive = drive + jnp.where(inside, decay * pltpu.roll(drive, turn, 0), 0.0)
        decay = decay * jnp.where(inside, pltpu.roll(decay, turn, 0), 1.0)
        step *= 2
    return decay, drive


def gate_values(gate, soft):
    half = gate.shape[1] // 2
    rec_gate = jax.nn.sigmoid(gate[:, :half])
    in_gate = jax.nn.sigmoid(gate[:, half:])
    log_decay = -RATE * rec_gate * soft
    square = jnp.exp(2.0 * log_decay)
    return rec_gate, in_gate, jnp.exp(log_decay), square, jnp.sqrt(1.0 - square + GUARD)


def main_rows(i, span, micro):
    return pl.ds(i // micro * micro * (span + HALO) + i % micro * span, span)


def with_halo(pre, i, span, micro):
    start = i // micro * micro * (span + HALO) + micro * span + i % micro * HALO
    both = [pre[pl.ds(start, HALO)], pre[main_rows(i, span, micro)]]
    return jnp.concatenate(both, axis=0)


def recur_head(span, micro, pre, rows, block, conv, gate, state, prod, sums):
    count = conv.shape[0] // span
    soft, taps = rows[0:1], [rows[k + 2 : k + 3] for k in range(4)]
    for i in range(count):
        vals = with_halo(pre, i, span, micro).astype(BF).astype(F32)
        total = taps[0] * vals
        for k in range(1, 4):
            total = total + taps[k] * pltpu.roll(vals, k, 0)
        conv[pl.ds(i * span, span)] = total[HALO:].astype(BF)
    gate[...] = dot_plain(conv[...], block[...])
    for i in range(count):
        here = pl.ds(i * span, span)
        _, in_gate, decay, _, root = gate_values(gate[here], soft)
        decay, local = span_scan(decay, root * in_gate * conv[here].astype(F32), False)
        state[here] = local
        prod[here] = decay
        sums[0, i : i + 1] = decay[span - 1 :]
        sums[1, i : i + 1] = local[span - 1 :]


def columns(ref, h, width):
    return ref.at[:, pl.ds(pl.multiple_of(h * width, 128), width)]


def by_heads(count, body):
    def turn(h, _):
        body(h)
        return 0

    lax.fori_loop(0, count, turn, 0)


def recur_kernel(
    dims, x_all, mix_w, small, rows, mixed, pre, conv, gate, state, prod, sums,
    small_w, gl_w, block_w, mixed_all, sems,
):
    span, micro, heads, held, bw, taps = dims
    part = held * bw
    p = Place()
    start = pl.multiple_of(p.z * heads // TP * bw, 128)
    pieces = (
        (mix_w.at[:, pl.ds(3 * part + 2 * bw, 128)], small_w),
        (mix_w.at[:, pl.ds(0, 2 * part)], gl_w),
        (mix_w.at[pl.ds(start, part), pl.ds(3 * part, 2 * bw)], block_w),
    )
    loads = [pltpu.make_async_copy(src, dst, sems.at[i]) for i, (src, dst) in enumerate(pieces)]
    for load in loads:
        load.start()
    loads[0].wait()
    row = lax.broadcasted_iota(jnp.int32, (8, 128), 0)
    lane = lax.broadcasted_iota(jnp.int32, (8, 128), 1)
    small[...] = dot_right_t(jnp.where(row == lane, 1.0, 0.0).astype(BF), small_w[...])
    own = small[:, pl.ds(start, part)]
    decay = -own[2:3]
    feature = lax.broadcasted_iota(jnp.int32, (1, part), 1)
    count = ((p.z + 1) * heads // TP - p.z * heads // TP) * bw
    rows[0:1] = jnp.maximum(decay, 0.0) + jnp.log1p(jnp.exp(-jnp.abs(decay)))
    rows[1:2] = jax.nn.sigmoid(decay)
    rows[2 : 2 + taps] = own[3 : 3 + taps]
    rows[6:7] = jnp.where(feature < count, 1.0, 0.0)
    rows[7:8] = jnp.zeros((1, part), F32)
    gain, wide, step = small[0:1], micro * (span + HALO), 16

    def norm(z, _):
        for k in range(0, wide, step):
            vals = x_all[pl.ds(pl.multiple_of(z * wide + k, step), step)].astype(F32)
            vals = normed(vals, gain).astype(BF)
            mixed_all[pl.ds(pl.multiple_of(z * wide + k, step), step)] = vals
            if k < micro * span:
                mixed[pl.ds(pl.multiple_of(z * micro * span + k, step), step)] = vals
        return 0

    lax.fori_loop(0, TP, norm, 0)
    loads[1].wait()

    def project(h):
        cols = pl.ds(pl.multiple_of(h * bw, 128), bw)
        pre[:, cols] = dot_plain(mixed_all[...], gl_w[:, cols])

    by_heads(2 * held, project)
    loads[2].wait()

    def one_head(h):
        block = block_w.at[pl.ds(pl.multiple_of(h * bw, 128), bw)]
        sums_h = sums.at[:, :, pl.ds(pl.multiple_of(h * bw, 128), bw)]
        recur_head(
            span, micro, columns(pre, held + h, bw), columns(rows, h, bw), block,
            columns(conv, h, bw), columns(gate, h, 2 * bw), columns(state, h, bw),
            columns(prod, h, bw), sums_h,
        )

    by_heads(held, one_head)


def recur(x_all, mix_w, dims):
    span, micro, _, held, bw, _ = dims
    part, width = held * bw, x_all.shape[1]
    tokens = x_all.shape[0] // (span + HALO) * span
    shapes = [((8, width), F32), ((8, part), F32), ((tokens, width), BF)]
    shapes += [((x_all.shape[0], 2 * part), F32), ((tokens, part), BF), ((tokens, 2 * part), F32)]
    shapes += [((tokens, part), F32), ((tokens, part), F32), ((2, tokens // span, part), F32)]
    return pl.pallas_call(
        functools.partial(recur_kernel, dims),
        in_specs=[VMEM, ANY],
        out_specs=[VMEM] * len(shapes),
        out_shape=[jax.ShapeDtypeStruct(*shape) for shape in shapes],
        scratch_shapes=[
            pltpu.VMEM((width, 128), BF),
            pltpu.VMEM((width, 2 * part), BF),
            pltpu.VMEM((part, 2 * bw), BF),
            pltpu.VMEM(x_all.shape, BF),
            pltpu.SemaphoreType.DMA((3,)),
        ],
        cost_estimate=FREE,
        compiler_params=pltpu.CompilerParams(vmem_limit_bytes=GRANT),
    )(x_all, mix_w)


def recur_mix_kernel(dims, pre, rows, state, prod, start, mix_w, mix, parts, out_w, sem):
    span, micro, _, held, bw, _ = dims
    part = held * bw
    load = pltpu.make_async_copy(mix_w.at[:, pl.ds(2 * part, part)], out_w, sem.at[0])
    load.start()

    def one_head(h):
        pre_h, state_h, prod_h = columns(pre, h, bw), columns(state, h, bw), columns(prod, h, bw)
        rows_h, start_h, mix_h = columns(rows, h, bw), columns(start, h, bw), columns(mix, h, bw)
        for i in range(state.shape[0] // span):
            here = pl.ds(i * span, span)
            act, _ = gelu_pair(pre_h[main_rows(i, span, micro)])
            states = state_h[here] + prod_h[here] * start_h[i : i + 1]
            mix_h[here] = (states * act * rows_h[6:7]).astype(BF)

    by_heads(held, one_head)
    load.wait()

    def project(j):
        cols = pl.ds(pl.multiple_of(j * 256, 256), 256)
        parts[:, cols] = dot_right_t(mix[...], out_w[cols]).astype(BF)

    by_heads(out_w.shape[0] // 256, project)


def recur_mix(pre, rows, state, prod, start, mix_w, dims):
    tokens, part = state.shape
    width = mix_w.shape[0]
    return pl.pallas_call(
        functools.partial(recur_mix_kernel, dims),
        in_specs=[VMEM] * 5 + [ANY],
        out_specs=[VMEM, VMEM],
        out_shape=[
            jax.ShapeDtypeStruct((tokens, part), BF),
            jax.ShapeDtypeStruct((tokens, width), BF),
        ],
        scratch_shapes=[pltpu.VMEM((width, part), BF), pltpu.SemaphoreType.DMA((1,))],
        cost_estimate=FREE,
        compiler_params=pltpu.CompilerParams(vmem_limit_bytes=GRANT),
    )(pre, rows, state, prod, start, mix_w)


def recur_back_kernel(
    dims, grad, pre, rows, state, prod, start, gate, mix_w, gelu, local, prods, sums, back, out_w, sem
):
    span, micro, _, held, bw, _ = dims
    part = held * bw
    load = pltpu.make_async_copy(mix_w.at[:, pl.ds(2 * part, part)], out_w, sem.at[0])
    load.start()
    load.wait()

    def one_head(h):
        back[...] = dot_plain(grad[...], out_w[:, pl.ds(pl.multiple_of(h * bw, 128), bw)])
        pre_h, state_h, prod_h = columns(pre, h, bw), columns(state, h, bw), columns(prod, h, bw)
        rows_h, start_h, gate_h = columns(rows, h, bw), columns(start, h, bw), columns(gate, h, 2 * bw)
        gelu_h, local_h = columns(gelu, h, bw), columns(local, h, bw)
        prods_h, sums_h = columns(prods, h, bw), columns(sums, h, bw)
        soft = rows_h[0:1]
        for i in range(back.shape[0] // span):
            here = pl.ds(i * span, span)
            act, slope = gelu_pair(pre_h[main_rows(i, span, micro)])
            states = state_h[here] + prod_h[here] * start_h[i : i + 1]
            gelu_h[here] = (back[here] * states * slope * rows_h[6:7]).astype(BF)
            _, _, decay, _, _ = gate_values(gate_h[here], soft)
            row = lax.broadcasted_iota(jnp.int32, decay.shape, 0)
            later = jnp.where(row < span - 1, pltpu.roll(decay, span - 1, 0), 1.0)
            later, adjoint = span_scan(later, back[here] * act, True)
            local_h[here] = adjoint
            prods_h[here] = later
            sums_h[i : i + 1] = decay[:1] * adjoint[:1]

    by_heads(held, one_head)


def recur_back(grad, pre, rows, state, prod, start, gate, mix_w, dims):
    tokens, part = state.shape
    shapes = [((tokens, part), BF), ((tokens, part), F32), ((tokens, part), F32), (start.shape, F32)]
    return pl.pallas_call(
        functools.partial(recur_back_kernel, dims),
        in_specs=[VMEM] * 7 + [ANY],
        out_specs=[VMEM] * 4,
        out_shape=[jax.ShapeDtypeStruct(*shape) for shape in shapes],
        scratch_shapes=[
            pltpu.VMEM((tokens, dims[4]), F32),
            pltpu.VMEM((mix_w.shape[0], part), BF),
            pltpu.SemaphoreType.DMA((1,)),
        ],
        cost_estimate=FREE,
        compiler_params=pltpu.CompilerParams(vmem_limit_bytes=GRANT),
    )(grad, pre, rows, state, prod, start, gate, mix_w)


def recur_grad_kernel(
    span, micro, local, prods, carried, state, prod, start, gate, conv, pre, rows, block,
    blocks_out, lru_out, spill_out, rows_out, gate_grad, conv_grad,
):
    count = local.shape[0] // span
    soft, sig, own = rows[0:1], rows[1:2], rows[6:7]
    taps = [rows[k + 2 : k + 3] for k in range(4)]
    width = local.shape[1]
    add_up = lambda v: jnp.sum(v, axis=0, keepdims=True)
    decay_sum = jnp.zeros((1, width), F32)
    for i in range(count):
        here = pl.ds(i * span, span)
        adjoint = local[here] + prods[here] * carried[i : i + 1]
        states = state[here] + prod[here] * start[i : i + 1]
        row = lax.broadcasted_iota(jnp.int32, states.shape, 0)
        earlier = jnp.where(row >= 1, pltpu.roll(states, 1, 0), start[i : i + 1])
        rec_gate, in_gate, decay, square, root = gate_values(gate[here], soft)
        conv_vals = conv[here].astype(F32)
        drive = adjoint * conv_vals
        grad_log = adjoint * earlier * decay - drive * in_gate * square / root
        decay_sum = decay_sum + add_up(grad_log * rec_gate)
        gate_grad[here, :width] = (-RATE * soft * grad_log * rec_gate * (1.0 - rec_gate)).astype(BF)
        gate_grad[here, width:] = (drive * root * in_gate * (1.0 - in_gate)).astype(BF)
        conv_grad[here] = adjoint * root * in_gate
    blocks_out[...] = lax.dot_general(
        conv[...], gate_grad[...], (((0,), (0,)), ((), ())), preferred_element_type=F32
    )
    conv_grad[...] += dot_right_t(gate_grad[...], block[0])
    tap_sums = [jnp.zeros((1, width), F32) for _ in range(4)]
    for i in range(count):
        here = pl.ds(i * span, span)
        grad = conv_grad[here]
        vals = with_halo(pre, i, span, micro).astype(BF).astype(F32)
        wide = jnp.concatenate([jnp.zeros((HALO, width), F32), grad], axis=0)
        total = taps[0] * wide
        tap_sums[0] = tap_sums[0] + add_up(grad * vals[HALO:])
        for k in range(1, 4):
            total = total + taps[k] * pltpu.roll(wide, span + HALO - k, 0)
            tap_sums[k] = tap_sums[k] + add_up(grad * pltpu.roll(vals, k, 0)[HALO:])
        lru_out[here] = total[HALO:]
        spill_out[pl.ds(i * HALO, HALO)] = total[:HALO]
    rows_out[...] = jnp.zeros(rows_out.shape, F32)
    rows_out[0:1] = decay_sum * sig * own * RATE
    for k in range(4):
        rows_out[k + 1 : k + 2] = tap_sums[k] * own


def recur_grad(local, prods, carried, state, prod, start, gate, conv, pre, rows, blocks, dims):
    tokens, part = state.shape
    span, micro, _, held, bw, _ = dims
    column = lambda h: (0, h)
    whole = pl.BlockSpec((tokens, bw), column)
    ends = pl.BlockSpec((start.shape[0], bw), column)
    return pl.pallas_call(
        functools.partial(recur_grad_kernel, span, micro),
        grid=(held,),
        in_specs=[
            whole,
            whole,
            ends,
            whole,
            whole,
            ends,
            pl.BlockSpec((tokens, 2 * bw), column),
            whole,
            pl.BlockSpec((pre.shape[0], bw), lambda h: (0, held + h)),
            pl.BlockSpec((8, bw), column),
            pl.BlockSpec((1, bw, 2 * bw), lambda h: (h, 0, 0)),
        ],
        out_specs=[
            pl.BlockSpec((bw, 2 * bw), lambda h: (h, 0)),
            whole,
            pl.BlockSpec((start.shape[0] * HALO, bw), column),
            pl.BlockSpec((8, bw), column),
        ],
        out_shape=[
            jax.ShapeDtypeStruct((part, 2 * bw), F32),
            jax.ShapeDtypeStruct((tokens, part), F32),
            jax.ShapeDtypeStruct((start.shape[0] * HALO, part), F32),
            jax.ShapeDtypeStruct((8, part), F32),
        ],
        scratch_shapes=[pltpu.VMEM((tokens, 2 * bw), BF), pltpu.VMEM((tokens, bw), F32)],
        cost_estimate=FREE,
        compiler_params=pltpu.CompilerParams(vmem_limit_bytes=GRANT),
    )(local, prods, carried, state, prod, start, gate, conv, pre, rows, blocks)


def recur_in_kernel(
    dims, gelu, lru, spill, rows, small, mixed, mix_w, pair, parts, gains, gl_w, sem
):
    span, _, _, held, bw, _ = dims
    part = held * bw
    load = pltpu.make_async_copy(mix_w.at[:, pl.ds(0, 2 * part)], gl_w, sem.at[0])
    load.start()
    pair[:, :part] = gelu[...]

    def one_head(h):
        lru_h, spill_h, own = columns(lru, h, bw), columns(spill, h, bw), columns(rows, h, bw)[6:7]
        for i in range(lru.shape[0] // span):
            vals = lru_h[pl.ds(i * span, span)]
            late = vals[span - HALO :] + spill_h[pl.ds(i * HALO, HALO)]
            vals = jnp.concatenate([vals[: span - HALO], late], axis=0) * own
            pair[pl.ds(i * span, span), pl.ds(pl.multiple_of((held + h) * bw, 128), bw)] = vals.astype(BF)

    by_heads(held, one_head)
    load.wait()

    def project(j):
        cols = pl.ds(pl.multiple_of(j * 256, 256), 256)
        grad = dot_right_t(pair[...], gl_w[cols])
        parts[:, cols] = grad.astype(BF)
        gain = jnp.sum(grad * mixed[:, cols].astype(F32), axis=0, keepdims=True)
        gains[0:1, cols] = gain / small[0:1, cols]

    by_heads(gl_w.shape[0] // 256, project)


def recur_in(gelu, lru, spill, rows, small, mixed, mix_w, dims):
    tokens, part = gelu.shape
    width = mix_w.shape[0]
    return pl.pallas_call(
        functools.partial(recur_in_kernel, dims),
        in_specs=[VMEM] * 6 + [ANY],
        out_specs=[VMEM] * 3,
        out_shape=[
            jax.ShapeDtypeStruct((tokens, 2 * part), BF),
            jax.ShapeDtypeStruct((tokens, width), BF),
            jax.ShapeDtypeStruct((8, width), F32),
        ],
        scratch_shapes=[pltpu.VMEM((width, 2 * part), BF), pltpu.SemaphoreType.DMA((1,))],
        cost_estimate=FREE,
        compiler_params=pltpu.CompilerParams(vmem_limit_bytes=GRANT),
    )(gelu, lru, spill, rows, small, mixed, mix_w)


def device(p, f=None, z=None, x=None, c=None):
    f, z = p.f if f is None else f, p.z if z is None else z
    x, c = p.x if x is None else x, p.c if c is None else c
    return (f, ((p.r * TP + z) * 2 + x) * 2 + c)


def copy_to(src, dst, sems, index, dev):
    return pltpu.make_async_remote_copy(
        src_ref=src,
        dst_ref=dst,
        send_sem=sems[0].at[index],
        recv_sem=sems[1].at[index],
        device_id=dev,
        device_id_type=MESH,
    )


def pairs(*shape):
    return [pltpu.SemaphoreType.DMA(shape), pltpu.SemaphoreType.DMA(shape)]


def greet(devices):
    barrier = pltpu.get_barrier_semaphore()
    for dev in devices:
        pl.semaphore_signal(barrier, inc=1, device_id=dev, device_id_type=MESH)
    pl.semaphore_wait(barrier, len(devices))


def by_rows(count, body, step=16):
    def turn(i, _):
        body(pl.ds(pl.multiple_of(i * step, step), step))
        return 0

    assert count % step == 0
    lax.fori_loop(0, count // step, turn, 0)


class Gather:
    def __init__(self, p, out, ups, downs):
        self.p, self.out, self.ups, self.downs = p, out, ups, downs
        self.up = device(p, z=jnp.minimum(p.z + 1, TP - 1))
        self.down = device(p, z=jnp.maximum(p.z - 1, 0))

    def begin(self, h, src):
        z = self.p.z

        @pl.when(z < TP - 1)
        def _():
            copy_to(src, self.out.at[z, h], self.ups, (0, h), self.up).start()

        @pl.when(z > 0)
        def _():
            copy_to(src, self.out.at[z, h], self.downs, (0, h), self.down).start()

    def step(self, k, h):
        z, out = self.p.z, self.out

        @pl.when(z >= k)
        def _():
            block = out.at[z - k, h]
            copy_to(block, block, self.ups, (k - 1, h), self.up).wait_recv()
            if k < TP - 1:

                @pl.when(z < TP - 1)
                def _():
                    copy_to(block, block, self.ups, (k, h), self.up).start()

        @pl.when(z <= TP - 1 - k)
        def _():
            block = out.at[z + k, h]
            copy_to(block, block, self.downs, (k - 1, h), self.down).wait_recv()
            if k < TP - 1:

                @pl.when(z > 0)
                def _():
                    copy_to(block, block, self.downs, (k, h), self.down).start()

    def close(self, halves):
        z, block = self.p.z, self.out.at[0, 0]
        for h in range(halves):
            for k in range(TP - 1):

                @pl.when((z >= k) & (z < TP - 1))
                def _():
                    copy_to(block, block, self.ups, (k, h), self.up).wait_send()

                @pl.when((z <= TP - 1 - k) & (z > 0))
                def _():
                    copy_to(block, block, self.downs, (k, h), self.down).wait_send()


class LineSum:
    def __init__(self, p, parts, scratch):
        self.p, self.parts = p, parts
        self.got_up, self.got_down, self.out_up, self.out_down = scratch[:4]
        self.ups, self.downs = scratch[4:6], scratch[6:8]
        self.halves, self.rows = parts.shape[1:3]
        self.up = device(p, z=jnp.minimum(p.z + 1, TP - 1))
        self.down = device(p, z=jnp.maximum(p.z - 1, 0))

    @staticmethod
    def scratch(parts):
        block = parts[1:]
        return [
            pltpu.VMEM((TP - 1,) + block, BF),
            pltpu.VMEM((TP - 1,) + block, BF),
            pltpu.VMEM((TP - 2,) + block, BF),
            pltpu.VMEM((TP - 2,) + block, BF),
            *pairs(TP - 1, parts[1]),
            *pairs(TP - 1, parts[1]),
        ]

    def clear(self):
        z = self.p.z

        @pl.when(z == 0)
        def _():
            for h in range(self.halves):
                by_rows(self.rows, lambda at: self.fill(self.got_up, h, at))

        @pl.when(z == TP - 1)
        def _():
            for h in range(self.halves):
                by_rows(self.rows, lambda at: self.fill(self.got_down, h, at))

    def fill(self, ref, h, at):
        ref[0, h, at] = jnp.zeros((at.size, ref.shape[-1]), BF)

    def one_way(self, k, h, place, block, got, out, sems, dev):
        @pl.when(place == 0)
        def _():
            copy_to(self.parts.at[block, h], got.at[k - 1, h], sems, (k - 1, h), dev).start()

        if k < TP - 1:

            @pl.when((place >= 1) & (place + k <= TP - 1))
            def _():
                copy_to(got.at[k, h], got.at[k, h], sems, (k, h), dev).wait_recv()

                def add(at):
                    total = self.parts[block, h, at].astype(F32) + got[k, h, at].astype(F32)
                    out[k - 1, h, at] = total.astype(BF)

                by_rows(self.rows, add)
                copy_to(out.at[k - 1, h], got.at[k - 1, h], sems, (k - 1, h), dev).start()

    def step(self, k, h):
        z = self.p.z
        block = jnp.minimum(z + k, TP - 1)
        self.one_way(k, h, z, block, self.got_up, self.out_up, self.ups, self.up)
        block = jnp.maximum(z - k, 0)
        self.one_way(k, h, TP - 1 - z, block, self.got_down, self.out_down, self.downs, self.down)

    def arrive(self, h):
        z = self.p.z

        @pl.when(z >= 1)
        def _():
            got = self.got_up.at[0, h]
            copy_to(got, got, self.ups, (0, h), self.up).wait_recv()

        @pl.when(z <= TP - 2)
        def _():
            got = self.got_down.at[0, h]
            copy_to(got, got, self.downs, (0, h), self.down).wait_recv()

    def total(self, h, at):
        total = self.parts[self.p.z, h, at].astype(F32) + self.got_up[0, h, at].astype(F32)
        return total + self.got_down[0, h, at].astype(F32)

    def close(self):
        z, got = self.p.z, self.got_up.at[0, 0]
        for h in range(self.halves):
            for k in range(1, TP):

                @pl.when(z + k <= TP - 1)
                def _():
                    copy_to(got, got, self.ups, (k - 1, h), self.up).wait_send()

                @pl.when(z - k >= 0)
                def _():
                    copy_to(got, got, self.downs, (k - 1, h), self.down).wait_send()


def greet_line(p, others=()):
    barrier = pltpu.get_barrier_semaphore()
    for dev in others:
        pl.semaphore_signal(barrier, inc=1, device_id=dev, device_id_type=MESH)

    @pl.when(p.z > 0)
    def _():
        pl.semaphore_signal(barrier, inc=1, device_id=device(p, z=p.z - 1), device_id_type=MESH)

    @pl.when(p.z < TP - 1)
    def _():
        pl.semaphore_signal(barrier, inc=1, device_id=device(p, z=p.z + 1), device_id_type=MESH)

    inner = (p.z > 0) & (p.z < TP - 1)

    @pl.when(inner)
    def _():
        pl.semaphore_wait(barrier, len(others) + 2)

    @pl.when(jnp.logical_not(inner))
    def _():
        pl.semaphore_wait(barrier, len(others) + 1)


class Spread:
    KINDS = ((0, 0), (0, 1), (1, 0), (1, 1))

    def __init__(self, p, whole, sems):
        self.p, self.whole, self.started = p, whole, []
        self.xs, self.fs, self.gs, self.cs = sems[0:2], sems[2:4], sems[4:6], sems[6:8]
        self.to_x, self.to_f = device(p, x=1 - p.x), device(p, f=1 - p.f)
        self.to_c = device(p, c=1 - p.c)

    @staticmethod
    def scratch():
        return [*pairs(TP), *pairs(TP), *pairs(TP), *pairs(4, TP)]

    def slot(self, kind, d, other_core=False):
        p, (f, x) = self.p, self.KINDS[kind]
        c = 1 - p.c if other_core else p.c
        return self.whole.at[(p.f + f) % 2, 0, (p.z - d) % TP, (p.x + x) % 2, c]

    def send(self, src, dst, sems, index, dev):
        copy = copy_to(src, dst, sems, index, dev)
        copy.start()
        self.started.append(copy)

    def wait(self, ref, sems, index):
        copy_to(ref, ref, sems, index, self.to_x).wait_recv()

    def spread(self, d, src=None):
        dst = self.slot(0, d)
        src = dst if src is None else src
        self.send(src, dst, self.xs, (d,), self.to_x)
        self.send(src, dst, self.fs, (d,), self.to_f)
        self.send(src, dst, self.cs, (0, d), self.to_c)

    def given(self, d, own, by_x, by_f):
        self.send(own, self.slot(0, d), self.cs, (0, d), self.to_c)
        self.send(by_x, self.slot(1, d), self.cs, (1, d), self.to_c)
        self.send(by_f, self.slot(2, d), self.cs, (2, d), self.to_c)
        if d % 2 == 0:
            self.send(by_x, self.slot(1, d), self.gs, (d,), self.to_f)
        else:
            self.send(by_f, self.slot(2, d), self.gs, (d,), self.to_x)

    def sides(self, d):
        ref = self.slot(1, d)
        self.wait(ref, self.xs, (d,))
        if d % 2 == 0:
            self.send(ref, ref, self.gs, (d,), self.to_f)
        self.send(ref, ref, self.cs, (1, d), self.to_c)
        ref = self.slot(2, d)
        self.wait(ref, self.fs, (d,))
        if d % 2 == 1:
            self.send(ref, ref, self.gs, (d,), self.to_x)
        self.send(ref, ref, self.cs, (2, d), self.to_c)

    def corner(self, d):
        ref = self.slot(3, d)
        self.wait(ref, self.gs, (d,))
        self.send(ref, ref, self.cs, (3, d), self.to_c)

    def close(self, pieces):
        for kind in range(4):
            for d in pieces:
                self.wait(self.slot(kind, d, True), self.cs, (kind, d))
        for copy in self.started:
            copy.wait_send()


def pack_kernel(bw, gelu, lru, out_t, blocks, small, gate, up, down_t, mix, *ffw):
    p = Place()
    heads = gelu.shape[1] // bw
    part, ffw_part = -(-heads // TP) * bw, gate.shape[1] // TP
    for d in range(TP):
        z = (p.z + d) % TP
        cols = pl.ds(pl.multiple_of(z * heads // TP * bw, 128), part)
        sources = [gelu[:, cols], lru[:, cols], out_t[:, cols], blocks[...], small[...]]
        offset = 0
        for source in sources:
            mix[d, :, offset : offset + source.shape[1]] = source
            offset += source.shape[1]
        cols = pl.ds(pl.multiple_of(z * ffw_part, 128), ffw_part)
        for i, source in enumerate((gate, up, down_t)):
            ffw[d][:, i * ffw_part : (i + 1) * ffw_part] = source[:, cols]


def pack(weights, bw):
    rows, lru_width = weights[0].shape
    part = -(-lru_width // bw // TP) * bw
    mix_cols = 3 * part + weights[3].shape[1] + weights[4].shape[1]
    piece = jax.ShapeDtypeStruct((rows, 3 * weights[5].shape[1] // TP), BF)
    mix, *ffw = pl.pallas_call(
        functools.partial(pack_kernel, bw),
        in_specs=[VMEM] * 8,
        out_specs=[VMEM] * (1 + TP),
        out_shape=[jax.ShapeDtypeStruct((TP, rows, mix_cols), BF), *[piece] * TP],
        compiler_params=pltpu.CompilerParams(vmem_limit_bytes=GRANT),
    )(*weights)
    return mix, ffw


def intake_kernel(
    mix_p, ffw_0, ffw_1, x_p, mix_w, ffw_w, piece_1, x_all, zs, zr, us, ur, vs, vr, local, *sems
):
    p = Place()
    mix, ffw = Spread(p, mix_w, sems[:8]), Spread(p, ffw_w, sems[8:])
    to_z = [device(p, z=(p.z + d) % TP) for d in range(TP)]
    greet(to_z[1:] + [mix.to_x, mix.to_f, mix.to_c])
    started = []

    def along_z(i, src, dst, d):
        copy = copy_to(src, dst, (zs, zr), (i,), to_z[d])
        copy.start()
        started.append(copy)

    def from_z(i, ref):
        copy_to(ref, ref, (zs, zr), (i,), to_z[1]).wait_recv()

    for d in (1, 3, 2):
        along_z(d, mix_p.at[d], mix.slot(0, 0), d)
    mix.spread(0, mix_p.at[0])
    ffw.spread(0, ffw_0)
    stays = [
        pltpu.make_async_copy(mix_p.at[0], mix.slot(0, 0), local.at[0]),
        pltpu.make_async_copy(ffw_0, ffw.slot(0, 0), local.at[1]),
        pltpu.make_async_copy(x_p, x_all.at[p.z, 0], local.at[2]),
    ]
    for copy in stays:
        copy.start()
    line = Gather(p, x_all, (us, ur), (vs, vr))
    for d in (1, 3, 2):
        from_z(d, mix.slot(0, d))
        mix.spread(d)
    line.begin(0, x_p)
    along_z(0, ffw_1, piece_1, 1)
    mix.sides(0)
    ffw.sides(0)
    mix.corner(0)
    line.step(1, 0)
    for d in (1, 3):
        mix.sides(d)
    ffw.corner(0)
    line.step(2, 0)
    for d in (1, 3):
        mix.corner(d)
    mix.sides(2)
    line.step(3, 0)
    mix.corner(2)
    from_z(0, piece_1)
    mix.close(range(TP))
    ffw.close((0,))
    for copy in started:
        copy.wait_send()
    line.close(1)
    for copy in stays:
        copy.wait()


def intake(mix_p, ffw_0, ffw_1, x_p, p):
    whole = lambda v: jax.ShapeDtypeStruct((p.fs, 1, TP, 2, 2) + v.shape[-2:], BF)
    mix_w, ffw_w, piece_1, x_all = pl.pallas_call(
        intake_kernel,
        in_specs=[ANY] * 4,
        out_specs=[ANY] * 4,
        out_shape=[
            whole(mix_p),
            whole(ffw_0),
            jax.ShapeDtypeStruct(ffw_1.shape, BF),
            jax.ShapeDtypeStruct((TP, 1) + x_p.shape, BF),
        ],
        scratch_shapes=[
            *pairs(TP),
            *pairs(TP - 1, 1),
            *pairs(TP - 1, 1),
            pltpu.SemaphoreType.DMA((3,)),
            *Spread.scratch(),
            *Spread.scratch(),
        ],
        compiler_params=pltpu.CompilerParams(collective_id=0, has_side_effects=True),
    )(mix_p, ffw_0, ffw_1, x_p)
    return mix_w.reshape(-1, mix_p.shape[-1]), ffw_w, piece_1, x_all[:, 0]


class Stream:
    def __init__(self, pick, count, buffers, sems):
        self.pick, self.count, self.buffers, self.sems = pick, count, buffers, sems

    def load(self, i):
        slot = i % 2
        return pltpu.make_async_copy(self.pick(i), self.buffers.at[slot], self.sems.at[slot])

    def start(self):
        self.load(0).start()

    def run(self, low, high, body):
        def turn(i, _):
            @pl.when(i + 1 < self.count)
            def _():
                self.load(i + 1).start()

            self.load(i).wait()
            body(i, self.buffers.at[i % 2])
            return 0

        lax.fori_loop(low, high, turn, 0)


def flat(block):
    return block.reshape(-1, block.shape[-1])


FFW_CHUNK = 256


def ffw_streams(ffw_w, part, buffers):
    chunks, rest = part // FFW_CHUNK, part % FFW_CHUNK
    col = lambda base, i: pl.ds(pl.multiple_of(base + i * FFW_CHUNK, 128), FFW_CHUNK)
    pick = lambda base: lambda i: ffw_w.at[:, 0, :, :, :, :, col(base, i)]
    half = TP // 2
    rows = lambda cols: lambda i: ffw_w.at[i // 2, 0, pl.ds(i % 2 * half, half), :, :, :, cols]
    gate = Stream(pick(0), chunks, buffers[0], buffers[1])
    up = Stream(pick(part), chunks, buffers[2], buffers[3])
    down = Stream(pick(2 * part), chunks, buffers[0], buffers[1])
    down_rows = Stream(rows(pl.ds(2 * part, part)), 4, buffers[4], buffers[5])
    both_rows = Stream(rows(pl.ds(0, 2 * part)), 4, buffers[6], buffers[7])
    return gate, up, down, down_rows, both_rows


class Feed:
    def __init__(self, x, cot, ffw_w, outs, vals, scratch):
        self.x, self.cot, self.vals = x, cot, vals
        self.hidden, self.grad_pair, self.out_parts, self.in_parts = outs
        self.part = part = self.hidden.shape[1]
        self.chunks, self.rest = part // FFW_CHUNK, part % FFW_CHUNK
        streams = ffw_streams(ffw_w, part, scratch[:8])
        self.gate, self.up, self.down, self.down_rows, self.both_rows = streams
        self.tails, tail_sems = scratch[8:10]
        self.last = last = self.chunks * FFW_CHUNK
        self.loads = [
            pltpu.make_async_copy(
                ffw_w.at[:, 0, :, :, :, :, pl.ds(k * part + last, self.rest)],
                self.tails.at[k],
                tail_sems.at[k],
            )
            for k in range(3)
        ]

    def begin(self):
        self.gate.start()
        self.up.start()
        for load in self.loads:
            load.start()
        self.down_rows.start()
        self.both_rows.start()

    def cols(self, i, base):
        return pl.ds(pl.multiple_of(base + i * FFW_CHUNK, 128), FFW_CHUNK)

    def forward_cols(self, cols, other, gate_w, up_w):
        gate_vals = dot_plain(self.x[...], gate_w)
        up_vals = dot_plain(self.x[...], up_w)
        self.vals[:, cols] = gate_vals
        self.vals[:, other] = up_vals
        self.hidden[:, cols] = (gelu_pair(gate_vals)[0] * up_vals).astype(BF)

    def forward(self, low, high):
        def turn(i, _):
            for stream in (self.gate, self.up):

                @pl.when(i + 1 < self.chunks)
                def _(stream=stream):
                    stream.load(i + 1).start()

                stream.load(i).wait()
            weights = [flat(stream.buffers[i % 2]) for stream in (self.gate, self.up)]
            self.forward_cols(self.cols(i, 0), self.cols(i, self.part), *weights)
            return 0

        lax.fori_loop(low, high, turn, 0)

    def forward_end(self):
        self.down.start()
        for load in self.loads:
            load.wait()
        cols = pl.ds(self.last, self.rest), pl.ds(self.part + self.last, self.rest)
        self.forward_cols(*cols, flat(self.tails[0]), flat(self.tails[1]))

    def by_weight_rows(self, stream, source, out):
        def body(i, buffer):
            weights = flat(buffer[...])
            count = weights.shape[0]
            cols = pl.ds(pl.multiple_of(i * count, 128), count)
            out[:, cols] = dot_right_t(source[...], weights).astype(BF)

        stream.run(0, 4, body)

    def forward_out(self):
        self.by_weight_rows(self.down_rows, self.hidden, self.out_parts)

    def backward_cols(self, cols, other, weights):
        grad = dot_plain(self.cot[...], weights)
        act, slope = gelu_pair(self.vals[:, cols])
        self.grad_pair[:, cols] = (grad * self.vals[:, other] * slope).astype(BF)
        self.grad_pair[:, other] = (grad * act).astype(BF)

    def backward(self):
        def body(i, buffer):
            self.backward_cols(self.cols(i, 0), self.cols(i, self.part), flat(buffer[...]))

        self.down.run(0, self.chunks, body)
        cols = pl.ds(self.last, self.rest), pl.ds(self.part + self.last, self.rest)
        self.backward_cols(*cols, flat(self.tails[2]))
        self.by_weight_rows(self.both_rows, self.grad_pair, self.in_parts)


def ffw_scratch(ffw_w, part):
    f, _, z, x, c, rows, _ = ffw_w.shape
    column = lambda width: pltpu.VMEM((2, f, z, x, c, rows, width), BF)
    wide = lambda width: pltpu.VMEM((2, z // 2, x, c, rows, width), BF)
    pair = pltpu.SemaphoreType.DMA((2,))
    return [
        column(FFW_CHUNK), pair, column(FFW_CHUNK), pair, wide(part), pair, wide(2 * part), pair,
        pltpu.VMEM((3, f, z, x, c, rows, part % FFW_CHUNK), BF),
        pltpu.SemaphoreType.DMA((3,)),
    ]


def middle_kernel(with_ffw, *refs):
    parts, x_zero, gain, cot_p, piece_1, by_x, by_f, piece_2, piece_3, _ = refs[:10]
    x_one, ffw_all, cot_all, ffw_w, *refs = refs[10:]
    if with_ffw:
        outs, refs = refs[:4], refs[4:]
    own, local, gu0, gu1, gd0, gd1, cu0, cu1, cd0, cd1 = refs[:10]
    p = Place()
    line = LineSum(p, parts, refs[10:18])
    out = Gather(p, ffw_all, (gu0, gu1), (gd0, gd1))
    cot = Gather(p, cot_all, (cu0, cu1), (cd0, cd1))
    halves, rows = parts.shape[1:3]
    line.clear()
    stays = []

    def stay(src, dst):
        copy = pltpu.make_async_copy(src, dst, local.at[len(stays)])
        copy.start()
        stays.append(copy)

    if with_ffw:
        ffw = Spread(p, ffw_w, refs[18:26])
        greet_line(p, (ffw.to_x, ffw.to_f, ffw.to_c))
    else:
        greet_line(p)
    side = lambda name, *args: getattr(ffw, name)(*args) if with_ffw else None
    for h in range(halves):
        line.step(TP - 1, h)
    side("given", 1, piece_1, by_x, by_f)
    side("spread", 3, piece_3)
    side("spread", 2, piece_2)
    if with_ffw:
        bounce, bounce_sems = refs[37:39]
        moves = [(piece_1, 0, 1), (by_x, 1, 1), (by_f, 2, 1), (piece_3, 0, 3), (piece_2, 0, 2)]
        for i, (src, kind, d) in enumerate(moves):
            slot, dst = bounce.at[i % 2], ffw.slot(kind, d)
            if i >= 2:
                pltpu.make_async_copy(slot, dst, bounce_sems.at[i % 2]).wait()
            load = pltpu.make_async_copy(src, slot, bounce_sems.at[2])
            load.start()
            load.wait()
            pltpu.make_async_copy(slot, dst, bounce_sems.at[i % 2]).start()
        for i in range(2):
            pltpu.make_async_copy(bounce.at[i], ffw.slot(0, 0), bounce_sems.at[i]).wait()
    for k in range(TP - 2, 0, -1):
        for h in range(halves):
            line.step(k, h)
    for h in range(halves):
        line.arrive(h)

        def finish(at, h=h):
            value = x_zero[h, at].astype(F32) + line.total(h, at)
            x_one[h, at] = value
            own[h, at] = normed(value, gain[...]).astype(BF)

        by_rows(rows, finish)
        out.begin(h, own.at[h])
        stay(own.at[h], ffw_all.at[p.z, h])
    for h in range(halves):
        out.step(1, h)
    for d in (3, 2):
        side("sides", d)
    for h in range(halves):
        out.step(2, h)
    cot.begin(0, cot_p)
    stay(cot_p, cot_all.at[p.z, 0])
    side("corner", 1)
    for d in (3, 2):
        side("corner", d)
    for h in range(halves):
        out.step(3, h)
    cot.step(1, 0)
    side("close", (1, 2, 3))
    if not with_ffw:
        cot.step(2, 0)
        cot.step(3, 0)
    for copy in stays:
        copy.wait()
    if with_ffw:
        tokens = lambda ref: ref.reshape(TP * halves * rows, parts.shape[3])
        feed = Feed(tokens(ffw_all), tokens(cot_all), ffw_w, outs, refs[26], refs[27:37])
        feed.begin()
        feed.forward(0, 2)
        cot.step(2, 0)
        feed.forward(2, 6)
        cot.step(3, 0)
        feed.forward(6, feed.chunks)
        feed.forward_end()
        feed.forward_out()
        feed.backward()
    line.close()
    out.close(halves)
    cot.close(1)


def middle(parts, x_zero, gain, cot_p, pieces, ffw_w):
    shape = parts.shape
    with_ffw = ffw_w is not None
    outs, extra = [], []
    if with_ffw:
        tokens, part = shape[0] * shape[1] * shape[2], ffw_w.shape[-1] // 3
        assert part // FFW_CHUNK >= 6 and part % FFW_CHUNK
        outs = [(tokens, part), (tokens, 2 * part), (tokens, shape[3]), (tokens, shape[3])]
        extra = [*Spread.scratch(), pltpu.VMEM((tokens, 2 * part), F32), *ffw_scratch(ffw_w, part)]
        extra += [pltpu.VMEM((2,) + pieces[0].shape, BF), pltpu.SemaphoreType.DMA((3,))]
    else:
        ffw_w = jnp.zeros((16, 128), BF)
        pieces = [ffw_w] * 5
    here = VMEM if with_ffw else ANY
    return pl.pallas_call(
        functools.partial(middle_kernel, with_ffw),
        in_specs=[VMEM] * 3 + [ANY] * 7,
        out_specs=[VMEM, here, here, ANY] + [VMEM] * len(outs),
        out_shape=[
            jax.ShapeDtypeStruct(shape[1:], F32),
            jax.ShapeDtypeStruct(shape, BF),
            jax.ShapeDtypeStruct((TP, 1) + cot_p.shape, BF),
            jax.ShapeDtypeStruct(ffw_w.shape, BF),
            *(jax.ShapeDtypeStruct(out, BF) for out in outs),
        ],
        input_output_aliases={9: 3},
        scratch_shapes=[
            pltpu.VMEM(shape[1:], BF),
            pltpu.SemaphoreType.DMA((shape[1] + 3,)),
            *pairs(TP - 1, shape[1]),
            *pairs(TP - 1, shape[1]),
            *pairs(TP - 1, 1),
            *pairs(TP - 1, 1),
            *LineSum.scratch(shape),
            *extra,
        ],
        compiler_params=pltpu.CompilerParams(
            collective_id=1, has_side_effects=True, vmem_limit_bytes=GRANT
        ),
    )(parts, x_zero, gain, cot_p, *pieces, ffw_w)


def norm_back(values, gain, grad):
    inv = lax.rsqrt(jnp.mean(values * values, axis=-1, keepdims=True) + EPS)
    unit = values * inv
    through = grad * gain
    inner = jnp.mean(through * unit, axis=-1, keepdims=True)
    return inv * (through - unit * inner), grad * unit


class Fold:
    ORDER = ((0, 1, 1), (1, 1, 1), (0, 0, 1), (1, 1, 0), (0, 1, 0), (1, 0, 1), (0, 0, 0), (1, 0, 0))

    def __init__(self, p, grad, cores, scratch):
        self.p, self.grad, self.cores = p, grad, cores
        self.sums, self.stage, self.got, self.got_late = scratch[:4]
        self.near, self.staged = scratch[4:6]
        self.core_sems, self.early, self.late = scratch[6:8], scratch[8:10], scratch[10:12]
        self.to = (device(p, x=1 - p.x), device(p, f=1 - p.f))
        self.to_c = device(p, c=1 - p.c)

    @staticmethod
    def shapes(grad, staged):
        block = (TP // 2,) + grad.shape[-2:]
        waiting = (2,) if staged else (2, 2, 2)
        return jax.ShapeDtypeStruct((2, 2, 2) + block, BF), [
            pltpu.VMEM((2, 2, 2) + block, BF),
            pltpu.VMEM(waiting + block, BF),
            pltpu.VMEM((2, 2) + block, BF),
            pltpu.VMEM((2,) + block, BF),
            pltpu.SemaphoreType.DMA((8,)),
            pltpu.SemaphoreType.DMA((2,)),
            *pairs(8),
            *pairs(2, 2),
            *pairs(2),
        ]

    def block(self, way, f_rel, x_rel, c):
        p, half = self.p, TP // 2
        f, x = (p.f + f_rel) % 2, (p.x + x_rel) % 2
        return self.grad.at[f, 0, pl.ds(way * half, half), x, c]

    def cross(self, i):
        name = self.ORDER[i]
        src = self.block(*name, 1 - self.p.c)
        dst = self.stage if self.cores is None else self.cores
        return copy_to(src, dst.at[name], self.core_sems, (i,), self.to_c)

    def load(self, i):
        name = self.ORDER[i]
        return pltpu.make_async_copy(
            self.block(*name, self.p.c), self.sums.at[name], self.near.at[i]
        )

    def fetch(self, i):
        src = self.cores.at[self.ORDER[i]]
        return pltpu.make_async_copy(src, self.stage.at[i % 2], self.staged.at[i % 2])

    def first(self, way, block):
        src = self.sums.at[(0, block, 1) if way == 0 else (1, 1, block)]
        return copy_to(src, self.got.at[way, block], self.early, (way, block), self.to[way])

    def second(self, way):
        src = self.sums.at[(0, 1, 0) if way == 0 else (1, 0, 1)]
        return copy_to(src, self.got_late.at[way], self.late, (way,), self.to[1 - way])

    def add(self, name, *others):
        rows = self.sums.shape[-2]

        def turn(at):
            for k in range(TP // 2):
                total = self.sums[(*name, k, at)].astype(F32)
                for other in others:
                    total = total + other[k, at].astype(F32)
                self.sums[(*name, k, at)] = total.astype(BF)

        by_rows(rows, turn)

    def begin(self):
        for i in range(8):
            self.cross(i).start()
            self.load(i).start()

    def issue(self, i):
        self.cross(i).wait_recv()
        self.fetch(i).start()

    def join(self, i):
        if self.cores is None:
            self.cross(i).wait_recv()
            self.load(i).wait()
            self.add(self.ORDER[i], self.stage.at[self.ORDER[i]])
        else:
            if i == 0:
                self.issue(0)
            if i + 1 < 8:
                self.issue(i + 1)
            self.fetch(i).wait()
            self.load(i).wait()
            self.add(self.ORDER[i], self.stage.at[i % 2])
        if i < 4:
            way = self.ORDER[i][0]
            self.first(way, self.ORDER[i][1 + way]).start()

    def middle(self):
        for way in range(2):
            self.first(way, 1).wait_recv()
            self.add((0, 1, 0) if way == 0 else (1, 0, 1), self.got.at[way, 1])
            self.second(way).start()

    def finish(self):
        for way in range(2):
            self.first(way, 0).wait_recv()
            self.second(way).wait_recv()
            self.add((way, 0, 0), self.got.at[way, 0], self.got_late.at[way])

    def result(self, z):
        return self.sums.at[z // (TP // 2), 0, 0, z % (TP // 2)]

    def close(self):
        for i in range(8):
            self.cross(i).wait_send()
        for way in range(2):
            self.second(way).wait_send()
            for block in range(2):
                self.first(way, block).wait_send()


def folds_of(p, grads, cores, scratch):
    return [Fold(p, g, c, scratch[12 * i : 12 * i + 12]) for i, (g, c) in enumerate(zip(grads, cores))]


GRAD_CHUNK = 640


class Outer:
    def __init__(self, grad, left, right, turned, buffers, sems):
        self.grad, self.left, self.right, self.turned = grad, left, right, turned
        self.buffers, self.sems = buffers, sems
        self.across = grad.shape[-1] // GRAD_CHUNK
        self.count = 4 * self.across

    def store(self, i):
        k, half = i // self.across, TP // 2
        cols = pl.ds(pl.multiple_of(i % self.across * GRAD_CHUNK, 128), GRAD_CHUNK)
        dst = self.grad.at[k // 2, 0, pl.ds(k % 2 * half, half), :, :, :, cols]
        return pltpu.make_async_copy(self.buffers.at[i % 2], dst, self.sems.at[i % 2])

    def run(self, low, high):
        rows = self.turned.shape[0]

        def turn(i, _):
            @pl.when(i % self.across == 0)
            def _():
                cols = pl.ds(pl.multiple_of(i // self.across * rows, 128), rows)
                self.turned[...] = jnp.transpose(self.left[:, cols])

            @pl.when(i >= 2)
            def _():
                self.store(i - 2).wait()

            cols = pl.ds(pl.multiple_of(i % self.across * GRAD_CHUNK, 128), GRAD_CHUNK)
            chunk = dot_plain(self.turned[...], self.right[:, cols]).astype(BF)
            self.buffers[i % 2] = chunk.reshape(self.buffers.shape[1:])
            self.store(i).start()
            return 0

        lax.fori_loop(low, high, turn, 0)

    def close(self):
        for i in (self.count - 2, self.count - 1):
            self.store(i).wait()


def turn_kernel(count, *refs):
    parts, out_parts, x_one, cot, gain = refs[:5]
    factors, refs = refs[5 : 5 + (4 if count else 0)], refs[5 + (4 if count else 0) :]
    mixed_out, grad_x_one, grad_gain, mix_all = refs[:4]
    pieces, refs = refs[4 : 4 + TP], refs[4 + TP :]
    grads, cores, refs = refs[:count], refs[count : 2 * count], refs[2 * count :]
    own, local, gu0, gu1, gd0, gd1 = refs[:6]
    p = Place()
    line, late = LineSum(p, parts, refs[6:14]), LineSum(p, out_parts, refs[14:22])
    folds = folds_of(p, grads, cores, refs[22 : 22 + 12 * count])
    out = Gather(p, mix_all, (gu0, gu1), (gd0, gd1))
    halves, rows = parts.shape[1:3]
    line.clear()
    late.clear()
    greet_line(p, (*folds[0].to, folds[0].to_c) if folds else ())
    stays = []

    def stay(src, dst):
        copy = pltpu.make_async_copy(src, dst, local.at[len(stays)])
        copy.start()
        stays.append(copy)

    if folds:
        left, right, turned, buffers, chunk_sems, load_sems = refs[22 + 12 * count :]
        part = factors[1].shape[1]
        outers = [
            Outer(grads[m], left, right.at[:, pl.ds(m // 2 * part, part)], turned, buffers, chunk_sems)
            for m in range(3)
        ]
        down, gate, up = folds
        size = outers[0].count
        half = size // 2

    def load(m):
        cols = right.at[:, pl.ds(0, factors[2 * m + 1].shape[1])]
        copies = [
            pltpu.make_async_copy(factors[2 * m], left, load_sems.at[0]),
            pltpu.make_async_copy(factors[2 * m + 1], cols, load_sems.at[1]),
        ]
        for copy in copies:
            copy.start()
        for copy in copies:
            copy.wait()

    def outer(m, low, high):
        outers[m].run(low, high)
        if high == size:
            outers[m].close()
            folds[m].begin()

    def join(fold, *blocks):
        for i in blocks:
            fold.join(i)

    def line_step(k):
        for h in range(halves):
            line.step(k, h)

    line_step(3)
    for h in range(halves):
        late.step(TP - 1, h)
    if folds:
        load(0)
        outer(0, 0, size)
        load(1)
        outer(1, 0, half)
        join(down, 0, 1, 2, 3)
    line_step(2)
    if folds:
        outer(1, half, size)
        join(down, 4, 5)
        outer(2, 0, half)
        join(gate, 0, 1)
        down.middle()
        join(gate, 2, 3)
    line_step(1)
    if folds:
        outer(2, half, size)
        join(gate, 4, 5)
    grad_gain[...] = jnp.zeros(grad_gain.shape, F32)
    for h in range(halves):
        line.arrive(h)

        def finish(at, h=h):
            grad, gains = norm_back(x_one[h, at], gain[...], line.total(h, at))
            grad = grad + cot[h, at].astype(F32)
            grad_x_one[h, at] = grad
            own[h, at] = grad.astype(BF)
            grad_gain[0:1] += jnp.sum(gains, axis=0, keepdims=True)

        by_rows(rows, finish)
        out.begin(h, own.at[h])
        stay(own.at[h], mix_all.at[p.z, h])
    if folds:
        join(up, 0, 1)
        gate.middle()
        join(up, 2, 3)
    for h in range(halves):
        out.step(1, h)
        late.step(2, h)
    if folds:
        join(down, 6, 7)
        join(up, 4, 5)
        join(gate, 6, 7)
    for h in range(halves):
        out.step(2, h)
        late.step(1, h)
    if folds:
        join(up, 6, 7)
        up.middle()
    for h in range(halves):
        out.step(3, h)
    for h in range(halves):
        late.arrive(h)

        def store(at, h=h):
            mixed_out[h, at] = (x_one[h, at] + late.total(h, at)).astype(BF)

        by_rows(rows, store)
    offset = 0
    for fold in folds:
        fold.finish()
        cols = fold.grad.shape[-1]
        for d in range(TP):
            stay(fold.result((p.z + d) % TP), pieces[d].at[:, pl.ds(offset, cols)])
        offset += cols
    for fold in folds:
        fold.close()
    line.close()
    late.close()
    out.close(halves)
    for copy in stays:
        copy.wait()


def turn(parts, out_parts, x_one, cot, gain, factors, p):
    shape, count, width = parts.shape, 3 if factors else 0, parts.shape[-1]
    rows = width // (p.fs * TP * 4)
    sizes = [factors[1].shape[1]] * count if factors else []
    grads = [jax.ShapeDtypeStruct((p.fs, 1, TP, 2, 2, rows, size), BF) for size in sizes]
    folded = [Fold.shapes(grad, True) for grad in grads]
    piece = jax.ShapeDtypeStruct((rows, sum(sizes)) if factors else (16, 128), BF)
    extra = []
    if factors:
        assert all(size % GRAD_CHUNK == 0 for size in sizes)
        tokens, deep = factors[0].shape[0], width // 4
        extra = [
            pltpu.VMEM((tokens, width), BF),
            pltpu.VMEM((tokens, 2 * sizes[0]), BF),
            pltpu.VMEM((deep, tokens), BF),
            pltpu.VMEM((2, TP // 2, 2, 2, rows, GRAD_CHUNK), BF),
            pltpu.SemaphoreType.DMA((2,)),
            pltpu.SemaphoreType.DMA((2,)),
        ]
    results = pl.pallas_call(
        functools.partial(turn_kernel, count),
        in_specs=[VMEM] * 5 + [ANY] * len(factors),
        out_specs=[VMEM, VMEM, VMEM, ANY] + [ANY] * (TP + 2 * count),
        out_shape=[
            jax.ShapeDtypeStruct(shape[1:], BF),
            jax.ShapeDtypeStruct(shape[1:], F32),
            jax.ShapeDtypeStruct((8, width), F32),
            jax.ShapeDtypeStruct(shape, BF),
            *[piece] * TP,
            *grads,
            *(cores for cores, _ in folded),
        ],
        scratch_shapes=[
            pltpu.VMEM(shape[1:], BF),
            pltpu.SemaphoreType.DMA((shape[1] + TP * count,)),
            *pairs(TP - 1, shape[1]),
            *pairs(TP - 1, shape[1]),
            *LineSum.scratch(shape),
            *LineSum.scratch(shape),
            *(item for _, scratch in folded for item in scratch),
            *extra,
        ],
        compiler_params=pltpu.CompilerParams(
            collective_id=2, has_side_effects=True, vmem_limit_bytes=GRANT
        ),
    )(parts, out_parts, x_one, cot, gain, *factors)
    return results[: 4 + TP]


def final_kernel(count, *refs):
    parts, x_zero, gain, grad_x_one, vectors = refs[:5]
    grads, refs = refs[5 : 5 + count], refs[5 + count :]
    grad_in, sums = refs[:2]
    outs, cores, refs = refs[2 : 2 + count], [None] * count, refs[2 + count :]
    acc, got, vs, vr, zs, zr, local = refs[:7]
    p = Place()
    line = LineSum(p, parts, refs[7:15])
    folds = folds_of(p, grads, cores, refs[15:])
    halves, rows = parts.shape[1:3]
    line.clear()
    to_z = [device(p, z=(p.z + d) % TP) for d in range(TP)]
    (to_x, to_f), to_c = folds[0].to, folds[0].to_c
    greet(to_z[1:] + [to_x, to_f, to_c])
    partners = [to_c, to_x, to_f] + [
        device(p, z=p.z + bit * (1 - 2 * (p.z // bit % 2))) for bit in (1, 2)
    ]

    def vector(i):
        return copy_to(acc.at[i], got.at[i], (vs, vr), (i,), partners[i])

    def next_vector(i):
        vector(i).wait_recv()
        if i < 4:
            acc[i + 1] = acc[i] + got[i]
            vector(i + 1).start()
        else:
            sums[...] = acc[i] + got[i]

    acc[0] = vectors[...]
    vector(0).start()
    for fold in folds:
        fold.begin()
    for h in range(halves):
        line.step(TP - 1, h)
    started, stays = [], []

    def send_on(m):
        folds[m].finish()
        for d in (1, 3, 2):
            src = folds[m].result((p.z + d) % TP)
            copy = copy_to(src, outs[m].at[p.z], (zs, zr), (m, d - 1), to_z[d])
            copy.start()
            started.append(copy)
        stays.append(pltpu.make_async_copy(folds[m].result(p.z), outs[m].at[p.z], local.at[m]))
        stays[-1].start()

    for i in range(4):
        folds[0].join(i)
    for m, fold in enumerate(folds):
        fold.join(4)
        fold.join(5)
        if m + 1 < count:
            folds[m + 1].join(0)
            folds[m + 1].join(1)
        fold.middle()
        if m + 1 < count:
            folds[m + 1].join(2)
            folds[m + 1].join(3)
        fold.join(6)
        fold.join(7)
        if m < TP - 2:
            for h in range(halves):
                line.step(TP - 2 - m, h)
        next_vector(m)
        if m > 0:
            send_on(m - 1)
    next_vector(3)
    for h in range(halves):
        line.arrive(h)

        def finish(at, h=h):
            grad, _ = norm_back(x_zero[h, at].astype(F32), gain[...], line.total(h, at))
            grad_in[h, at] = grad_x_one[h, at] + grad

        by_rows(rows, finish)
    next_vector(4)
    send_on(count - 1)
    for m in range(count):
        for d in range(1, TP):
            ref = outs[m].at[(p.z - d) % TP]
            copy_to(ref, ref, (zs, zr), (m, d - 1), to_z[1]).wait_recv()
    for copy in started:
        copy.wait_send()
    for i in range(5):
        vector(i).wait_send()
    for fold in folds:
        fold.close()
    line.close()
    for copy in stays:
        copy.wait()


def final(parts, x_zero, gain, grad_x_one, vectors, grads):
    shape, count = parts.shape, len(grads)
    folded = [Fold.shapes(grad, False) for grad in grads]
    results = pl.pallas_call(
        functools.partial(final_kernel, count),
        in_specs=[VMEM] * 5 + [ANY] * count,
        out_specs=[VMEM, VMEM] + [ANY] * count,
        out_shape=[
            jax.ShapeDtypeStruct(shape[1:], F32),
            jax.ShapeDtypeStruct(vectors.shape, F32),
            *(jax.ShapeDtypeStruct((TP,) + grad.shape[-2:], BF) for grad in grads),
        ],
        scratch_shapes=[
            pltpu.VMEM((5,) + vectors.shape, F32),
            pltpu.VMEM((5,) + vectors.shape, F32),
            *pairs(5),
            *pairs(count, TP - 1),
            pltpu.SemaphoreType.DMA((count,)),
            *LineSum.scratch(shape),
            *(item for _, scratch in folded for item in scratch),
        ],
        compiler_params=pltpu.CompilerParams(
            collective_id=3, has_side_effects=True, vmem_limit_bytes=GRANT
        ),
    )(parts, x_zero, gain, grad_x_one, vectors, *grads)
    return results[0], results[1], results[2 : 2 + count]


def chain_kernel(backward, sums, *refs):
    if backward:
        known, start, spans, send, recv = refs
    else:
        start, spans, send, recv = refs
    p = Place()
    peers = [device_q(p, (p.q + d) % NQ) for d in range(NQ)]
    greet(peers[1:])
    spans[p.q] = sums[...]
    copies = []
    for d in range(1, NQ):
        copies.append(copy_to(spans.at[p.q], spans.at[p.q], (send, recv), (d,), peers[d]))
        copies[-1].start()
    for d in range(1, NQ):
        ref = spans.at[(p.q - d) % NQ]
        copy_to(ref, ref, (send, recv), (d,), peers[d]).wait_recv()
    micro = sums.shape[1] // TP
    carry = jnp.zeros((micro, sums.shape[2]), F32)
    order = [(z, q) for z in range(TP) for q in range(NQ)]
    for z, q in reversed(order) if backward else order:
        here = slice(z * micro, (z + 1) * micro)

        @pl.when(p.q == q)
        def _(carry=carry, here=here):
            start[here] = carry

        decay = known[q, 0, here] if backward else spans[q, 0, here]
        carry = decay * carry + spans[q, 0 if backward else 1, here]
    for copy in copies:
        copy.wait_send()


def device_q(p, q):
    return device(p, x=q // 2, c=q % 2)


def chain(sums, known=None):
    backward = known is not None
    every = (NQ,) + sums.shape
    return pl.pallas_call(
        functools.partial(chain_kernel, backward),
        in_specs=[VMEM] * (2 if backward else 1),
        out_specs=[VMEM, VMEM],
        out_shape=[
            jax.ShapeDtypeStruct(sums.shape[1:], F32),
            jax.ShapeDtypeStruct(every, F32),
        ],
        scratch_shapes=pairs(NQ),
        cost_estimate=FREE,
        compiler_params=pltpu.CompilerParams(
            collective_id=5 if backward else 4, has_side_effects=True
        ),
    )(*((sums, known) if backward else (sums,)))


def unpack_kernel(own, one, two, three, *outs):
    p = Place()
    part = own.shape[1] // len(outs)
    for d, piece in enumerate((own, one, two, three)):
        cols = pl.ds(pl.multiple_of((p.z - d) % TP * part, 128), part)
        for i, out in enumerate(outs):
            out[:, cols] = piece[:, i * part : (i + 1) * part].astype(F32)


def unpack(pieces, count):
    rows, cols = pieces[0].shape
    return pl.pallas_call(
        unpack_kernel,
        in_specs=[VMEM] * TP,
        out_specs=[VMEM] * count,
        out_shape=[jax.ShapeDtypeStruct((rows, cols // count * TP), F32)] * count,
        compiler_params=pltpu.CompilerParams(vmem_limit_bytes=GRANT),
    )(*pieces)


def geglu(gate_vals, up_vals):
    return jax.nn.gelu(gate_vals) * up_vals


def all_spans(value, p):
    by_q = everywhere(value, shift_q, p.q, NQ)
    by_r = everywhere(by_q, shift_r, p.r, p.rests)
    return jnp.swapaxes(by_r, 1, 2).reshape((-1,) + value.shape[1:])


def own_spans(spans, p):
    split = spans.reshape((p.rests, TP, NQ) + spans.shape[1:])
    return lax.dynamic_index_in_dim(at(split, p.r), p.q, 1, keepdims=False)


def on_device(
    inputs,
    cotangent,
    proj_gelu,
    proj_lru,
    gate_blocks,
    proj_out,
    ffw_gate,
    ffw_up,
    ffw_down,
    norm_mix,
    norm_ffw,
    decay_param,
    conv_taps,
):
    p = Place()
    micro, span, width = inputs.shape[0], inputs.shape[2], inputs.shape[3]
    lru_width = proj_gelu.shape[1]
    tap_count = conv_taps.shape[1]
    block_width = gate_blocks.shape[1] // 2
    heads = lru_width // block_width
    ffw_part = ffw_gate.shape[1] // TP
    rows = proj_gelu.shape[0]
    held = -(-heads // TP)
    first = [k * heads // TP for k in range(TP)]
    owned = [range(first[k], first[k + 1] if k + 1 < TP else heads) for k in range(TP)]
    part = held * block_width

    out_t, down_t = proj_out.T, ffw_down.T
    small = jnp.concatenate([norm_mix[None], norm_ffw[None], decay_param[None], conv_taps.T])
    small = jnp.pad(small, ((0, 128 - small.shape[0]), (0, 0))).T
    x_rows, cot = inputs[:, 0], cotangent[:, 0]
    one = 1 if p.rests == 1 else 0
    edge = lax.ppermute(
        x_rows[:, span - (tap_count - 1) :],
        "seq",
        [(i, i + 1) for i in range(lax.axis_size("seq") - 1)],
    )
    edge = jnp.pad(edge, ((0, 0), (HALO - (tap_count - 1), 0), (0, 0)))
    x_wide = jnp.concatenate([x_rows.reshape(-1, width), edge.reshape(-1, width)])
    if p.rests == 1:
        weights = (proj_gelu, proj_lru, out_t, gate_blocks, small, ffw_gate, ffw_up, down_t)
        mix_pieces, ffw_pieces = pack(weights, block_width)
        mix_w, ffw_w, piece_1, x_all = intake(
            mix_pieces, ffw_pieces[0], ffw_pieces[1], x_wide, p
        )
        piece_2, piece_3, x_all = lax.optimization_barrier((*ffw_pieces[2:], x_all))
        piece_3, piece_2 = shift_z(piece_3, 3), shift_z(piece_2, 2)
        passed = (piece_1, swap_x(piece_1), swap_f(piece_1), piece_2, piece_3)
    else:
        mix_pieces, ffw_pieces = [], []
        for k in range(TP):
            cols = slice(first[k] * block_width, first[k] * block_width + part)
            pieces = [proj_gelu[:, cols], proj_lru[:, cols], out_t[:, cols], gate_blocks, small]
            mix_pieces.append(jnp.concatenate(pieces, axis=1))
            cols = slice(k * ffw_part, (k + 1) * ffw_part)
            pieces = [ffw_gate[:, cols], ffw_up[:, cols], down_t[:, cols]]
            ffw_pieces.append(jnp.concatenate(pieces, axis=1))
        mix_w = weights_in(jnp.stack(mix_pieces), p)
        whole_ffw = weights_in(jnp.stack(ffw_pieces), p)
        x_all, passed, ffw_w = gather_z(x_wide, p), None, None
    dims = (span, micro, heads, held, block_width, tap_count)
    small_w, rows_w, mixed, pre, conv, gate, state, prod, sums = recur(
        x_all.reshape(-1, width), mix_w, dims
    )
    mix_gain, ffw_gain = small_w[0:1], small_w[1:2]
    start = sum(jnp.where(p.z == k, first[k] * block_width, 0) for k in range(TP))

    ends = (TP, micro, part)
    if p.rests == 1:
        state_in, every_sum = chain(sums)
    else:
        sums = all_spans(jnp.stack([sums[0].reshape(ends), sums[1].reshape(ends)], axis=1), p)
        carry, carries = jnp.zeros_like(sums[0, 0]), []
        for k in range(sums.shape[0]):
            carries.append(carry)
            carry = sums[k, 0] * carry + sums[k, 1]
        state_in = own_spans(jnp.stack(carries), p).reshape(-1, part)
    mix_bf, out_parts = recur_mix(pre, rows_w, state, prod, state_in, mix_w, dims)
    blocked = (TP, micro, span, width)
    out_parts = out_parts.reshape(blocked)
    x_one, ffw_bf, cot_all, _, *fed = middle(
        out_parts, x_rows, ffw_gain, cot.reshape(-1, width), passed, ffw_w
    )
    cot_all = cot_all.reshape(-1, width)

    ffw_bf = ffw_bf.reshape(-1, width)
    if p.rests == 1:
        hidden_bf, grad_gate_up, ffw_parts, grad_in_parts = fed
    else:
        gate_up_w, down_w = whole_ffw[:, : 2 * ffw_part], whole_ffw[:, 2 * ffw_part :]
        gate_up = dot_plain(ffw_bf, gate_up_w)
        gate_vals, up_vals = gate_up[:, :ffw_part], gate_up[:, ffw_part:]
        hidden_bf = geglu(gate_vals, up_vals).astype(BF)
        grad_hidden = dot_plain(cot_all, down_w)
        _, pull_back = jax.vjp(geglu, gate_vals, up_vals)
        grad_gate_up = jnp.concatenate(pull_back(grad_hidden), axis=1).astype(BF)
        ffw_parts = dot_right_t(hidden_bf, down_w).astype(BF)
        grad_in_parts = dot_right_t(grad_gate_up, gate_up_w).astype(BF)
    ffw_parts, grad_in_parts = ffw_parts.reshape(blocked), grad_in_parts.reshape(blocked)
    factors = [cot_all, hidden_bf, ffw_bf, grad_gate_up]
    mixed_out, grad_x_one, gain_rows, grad_mix, *ffw_pieces = turn(
        grad_in_parts, ffw_parts, x_one, cot, ffw_gain, factors * one, p
    )
    if p.rests == 1:
        for d in (1, 3, 2):
            ffw_pieces[d] = shift_z(ffw_pieces[d], d)
    grad_mix = grad_mix.reshape(-1, width)

    grad_gelu_bf, local_back, prod_back, back_sums = recur_back(
        grad_mix, pre, rows_w, state, prod, state_in, gate, mix_w, dims
    )
    if p.rests == 1:
        carried, _ = chain(back_sums[None], every_sum)
    else:
        back_sums = all_spans(back_sums.reshape(ends), p)
        carry, carries = jnp.zeros_like(sums[0, 0]), []
        for k in range(sums.shape[0] - 1, -1, -1):
            carries.append(carry)
            carry = sums[k, 0] * carry + back_sums[k]
        carried = own_spans(jnp.stack(carries[::-1]), p).reshape(-1, part)
    block_mats = lax.dynamic_slice(mix_w, (start, 3 * part), (part, 2 * block_width))
    grad_blocks, grad_lru, spill, row_grads = recur_grad(
        local_back, prod_back, carried, state, prod, state_in, gate, conv, pre, rows_w,
        block_mats.reshape(held, block_width, 2 * block_width), dims,
    )
    spill = spill.reshape(TP, micro, HALO, part)
    from_next = shift_q(spill, -1)
    last = jnp.zeros_like(spill[:1])
    if p.rests > 1:
        last = move(spill[:1], lambda r, z, q: (r - 1, z, NQ - 1) if q == 0 and r > 0 else None)
    from_next = jnp.where(
        p.q == NQ - 1, jnp.concatenate([from_next[1:], last], axis=0), from_next
    )
    grad_pair, grad_mixed_parts, mix_gain_rows = recur_in(
        grad_gelu_bf, grad_lru, from_next.reshape(-1, part), rows_w, small_w, mixed, mix_w, dims
    )
    grad_mixed_parts = grad_mixed_parts.reshape(blocked)

    blocks_all = lax.dynamic_update_slice_in_dim(
        jnp.zeros((lru_width, 2 * block_width), BF),
        (grad_blocks * rows_w[6][:, None]).astype(BF),
        start,
        0,
    )
    mix_grads = [dot_left_t(mixed, grad_pair), dot_left_t(grad_mix, mix_bf), blocks_all]
    mix_grads = [grad.astype(BF) for grad in mix_grads]
    vectors = lax.dynamic_update_slice_in_dim(
        jnp.zeros((1 + tap_count, lru_width), F32), row_grads[: 1 + tap_count], start, 1
    )
    vectors = jnp.concatenate([mix_gain_rows[:1], gain_rows[:1], vectors], axis=0)
    vectors = jnp.pad(vectors, ((0, -vectors.shape[0] % 8), (0, 0)))
    if p.rests == 1:
        grad_inputs, vectors, mix_grads = final(
            grad_mixed_parts, x_rows, mix_gain, grad_x_one, vectors,
            [by_owner(grad, p) for grad in mix_grads],
        )
    else:
        mix_grads = [grads_out(grad, p) for grad in mix_grads]
        grad_mixed_own = scatter_z(grad_mixed_parts, p)
        grad_inputs = grad_x_one + norm_back(x_rows.astype(F32), mix_gain, grad_mixed_own)[0]
        for exchange in (swap_core, swap_x, swap_f):
            vectors = vectors + exchange(vectors)
        for bit in (1, 2):
            vectors = vectors + move(vectors, lambda r, z, q, bit=bit: (r, z ^ bit, q))
        total = vectors
        for d in range(1, p.rests):
            total = total + shift_r(vectors, d)
        vectors = total
    vectors = lax.dynamic_slice_in_dim(vectors, p.index * rows, rows, 1)

    def mix_columns(grad, offset):
        picked = [
            grad[k][
                :,
                offset + (owned[k][0] - first[k]) * block_width : offset
                + (owned[k][-1] + 1 - first[k]) * block_width,
            ]
            for k in range(TP)
        ]
        return jnp.concatenate(picked, axis=1).astype(F32)

    if p.rests == 1:
        share_down, share_gate, share_up = unpack(ffw_pieces, 3)
    else:
        ffw_grads = [dot_left_t(*factors[:2]), dot_left_t(*factors[2:])]
        ffw_grads = [grads_out(grad.astype(BF), p) for grad in ffw_grads]
        beside = lambda v: jnp.swapaxes(v, 0, 1).reshape(rows, -1).astype(F32)
        share_gate = beside(ffw_grads[1][:, :, :ffw_part])
        share_up = beside(ffw_grads[1][:, :, ffw_part:])
        share_down = beside(ffw_grads[0])
    shape = (micro, 1, span, width)
    return (
        mixed_out.reshape(shape),
        grad_inputs.reshape(shape),
        mix_columns(mix_grads[0], 0),
        mix_columns(mix_grads[0], part),
        jnp.sum(mix_grads[2].astype(F32), axis=0),
        mix_columns(mix_grads[1], 0).T,
        share_gate,
        share_up,
        share_down.T,
        vectors[0],
        vectors[1],
        vectors[2],
        vectors[3 : 3 + tap_count].T,
    )


def solution(mesh):
    in_specs = (
        P(None, "fsdp", "seq", None),
        P(None, "fsdp", "seq", None),
        P(("fsdp", "seq"), None),
        P(("fsdp", "seq"), None),
        P(("fsdp", "seq"), None),
        P(None, ("fsdp", "seq")),
        P(("fsdp", "seq"), None),
        P(("fsdp", "seq"), None),
        P(None, ("fsdp", "seq")),
        P(("fsdp", "seq")),
        P(("fsdp", "seq")),
        P(("fsdp", "seq")),
        P(("fsdp", "seq"), None),
    )
    out_specs = (
        P(None, "fsdp", "seq", None),
        P(None, "fsdp", "seq", None),
        P(("fsdp", "seq"), None),
        P(("fsdp", "seq"), None),
        P(("fsdp", "seq"), None),
        P(None, ("fsdp", "seq")),
        P(("fsdp", "seq"), None),
        P(("fsdp", "seq"), None),
        P(None, ("fsdp", "seq")),
        P(("fsdp", "seq")),
        P(("fsdp", "seq")),
        P(("fsdp", "seq")),
        P(("fsdp", "seq"), None),
    )
    return jax.shard_map(
        on_device, mesh=mesh, in_specs=in_specs, out_specs=out_specs, check_vma=False
    )
```

```python
import functools

import jax
import jax.numpy as jnp
from jax import lax
from jax.experimental import pallas as pl
from jax.experimental.pallas import tpu as pltpu
from jax.sharding import PartitionSpec as P

EPS = 1e-06
GUARD = 0.001
RATE = 8.0
TP = 4
NQ = 4
HALO = 8
BF = jnp.bfloat16
F32 = jnp.float32
MESH = pl.DeviceIdType.MESH
ANY = pl.BlockSpec(memory_space=pl.ANY)
VMEM = pl.BlockSpec(memory_space=pltpu.VMEM)
GRANT = 60 * 1024 * 1024
CUTS = 2
FREE = pl.CostEstimate(flops=0, bytes_accessed=0, transcendentals=0)


def move(value, step):
    pairs = []
    for here in range(lax.axis_size("seq")):
        there = step(here // (TP * NQ), here // NQ % TP, here % NQ)
        if there is not None:
            pairs.append((here, (there[0] * TP + there[1]) * NQ + there[2]))
    return lax.ppermute(value, "seq", pairs)


def swap_core(value):
    return move(value, lambda r, z, q: (r, z, q ^ 1))


def swap_x(value):
    return move(value, lambda r, z, q: (r, z, q ^ 2))


def swap_f(value):
    return lax.ppermute(value, "fsdp", [(0, 1), (1, 0)])


def shift_z(value, d):
    return move(value, lambda r, z, q: (r, (z + d) % TP, q))


def shift_q(value, d):
    return move(value, lambda r, z, q: (r, z, (q + d) % NQ))


def shift_r(value, d):
    count = lax.axis_size("seq") // (TP * NQ)
    return move(value, lambda r, z, q: ((r + d) % count, z, q))


def hop(value, d, low, high):
    return move(value, lambda r, z, q: (r, z + d, q) if low <= z <= high else None)


class Place:
    def __init__(self):
        seq = lax.axis_index("seq")
        self.f = lax.axis_index("fsdp")
        self.r, self.z, self.q = seq // (TP * NQ), seq // NQ % TP, seq % NQ
        self.x, self.c = self.q // 2, self.q % 2
        self.rests = lax.axis_size("seq") // (TP * NQ)
        self.fs = lax.axis_size("fsdp")
        self.index = self.f * lax.axis_size("seq") + seq


def at(value, index):
    return lax.dynamic_index_in_dim(value, index, 0, keepdims=False)


def put(base, value, *index):
    starts = [jnp.int32(0) if i is None else jnp.int32(i) for i in index]
    starts += [jnp.int32(0)] * (base.ndim - len(index))
    for dim, i in enumerate(index):
        if i is not None:
            value = jnp.expand_dims(value, dim)
    return lax.dynamic_update_slice(base, value, starts)


def everywhere(value, shifter, mine, count):
    out = put(jnp.zeros((count,) + value.shape, value.dtype), value, mine)
    for d in range(1, count):
        out = put(out, shifter(value, d), (mine - d) % count)
    return out


def gather_z(value, p):
    ups, downs = [], []
    up = down = value
    for k in range(1, TP):
        up = hop(up, 1, k - 1, TP - 2)
        down = hop(down, -1, 1, TP - k)
        ups.append(up)
        downs.append(down)
    out = put(jnp.zeros((TP,) + value.shape, value.dtype), value, p.z)
    for k in range(1, TP):
        out = put(out, downs[k - 1] + ups[TP - 1 - k], (p.z + k) % TP)
    return out


def scatter_z(parts, p):
    right = left = None
    for k in range(TP - 1, 0, -1):
        send = at(parts, (p.z + k) % TP)
        if right is not None:
            send = (send.astype(F32) + right.astype(F32)).astype(BF)
        right = hop(send, 1, 0, TP - 1 - k)
        send = at(parts, (p.z - k) % TP)
        if left is not None:
            send = (send.astype(F32) + left.astype(F32)).astype(BF)
        left = hop(send, -1, k, TP - 1)
    return at(parts, p.z).astype(F32) + right.astype(F32) + left.astype(F32)


def weights_in(pieces, p):
    rows, cols = pieces.shape[1:]
    mine = put(jnp.zeros(pieces.shape, BF), at(pieces, p.z), p.z)
    for d in range(1, TP):
        mine = put(mine, shift_z(at(pieces, (p.z + d) % TP), d), (p.z - d) % TP)
    mine = everywhere(mine, shift_r, p.r, p.rests)
    half = TP // 2
    by_x, by_f = swap_x(mine), swap_f(mine)
    corner = (swap_f(by_x[:, :half]), swap_x(by_f[:, half:]))
    whole = jnp.zeros((p.fs, p.rests, TP, 2, 2, rows, cols), BF)
    for block, f, x, z in (
        (mine, p.f, p.x, 0),
        (by_x, p.f, 1 - p.x, 0),
        (by_f, 1 - p.f, p.x, 0),
        (corner[0], 1 - p.f, 1 - p.x, 0),
        (corner[1], 1 - p.f, 1 - p.x, half),
    ):
        other = swap_core(block)
        for part, c in ((block, p.c), (other, 1 - p.c)):
            part = part[None, :, :, None, None]
            whole = lax.dynamic_update_slice(
                whole, part, [jnp.int32(i) for i in (f, 0, z, x, c, 0, 0)]
            )
    return whole.reshape(-1, cols)


def by_owner(grad, p):
    return grad.reshape(p.fs, p.rests, TP, 2, 2, -1, grad.shape[1])


def to_owner_z(total, p):
    out = put(jnp.zeros(total.shape, BF), at(total, p.z), p.z)
    for d in (1, 3, 2):
        out = put(out, shift_z(at(total, (p.z + d) % TP), d), (p.z - d) % TP)
    return out


def grads_out(grad, p):
    plus = lambda a, b: (a.astype(F32) + b.astype(F32)).astype(BF)
    pick = lambda v, dim, i: lax.dynamic_index_in_dim(v, i, dim, keepdims=False)
    total = by_owner(grad, p)
    total = plus(pick(total, 4, p.c), swap_core(pick(total, 4, 1 - p.c)))
    total = plus(pick(total, 3, p.x), swap_x(pick(total, 3, 1 - p.x)))
    total = plus(at(total, p.f), swap_f(at(total, 1 - p.f)))
    mine = at(total, p.r)
    for d in range(1, p.rests):
        mine = plus(mine, shift_r(at(total, (p.r + d) % p.rests), d))
    return to_owner_z(mine, p)


def dot_left_t(left_mat, right_mat):
    return lax.dot_general(
        left_mat, right_mat, (((0,), (0,)), ((), ())), preferred_element_type=F32
    )


def dot_plain(left_mat, right_mat):
    return jnp.dot(left_mat, right_mat, preferred_element_type=F32)


def dot_right_t(left_mat, right_mat):
    return lax.dot_general(
        left_mat, right_mat, (((1,), (1,)), ((), ())), preferred_element_type=F32
    )


def normed(values, gain_vec):
    return values * lax.rsqrt(jnp.mean(values * values, axis=-1, keepdims=True) + EPS) * gain_vec


def gelu_pair(v):
    scale = 0.7978845608028654
    inner = jnp.tanh(scale * (v + 0.044715 * v * v * v))
    slope = 0.5 * v * (1.0 - inner * inner) * scale * (1.0 + 0.134145 * v * v)
    return 0.5 * v * (1.0 + inner), 0.5 * (1.0 + inner) + slope


def span_scan(decay, drive, backward):
    count = decay.shape[0]
    row = lax.broadcasted_iota(jnp.int32, decay.shape, 0)
    step = 1
    while step < count:
        inside = row < count - step if backward else row >= step
        turn = count - step if backward else step
        drive = drive + jnp.where(inside, decay * pltpu.roll(drive, turn, 0), 0.0)
        decay = decay * jnp.where(inside, pltpu.roll(decay, turn, 0), 1.0)
        step *= 2
    return decay, drive


def gate_values(gate, soft):
    half = gate.shape[1] // 2
    rec_gate = jax.nn.sigmoid(gate[:, :half])
    in_gate = jax.nn.sigmoid(gate[:, half:])
    log_decay = -RATE * rec_gate * soft
    square = jnp.exp(2.0 * log_decay)
    return rec_gate, in_gate, jnp.exp(log_decay), square, jnp.sqrt(1.0 - square + GUARD)


def main_rows(i, span, micro):
    return pl.ds(i // micro * micro * (span + HALO) + i % micro * span, span)


def with_halo(pre, i, span, micro):
    start = i // micro * micro * (span + HALO) + micro * span + i % micro * HALO
    both = [pre[pl.ds(start, HALO)], pre[main_rows(i, span, micro)]]
    return jnp.concatenate(both, axis=0)


def recur_head(span, micro, pre, rows, block, conv, gate, state, prod, sums):
    count = conv.shape[0] // span
    soft, taps = rows[0:1], [rows[k + 2 : k + 3] for k in range(4)]
    for i in range(count):
        vals = with_halo(pre, i, span, micro).astype(BF).astype(F32)
        total = taps[0] * vals
        for k in range(1, 4):
            total = total + taps[k] * pltpu.roll(vals, k, 0)
        conv[pl.ds(i * span, span)] = total[HALO:].astype(BF)
    gate[...] = dot_plain(conv[...], block[...])
    for i in range(count):
        here = pl.ds(i * span, span)
        _, in_gate, decay, _, root = gate_values(gate[here], soft)
        decay, local = span_scan(decay, root * in_gate * conv[here].astype(F32), False)
        state[here] = local
        prod[here] = decay
        sums[0, i : i + 1] = decay[span - 1 :]
        sums[1, i : i + 1] = local[span - 1 :]


def columns(ref, h, width):
    return ref.at[:, pl.ds(pl.multiple_of(h * width, 128), width)]


def by_heads(count, body):
    def turn(h, _):
        body(h)
        return 0

    lax.fori_loop(0, count, turn, 0)


def recur_kernel(
    dims, x_all, mix_w, small, rows, mixed, pre, conv, gate, state, prod, sums,
    small_w, gl_w, block_w, mixed_all, sems,
):
    span, micro, heads, held, bw, taps = dims
    part = held * bw
    p = Place()
    start = pl.multiple_of(p.z * heads // TP * bw, 128)
    pieces = (
        (mix_w.at[:, pl.ds(3 * part + 2 * bw, 128)], small_w),
        (mix_w.at[:, pl.ds(0, 2 * part)], gl_w),
        (mix_w.at[pl.ds(start, part), pl.ds(3 * part, 2 * bw)], block_w),
    )
    loads = [pltpu.make_async_copy(src, dst, sems.at[i]) for i, (src, dst) in enumerate(pieces)]
    for load in loads:
        load.start()
    loads[0].wait()
    row = lax.broadcasted_iota(jnp.int32, (8, 128), 0)
    lane = lax.broadcasted_iota(jnp.int32, (8, 128), 1)
    small[...] = dot_right_t(jnp.where(row == lane, 1.0, 0.0).astype(BF), small_w[...])
    own = small[:, pl.ds(start, part)]
    decay = -own[2:3]
    feature = lax.broadcasted_iota(jnp.int32, (1, part), 1)
    count = ((p.z + 1) * heads // TP - p.z * heads // TP) * bw
    rows[0:1] = jnp.maximum(decay, 0.0) + jnp.log1p(jnp.exp(-jnp.abs(decay)))
    rows[1:2] = jax.nn.sigmoid(decay)
    rows[2 : 2 + taps] = own[3 : 3 + taps]
    rows[6:7] = jnp.where(feature < count, 1.0, 0.0)
    rows[7:8] = jnp.zeros((1, part), F32)
    gain, wide, step = small[0:1], micro * (span + HALO), 16

    def norm(z, _):
        for k in range(0, wide, step):
            vals = x_all[pl.ds(pl.multiple_of(z * wide + k, step), step)].astype(F32)
            vals = normed(vals, gain).astype(BF)
            mixed_all[pl.ds(pl.multiple_of(z * wide + k, step), step)] = vals
            if k < micro * span:
                mixed[pl.ds(pl.multiple_of(z * micro * span + k, step), step)] = vals
        return 0

    lax.fori_loop(0, TP, norm, 0)
    loads[1].wait()

    def project(h):
        cols = pl.ds(pl.multiple_of(h * bw, 128), bw)
        pre[:, cols] = dot_plain(mixed_all[...], gl_w[:, cols])

    by_heads(2 * held, project)
    loads[2].wait()

    def one_head(h):
        block = block_w.at[pl.ds(pl.multiple_of(h * bw, 128), bw)]
        sums_h = sums.at[:, :, pl.ds(pl.multiple_of(h * bw, 128), bw)]
        recur_head(
            span, micro, columns(pre, held + h, bw), columns(rows, h, bw), block,
            columns(conv, h, bw), columns(gate, h, 2 * bw), columns(state, h, bw),
            columns(prod, h, bw), sums_h,
        )

    by_heads(held, one_head)


def recur(x_all, mix_w, dims):
    span, micro, _, held, bw, _ = dims
    part, width = held * bw, x_all.shape[1]
    tokens = x_all.shape[0] // (span + HALO) * span
    shapes = [((8, width), F32), ((8, part), F32), ((tokens, width), BF)]
    shapes += [((x_all.shape[0], 2 * part), F32), ((tokens, part), BF), ((tokens, 2 * part), F32)]
    shapes += [((tokens, part), F32), ((tokens, part), F32), ((2, tokens // span, part), F32)]
    return pl.pallas_call(
        functools.partial(recur_kernel, dims),
        in_specs=[VMEM, ANY],
        out_specs=[VMEM] * len(shapes),
        out_shape=[jax.ShapeDtypeStruct(*shape) for shape in shapes],
        scratch_shapes=[
            pltpu.VMEM((width, 128), BF),
            pltpu.VMEM((width, 2 * part), BF),
            pltpu.VMEM((part, 2 * bw), BF),
            pltpu.VMEM(x_all.shape, BF),
            pltpu.SemaphoreType.DMA((3,)),
        ],
        cost_estimate=FREE,
        compiler_params=pltpu.CompilerParams(vmem_limit_bytes=GRANT),
    )(x_all, mix_w)


def recur_mix_kernel(dims, pre, rows, state, prod, start, mix_w, mix, parts, out_w, sem):
    span, micro, _, held, bw, _ = dims
    part = held * bw
    load = pltpu.make_async_copy(mix_w.at[:, pl.ds(2 * part, part)], out_w, sem.at[0])
    load.start()

    def one_head(h):
        pre_h, state_h, prod_h = columns(pre, h, bw), columns(state, h, bw), columns(prod, h, bw)
        rows_h, start_h, mix_h = columns(rows, h, bw), columns(start, h, bw), columns(mix, h, bw)
        for i in range(state.shape[0] // span):
            here = pl.ds(i * span, span)
            act, _ = gelu_pair(pre_h[main_rows(i, span, micro)])
            states = state_h[here] + prod_h[here] * start_h[i : i + 1]
            mix_h[here] = (states * act * rows_h[6:7]).astype(BF)

    by_heads(held, one_head)
    load.wait()

    def project(j):
        cols = pl.ds(pl.multiple_of(j * 256, 256), 256)
        parts[:, cols] = dot_right_t(mix[...], out_w[cols]).astype(BF)

    by_heads(out_w.shape[0] // 256, project)


def recur_mix(pre, rows, state, prod, start, mix_w, dims):
    tokens, part = state.shape
    width = mix_w.shape[0]
    return pl.pallas_call(
        functools.partial(recur_mix_kernel, dims),
        in_specs=[VMEM] * 5 + [ANY],
        out_specs=[VMEM, VMEM],
        out_shape=[
            jax.ShapeDtypeStruct((tokens, part), BF),
            jax.ShapeDtypeStruct((tokens, width), BF),
        ],
        scratch_shapes=[pltpu.VMEM((width, part), BF), pltpu.SemaphoreType.DMA((1,))],
        cost_estimate=FREE,
        compiler_params=pltpu.CompilerParams(vmem_limit_bytes=GRANT),
    )(pre, rows, state, prod, start, mix_w)


def recur_back_kernel(
    dims, grad, pre, rows, state, prod, start, gate, mix_w, gelu, local, prods, sums, back, out_w, sem
):
    span, micro, _, held, bw, _ = dims
    part = held * bw
    load = pltpu.make_async_copy(mix_w.at[:, pl.ds(2 * part, part)], out_w, sem.at[0])
    load.start()
    load.wait()

    def one_head(h):
        back[...] = dot_plain(grad[...], out_w[:, pl.ds(pl.multiple_of(h * bw, 128), bw)])
        pre_h, state_h, prod_h = columns(pre, h, bw), columns(state, h, bw), columns(prod, h, bw)
        rows_h, start_h, gate_h = columns(rows, h, bw), columns(start, h, bw), columns(gate, h, 2 * bw)
        gelu_h, local_h = columns(gelu, h, bw), columns(local, h, bw)
        prods_h, sums_h = columns(prods, h, bw), columns(sums, h, bw)
        soft = rows_h[0:1]
        for i in range(back.shape[0] // span):
            here = pl.ds(i * span, span)
            act, slope = gelu_pair(pre_h[main_rows(i, span, micro)])
            states = state_h[here] + prod_h[here] * start_h[i : i + 1]
            gelu_h[here] = (back[here] * states * slope * rows_h[6:7]).astype(BF)
            _, _, decay, _, _ = gate_values(gate_h[here], soft)
            row = lax.broadcasted_iota(jnp.int32, decay.shape, 0)
            later = jnp.where(row < span - 1, pltpu.roll(decay, span - 1, 0), 1.0)
            later, adjoint = span_scan(later, back[here] * act, True)
            local_h[here] = adjoint
            prods_h[here] = later
            sums_h[i : i + 1] = decay[:1] * adjoint[:1]

    by_heads(held, one_head)


def recur_back(grad, pre, rows, state, prod, start, gate, mix_w, dims):
    tokens, part = state.shape
    shapes = [((tokens, part), BF), ((tokens, part), F32), ((tokens, part), F32), (start.shape, F32)]
    return pl.pallas_call(
        functools.partial(recur_back_kernel, dims),
        in_specs=[VMEM] * 7 + [ANY],
        out_specs=[VMEM] * 4,
        out_shape=[jax.ShapeDtypeStruct(*shape) for shape in shapes],
        scratch_shapes=[
            pltpu.VMEM((tokens, dims[4]), F32),
            pltpu.VMEM((mix_w.shape[0], part), BF),
            pltpu.SemaphoreType.DMA((1,)),
        ],
        cost_estimate=FREE,
        compiler_params=pltpu.CompilerParams(vmem_limit_bytes=GRANT),
    )(grad, pre, rows, state, prod, start, gate, mix_w)


def recur_grad_kernel(
    span, micro, local, prods, carried, state, prod, start, gate, conv, pre, rows, block,
    blocks_out, lru_out, spill_out, rows_out, gate_grad, conv_grad,
):
    count = local.shape[0] // span
    soft, sig, own = rows[0:1], rows[1:2], rows[6:7]
    taps = [rows[k + 2 : k + 3] for k in range(4)]
    width = local.shape[1]
    add_up = lambda v: jnp.sum(v, axis=0, keepdims=True)
    decay_sum = jnp.zeros((1, width), F32)
    for i in range(count):
        here = pl.ds(i * span, span)
        adjoint = local[here] + prods[here] * carried[i : i + 1]
        states = state[here] + prod[here] * start[i : i + 1]
        row = lax.broadcasted_iota(jnp.int32, states.shape, 0)
        earlier = jnp.where(row >= 1, pltpu.roll(states, 1, 0), start[i : i + 1])
        rec_gate, in_gate, decay, square, root = gate_values(gate[here], soft)
        conv_vals = conv[here].astype(F32)
        drive = adjoint * conv_vals
        grad_log = adjoint * earlier * decay - drive * in_gate * square / root
        decay_sum = decay_sum + add_up(grad_log * rec_gate)
        gate_grad[here, :width] = (-RATE * soft * grad_log * rec_gate * (1.0 - rec_gate)).astype(BF)
        gate_grad[here, width:] = (drive * root * in_gate * (1.0 - in_gate)).astype(BF)
        conv_grad[here] = adjoint * root * in_gate
    blocks_out[...] = lax.dot_general(
        conv[...], gate_grad[...], (((0,), (0,)), ((), ())), preferred_element_type=F32
    )
    conv_grad[...] += dot_right_t(gate_grad[...], block[0])
    tap_sums = [jnp.zeros((1, width), F32) for _ in range(4)]
    for i in range(count):
        here = pl.ds(i * span, span)
        grad = conv_grad[here]
        vals = with_halo(pre, i, span, micro).astype(BF).astype(F32)
        wide = jnp.concatenate([jnp.zeros((HALO, width), F32), grad], axis=0)
        total = taps[0] * wide
        tap_sums[0] = tap_sums[0] + add_up(grad * vals[HALO:])
        for k in range(1, 4):
            total = total + taps[k] * pltpu.roll(wide, span + HALO - k, 0)
            tap_sums[k] = tap_sums[k] + add_up(grad * pltpu.roll(vals, k, 0)[HALO:])
        lru_out[here] = total[HALO:]
        spill_out[pl.ds(i * HALO, HALO)] = total[:HALO]
    rows_out[...] = jnp.zeros(rows_out.shape, F32)
    rows_out[0:1] = decay_sum * sig * own * RATE
    for k in range(4):
        rows_out[k + 1 : k + 2] = tap_sums[k] * own


def recur_grad(local, prods, carried, state, prod, start, gate, conv, pre, rows, blocks, dims):
    tokens, part = state.shape
    span, micro, _, held, bw, _ = dims
    column = lambda h: (0, h)
    whole = pl.BlockSpec((tokens, bw), column)
    ends = pl.BlockSpec((start.shape[0], bw), column)
    return pl.pallas_call(
        functools.partial(recur_grad_kernel, span, micro),
        grid=(held,),
        in_specs=[
            whole,
            whole,
            ends,
            whole,
            whole,
            ends,
            pl.BlockSpec((tokens, 2 * bw), column),
            whole,
            pl.BlockSpec((pre.shape[0], bw), lambda h: (0, held + h)),
            pl.BlockSpec((8, bw), column),
            pl.BlockSpec((1, bw, 2 * bw), lambda h: (h, 0, 0)),
        ],
        out_specs=[
            pl.BlockSpec((bw, 2 * bw), lambda h: (h, 0)),
            whole,
            pl.BlockSpec((start.shape[0] * HALO, bw), column),
            pl.BlockSpec((8, bw), column),
        ],
        out_shape=[
            jax.ShapeDtypeStruct((part, 2 * bw), F32),
            jax.ShapeDtypeStruct((tokens, part), F32),
            jax.ShapeDtypeStruct((start.shape[0] * HALO, part), F32),
            jax.ShapeDtypeStruct((8, part), F32),
        ],
        scratch_shapes=[pltpu.VMEM((tokens, 2 * bw), BF), pltpu.VMEM((tokens, bw), F32)],
        cost_estimate=FREE,
        compiler_params=pltpu.CompilerParams(vmem_limit_bytes=GRANT),
    )(local, prods, carried, state, prod, start, gate, conv, pre, rows, blocks)


def recur_in_kernel(
    dims, gelu, lru, spill, rows, small, mixed, mix_w, pair, parts, gains, gl_w, sem
):
    span, _, _, held, bw, _ = dims
    part = held * bw
    load = pltpu.make_async_copy(mix_w.at[:, pl.ds(0, 2 * part)], gl_w, sem.at[0])
    load.start()
    pair[:, :part] = gelu[...]

    def one_head(h):
        lru_h, spill_h, own = columns(lru, h, bw), columns(spill, h, bw), columns(rows, h, bw)[6:7]
        for i in range(lru.shape[0] // span):
            vals = lru_h[pl.ds(i * span, span)]
            late = vals[span - HALO :] + spill_h[pl.ds(i * HALO, HALO)]
            vals = jnp.concatenate([vals[: span - HALO], late], axis=0) * own
            pair[pl.ds(i * span, span), pl.ds(pl.multiple_of((held + h) * bw, 128), bw)] = vals.astype(BF)

    by_heads(held, one_head)
    load.wait()

    def project(j):
        cols = pl.ds(pl.multiple_of(j * 256, 256), 256)
        grad = dot_right_t(pair[...], gl_w[cols])
        parts[:, cols] = grad.astype(BF)
        gain = jnp.sum(grad * mixed[:, cols].astype(F32), axis=0, keepdims=True)
        gains[0:1, cols] = gain / small[0:1, cols]

    by_heads(gl_w.shape[0] // 256, project)


def recur_in(gelu, lru, spill, rows, small, mixed, mix_w, dims):
    tokens, part = gelu.shape
    width = mix_w.shape[0]
    return pl.pallas_call(
        functools.partial(recur_in_kernel, dims),
        in_specs=[VMEM] * 6 + [ANY],
        out_specs=[VMEM] * 3,
        out_shape=[
            jax.ShapeDtypeStruct((tokens, 2 * part), BF),
            jax.ShapeDtypeStruct((tokens, width), BF),
            jax.ShapeDtypeStruct((8, width), F32),
        ],
        scratch_shapes=[pltpu.VMEM((width, 2 * part), BF), pltpu.SemaphoreType.DMA((1,))],
        cost_estimate=FREE,
        compiler_params=pltpu.CompilerParams(vmem_limit_bytes=GRANT),
    )(gelu, lru, spill, rows, small, mixed, mix_w)


def device(p, f=None, z=None, x=None, c=None):
    f, z = p.f if f is None else f, p.z if z is None else z
    x, c = p.x if x is None else x, p.c if c is None else c
    return (f, ((p.r * TP + z) * 2 + x) * 2 + c)


def copy_to(src, dst, sems, index, dev):
    return pltpu.make_async_remote_copy(
        src_ref=src,
        dst_ref=dst,
        send_sem=sems[0].at[index],
        recv_sem=sems[1].at[index],
        device_id=dev,
        device_id_type=MESH,
    )


def pairs(*shape):
    return [pltpu.SemaphoreType.DMA(shape), pltpu.SemaphoreType.DMA(shape)]


def greet(devices):
    barrier = pltpu.get_barrier_semaphore()
    for dev in devices:
        pl.semaphore_signal(barrier, inc=1, device_id=dev, device_id_type=MESH)
    pl.semaphore_wait(barrier, len(devices))


def by_rows(count, body, step=16):
    def turn(i, _):
        body(pl.ds(pl.multiple_of(i * step, step), step))
        return 0

    assert count % step == 0
    lax.fori_loop(0, count // step, turn, 0)


class Gather:
    def __init__(self, p, out, ups, downs):
        self.p, self.out, self.ups, self.downs = p, out, ups, downs
        self.up = device(p, z=jnp.minimum(p.z + 1, TP - 1))
        self.down = device(p, z=jnp.maximum(p.z - 1, 0))

    def begin(self, h, src):
        z = self.p.z

        @pl.when(z < TP - 1)
        def _():
            copy_to(src, self.out.at[z, h], self.ups, (0, h), self.up).start()

        @pl.when(z > 0)
        def _():
            copy_to(src, self.out.at[z, h], self.downs, (0, h), self.down).start()

    def step(self, k, h):
        z, out = self.p.z, self.out

        @pl.when(z >= k)
        def _():
            block = out.at[z - k, h]
            copy_to(block, block, self.ups, (k - 1, h), self.up).wait_recv()
            if k < TP - 1:

                @pl.when(z < TP - 1)
                def _():
                    copy_to(block, block, self.ups, (k, h), self.up).start()

        @pl.when(z <= TP - 1 - k)
        def _():
            block = out.at[z + k, h]
            copy_to(block, block, self.downs, (k - 1, h), self.down).wait_recv()
            if k < TP - 1:

                @pl.when(z > 0)
                def _():
                    copy_to(block, block, self.downs, (k, h), self.down).start()

    def close(self, halves):
        z, block = self.p.z, self.out.at[0, 0]
        for h in range(halves) if isinstance(halves, int) else halves:
            for k in range(TP - 1):

                @pl.when((z >= k) & (z < TP - 1))
                def _():
                    copy_to(block, block, self.ups, (k, h), self.up).wait_send()

                @pl.when((z <= TP - 1 - k) & (z > 0))
                def _():
                    copy_to(block, block, self.downs, (k, h), self.down).wait_send()


class LineSum:
    def __init__(self, p, parts, scratch):
        self.p, self.parts = p, parts
        self.got_up, self.got_down, self.out_up, self.out_down = scratch[:4]
        self.ups, self.downs = scratch[4:6], scratch[6:8]
        self.halves, self.rows = parts.shape[1:3]
        self.up = device(p, z=jnp.minimum(p.z + 1, TP - 1))
        self.down = device(p, z=jnp.maximum(p.z - 1, 0))

    @staticmethod
    def scratch(parts):
        block = parts[1:]
        return [
            pltpu.VMEM((TP - 1,) + block, BF),
            pltpu.VMEM((TP - 1,) + block, BF),
            pltpu.VMEM((TP - 2,) + block, BF),
            pltpu.VMEM((TP - 2,) + block, BF),
            *pairs(TP - 1, parts[1]),
            *pairs(TP - 1, parts[1]),
        ]

    def clear(self):
        z = self.p.z

        @pl.when(z == 0)
        def _():
            for h in range(self.halves):
                by_rows(self.rows, lambda at: self.fill(self.got_up, h, at))

        @pl.when(z == TP - 1)
        def _():
            for h in range(self.halves):
                by_rows(self.rows, lambda at: self.fill(self.got_down, h, at))

    def fill(self, ref, h, at):
        ref[0, h, at] = jnp.zeros((at.size, ref.shape[-1]), BF)

    def one_way(self, k, h, place, block, got, out, sems, dev):
        @pl.when(place == 0)
        def _():
            copy_to(self.parts.at[block, h], got.at[k - 1, h], sems, (k - 1, h), dev).start()

        if k < TP - 1:

            @pl.when((place >= 1) & (place + k <= TP - 1))
            def _():
                copy_to(got.at[k, h], got.at[k, h], sems, (k, h), dev).wait_recv()

                def add(at):
                    total = self.parts[block, h, at].astype(F32) + got[k, h, at].astype(F32)
                    out[k - 1, h, at] = total.astype(BF)

                by_rows(self.rows, add)
                copy_to(out.at[k - 1, h], got.at[k - 1, h], sems, (k - 1, h), dev).start()

    def step(self, k, h):
        z = self.p.z
        block = jnp.minimum(z + k, TP - 1)
        self.one_way(k, h, z, block, self.got_up, self.out_up, self.ups, self.up)
        block = jnp.maximum(z - k, 0)
        self.one_way(k, h, TP - 1 - z, block, self.got_down, self.out_down, self.downs, self.down)

    def arrive(self, h):
        z = self.p.z

        @pl.when(z >= 1)
        def _():
            got = self.got_up.at[0, h]
            copy_to(got, got, self.ups, (0, h), self.up).wait_recv()

        @pl.when(z <= TP - 2)
        def _():
            got = self.got_down.at[0, h]
            copy_to(got, got, self.downs, (0, h), self.down).wait_recv()

    def total(self, h, at):
        total = self.parts[self.p.z, h, at].astype(F32) + self.got_up[0, h, at].astype(F32)
        return total + self.got_down[0, h, at].astype(F32)

    def close(self):
        z, got = self.p.z, self.got_up.at[0, 0]
        for h in range(self.halves):
            for k in range(1, TP):

                @pl.when(z + k <= TP - 1)
                def _():
                    copy_to(got, got, self.ups, (k - 1, h), self.up).wait_send()

                @pl.when(z - k >= 0)
                def _():
                    copy_to(got, got, self.downs, (k - 1, h), self.down).wait_send()


def greet_line(p, others=()):
    barrier = pltpu.get_barrier_semaphore()
    for dev in others:
        pl.semaphore_signal(barrier, inc=1, device_id=dev, device_id_type=MESH)

    @pl.when(p.z > 0)
    def _():
        pl.semaphore_signal(barrier, inc=1, device_id=device(p, z=p.z - 1), device_id_type=MESH)

    @pl.when(p.z < TP - 1)
    def _():
        pl.semaphore_signal(barrier, inc=1, device_id=device(p, z=p.z + 1), device_id_type=MESH)

    inner = (p.z > 0) & (p.z < TP - 1)

    @pl.when(inner)
    def _():
        pl.semaphore_wait(barrier, len(others) + 2)

    @pl.when(jnp.logical_not(inner))
    def _():
        pl.semaphore_wait(barrier, len(others) + 1)


class Spread:
    KINDS = ((0, 0), (0, 1), (1, 0), (1, 1))

    def __init__(self, p, whole, sems):
        self.p, self.whole, self.started = p, whole, []
        self.xs, self.fs, self.gs, self.cs = sems[0:2], sems[2:4], sems[4:6], sems[6:8]
        self.to_x, self.to_f = device(p, x=1 - p.x), device(p, f=1 - p.f)
        self.to_c = device(p, c=1 - p.c)

    @staticmethod
    def scratch():
        return [*pairs(TP), *pairs(TP), *pairs(TP), *pairs(4, TP)]

    def slot(self, kind, d, other_core=False):
        p, (f, x) = self.p, self.KINDS[kind]
        c = 1 - p.c if other_core else p.c
        return self.whole.at[(p.f + f) % 2, 0, (p.z - d) % TP, (p.x + x) % 2, c]

    def send(self, src, dst, sems, index, dev):
        copy = copy_to(src, dst, sems, index, dev)
        copy.start()
        self.started.append(copy)

    def wait(self, ref, sems, index):
        copy_to(ref, ref, sems, index, self.to_x).wait_recv()

    def spread(self, d, src=None):
        dst = self.slot(0, d)
        src = dst if src is None else src
        self.send(src, dst, self.xs, (d,), self.to_x)
        self.send(src, dst, self.fs, (d,), self.to_f)
        self.send(src, dst, self.cs, (0, d), self.to_c)

    def given(self, d, own, by_x, by_f):
        self.send(own, self.slot(0, d), self.cs, (0, d), self.to_c)
        self.send(by_x, self.slot(1, d), self.cs, (1, d), self.to_c)
        self.send(by_f, self.slot(2, d), self.cs, (2, d), self.to_c)
        if d % 2 == 0:
            self.send(by_x, self.slot(1, d), self.gs, (d,), self.to_f)
        else:
            self.send(by_f, self.slot(2, d), self.gs, (d,), self.to_x)

    def sides(self, d):
        ref = self.slot(1, d)
        self.wait(ref, self.xs, (d,))
        if d % 2 == 0:
            self.send(ref, ref, self.gs, (d,), self.to_f)
        self.send(ref, ref, self.cs, (1, d), self.to_c)
        ref = self.slot(2, d)
        self.wait(ref, self.fs, (d,))
        if d % 2 == 1:
            self.send(ref, ref, self.gs, (d,), self.to_x)
        self.send(ref, ref, self.cs, (2, d), self.to_c)

    def corner(self, d):
        ref = self.slot(3, d)
        self.wait(ref, self.gs, (d,))
        self.send(ref, ref, self.cs, (3, d), self.to_c)

    def close(self, pieces):
        for kind in range(4):
            for d in pieces:
                self.wait(self.slot(kind, d, True), self.cs, (kind, d))
        for copy in self.started:
            copy.wait_send()


def pack_kernel(bw, gelu, lru, out_t, blocks, small, gate, up, down_t, mix, *ffw):
    p = Place()
    heads = gelu.shape[1] // bw
    part, ffw_part = -(-heads // TP) * bw, gate.shape[1] // TP
    for d in range(TP):
        z = (p.z + d) % TP
        cols = pl.ds(pl.multiple_of(z * heads // TP * bw, 128), part)
        sources = [gelu[:, cols], lru[:, cols], out_t[:, cols], blocks[...], small[...]]
        offset = 0
        for source in sources:
            mix[d, :, offset : offset + source.shape[1]] = source
            offset += source.shape[1]
        cols = pl.ds(pl.multiple_of(z * ffw_part, 128), ffw_part)
        for i, source in enumerate((gate, up, down_t)):
            ffw[d][:, i * ffw_part : (i + 1) * ffw_part] = source[:, cols]


def pack(weights, bw):
    rows, lru_width = weights[0].shape
    part = -(-lru_width // bw // TP) * bw
    mix_cols = 3 * part + weights[3].shape[1] + weights[4].shape[1]
    piece = jax.ShapeDtypeStruct((rows, 3 * weights[5].shape[1] // TP), BF)
    mix, *ffw = pl.pallas_call(
        functools.partial(pack_kernel, bw),
        in_specs=[VMEM] * 8,
        out_specs=[VMEM] * (1 + TP),
        out_shape=[jax.ShapeDtypeStruct((TP, rows, mix_cols), BF), *[piece] * TP],
        compiler_params=pltpu.CompilerParams(vmem_limit_bytes=GRANT),
    )(*weights)
    return mix, ffw


def intake_kernel(
    mix_p, ffw_0, ffw_1, x_p, cot_p, mix_w, ffw_w, piece_1, x_all, cot_all,
    zs, zr, us, ur, vs, vr, cus, cur, cvs, cvr, local, *sems
):
    p = Place()
    mix, ffw = Spread(p, mix_w, sems[:8]), Spread(p, ffw_w, sems[8:])
    to_z = [device(p, z=(p.z + d) % TP) for d in range(TP)]
    greet(to_z[1:] + [mix.to_x, mix.to_f, mix.to_c])
    started = []

    def along_z(i, src, dst, d):
        copy = copy_to(src, dst, (zs, zr), (i,), to_z[d])
        copy.start()
        started.append(copy)

    def from_z(i, ref):
        copy_to(ref, ref, (zs, zr), (i,), to_z[1]).wait_recv()

    for d in (1, 3, 2):
        along_z(d, mix_p.at[d], mix.slot(0, 0), d)
    mix.spread(0, mix_p.at[0])
    ffw.spread(0, ffw_0)
    stays = [
        pltpu.make_async_copy(mix_p.at[0], mix.slot(0, 0), local.at[0]),
        pltpu.make_async_copy(ffw_0, ffw.slot(0, 0), local.at[1]),
        pltpu.make_async_copy(x_p, x_all.at[p.z, 0], local.at[2]),
        pltpu.make_async_copy(cot_p, cot_all.at[p.z, 0], local.at[3]),
    ]
    for copy in stays:
        copy.start()
    line = Gather(p, x_all, (us, ur), (vs, vr))
    cot = Gather(p, cot_all, (cus, cur), (cvs, cvr))
    for d in (1, 3):
        from_z(d, mix.slot(0, d))
        mix.spread(d)
    line.begin(0, x_p)
    cot.begin(0, cot_p)
    from_z(2, mix.slot(0, 2))
    mix.spread(2)
    along_z(0, ffw_1, piece_1, 1)
    mix.sides(0)
    ffw.sides(0)
    mix.corner(0)
    line.step(1, 0)
    cot.step(1, 0)
    for d in (1, 3):
        mix.sides(d)
    ffw.corner(0)
    line.step(2, 0)
    cot.step(2, 0)
    for d in (1, 3):
        mix.corner(d)
    mix.sides(2)
    line.step(3, 0)
    cot.step(3, 0)
    mix.corner(2)
    from_z(0, piece_1)
    mix.close(range(TP))
    ffw.close((0,))
    for copy in started:
        copy.wait_send()
    line.close(1)
    cot.close(1)
    for copy in stays:
        copy.wait()


def intake(mix_p, ffw_0, ffw_1, x_p, cot_p, p):
    whole = lambda v: jax.ShapeDtypeStruct((p.fs, 1, TP, 2, 2) + v.shape[-2:], BF)
    mix_w, ffw_w, piece_1, x_all, cot_all = pl.pallas_call(
        intake_kernel,
        in_specs=[ANY] * 5,
        out_specs=[ANY] * 5,
        out_shape=[
            whole(mix_p),
            whole(ffw_0),
            jax.ShapeDtypeStruct(ffw_1.shape, BF),
            jax.ShapeDtypeStruct((TP, 1) + x_p.shape, BF),
            jax.ShapeDtypeStruct((TP, 1) + cot_p.shape, BF),
        ],
        scratch_shapes=[
            *pairs(TP),
            *pairs(TP - 1, 1),
            *pairs(TP - 1, 1),
            *pairs(TP - 1, 1),
            *pairs(TP - 1, 1),
            pltpu.SemaphoreType.DMA((4,)),
            *Spread.scratch(),
            *Spread.scratch(),
        ],
        compiler_params=pltpu.CompilerParams(collective_id=0, has_side_effects=True),
    )(mix_p, ffw_0, ffw_1, x_p, cot_p)
    return mix_w.reshape(-1, mix_p.shape[-1]), ffw_w, piece_1, x_all[:, 0], cot_all


class Stream:
    def __init__(self, pick, count, buffers, sems):
        self.pick, self.count, self.buffers, self.sems = pick, count, buffers, sems

    def load(self, i):
        slot = i % 2
        return pltpu.make_async_copy(self.pick(i), self.buffers.at[slot], self.sems.at[slot])

    def start(self):
        self.load(0).start()

    def run(self, low, high, body):
        def turn(i, _):
            @pl.when(i + 1 < self.count)
            def _():
                self.load(i + 1).start()

            self.load(i).wait()
            body(i, self.buffers.at[i % 2])
            return 0

        lax.fori_loop(low, high, turn, 0)


def flat(block):
    return block.reshape(-1, block.shape[-1])


FFW_CHUNK = 256


def ffw_streams(ffw_w, part, buffers):
    chunks, rest = part // FFW_CHUNK, part % FFW_CHUNK
    col = lambda base, i: pl.ds(pl.multiple_of(base + i * FFW_CHUNK, 128), FFW_CHUNK)
    pick = lambda base: lambda i: ffw_w.at[:, 0, :, :, :, :, col(base, i)]
    half = TP // 2
    rows = lambda cols: lambda i: ffw_w.at[i // 2, 0, pl.ds(i % 2 * half, half), :, :, :, cols]
    gate = Stream(pick(0), chunks, buffers[0], buffers[1])
    up = Stream(pick(part), chunks, buffers[2], buffers[3])
    down = Stream(pick(2 * part), chunks, buffers[0], buffers[1])
    down_rows = Stream(rows(pl.ds(2 * part, part)), 4, buffers[4], buffers[5])
    both_rows = Stream(rows(pl.ds(0, 2 * part)), 4, buffers[6], buffers[7])
    return gate, up, down, down_rows, both_rows


class Feed:
    def __init__(self, x, cot, ffw_w, outs, vals, scratch):
        self.x, self.cot, self.vals = x, cot, vals
        self.hidden, self.grad_pair, self.out_parts, self.in_parts = outs
        self.part = part = self.hidden.shape[1]
        self.chunks, self.rest = part // FFW_CHUNK, part % FFW_CHUNK
        streams = ffw_streams(ffw_w, part, scratch[:8])
        self.gate, self.up, self.down, self.down_rows, self.both_rows = streams
        self.tails, tail_sems = scratch[8:10]
        self.last = last = self.chunks * FFW_CHUNK
        self.loads = [
            pltpu.make_async_copy(
                ffw_w.at[:, 0, :, :, :, :, pl.ds(k * part + last, self.rest)],
                self.tails.at[k],
                tail_sems.at[k],
            )
            for k in range(3)
        ]

    def begin(self):
        self.gate.start()
        self.up.start()
        for load in self.loads:
            load.start()
        self.down_rows.start()
        self.both_rows.start()

    def cols(self, i, base):
        return pl.ds(pl.multiple_of(base + i * FFW_CHUNK, 128), FFW_CHUNK)

    def forward_cols(self, cols, other, gate_w, up_w):
        gate_vals = dot_plain(self.x[...], gate_w)
        up_vals = dot_plain(self.x[...], up_w)
        self.vals[:, cols] = gate_vals
        self.vals[:, other] = up_vals
        self.hidden[:, cols] = (gelu_pair(gate_vals)[0] * up_vals).astype(BF)

    def forward(self, low, high):
        def turn(i, _):
            for stream in (self.gate, self.up):

                @pl.when(i + 1 < self.chunks)
                def _(stream=stream):
                    stream.load(i + 1).start()

                stream.load(i).wait()
            weights = [flat(stream.buffers[i % 2]) for stream in (self.gate, self.up)]
            self.forward_cols(self.cols(i, 0), self.cols(i, self.part), *weights)
            return 0

        lax.fori_loop(low, high, turn, 0)

    def forward_end(self):
        self.down.start()
        for load in self.loads:
            load.wait()
        cols = pl.ds(self.last, self.rest), pl.ds(self.part + self.last, self.rest)
        self.forward_cols(*cols, flat(self.tails[0]), flat(self.tails[1]))

    def by_weight_rows(self, stream, source, out, low=0, high=4):
        def body(i, buffer):
            weights = flat(buffer[...])
            count = weights.shape[0]
            cols = pl.ds(pl.multiple_of(i * count, 128), count)
            out[:, cols] = dot_right_t(source[...], weights).astype(BF)

        stream.run(low, high, body)

    def forward_out(self):
        self.by_weight_rows(self.down_rows, self.hidden, self.out_parts)

    def backward_cols(self, cols, other, weights):
        grad = dot_plain(self.cot[...], weights)
        act, slope = gelu_pair(self.vals[:, cols])
        self.grad_pair[:, cols] = (grad * self.vals[:, other] * slope).astype(BF)
        self.grad_pair[:, other] = (grad * act).astype(BF)

    def backward(self, low, high):
        def body(i, buffer):
            self.backward_cols(self.cols(i, 0), self.cols(i, self.part), flat(buffer[...]))

        self.down.run(low, high, body)

    def backward_end(self):
        cols = pl.ds(self.last, self.rest), pl.ds(self.part + self.last, self.rest)
        self.backward_cols(*cols, flat(self.tails[2]))

    def backward_in(self, low, high):
        self.by_weight_rows(self.both_rows, self.grad_pair, self.in_parts, low, high)


def ffw_scratch(ffw_w, part):
    f, _, z, x, c, rows, _ = ffw_w.shape
    column = lambda width: pltpu.VMEM((2, f, z, x, c, rows, width), BF)
    wide = lambda width: pltpu.VMEM((2, z // 2, x, c, rows, width), BF)
    pair = pltpu.SemaphoreType.DMA((2,))
    return [
        column(FFW_CHUNK), pair, column(FFW_CHUNK), pair, wide(part), pair, wide(2 * part), pair,
        pltpu.VMEM((3, f, z, x, c, rows, part % FFW_CHUNK), BF),
        pltpu.SemaphoreType.DMA((3,)),
    ]


def middle_kernel(with_ffw, *refs):
    parts, x_zero, gain, cot_p, cot_first, piece_1, by_x, by_f, piece_2, piece_3, _ = refs[:11]
    x_one_out, ffw_out, cot_out, ffw_w, *refs = refs[11:]
    if with_ffw:
        hidden_out, pair_out, parts_out, in_out, *refs = refs
    x_one, ffw_all, cot_all, own, local, gu0, gu1, gd0, gd1, cu0, cu1, cd0, cd1 = refs[:13]
    p = Place()
    line = LineSum(p, parts, refs[13:21])
    out = Gather(p, ffw_all, (gu0, gu1), (gd0, gd1))
    cot = Gather(p, cot_all, (cu0, cu1), (cd0, cd1))
    halves, rows = parts.shape[1:3]
    line.clear()
    stays = []

    def stay(src, dst):
        copy = pltpu.make_async_copy(src, dst, local.at[len(stays)])
        copy.start()
        stays.append(copy)

    if with_ffw:
        ffw = Spread(p, ffw_w, refs[21:29])
        outs, vals, buffers = refs[29:33], refs[33], refs[34:44]
        bounce_sems = refs[44]
        greet_line(p, (ffw.to_x, ffw.to_f, ffw.to_c))
    else:
        greet_line(p)
    side = lambda name, *args: getattr(ffw, name)(*args) if with_ffw else None
    for h in range(halves):
        line.step(TP - 1, h)
    stay(cot_first, cot_all.at[:, pl.ds(0, 1)])
    side("given", 1, piece_1, by_x, by_f)
    side("spread", 3, piece_3)
    side("spread", 2, piece_2)
    if with_ffw:
        part = vals.shape[1] // 2
        moves = [(piece_1, 0, 1), (by_x, 1, 1), (by_f, 2, 1), (piece_3, 0, 3), (piece_2, 0, 2)]
        steps = [(src, ffw.slot(kind, d), k) for src, kind, d in moves for k in range(2)]

        def bounce(i, out):
            src, dst, k = steps[i]
            cols = pl.ds(0, 2 * part) if k == 0 else pl.ds(2 * part, part)
            space = buffers[6 - 2 * k].at[i // 2 % 2, 0, 0, 0]
            if out:
                return pltpu.make_async_copy(space, dst.at[:, cols], bounce_sems.at[i % 4])
            return pltpu.make_async_copy(src.at[:, cols], space, bounce_sems.at[4])

        for i in range(len(steps)):
            if i >= 4:
                bounce(i - 4, True).wait()
            bounce(i, False).start()
            bounce(i, False).wait()
            bounce(i, True).start()
        for i in range(len(steps) - 4, len(steps)):
            bounce(i, True).wait()
    for k in range(TP - 2, 0, -1):
        for h in range(halves):
            line.step(k, h)
    for h in range(halves):
        line.arrive(h)

        def finish(at, h=h):
            value = x_zero[h, at].astype(F32) + line.total(h, at)
            x_one[h, at] = value
            own[h, at] = normed(value, gain[...]).astype(BF)

        by_rows(rows, finish)
        out.begin(h, own.at[h])
        stay(own.at[h], ffw_all.at[p.z, h])
    for h in range(halves):
        out.step(1, h)
    for d in (3, 2):
        side("sides", d)
    for h in range(halves):
        out.step(2, h)
    cot.begin(1, cot_p)
    stay(cot_p, cot_all.at[p.z, 1])
    side("corner", 1)
    for d in (3, 2):
        side("corner", d)
    for h in range(halves):
        out.step(3, h)
    cot.step(1, 1)
    side("close", (1, 2, 3))
    if not with_ffw:
        cot.step(2, 1)
        cot.step(3, 1)
    for copy in stays:
        copy.wait()
    done = len(stays)
    stay(x_one, x_one_out)
    stay(ffw_all, ffw_out)
    if not with_ffw:
        stay(cot_all, cot_out)
    else:
        tokens = lambda ref: ref.reshape(TP * halves * rows, parts.shape[3])
        hidden, pair, out_parts, in_parts = outs
        flat_outs = (hidden, pair, tokens(out_parts), in_parts)
        feed = Feed(tokens(ffw_all), tokens(cot_all), ffw_w, flat_outs, vals, buffers)
        feed.begin()
        feed.forward(0, 2)
        cot.step(2, 1)
        feed.forward(2, 6)
        cot.step(3, 1)
        stay(cot_all, cot_out)
        feed.forward(6, feed.chunks)
        feed.forward_end()
        feed.forward_out()
        stay(hidden, hidden_out)
        stay(out_parts, parts_out)
        feed.backward(0, feed.chunks)
        feed.backward_end()
        stay(pair, pair_out)
        feed.backward_in(0, 4)
        stay(in_parts, in_out)
    line.close()
    out.close(halves)
    cot.close((1,))
    for copy in stays[done:]:
        copy.wait()


def middle(parts, x_zero, gain, cot_p, cot_first, pieces, ffw_w):
    shape = parts.shape
    with_ffw = ffw_w is not None
    line = (TP, 2) + cot_p.shape
    outs, extra = [], []
    if with_ffw:
        tokens, part = shape[0] * shape[1] * shape[2], ffw_w.shape[-1] // 3
        assert part // FFW_CHUNK >= 6 and part % FFW_CHUNK
        outs = [(tokens, part), (tokens, 2 * part), shape, (tokens, shape[3])]
        extra = [
            *Spread.scratch(),
            *(pltpu.VMEM(kept, BF) for kept in outs),
            pltpu.VMEM((tokens, 2 * part), F32),
            *ffw_scratch(ffw_w, part),
            pltpu.SemaphoreType.DMA((5,)),
        ]
    else:
        ffw_w = jnp.zeros((16, 128), BF)
        pieces = [ffw_w] * 5
    return pl.pallas_call(
        functools.partial(middle_kernel, with_ffw),
        in_specs=[VMEM] * 3 + [ANY] * 8,
        out_specs=[ANY] * (4 + len(outs)),
        out_shape=[
            jax.ShapeDtypeStruct(shape[1:], F32),
            jax.ShapeDtypeStruct(shape, BF),
            jax.ShapeDtypeStruct(line, BF),
            jax.ShapeDtypeStruct(ffw_w.shape, BF),
            *(jax.ShapeDtypeStruct(out, BF) for out in outs),
        ],
        input_output_aliases={10: 3},
        scratch_shapes=[
            pltpu.VMEM(shape[1:], F32),
            pltpu.VMEM(shape, BF),
            pltpu.VMEM(line, BF),
            pltpu.VMEM(shape[1:], BF),
            pltpu.SemaphoreType.DMA((shape[1] + 10,)),
            *pairs(TP - 1, shape[1]),
            *pairs(TP - 1, shape[1]),
            *pairs(TP - 1, 2),
            *pairs(TP - 1, 2),
            *LineSum.scratch(shape),
            *extra,
        ],
        compiler_params=pltpu.CompilerParams(
            collective_id=1, has_side_effects=True, vmem_limit_bytes=GRANT
        ),
    )(parts, x_zero, gain, cot_p, cot_first, *pieces, ffw_w)


def norm_back(values, gain, grad):
    inv = lax.rsqrt(jnp.mean(values * values, axis=-1, keepdims=True) + EPS)
    unit = values * inv
    through = grad * gain
    inner = jnp.mean(through * unit, axis=-1, keepdims=True)
    return inv * (through - unit * inner), grad * unit


class Fold:
    ORDER = ((0, 1, 1), (1, 1, 1), (0, 0, 1), (1, 1, 0), (0, 1, 0), (1, 0, 1), (0, 0, 0), (1, 0, 0))

    def __init__(self, p, grad, cores, scratch):
        self.p, self.grad, self.cores = p, grad, cores
        self.sums, self.stage, self.got, self.got_late = scratch[:4]
        self.near, self.staged = scratch[4:6]
        self.core_sems, self.early, self.late = scratch[6:8], scratch[8:10], scratch[10:12]
        self.to = (device(p, x=1 - p.x), device(p, f=1 - p.f))
        self.to_c = device(p, c=1 - p.c)

    @staticmethod
    def shapes(grad, staged):
        block = (TP // 2,) + grad.shape[-2:]
        waiting = (2,) if staged else (2, 2, 2)
        return jax.ShapeDtypeStruct((2, 2, 2) + block, BF), [
            pltpu.VMEM((2, 2, 2) + block, BF),
            pltpu.VMEM(waiting + block, BF),
            pltpu.VMEM((2, 2) + block, BF),
            pltpu.VMEM((2,) + block, BF),
            pltpu.SemaphoreType.DMA((8,)),
            pltpu.SemaphoreType.DMA((2,)),
            *pairs(8),
            *pairs(2, 2),
            *pairs(2),
        ]

    def block(self, way, f_rel, x_rel, c):
        p, half = self.p, TP // 2
        f, x = (p.f + f_rel) % 2, (p.x + x_rel) % 2
        return self.grad.at[f, 0, pl.ds(way * half, half), x, c]

    def cross(self, i):
        name = self.ORDER[i]
        src = self.block(*name, 1 - self.p.c)
        dst = self.stage if self.cores is None else self.cores
        return copy_to(src, dst.at[name], self.core_sems, (i,), self.to_c)

    def load(self, i):
        name = self.ORDER[i]
        return pltpu.make_async_copy(
            self.block(*name, self.p.c), self.sums.at[name], self.near.at[i]
        )

    def fetch(self, i):
        src = self.cores.at[self.ORDER[i]]
        return pltpu.make_async_copy(src, self.stage.at[i % 2], self.staged.at[i % 2])

    def first(self, way, block):
        src = self.sums.at[(0, block, 1) if way == 0 else (1, 1, block)]
        return copy_to(src, self.got.at[way, block], self.early, (way, block), self.to[way])

    def second(self, way):
        src = self.sums.at[(0, 1, 0) if way == 0 else (1, 0, 1)]
        return copy_to(src, self.got_late.at[way], self.late, (way,), self.to[1 - way])

    def add(self, name, *others):
        rows = self.sums.shape[-2]

        def turn(at):
            for k in range(TP // 2):
                total = self.sums[(*name, k, at)].astype(F32)
                for other in others:
                    total = total + other[k, at].astype(F32)
                self.sums[(*name, k, at)] = total.astype(BF)

        by_rows(rows, turn)

    def begin(self, blocks=range(8)):
        for i in blocks:
            self.cross(i).start()
            self.load(i).start()

    def issue(self, i):
        self.cross(i).wait_recv()
        self.fetch(i).start()

    def join(self, i):
        if self.cores is None:
            self.cross(i).wait_recv()
            self.load(i).wait()
            self.add(self.ORDER[i], self.stage.at[self.ORDER[i]])
        else:
            if i == 0:
                self.issue(0)
            if i + 1 < 8:
                self.issue(i + 1)
            self.fetch(i).wait()
            self.load(i).wait()
            self.add(self.ORDER[i], self.stage.at[i % 2])
        if i < 4:
            way = self.ORDER[i][0]
            self.first(way, self.ORDER[i][1 + way]).start()

    def middle(self):
        for way in range(2):
            self.first(way, 1).wait_recv()
            self.add((0, 1, 0) if way == 0 else (1, 0, 1), self.got.at[way, 1])
            self.second(way).start()

    def finish(self):
        for way in range(2):
            self.first(way, 0).wait_recv()
            self.second(way).wait_recv()
            self.add((way, 0, 0), self.got.at[way, 0], self.got_late.at[way])

    def result(self, z):
        return self.sums.at[z // (TP // 2), 0, 0, z % (TP // 2)]

    def close(self):
        for i in range(8):
            self.cross(i).wait_send()
        for way in range(2):
            self.second(way).wait_send()
            for block in range(2):
                self.first(way, block).wait_send()


def folds_of(p, grads, cores, scratch):
    return [Fold(p, g, c, scratch[12 * i : 12 * i + 12]) for i, (g, c) in enumerate(zip(grads, cores))]


GRAD_CHUNK = 640


class Outer:
    def __init__(self, grad, left, right, turned, buffers, sems):
        self.grad, self.left, self.right, self.turned = grad, left, right, turned
        self.buffers, self.sems = buffers, sems
        self.wide = buffers.shape[-1]
        self.across = grad.shape[-1] // self.wide
        self.count = 4 * self.across

    def place(self, i):
        return (lax.axis_index("fsdp") * 2 + 2 + i // self.across) % 4

    def store(self, i):
        k, half = self.place(i), TP // 2
        cols = pl.ds(pl.multiple_of(i % self.across * self.wide, 128), self.wide)
        dst = self.grad.at[k // 2, 0, pl.ds(k % 2 * half, half), :, :, :, cols]
        return pltpu.make_async_copy(self.buffers.at[i % 2], dst, self.sems.at[i % 2])

    def run(self, low, high):
        rows = self.turned.shape[0]

        def turn(i, _):
            @pl.when(i % self.across == 0)
            def _():
                cols = pl.ds(pl.multiple_of(self.place(i) * rows, 128), rows)
                self.turned[...] = jnp.transpose(self.left[:, cols])

            @pl.when(i >= low + 2)
            def _():
                self.store(i - 2).wait()

            cols = pl.ds(pl.multiple_of(i % self.across * self.wide, 128), self.wide)
            chunk = dot_plain(self.turned[...], self.right[:, cols]).astype(BF)
            self.buffers[i % 2] = chunk.reshape(self.buffers.shape[1:])
            self.store(i).start()
            return 0

        lax.fori_loop(low, high, turn, 0)

    def flush(self, done):
        for i in (done - 2, done - 1):
            self.store(i).wait()


def turn_kernel(count, *refs):
    parts, out_parts, x_one, cot, gain = refs[:5]
    factors, refs = refs[5 : 5 + (4 if count else 0)], refs[5 + (4 if count else 0) :]
    mixed_out, grad_x_one, grad_gain, mix_all = refs[:4]
    pieces, refs = refs[4 : 4 + TP], refs[4 + TP :]
    grads, cores, refs = refs[:count], refs[count : 2 * count], refs[2 * count :]
    own, local, gu0, gu1, gd0, gd1 = refs[:6]
    p = Place()
    line, late = LineSum(p, parts, refs[6:14]), LineSum(p, out_parts, refs[14:22])
    folds = folds_of(p, grads, cores, refs[22 : 22 + 12 * count])
    out = Gather(p, mix_all, (gu0, gu1), (gd0, gd1))
    halves, rows = parts.shape[1:3]
    line.clear()
    late.clear()
    greet_line(p, (*folds[0].to, folds[0].to_c) if folds else ())
    stays = []

    def stay(src, dst):
        copy = pltpu.make_async_copy(src, dst, local.at[len(stays)])
        copy.start()
        stays.append(copy)

    if folds:
        left, right, turned, buffers, chunk_sems, load_sems = refs[22 + 12 * count :]
        part = factors[1].shape[1]
        outers = [
            Outer(grads[m], left, right.at[:, pl.ds(m // 2 * part, part)], turned, buffers, chunk_sems)
            for m in range(3)
        ]
        down, gate, up = folds
        size = outers[0].count
        half = size // 2

    def load(m):
        cols = right.at[:, pl.ds(0, factors[2 * m + 1].shape[1])]
        copies = [
            pltpu.make_async_copy(factors[2 * m], left, load_sems.at[0]),
            pltpu.make_async_copy(factors[2 * m + 1], cols, load_sems.at[1]),
        ]
        for copy in copies:
            copy.start()
        for copy in copies:
            copy.wait()

    def outer(m, low, high):
        outers[m].run(low, high)
        outers[m].flush(high)
        folds[m].begin((0, 1, 3, 4) if high == half else (2, 5, 6, 7))

    def join(fold, *blocks):
        for i in blocks:
            fold.join(i)

    def line_step(k):
        for h in range(halves):
            line.step(k, h)

    line_step(3)
    for h in range(halves):
        late.step(TP - 1, h)
    if folds:
        load(0)
        outer(0, 0, half)
        outer(0, half, size)
        join(down, 0, 1)
        load(1)
        outer(1, 0, half)
        join(down, 2, 3)
    line_step(2)
    if folds:
        outer(1, half, size)
        join(down, 4, 5)
        outer(2, 0, half)
        join(gate, 0, 1)
        down.middle()
        join(gate, 2, 3)
    line_step(1)
    if folds:
        outer(2, half, size)
        join(gate, 4, 5)
    grad_gain[...] = jnp.zeros(grad_gain.shape, F32)
    for h in range(halves):
        line.arrive(h)

        def finish(at, h=h):
            grad, gains = norm_back(x_one[h, at], gain[...], line.total(h, at))
            grad = grad + cot[h, at].astype(F32)
            grad_x_one[h, at] = grad
            own[h, at] = grad.astype(BF)
            grad_gain[0:1] += jnp.sum(gains, axis=0, keepdims=True)

        by_rows(rows, finish)
        out.begin(h, own.at[h])
        stay(own.at[h], mix_all.at[p.z, h])
    if folds:
        join(up, 0, 1)
        gate.middle()
        join(up, 2, 3)
    for h in range(halves):
        out.step(1, h)
        late.step(2, h)
    if folds:
        join(down, 6, 7)
        join(up, 4, 5)
        join(gate, 6, 7)
    for h in range(halves):
        out.step(2, h)
        late.step(1, h)
    if folds:
        join(up, 6, 7)
        up.middle()
    for h in range(halves):
        out.step(3, h)
    for h in range(halves):
        late.arrive(h)

        def store(at, h=h):
            mixed_out[h, at] = (x_one[h, at] + late.total(h, at)).astype(BF)

        by_rows(rows, store)
    offset = 0
    for fold in folds:
        fold.finish()
        cols = fold.grad.shape[-1]
        for d in range(TP):
            stay(fold.result((p.z + d) % TP), pieces[d].at[:, pl.ds(offset, cols)])
        offset += cols
    for fold in folds:
        fold.close()
    line.close()
    late.close()
    out.close(halves)
    for copy in stays:
        copy.wait()


def turn(parts, out_parts, x_one, cot, gain, factors, p):
    shape, count, width = parts.shape, 3 if factors else 0, parts.shape[-1]
    rows = width // (p.fs * TP * 4)
    sizes = [factors[1].shape[1]] * count if factors else []
    grads = [jax.ShapeDtypeStruct((p.fs, 1, TP, 2, 2, rows, size), BF) for size in sizes]
    folded = [Fold.shapes(grad, True) for grad in grads]
    piece = jax.ShapeDtypeStruct((rows, sum(sizes)) if factors else (16, 128), BF)
    extra = []
    if factors:
        assert all(size % GRAD_CHUNK == 0 for size in sizes)
        tokens, deep = factors[0].shape[0], width // 4
        extra = [
            pltpu.VMEM((tokens, width), BF),
            pltpu.VMEM((tokens, 2 * sizes[0]), BF),
            pltpu.VMEM((deep, tokens), BF),
            pltpu.VMEM((2, TP // 2, 2, 2, rows, GRAD_CHUNK), BF),
            pltpu.SemaphoreType.DMA((2,)),
            pltpu.SemaphoreType.DMA((2,)),
        ]
    results = pl.pallas_call(
        functools.partial(turn_kernel, count),
        in_specs=[VMEM] * 5 + [ANY] * len(factors),
        out_specs=[VMEM, VMEM, VMEM, ANY] + [ANY] * (TP + 2 * count),
        out_shape=[
            jax.ShapeDtypeStruct(shape[1:], BF),
            jax.ShapeDtypeStruct(shape[1:], F32),
            jax.ShapeDtypeStruct((8, width), F32),
            jax.ShapeDtypeStruct(shape, BF),
            *[piece] * TP,
            *grads,
            *(cores for cores, _ in folded),
        ],
        scratch_shapes=[
            pltpu.VMEM(shape[1:], BF),
            pltpu.SemaphoreType.DMA((shape[1] + TP * count,)),
            *pairs(TP - 1, shape[1]),
            *pairs(TP - 1, shape[1]),
            *LineSum.scratch(shape),
            *LineSum.scratch(shape),
            *(item for _, scratch in folded for item in scratch),
            *extra,
        ],
        compiler_params=pltpu.CompilerParams(
            collective_id=2, has_side_effects=True, vmem_limit_bytes=GRANT
        ),
    )(parts, out_parts, x_one, cot, gain, *factors)
    return results[: 4 + TP]


def final_kernel(*refs):
    parts, x_zero, gain, grad_x_one, vectors, blocks = refs[:6]
    factors, refs = refs[6:10], refs[10:]
    grad_in, sums = refs[:2]
    outs, grads, refs = refs[2:6], (blocks, *refs[6:9]), refs[9:]
    acc, got, vs, vr, zs, zr, local, left, right, turned, buffers, chunk_sems, load_sems = refs[:13]
    p = Place()
    line = LineSum(p, parts, refs[13:21])
    folds = folds_of(p, grads, [None] * 4, refs[21:])
    halves, rows = parts.shape[1:3]
    line.clear()
    to_z = [device(p, z=(p.z + d) % TP) for d in range(TP)]
    (to_x, to_f), to_c = folds[0].to, folds[0].to_c
    greet(to_z[1:] + [to_x, to_f, to_c])
    partners = [to_c, to_x, to_f] + [
        device(p, z=p.z + bit * (1 - 2 * (p.z // bit % 2))) for bit in (1, 2)
    ]
    part = factors[1].shape[1]
    outers = [
        Outer(grads[m], left, right.at[:, pl.ds(m // 3 * part, part)], turned, buffers, chunk_sems)
        for m in range(1, 4)
    ]

    def load(m):
        cols = right.at[:, pl.ds(0, factors[2 * m + 1].shape[1])]
        copies = [
            pltpu.make_async_copy(factors[2 * m], left, load_sems.at[0]),
            pltpu.make_async_copy(factors[2 * m + 1], cols, load_sems.at[1]),
        ]
        for copy in copies:
            copy.start()
        for copy in copies:
            copy.wait()

    def outer(m):
        outers[m - 1].run(0, outers[m - 1].count)
        outers[m - 1].flush(outers[m - 1].count)
        folds[m].begin()

    def join(m, *blocks):
        for i in blocks:
            folds[m].join(i)

    def line_step(k):
        for h in range(halves):
            line.step(k, h)

    def vector(i):
        return copy_to(acc.at[i], got.at[i], (vs, vr), (i,), partners[i])

    def next_vector(i):
        vector(i).wait_recv()
        if i < 4:
            acc[i + 1] = acc[i] + got[i]
            vector(i + 1).start()
        else:
            sums[...] = acc[i] + got[i]

    started, stays = [], []

    def send_on(m):
        folds[m].finish()
        for d in (1, 3, 2):
            src = folds[m].result((p.z + d) % TP)
            copy = copy_to(src, outs[m].at[p.z], (zs, zr), (m, d - 1), to_z[d])
            copy.start()
            started.append(copy)
        stays.append(pltpu.make_async_copy(folds[m].result(p.z), outs[m].at[p.z], local.at[m]))
        stays[-1].start()

    acc[0] = vectors[...]
    vector(0).start()
    folds[0].begin()
    line_step(3)
    load(0)
    outer(1)
    load(1)
    join(0, 0, 1, 2, 3)
    outer(2)
    join(0, 4, 5)
    join(1, 0, 1)
    folds[0].middle()
    join(1, 2, 3)
    outer(3)
    line_step(2)
    next_vector(0)
    for m in (1, 2):
        join(m - 1, 6, 7)
        join(m, 4, 5)
        join(m + 1, 0, 1)
        folds[m].middle()
        join(m + 1, 2, 3)
        if m == 1:
            line_step(1)
        next_vector(m)
        send_on(m - 1)
    join(2, 6, 7)
    join(3, 4, 5)
    folds[3].middle()
    join(3, 6, 7)
    send_on(2)
    next_vector(3)
    for h in range(halves):
        line.arrive(h)

        def finish(at, h=h):
            grad, _ = norm_back(x_zero[h, at].astype(F32), gain[...], line.total(h, at))
            grad_in[h, at] = grad_x_one[h, at] + grad

        by_rows(rows, finish)
    next_vector(4)
    send_on(3)
    for m in range(4):
        for d in range(1, TP):
            ref = outs[m].at[(p.z - d) % TP]
            copy_to(ref, ref, (zs, zr), (m, d - 1), to_z[1]).wait_recv()
    for copy in started:
        copy.wait_send()
    for i in range(5):
        vector(i).wait_send()
    for fold in folds:
        fold.close()
    line.close()
    for copy in stays:
        copy.wait()


def final(parts, x_zero, gain, grad_x_one, vectors, blocks, factors, p):
    shape = parts.shape
    rows, part = blocks.shape[-2], factors[1].shape[1]
    tokens, width = factors[0].shape
    shaped = jax.ShapeDtypeStruct
    grads = [shaped((p.fs, 1, TP, 2, 2, rows, part), BF)] * 3
    widths = [blocks.shape[-1]] + [part] * 3
    folded = [Fold.shapes(grad, False)[1] for grad in (blocks, *grads)]
    results = pl.pallas_call(
        final_kernel,
        in_specs=[VMEM] * 5 + [ANY] * 5,
        out_specs=[VMEM, VMEM] + [ANY] * 7,
        out_shape=[
            shaped(shape[1:], F32),
            shaped(vectors.shape, F32),
            *(shaped((TP, rows, wide), BF) for wide in widths),
            *grads,
        ],
        scratch_shapes=[
            pltpu.VMEM((5,) + vectors.shape, F32),
            pltpu.VMEM((5,) + vectors.shape, F32),
            *pairs(5),
            *pairs(4, TP - 1),
            pltpu.SemaphoreType.DMA((4,)),
            pltpu.VMEM((tokens, width), BF),
            pltpu.VMEM((tokens, 2 * part), BF),
            pltpu.VMEM((width // 4, tokens), BF),
            pltpu.VMEM((2, TP // 2, 2, 2, rows, part), BF),
            pltpu.SemaphoreType.DMA((2,)),
            pltpu.SemaphoreType.DMA((2,)),
            *LineSum.scratch(shape),
            *(item for scratch in folded for item in scratch),
        ],
        compiler_params=pltpu.CompilerParams(
            collective_id=3, has_side_effects=True, vmem_limit_bytes=GRANT
        ),
    )(parts, x_zero, gain, grad_x_one, vectors, blocks, *factors)
    return results[0], results[1], results[2:6]


def chain_kernel(backward, sums, *refs):
    if backward:
        known, start, spans, send, recv = refs
    else:
        start, spans, send, recv = refs
    p = Place()
    peers = [device_q(p, (p.q + d) % NQ) for d in range(NQ)]
    greet(peers[1:])
    spans[p.q] = sums[...]
    copies = []
    for d in range(1, NQ):
        copies.append(copy_to(spans.at[p.q], spans.at[p.q], (send, recv), (d,), peers[d]))
        copies[-1].start()
    for d in range(1, NQ):
        ref = spans.at[(p.q - d) % NQ]
        copy_to(ref, ref, (send, recv), (d,), peers[d]).wait_recv()
    micro = sums.shape[1] // TP
    carry = jnp.zeros((micro, sums.shape[2]), F32)
    order = [(z, q) for z in range(TP) for q in range(NQ)]
    for z, q in reversed(order) if backward else order:
        here = slice(z * micro, (z + 1) * micro)

        @pl.when(p.q == q)
        def _(carry=carry, here=here):
            start[here] = carry

        decay = known[q, 0, here] if backward else spans[q, 0, here]
        carry = decay * carry + spans[q, 0 if backward else 1, here]
    for copy in copies:
        copy.wait_send()


def device_q(p, q):
    return device(p, x=q // 2, c=q % 2)


def chain(sums, known=None):
    backward = known is not None
    every = (NQ,) + sums.shape
    return pl.pallas_call(
        functools.partial(chain_kernel, backward),
        in_specs=[VMEM] * (2 if backward else 1),
        out_specs=[VMEM, VMEM],
        out_shape=[
            jax.ShapeDtypeStruct(sums.shape[1:], F32),
            jax.ShapeDtypeStruct(every, F32),
        ],
        scratch_shapes=pairs(NQ),
        cost_estimate=FREE,
        compiler_params=pltpu.CompilerParams(
            collective_id=5 if backward else 4, has_side_effects=True
        ),
    )(*((sums, known) if backward else (sums,)))


def unpack_kernel(own, one, two, three, *outs):
    p = Place()
    part = own.shape[1] // len(outs)
    for d, piece in enumerate((own, one, two, three)):
        cols = pl.ds(pl.multiple_of((p.z - d) % TP * part, 128), part)
        for i, out in enumerate(outs):
            out[:, cols] = piece[:, i * part : (i + 1) * part].astype(F32)


def unpack(pieces, count):
    rows, cols = pieces[0].shape
    return pl.pallas_call(
        unpack_kernel,
        in_specs=[VMEM] * TP,
        out_specs=[VMEM] * count,
        out_shape=[jax.ShapeDtypeStruct((rows, cols // count * TP), F32)] * count,
        compiler_params=pltpu.CompilerParams(vmem_limit_bytes=GRANT),
    )(*pieces)


def geglu(gate_vals, up_vals):
    return jax.nn.gelu(gate_vals) * up_vals


def all_spans(value, p):
    by_q = everywhere(value, shift_q, p.q, NQ)
    by_r = everywhere(by_q, shift_r, p.r, p.rests)
    return jnp.swapaxes(by_r, 1, 2).reshape((-1,) + value.shape[1:])


def own_spans(spans, p):
    split = spans.reshape((p.rests, TP, NQ) + spans.shape[1:])
    return lax.dynamic_index_in_dim(at(split, p.r), p.q, 1, keepdims=False)


def on_device(
    inputs,
    cotangent,
    proj_gelu,
    proj_lru,
    gate_blocks,
    proj_out,
    ffw_gate,
    ffw_up,
    ffw_down,
    norm_mix,
    norm_ffw,
    decay_param,
    conv_taps,
):
    p = Place()
    micro, span, width = inputs.shape[0], inputs.shape[2], inputs.shape[3]
    lru_width = proj_gelu.shape[1]
    tap_count = conv_taps.shape[1]
    block_width = gate_blocks.shape[1] // 2
    heads = lru_width // block_width
    ffw_part = ffw_gate.shape[1] // TP
    rows = proj_gelu.shape[0]
    held = -(-heads // TP)
    first = [k * heads // TP for k in range(TP)]
    owned = [range(first[k], first[k + 1] if k + 1 < TP else heads) for k in range(TP)]
    part = held * block_width

    out_t, down_t = proj_out.T, ffw_down.T
    small = jnp.concatenate([norm_mix[None], norm_ffw[None], decay_param[None], conv_taps.T])
    small = jnp.pad(small, ((0, 128 - small.shape[0]), (0, 0))).T
    x_rows, cot = inputs[:, 0], cotangent[:, 0]
    one = 1 if p.rests == 1 else 0
    cot_halves = cot.reshape(2, -1, width)
    edge = lax.ppermute(
        x_rows[:, span - (tap_count - 1) :],
        "seq",
        [(i, i + 1) for i in range(lax.axis_size("seq") - 1)],
    )
    edge = jnp.pad(edge, ((0, 0), (HALO - (tap_count - 1), 0), (0, 0)))
    x_wide = jnp.concatenate([x_rows.reshape(-1, width), edge.reshape(-1, width)])
    if p.rests == 1:
        weights = (proj_gelu, proj_lru, out_t, gate_blocks, small, ffw_gate, ffw_up, down_t)
        mix_pieces, ffw_pieces = pack(weights, block_width)
        mix_w, ffw_w, piece_1, x_all, cot_first = intake(
            mix_pieces, ffw_pieces[0], ffw_pieces[1], x_wide, cot_halves[0], p
        )
        piece_2, piece_3, x_all = lax.optimization_barrier((*ffw_pieces[2:], x_all))
        piece_3, piece_2 = shift_z(piece_3, 3), shift_z(piece_2, 2)
        passed = (piece_1, swap_x(piece_1), swap_f(piece_1), piece_2, piece_3)
    else:
        mix_pieces, ffw_pieces = [], []
        for k in range(TP):
            cols = slice(first[k] * block_width, first[k] * block_width + part)
            pieces = [proj_gelu[:, cols], proj_lru[:, cols], out_t[:, cols], gate_blocks, small]
            mix_pieces.append(jnp.concatenate(pieces, axis=1))
            cols = slice(k * ffw_part, (k + 1) * ffw_part)
            pieces = [ffw_gate[:, cols], ffw_up[:, cols], down_t[:, cols]]
            ffw_pieces.append(jnp.concatenate(pieces, axis=1))
        mix_w = weights_in(jnp.stack(mix_pieces), p)
        whole_ffw = weights_in(jnp.stack(ffw_pieces), p)
        x_all, passed, ffw_w = gather_z(x_wide, p), None, None
        cot_first = gather_z(cot_halves[:1], p)
    dims = (span, micro, heads, held, block_width, tap_count)
    small_w, rows_w, mixed, pre, conv, gate, state, prod, sums = recur(
        x_all.reshape(-1, width), mix_w, dims
    )
    mix_gain, ffw_gain = small_w[0:1], small_w[1:2]
    start = sum(jnp.where(p.z == k, first[k] * block_width, 0) for k in range(TP))

    ends = (TP, micro, part)
    if p.rests == 1:
        state_in, every_sum = chain(sums)
    else:
        sums = all_spans(jnp.stack([sums[0].reshape(ends), sums[1].reshape(ends)], axis=1), p)
        carry, carries = jnp.zeros_like(sums[0, 0]), []
        for k in range(sums.shape[0]):
            carries.append(carry)
            carry = sums[k, 0] * carry + sums[k, 1]
        state_in = own_spans(jnp.stack(carries), p).reshape(-1, part)
    mix_bf, out_parts = recur_mix(pre, rows_w, state, prod, state_in, mix_w, dims)
    blocked = (TP, micro * CUTS, span // CUTS, width)
    x_own, cot_own = x_rows.reshape(blocked[1:]), cot.reshape(blocked[1:])
    out_parts = out_parts.reshape(blocked)
    x_one, ffw_bf, cot_all, _, *fed = middle(
        out_parts, x_own, ffw_gain, cot_halves[1], cot_first, passed, ffw_w
    )
    cot_all = cot_all.reshape(-1, width)

    ffw_bf = ffw_bf.reshape(-1, width)
    if p.rests == 1:
        hidden_bf, grad_gate_up, ffw_parts, grad_in_parts = fed
    else:
        gate_up_w, down_w = whole_ffw[:, : 2 * ffw_part], whole_ffw[:, 2 * ffw_part :]
        gate_up = dot_plain(ffw_bf, gate_up_w)
        gate_vals, up_vals = gate_up[:, :ffw_part], gate_up[:, ffw_part:]
        hidden_bf = geglu(gate_vals, up_vals).astype(BF)
        grad_hidden = dot_plain(cot_all, down_w)
        _, pull_back = jax.vjp(geglu, gate_vals, up_vals)
        grad_gate_up = jnp.concatenate(pull_back(grad_hidden), axis=1).astype(BF)
        ffw_parts = dot_right_t(hidden_bf, down_w).astype(BF)
        grad_in_parts = dot_right_t(grad_gate_up, gate_up_w).astype(BF)
    ffw_parts, grad_in_parts = ffw_parts.reshape(blocked), grad_in_parts.reshape(blocked)
    factors = [cot_all, hidden_bf, ffw_bf, grad_gate_up]
    mixed_out, grad_x_one, gain_rows, grad_mix, *ffw_pieces = turn(
        grad_in_parts, ffw_parts, x_one, cot_own, ffw_gain, factors * one, p
    )
    if p.rests == 1:
        for d in (1, 3, 2):
            ffw_pieces[d] = shift_z(ffw_pieces[d], d)
    grad_mix = grad_mix.reshape(-1, width)

    grad_gelu_bf, local_back, prod_back, back_sums = recur_back(
        grad_mix, pre, rows_w, state, prod, state_in, gate, mix_w, dims
    )
    if p.rests == 1:
        carried, _ = chain(back_sums[None], every_sum)
    else:
        back_sums = all_spans(back_sums.reshape(ends), p)
        carry, carries = jnp.zeros_like(sums[0, 0]), []
        for k in range(sums.shape[0] - 1, -1, -1):
            carries.append(carry)
            carry = sums[k, 0] * carry + back_sums[k]
        carried = own_spans(jnp.stack(carries[::-1]), p).reshape(-1, part)
    block_mats = lax.dynamic_slice(mix_w, (start, 3 * part), (part, 2 * block_width))
    grad_blocks, grad_lru, spill, row_grads = recur_grad(
        local_back, prod_back, carried, state, prod, state_in, gate, conv, pre, rows_w,
        block_mats.reshape(held, block_width, 2 * block_width), dims,
    )
    spill = spill.reshape(TP, micro, HALO, part)
    from_next = shift_q(spill, -1)
    last = jnp.zeros_like(spill[:1])
    if p.rests > 1:
        last = move(spill[:1], lambda r, z, q: (r - 1, z, NQ - 1) if q == 0 and r > 0 else None)
    from_next = jnp.where(
        p.q == NQ - 1, jnp.concatenate([from_next[1:], last], axis=0), from_next
    )
    grad_pair, grad_mixed_parts, mix_gain_rows = recur_in(
        grad_gelu_bf, grad_lru, from_next.reshape(-1, part), rows_w, small_w, mixed, mix_w, dims
    )
    grad_mixed_parts = grad_mixed_parts.reshape(blocked)

    blocks_all = lax.dynamic_update_slice_in_dim(
        jnp.zeros((lru_width, 2 * block_width), BF),
        (grad_blocks * rows_w[6][:, None]).astype(BF),
        start,
        0,
    )
    mix_factors = [grad_mix, mix_bf, mixed, grad_pair]
    vectors = lax.dynamic_update_slice_in_dim(
        jnp.zeros((1 + tap_count, lru_width), F32), row_grads[: 1 + tap_count], start, 1
    )
    vectors = jnp.concatenate([mix_gain_rows[:1], gain_rows[:1], vectors], axis=0)
    vectors = jnp.pad(vectors, ((0, -vectors.shape[0] % 8), (0, 0)))
    if p.rests == 1:
        grad_inputs, vectors, mix_grads = final(
            grad_mixed_parts, x_own, mix_gain, grad_x_one, vectors,
            by_owner(blocks_all, p), mix_factors, p,
        )
    else:
        products = [dot_left_t(*mix_factors[:2]), dot_left_t(*mix_factors[2:])]
        products = [blocks_all, products[0], products[1][:, :part], products[1][:, part:]]
        mix_grads = [grads_out(grad.astype(BF), p) for grad in products]
        grad_mixed_own = scatter_z(grad_mixed_parts, p)
        grad_inputs = grad_x_one + norm_back(x_own.astype(F32), mix_gain, grad_mixed_own)[0]
        for exchange in (swap_core, swap_x, swap_f):
            vectors = vectors + exchange(vectors)
        for bit in (1, 2):
            vectors = vectors + move(vectors, lambda r, z, q, bit=bit: (r, z ^ bit, q))
        total = vectors
        for d in range(1, p.rests):
            total = total + shift_r(vectors, d)
        vectors = total
    vectors = lax.dynamic_slice_in_dim(vectors, p.index * rows, rows, 1)

    def mix_columns(grad):
        picked = [grad[k][:, : len(owned[k]) * block_width] for k in range(TP)]
        return jnp.concatenate(picked, axis=1).astype(F32)

    if p.rests == 1:
        share_down, share_gate, share_up = unpack(ffw_pieces, 3)
    else:
        ffw_grads = [dot_left_t(*factors[:2]), dot_left_t(*factors[2:])]
        ffw_grads = [grads_out(grad.astype(BF), p) for grad in ffw_grads]
        beside = lambda v: jnp.swapaxes(v, 0, 1).reshape(rows, -1).astype(F32)
        share_gate = beside(ffw_grads[1][:, :, :ffw_part])
        share_up = beside(ffw_grads[1][:, :, ffw_part:])
        share_down = beside(ffw_grads[0])
    shape = (micro, 1, span, width)
    return (
        mixed_out.reshape(shape),
        grad_inputs.reshape(shape),
        mix_columns(mix_grads[2]),
        mix_columns(mix_grads[3]),
        jnp.sum(mix_grads[0].astype(F32), axis=0),
        mix_columns(mix_grads[1]).T,
        share_gate,
        share_up,
        share_down.T,
        vectors[0],
        vectors[1],
        vectors[2],
        vectors[3 : 3 + tap_count].T,
    )


def solution(mesh):
    in_specs = (
        P(None, "fsdp", "seq", None),
        P(None, "fsdp", "seq", None),
        P(("fsdp", "seq"), None),
        P(("fsdp", "seq"), None),
        P(("fsdp", "seq"), None),
        P(None, ("fsdp", "seq")),
        P(("fsdp", "seq"), None),
        P(("fsdp", "seq"), None),
        P(None, ("fsdp", "seq")),
        P(("fsdp", "seq")),
        P(("fsdp", "seq")),
        P(("fsdp", "seq")),
        P(("fsdp", "seq"), None),
    )
    out_specs = (
        P(None, "fsdp", "seq", None),
        P(None, "fsdp", "seq", None),
        P(("fsdp", "seq"), None),
        P(("fsdp", "seq"), None),
        P(("fsdp", "seq"), None),
        P(None, ("fsdp", "seq")),
        P(("fsdp", "seq"), None),
        P(("fsdp", "seq"), None),
        P(None, ("fsdp", "seq")),
        P(("fsdp", "seq")),
        P(("fsdp", "seq")),
        P(("fsdp", "seq")),
        P(("fsdp", "seq"), None),
    )
    return jax.shard_map(
        on_device, mesh=mesh, in_specs=in_specs, out_specs=out_specs, check_vma=False
    )
```

```python
import functools

import jax
import jax.numpy as jnp
from jax import lax
from jax.experimental import pallas as pl
from jax.experimental.pallas import tpu as pltpu
from jax.sharding import PartitionSpec as P

EPS = 1e-06
GUARD = 0.001
RATE = 8.0
TP = 4
NQ = 4
HALO = 8
BF = jnp.bfloat16
F32 = jnp.float32
MESH = pl.DeviceIdType.MESH
ANY = pl.BlockSpec(memory_space=pl.ANY)
VMEM = pl.BlockSpec(memory_space=pltpu.VMEM)
GRANT = 60 * 1024 * 1024
CUTS = 2
FREE = pl.CostEstimate(flops=0, bytes_accessed=0, transcendentals=0)


def move(value, step):
    pairs = []
    for here in range(lax.axis_size("seq")):
        there = step(here // (TP * NQ), here // NQ % TP, here % NQ)
        if there is not None:
            pairs.append((here, (there[0] * TP + there[1]) * NQ + there[2]))
    return lax.ppermute(value, "seq", pairs)


def swap_core(value):
    return move(value, lambda r, z, q: (r, z, q ^ 1))


def swap_x(value):
    return move(value, lambda r, z, q: (r, z, q ^ 2))


def swap_f(value):
    return lax.ppermute(value, "fsdp", [(0, 1), (1, 0)])


def shift_z(value, d):
    return move(value, lambda r, z, q: (r, (z + d) % TP, q))


def shift_q(value, d):
    return move(value, lambda r, z, q: (r, z, (q + d) % NQ))


def shift_r(value, d):
    count = lax.axis_size("seq") // (TP * NQ)
    return move(value, lambda r, z, q: ((r + d) % count, z, q))


def hop(value, d, low, high):
    return move(value, lambda r, z, q: (r, z + d, q) if low <= z <= high else None)


class Place:
    def __init__(self):
        seq = lax.axis_index("seq")
        self.f = lax.axis_index("fsdp")
        self.r, self.z, self.q = seq // (TP * NQ), seq // NQ % TP, seq % NQ
        self.x, self.c = self.q // 2, self.q % 2
        self.rests = lax.axis_size("seq") // (TP * NQ)
        self.fs = lax.axis_size("fsdp")
        self.index = self.f * lax.axis_size("seq") + seq


def at(value, index):
    return lax.dynamic_index_in_dim(value, index, 0, keepdims=False)


def put(base, value, *index):
    starts = [jnp.int32(0) if i is None else jnp.int32(i) for i in index]
    starts += [jnp.int32(0)] * (base.ndim - len(index))
    for dim, i in enumerate(index):
        if i is not None:
            value = jnp.expand_dims(value, dim)
    return lax.dynamic_update_slice(base, value, starts)


def everywhere(value, shifter, mine, count):
    out = put(jnp.zeros((count,) + value.shape, value.dtype), value, mine)
    for d in range(1, count):
        out = put(out, shifter(value, d), (mine - d) % count)
    return out


def gather_z(value, p):
    ups, downs = [], []
    up = down = value
    for k in range(1, TP):
        up = hop(up, 1, k - 1, TP - 2)
        down = hop(down, -1, 1, TP - k)
        ups.append(up)
        downs.append(down)
    out = put(jnp.zeros((TP,) + value.shape, value.dtype), value, p.z)
    for k in range(1, TP):
        out = put(out, downs[k - 1] + ups[TP - 1 - k], (p.z + k) % TP)
    return out


def scatter_z(parts, p):
    right = left = None
    for k in range(TP - 1, 0, -1):
        send = at(parts, (p.z + k) % TP)
        if right is not None:
            send = (send.astype(F32) + right.astype(F32)).astype(BF)
        right = hop(send, 1, 0, TP - 1 - k)
        send = at(parts, (p.z - k) % TP)
        if left is not None:
            send = (send.astype(F32) + left.astype(F32)).astype(BF)
        left = hop(send, -1, k, TP - 1)
    return at(parts, p.z).astype(F32) + right.astype(F32) + left.astype(F32)


def weights_in(pieces, p):
    rows, cols = pieces.shape[1:]
    mine = put(jnp.zeros(pieces.shape, BF), at(pieces, p.z), p.z)
    for d in range(1, TP):
        mine = put(mine, shift_z(at(pieces, (p.z + d) % TP), d), (p.z - d) % TP)
    mine = everywhere(mine, shift_r, p.r, p.rests)
    half = TP // 2
    by_x, by_f = swap_x(mine), swap_f(mine)
    corner = (swap_f(by_x[:, :half]), swap_x(by_f[:, half:]))
    whole = jnp.zeros((p.fs, p.rests, TP, 2, 2, rows, cols), BF)
    for block, f, x, z in (
        (mine, p.f, p.x, 0),
        (by_x, p.f, 1 - p.x, 0),
        (by_f, 1 - p.f, p.x, 0),
        (corner[0], 1 - p.f, 1 - p.x, 0),
        (corner[1], 1 - p.f, 1 - p.x, half),
    ):
        other = swap_core(block)
        for part, c in ((block, p.c), (other, 1 - p.c)):
            part = part[None, :, :, None, None]
            whole = lax.dynamic_update_slice(
                whole, part, [jnp.int32(i) for i in (f, 0, z, x, c, 0, 0)]
            )
    return whole.reshape(-1, cols)


def by_owner(grad, p):
    return grad.reshape(p.fs, p.rests, TP, 2, 2, -1, grad.shape[1])


def to_owner_z(total, p):
    out = put(jnp.zeros(total.shape, BF), at(total, p.z), p.z)
    for d in (1, 3, 2):
        out = put(out, shift_z(at(total, (p.z + d) % TP), d), (p.z - d) % TP)
    return out


def grads_out(grad, p):
    plus = lambda a, b: (a.astype(F32) + b.astype(F32)).astype(BF)
    pick = lambda v, dim, i: lax.dynamic_index_in_dim(v, i, dim, keepdims=False)
    total = by_owner(grad, p)
    total = plus(pick(total, 4, p.c), swap_core(pick(total, 4, 1 - p.c)))
    total = plus(pick(total, 3, p.x), swap_x(pick(total, 3, 1 - p.x)))
    total = plus(at(total, p.f), swap_f(at(total, 1 - p.f)))
    mine = at(total, p.r)
    for d in range(1, p.rests):
        mine = plus(mine, shift_r(at(total, (p.r + d) % p.rests), d))
    return to_owner_z(mine, p)


def dot_left_t(left_mat, right_mat):
    return lax.dot_general(
        left_mat, right_mat, (((0,), (0,)), ((), ())), preferred_element_type=F32
    )


def dot_plain(left_mat, right_mat):
    return jnp.dot(left_mat, right_mat, preferred_element_type=F32)


def dot_right_t(left_mat, right_mat):
    return lax.dot_general(
        left_mat, right_mat, (((1,), (1,)), ((), ())), preferred_element_type=F32
    )


def normed(values, gain_vec):
    return values * lax.rsqrt(jnp.mean(values * values, axis=-1, keepdims=True) + EPS) * gain_vec


def gelu_pair(v):
    scale = 0.7978845608028654
    inner = jnp.tanh(scale * (v + 0.044715 * v * v * v))
    slope = 0.5 * v * (1.0 - inner * inner) * scale * (1.0 + 0.134145 * v * v)
    return 0.5 * v * (1.0 + inner), 0.5 * (1.0 + inner) + slope


def span_scan(decay, drive, backward):
    count = decay.shape[0]
    row = lax.broadcasted_iota(jnp.int32, decay.shape, 0)
    step = 1
    while step < count:
        inside = row < count - step if backward else row >= step
        turn = count - step if backward else step
        drive = drive + jnp.where(inside, decay * pltpu.roll(drive, turn, 0), 0.0)
        decay = decay * jnp.where(inside, pltpu.roll(decay, turn, 0), 1.0)
        step *= 2
    return decay, drive


def gate_values(gate, soft):
    half = gate.shape[1] // 2
    rec_gate = jax.nn.sigmoid(gate[:, :half])
    in_gate = jax.nn.sigmoid(gate[:, half:])
    log_decay = -RATE * rec_gate * soft
    square = jnp.exp(2.0 * log_decay)
    return rec_gate, in_gate, jnp.exp(log_decay), square, jnp.sqrt(1.0 - square + GUARD)


def main_rows(i, span, micro):
    return pl.ds(i // micro * micro * (span + HALO) + i % micro * span, span)


def with_halo(pre, i, span, micro):
    start = i // micro * micro * (span + HALO) + micro * span + i % micro * HALO
    both = [pre[pl.ds(start, HALO)], pre[main_rows(i, span, micro)]]
    return jnp.concatenate(both, axis=0)


def recur_head(span, micro, pre, rows, block, conv, gate, state, prod, sums):
    count = conv.shape[0] // span
    soft, taps = rows[0:1], [rows[k + 2 : k + 3] for k in range(4)]
    for i in range(count):
        vals = with_halo(pre, i, span, micro).astype(BF).astype(F32)
        total = taps[0] * vals
        for k in range(1, 4):
            total = total + taps[k] * pltpu.roll(vals, k, 0)
        conv[pl.ds(i * span, span)] = total[HALO:].astype(BF)
    gate[...] = dot_plain(conv[...], block[...])
    for i in range(count):
        here = pl.ds(i * span, span)
        _, in_gate, decay, _, root = gate_values(gate[here], soft)
        decay, local = span_scan(decay, root * in_gate * conv[here].astype(F32), False)
        state[here] = local
        prod[here] = decay
        sums[0, i : i + 1] = decay[span - 1 :]
        sums[1, i : i + 1] = local[span - 1 :]


def columns(ref, h, width):
    return ref.at[:, pl.ds(pl.multiple_of(h * width, 128), width)]


def by_heads(count, body):
    def turn(h, _):
        body(h)
        return 0

    lax.fori_loop(0, count, turn, 0)


def recur_kernel(
    dims, x_all, gelu_w, lru_w, mix_w, small, rows, mixed, pre_gelu, pre_lru, conv, gate, state,
    prod, sums, small_w, block_w, mixed_all, sems,
):
    span, micro, heads, held, bw, taps = dims
    part, h = held * bw, pl.program_id(0)

    @pl.when(h == 0)
    def _():
        p = Place()
        start = pl.multiple_of(p.z * heads // TP * bw, 128)
        pieces = (
            (mix_w.at[:, pl.ds(3 * part + 2 * bw, 128)], small_w),
            (mix_w.at[pl.ds(start, part), pl.ds(3 * part, 2 * bw)], block_w),
        )
        loads = [pltpu.make_async_copy(src, dst, sems.at[i]) for i, (src, dst) in enumerate(pieces)]
        for load in loads:
            load.start()
        loads[0].wait()
        row = lax.broadcasted_iota(jnp.int32, (8, 128), 0)
        lane = lax.broadcasted_iota(jnp.int32, (8, 128), 1)
        small[...] = dot_right_t(jnp.where(row == lane, 1.0, 0.0).astype(BF), small_w[...])
        own = small[:, pl.ds(start, part)]
        decay = -own[2:3]
        feature = lax.broadcasted_iota(jnp.int32, (1, part), 1)
        count = ((p.z + 1) * heads // TP - p.z * heads // TP) * bw
        rows[0:1] = jnp.maximum(decay, 0.0) + jnp.log1p(jnp.exp(-jnp.abs(decay)))
        rows[1:2] = jax.nn.sigmoid(decay)
        rows[2 : 2 + taps] = own[3 : 3 + taps]
        rows[6:7] = jnp.where(feature < count, 1.0, 0.0)
        rows[7:8] = jnp.zeros((1, part), F32)
        gain, wide, step = small[0:1], micro * (span + HALO), 16

        def norm(z, _):
            for k in range(0, wide, step):
                vals = x_all[pl.ds(pl.multiple_of(z * wide + k, step), step)].astype(F32)
                vals = normed(vals, gain).astype(BF)
                mixed_all[pl.ds(pl.multiple_of(z * wide + k, step), step)] = vals
                if k < micro * span:
                    mixed[pl.ds(pl.multiple_of(z * micro * span + k, step), step)] = vals
            return 0

        lax.fori_loop(0, TP, norm, 0)
        loads[1].wait()

    pre_gelu[...] = dot_plain(mixed_all[...], gelu_w[...])
    pre_lru[...] = dot_plain(mixed_all[...], lru_w[...])
    block = block_w.at[pl.ds(pl.multiple_of(h * bw, 128), bw)]
    recur_head(span, micro, pre_lru, columns(rows, h, bw), block, conv, gate, state, prod, sums)


def recur(x_all, mix_w, dims):
    span, micro, _, held, bw, _ = dims
    part, width, wide = held * bw, x_all.shape[1], x_all.shape[0]
    tokens = wide // (span + HALO) * span
    whole = lambda shape: pl.BlockSpec(shape, lambda h: (0, 0))
    column = lambda rows, cols: pl.BlockSpec((rows, cols), lambda h: (0, h))
    shapes = [((8, width), F32), ((8, part), F32), ((tokens, width), BF)]
    shapes += [((wide, part), F32), ((wide, part), F32), ((tokens, part), BF)]
    shapes += [((tokens, 2 * part), F32), ((tokens, part), F32), ((tokens, part), F32)]
    shapes += [((2, tokens // span, part), F32)]
    return pl.pallas_call(
        functools.partial(recur_kernel, dims),
        grid=(held,),
        in_specs=[
            whole(x_all.shape),
            column(width, bw),
            pl.BlockSpec((width, bw), lambda h: (0, held + h)),
            ANY,
        ],
        out_specs=[
            whole((8, width)),
            whole((8, part)),
            whole((tokens, width)),
            column(wide, bw),
            column(wide, bw),
            column(tokens, bw),
            column(tokens, 2 * bw),
            column(tokens, bw),
            column(tokens, bw),
            pl.BlockSpec((2, tokens // span, bw), lambda h: (0, 0, h)),
        ],
        out_shape=[jax.ShapeDtypeStruct(*shape) for shape in shapes],
        scratch_shapes=[
            pltpu.VMEM((width, 128), BF),
            pltpu.VMEM((part, 2 * bw), BF),
            pltpu.VMEM(x_all.shape, BF),
            pltpu.SemaphoreType.DMA((2,)),
        ],
        cost_estimate=FREE,
        compiler_params=pltpu.CompilerParams(vmem_limit_bytes=GRANT),
    )(x_all, mix_w, mix_w, mix_w)


def recur_mix_kernel(dims, pre, rows, state, prod, start, mix_w, mix, parts, out_w, sem):
    span, micro, _, held, bw, _ = dims
    part = held * bw
    load = pltpu.make_async_copy(mix_w.at[:, pl.ds(2 * part, part)], out_w, sem.at[0])
    load.start()

    def one_head(h):
        pre_h, state_h, prod_h = columns(pre, h, bw), columns(state, h, bw), columns(prod, h, bw)
        rows_h, start_h, mix_h = columns(rows, h, bw), columns(start, h, bw), columns(mix, h, bw)
        for i in range(state.shape[0] // span):
            here = pl.ds(i * span, span)
            act, _ = gelu_pair(pre_h[main_rows(i, span, micro)])
            states = state_h[here] + prod_h[here] * start_h[i : i + 1]
            mix_h[here] = (states * act * rows_h[6:7]).astype(BF)

    by_heads(held, one_head)
    load.wait()

    def project(j):
        cols = pl.ds(pl.multiple_of(j * 256, 256), 256)
        parts[:, cols] = dot_right_t(mix[...], out_w[cols]).astype(BF)

    by_heads(out_w.shape[0] // 256, project)


def recur_mix(pre, rows, state, prod, start, mix_w, dims):
    tokens, part = state.shape
    width = mix_w.shape[0]
    return pl.pallas_call(
        functools.partial(recur_mix_kernel, dims),
        in_specs=[VMEM] * 5 + [ANY],
        out_specs=[VMEM, VMEM],
        out_shape=[
            jax.ShapeDtypeStruct((tokens, part), BF),
            jax.ShapeDtypeStruct((tokens, width), BF),
        ],
        scratch_shapes=[pltpu.VMEM((width, part), BF), pltpu.SemaphoreType.DMA((1,))],
        cost_estimate=FREE,
        compiler_params=pltpu.CompilerParams(vmem_limit_bytes=GRANT),
    )(pre, rows, state, prod, start, mix_w)


def recur_back_kernel(
    dims, grad, pre, rows, state, prod, start, gate, out_w, gelu, local, prods, sums, back
):
    span, micro = dims[:2]
    soft = rows[0:1]
    back[...] = dot_plain(grad[...], out_w[...])
    for i in range(back.shape[0] // span):
        here = pl.ds(i * span, span)
        act, slope = gelu_pair(pre[main_rows(i, span, micro)])
        states = state[here] + prod[here] * start[i : i + 1]
        gelu[here] = (back[here] * states * slope * rows[6:7]).astype(BF)
        _, _, decay, _, _ = gate_values(gate[here], soft)
        row = lax.broadcasted_iota(jnp.int32, decay.shape, 0)
        later = jnp.where(row < span - 1, pltpu.roll(decay, span - 1, 0), 1.0)
        later, adjoint = span_scan(later, back[here] * act, True)
        local[here] = adjoint
        prods[here] = later
        sums[i : i + 1] = decay[:1] * adjoint[:1]


def recur_back(grad, pre, rows, state, prod, start, gate, mix_w, dims):
    tokens, part = state.shape
    held, bw = dims[3:5]
    column = lambda h: (0, h)
    whole = pl.BlockSpec((tokens, bw), column)
    ends = pl.BlockSpec((start.shape[0], bw), column)
    shapes = [((tokens, part), BF), ((tokens, part), F32), ((tokens, part), F32), (start.shape, F32)]
    return pl.pallas_call(
        functools.partial(recur_back_kernel, dims),
        grid=(held,),
        in_specs=[
            pl.BlockSpec(grad.shape, lambda h: (0, 0)),
            pl.BlockSpec((pre.shape[0], bw), column),
            pl.BlockSpec((8, bw), column),
            whole,
            whole,
            ends,
            pl.BlockSpec((tokens, 2 * bw), column),
            pl.BlockSpec((mix_w.shape[0], bw), lambda h: (0, 2 * held + h)),
        ],
        out_specs=[whole, whole, whole, ends],
        out_shape=[jax.ShapeDtypeStruct(*shape) for shape in shapes],
        scratch_shapes=[pltpu.VMEM((tokens, bw), F32)],
        cost_estimate=FREE,
        compiler_params=pltpu.CompilerParams(vmem_limit_bytes=GRANT),
    )(grad, pre, rows, state, prod, start, gate, mix_w)


def recur_grad_kernel(
    span, micro, local, prods, carried, state, prod, start, gate, conv, pre, rows, block,
    blocks_out, lru_out, spill_out, rows_out, gate_grad, conv_grad,
):
    count = local.shape[0] // span
    soft, sig, own = rows[0:1], rows[1:2], rows[6:7]
    taps = [rows[k + 2 : k + 3] for k in range(4)]
    width = local.shape[1]
    add_up = lambda v: jnp.sum(v, axis=0, keepdims=True)
    decay_sum = jnp.zeros((1, width), F32)
    for i in range(count):
        here = pl.ds(i * span, span)
        adjoint = local[here] + prods[here] * carried[i : i + 1]
        states = state[here] + prod[here] * start[i : i + 1]
        row = lax.broadcasted_iota(jnp.int32, states.shape, 0)
        earlier = jnp.where(row >= 1, pltpu.roll(states, 1, 0), start[i : i + 1])
        rec_gate, in_gate, decay, square, root = gate_values(gate[here], soft)
        conv_vals = conv[here].astype(F32)
        drive = adjoint * conv_vals
        grad_log = adjoint * earlier * decay - drive * in_gate * square / root
        decay_sum = decay_sum + add_up(grad_log * rec_gate)
        gate_grad[here, :width] = (-RATE * soft * grad_log * rec_gate * (1.0 - rec_gate)).astype(BF)
        gate_grad[here, width:] = (drive * root * in_gate * (1.0 - in_gate)).astype(BF)
        conv_grad[here] = adjoint * root * in_gate
    blocks_out[...] = lax.dot_general(
        conv[...], gate_grad[...], (((0,), (0,)), ((), ())), preferred_element_type=F32
    )
    conv_grad[...] += dot_right_t(gate_grad[...], block[0])
    tap_sums = [jnp.zeros((1, width), F32) for _ in range(4)]
    for i in range(count):
        here = pl.ds(i * span, span)
        grad = conv_grad[here]
        vals = with_halo(pre, i, span, micro).astype(BF).astype(F32)
        wide = jnp.concatenate([jnp.zeros((HALO, width), F32), grad], axis=0)
        total = taps[0] * wide
        tap_sums[0] = tap_sums[0] + add_up(grad * vals[HALO:])
        for k in range(1, 4):
            total = total + taps[k] * pltpu.roll(wide, span + HALO - k, 0)
            tap_sums[k] = tap_sums[k] + add_up(grad * pltpu.roll(vals, k, 0)[HALO:])
        lru_out[here] = total[HALO:]
        spill_out[pl.ds(i * HALO, HALO)] = total[:HALO]
    rows_out[...] = jnp.zeros(rows_out.shape, F32)
    rows_out[0:1] = decay_sum * sig * own * RATE
    for k in range(4):
        rows_out[k + 1 : k + 2] = tap_sums[k] * own


def recur_grad(local, prods, carried, state, prod, start, gate, conv, pre, rows, blocks, dims):
    tokens, part = state.shape
    span, micro, _, held, bw, _ = dims
    column = lambda h: (0, h)
    whole = pl.BlockSpec((tokens, bw), column)
    ends = pl.BlockSpec((start.shape[0], bw), column)
    return pl.pallas_call(
        functools.partial(recur_grad_kernel, span, micro),
        grid=(held,),
        in_specs=[
            whole,
            whole,
            ends,
            whole,
            whole,
            ends,
            pl.BlockSpec((tokens, 2 * bw), column),
            whole,
            pl.BlockSpec((pre.shape[0], bw), column),
            pl.BlockSpec((8, bw), column),
            pl.BlockSpec((1, bw, 2 * bw), lambda h: (h, 0, 0)),
        ],
        out_specs=[
            pl.BlockSpec((bw, 2 * bw), lambda h: (h, 0)),
            whole,
            pl.BlockSpec((start.shape[0] * HALO, bw), column),
            pl.BlockSpec((8, bw), column),
        ],
        out_shape=[
            jax.ShapeDtypeStruct((part, 2 * bw), F32),
            jax.ShapeDtypeStruct((tokens, part), F32),
            jax.ShapeDtypeStruct((start.shape[0] * HALO, part), F32),
            jax.ShapeDtypeStruct((8, part), F32),
        ],
        scratch_shapes=[pltpu.VMEM((tokens, 2 * bw), BF), pltpu.VMEM((tokens, bw), F32)],
        cost_estimate=FREE,
        compiler_params=pltpu.CompilerParams(vmem_limit_bytes=GRANT),
    )(local, prods, carried, state, prod, start, gate, conv, pre, rows, blocks)


def recur_in_kernel(dims, gelu, lru, spill, rows, small, mixed, mix_w, pair, parts, gains):
    span, _, _, held, bw, _ = dims
    part = held * bw

    @pl.when(pl.program_id(0) == 0)
    def _():
        pair[:, :part] = gelu[...]

        def one_head(h):
            lru_h, spill_h, own = columns(lru, h, bw), columns(spill, h, bw), columns(rows, h, bw)[6:7]
            cols = pl.ds(pl.multiple_of((held + h) * bw, 128), bw)
            for i in range(lru.shape[0] // span):
                vals = lru_h[pl.ds(i * span, span)]
                late = vals[span - HALO :] + spill_h[pl.ds(i * HALO, HALO)]
                vals = jnp.concatenate([vals[: span - HALO], late], axis=0) * own
                pair[pl.ds(i * span, span), cols] = vals.astype(BF)

        by_heads(held, one_head)

    grad = dot_right_t(pair[...], mix_w[...])
    parts[...] = grad.astype(BF)
    gain = jnp.sum(grad * mixed[...].astype(F32), axis=0, keepdims=True)
    gains[0:1] = gain / small[0:1]


def recur_in(gelu, lru, spill, rows, small, mixed, mix_w, dims):
    tokens, part = gelu.shape
    width, chunk = mix_w.shape[0], 256
    whole = lambda v: pl.BlockSpec(v.shape, lambda j: (0, 0))
    column = lambda j: (0, j)
    return pl.pallas_call(
        functools.partial(recur_in_kernel, dims),
        grid=(width // chunk,),
        in_specs=[
            whole(gelu),
            whole(lru),
            whole(spill),
            whole(rows),
            pl.BlockSpec((8, chunk), column),
            pl.BlockSpec((tokens, chunk), column),
            pl.BlockSpec((chunk, 2 * part), lambda j: (j, 0)),
        ],
        out_specs=[
            pl.BlockSpec((tokens, 2 * part), lambda j: (0, 0)),
            pl.BlockSpec((tokens, chunk), column),
            pl.BlockSpec((8, chunk), column),
        ],
        out_shape=[
            jax.ShapeDtypeStruct((tokens, 2 * part), BF),
            jax.ShapeDtypeStruct((tokens, width), BF),
            jax.ShapeDtypeStruct((8, width), F32),
        ],
        cost_estimate=FREE,
        compiler_params=pltpu.CompilerParams(vmem_limit_bytes=GRANT),
    )(gelu, lru, spill, rows, small, mixed, mix_w)


def device(p, f=None, z=None, x=None, c=None):
    f, z = p.f if f is None else f, p.z if z is None else z
    x, c = p.x if x is None else x, p.c if c is None else c
    return (f, ((p.r * TP + z) * 2 + x) * 2 + c)


def copy_to(src, dst, sems, index, dev):
    return pltpu.make_async_remote_copy(
        src_ref=src,
        dst_ref=dst,
        send_sem=sems[0].at[index],
        recv_sem=sems[1].at[index],
        device_id=dev,
        device_id_type=MESH,
    )


def pairs(*shape):
    return [pltpu.SemaphoreType.DMA(shape), pltpu.SemaphoreType.DMA(shape)]


def greet(devices):
    barrier = pltpu.get_barrier_semaphore()
    for dev in devices:
        pl.semaphore_signal(barrier, inc=1, device_id=dev, device_id_type=MESH)
    pl.semaphore_wait(barrier, len(devices))


def by_rows(count, body, step=16):
    def turn(i, _):
        body(pl.ds(pl.multiple_of(i * step, step), step))
        return 0

    assert count % step == 0
    lax.fori_loop(0, count // step, turn, 0)


class Gather:
    def __init__(self, p, out, ups, downs):
        self.p, self.out, self.ups, self.downs = p, out, ups, downs
        self.up = device(p, z=jnp.minimum(p.z + 1, TP - 1))
        self.down = device(p, z=jnp.maximum(p.z - 1, 0))

    def begin(self, h, src):
        z = self.p.z

        @pl.when(z < TP - 1)
        def _():
            copy_to(src, self.out.at[z, h], self.ups, (0, h), self.up).start()

        @pl.when(z > 0)
        def _():
            copy_to(src, self.out.at[z, h], self.downs, (0, h), self.down).start()

    def step(self, k, h):
        z, out = self.p.z, self.out

        @pl.when(z >= k)
        def _():
            block = out.at[z - k, h]
            copy_to(block, block, self.ups, (k - 1, h), self.up).wait_recv()
            if k < TP - 1:

                @pl.when(z < TP - 1)
                def _():
                    copy_to(block, block, self.ups, (k, h), self.up).start()

        @pl.when(z <= TP - 1 - k)
        def _():
            block = out.at[z + k, h]
            copy_to(block, block, self.downs, (k - 1, h), self.down).wait_recv()
            if k < TP - 1:

                @pl.when(z > 0)
                def _():
                    copy_to(block, block, self.downs, (k, h), self.down).start()

    def close(self, halves):
        z, block = self.p.z, self.out.at[0, 0]
        for h in range(halves) if isinstance(halves, int) else halves:
            for k in range(TP - 1):

                @pl.when((z >= k) & (z < TP - 1))
                def _():
                    copy_to(block, block, self.ups, (k, h), self.up).wait_send()

                @pl.when((z <= TP - 1 - k) & (z > 0))
                def _():
                    copy_to(block, block, self.downs, (k, h), self.down).wait_send()


class LineSum:
    def __init__(self, p, parts, scratch):
        self.p, self.parts = p, parts
        self.got_up, self.got_down, self.out_up, self.out_down = scratch[:4]
        self.ups, self.downs = scratch[4:6], scratch[6:8]
        self.halves, self.rows = parts.shape[1:3]
        self.up = device(p, z=jnp.minimum(p.z + 1, TP - 1))
        self.down = device(p, z=jnp.maximum(p.z - 1, 0))

    @staticmethod
    def scratch(parts):
        block = parts[1:]
        return [
            pltpu.VMEM((TP - 1,) + block, BF),
            pltpu.VMEM((TP - 1,) + block, BF),
            pltpu.VMEM((TP - 2,) + block, BF),
            pltpu.VMEM((TP - 2,) + block, BF),
            *pairs(TP - 1, parts[1]),
            *pairs(TP - 1, parts[1]),
        ]

    def clear(self):
        z = self.p.z

        @pl.when(z == 0)
        def _():
            for h in range(self.halves):
                by_rows(self.rows, lambda at: self.fill(self.got_up, h, at))

        @pl.when(z == TP - 1)
        def _():
            for h in range(self.halves):
                by_rows(self.rows, lambda at: self.fill(self.got_down, h, at))

    def fill(self, ref, h, at):
        ref[0, h, at] = jnp.zeros((at.size, ref.shape[-1]), BF)

    def one_way(self, k, h, place, block, got, out, sems, dev):
        @pl.when(place == 0)
        def _():
            copy_to(self.parts.at[block, h], got.at[k - 1, h], sems, (k - 1, h), dev).start()

        if k < TP - 1:

            @pl.when((place >= 1) & (place + k <= TP - 1))
            def _():
                copy_to(got.at[k, h], got.at[k, h], sems, (k, h), dev).wait_recv()

                def add(at):
                    total = self.parts[block, h, at].astype(F32) + got[k, h, at].astype(F32)
                    out[k - 1, h, at] = total.astype(BF)

                by_rows(self.rows, add)
                copy_to(out.at[k - 1, h], got.at[k - 1, h], sems, (k - 1, h), dev).start()

    def step(self, k, h):
        z = self.p.z
        block = jnp.minimum(z + k, TP - 1)
        self.one_way(k, h, z, block, self.got_up, self.out_up, self.ups, self.up)
        block = jnp.maximum(z - k, 0)
        self.one_way(k, h, TP - 1 - z, block, self.got_down, self.out_down, self.downs, self.down)

    def arrive(self, h):
        z = self.p.z

        @pl.when(z >= 1)
        def _():
            got = self.got_up.at[0, h]
            copy_to(got, got, self.ups, (0, h), self.up).wait_recv()

        @pl.when(z <= TP - 2)
        def _():
            got = self.got_down.at[0, h]
            copy_to(got, got, self.downs, (0, h), self.down).wait_recv()

    def total(self, h, at):
        total = self.parts[self.p.z, h, at].astype(F32) + self.got_up[0, h, at].astype(F32)
        return total + self.got_down[0, h, at].astype(F32)

    def close(self):
        z, got = self.p.z, self.got_up.at[0, 0]
        for h in range(self.halves):
            for k in range(1, TP):

                @pl.when(z + k <= TP - 1)
                def _():
                    copy_to(got, got, self.ups, (k - 1, h), self.up).wait_send()

                @pl.when(z - k >= 0)
                def _():
                    copy_to(got, got, self.downs, (k - 1, h), self.down).wait_send()


def greet_line(p, others=()):
    barrier = pltpu.get_barrier_semaphore()
    for dev in others:
        pl.semaphore_signal(barrier, inc=1, device_id=dev, device_id_type=MESH)

    @pl.when(p.z > 0)
    def _():
        pl.semaphore_signal(barrier, inc=1, device_id=device(p, z=p.z - 1), device_id_type=MESH)

    @pl.when(p.z < TP - 1)
    def _():
        pl.semaphore_signal(barrier, inc=1, device_id=device(p, z=p.z + 1), device_id_type=MESH)

    inner = (p.z > 0) & (p.z < TP - 1)

    @pl.when(inner)
    def _():
        pl.semaphore_wait(barrier, len(others) + 2)

    @pl.when(jnp.logical_not(inner))
    def _():
        pl.semaphore_wait(barrier, len(others) + 1)


class Spread:
    KINDS = ((0, 0), (0, 1), (1, 0), (1, 1))

    def __init__(self, p, whole, sems):
        self.p, self.whole, self.started = p, whole, []
        self.xs, self.fs, self.gs, self.cs = sems[0:2], sems[2:4], sems[4:6], sems[6:8]
        self.to_x, self.to_f = device(p, x=1 - p.x), device(p, f=1 - p.f)
        self.to_c = device(p, c=1 - p.c)

    @staticmethod
    def scratch():
        return [*pairs(TP), *pairs(TP), *pairs(TP), *pairs(4, TP)]

    def slot(self, kind, d, other_core=False):
        p, (f, x) = self.p, self.KINDS[kind]
        c = 1 - p.c if other_core else p.c
        return self.whole.at[(p.f + f) % 2, 0, (p.z - d) % TP, (p.x + x) % 2, c]

    def send(self, src, dst, sems, index, dev):
        copy = copy_to(src, dst, sems, index, dev)
        copy.start()
        self.started.append(copy)

    def wait(self, ref, sems, index):
        copy_to(ref, ref, sems, index, self.to_x).wait_recv()

    def spread(self, d, src=None):
        dst = self.slot(0, d)
        src = dst if src is None else src
        self.send(src, dst, self.xs, (d,), self.to_x)
        self.send(src, dst, self.fs, (d,), self.to_f)
        self.send(src, dst, self.cs, (0, d), self.to_c)

    def given(self, d, own, by_x, by_f):
        self.send(own, self.slot(0, d), self.cs, (0, d), self.to_c)
        self.send(by_x, self.slot(1, d), self.cs, (1, d), self.to_c)
        self.send(by_f, self.slot(2, d), self.cs, (2, d), self.to_c)
        if d % 2 == 0:
            self.send(by_x, self.slot(1, d), self.gs, (d,), self.to_f)
        else:
            self.send(by_f, self.slot(2, d), self.gs, (d,), self.to_x)

    def sides(self, d):
        ref = self.slot(1, d)
        self.wait(ref, self.xs, (d,))
        if d % 2 == 0:
            self.send(ref, ref, self.gs, (d,), self.to_f)
        self.send(ref, ref, self.cs, (1, d), self.to_c)
        ref = self.slot(2, d)
        self.wait(ref, self.fs, (d,))
        if d % 2 == 1:
            self.send(ref, ref, self.gs, (d,), self.to_x)
        self.send(ref, ref, self.cs, (2, d), self.to_c)

    def corner(self, d):
        ref = self.slot(3, d)
        self.wait(ref, self.gs, (d,))
        self.send(ref, ref, self.cs, (3, d), self.to_c)

    def close(self, pieces):
        for kind in range(4):
            for d in pieces:
                self.wait(self.slot(kind, d, True), self.cs, (kind, d))
        for copy in self.started:
            copy.wait_send()


def pack_kernel(bw, gelu, lru, out_t, blocks, small, gate, up, down_t, mix, *ffw):
    p = Place()
    heads = gelu.shape[1] // bw
    part, ffw_part = -(-heads // TP) * bw, gate.shape[1] // TP
    for d in range(TP):
        z = (p.z + d) % TP
        cols = pl.ds(pl.multiple_of(z * heads // TP * bw, 128), part)
        sources = [gelu[:, cols], lru[:, cols], out_t[:, cols], blocks[...], small[...]]
        offset = 0
        for source in sources:
            mix[d, :, offset : offset + source.shape[1]] = source
            offset += source.shape[1]
        cols = pl.ds(pl.multiple_of(z * ffw_part, 128), ffw_part)
        for i, source in enumerate((gate, up, down_t)):
            ffw[d][:, i * ffw_part : (i + 1) * ffw_part] = source[:, cols]


def pack(weights, bw):
    rows, lru_width = weights[0].shape
    part = -(-lru_width // bw // TP) * bw
    mix_cols = 3 * part + weights[3].shape[1] + weights[4].shape[1]
    piece = jax.ShapeDtypeStruct((rows, 3 * weights[5].shape[1] // TP), BF)
    mix, *ffw = pl.pallas_call(
        functools.partial(pack_kernel, bw),
        in_specs=[VMEM] * 8,
        out_specs=[VMEM] * (1 + TP),
        out_shape=[jax.ShapeDtypeStruct((TP, rows, mix_cols), BF), *[piece] * TP],
        compiler_params=pltpu.CompilerParams(vmem_limit_bytes=GRANT),
    )(*weights)
    return mix, ffw


def intake_kernel(
    mix_p, ffw_0, ffw_1, x_p, cot_p, mix_w, ffw_w, piece_1, x_all, cot_all,
    zs, zr, us, ur, vs, vr, cus, cur, cvs, cvr, local, *sems
):
    p = Place()
    mix, ffw = Spread(p, mix_w, sems[:8]), Spread(p, ffw_w, sems[8:])
    to_z = [device(p, z=(p.z + d) % TP) for d in range(TP)]
    greet(to_z[1:] + [mix.to_x, mix.to_f, mix.to_c])
    started = []

    def along_z(i, src, dst, d):
        copy = copy_to(src, dst, (zs, zr), (i,), to_z[d])
        copy.start()
        started.append(copy)

    def from_z(i, ref):
        copy_to(ref, ref, (zs, zr), (i,), to_z[1]).wait_recv()

    for d in (1, 3, 2):
        along_z(d, mix_p.at[d], mix.slot(0, 0), d)
    mix.spread(0, mix_p.at[0])
    ffw.spread(0, ffw_0)
    stays = [
        pltpu.make_async_copy(mix_p.at[0], mix.slot(0, 0), local.at[0]),
        pltpu.make_async_copy(ffw_0, ffw.slot(0, 0), local.at[1]),
        pltpu.make_async_copy(x_p, x_all.at[p.z, 0], local.at[2]),
        pltpu.make_async_copy(cot_p, cot_all.at[p.z, 0], local.at[3]),
    ]
    for copy in stays:
        copy.start()
    line = Gather(p, x_all, (us, ur), (vs, vr))
    cot = Gather(p, cot_all, (cus, cur), (cvs, cvr))
    for d in (1, 3):
        from_z(d, mix.slot(0, d))
        mix.spread(d)
    line.begin(0, x_p)
    cot.begin(0, cot_p)
    from_z(2, mix.slot(0, 2))
    mix.spread(2)
    along_z(0, ffw_1, piece_1, 1)
    mix.sides(0)
    ffw.sides(0)
    mix.corner(0)
    line.step(1, 0)
    cot.step(1, 0)
    for d in (1, 3):
        mix.sides(d)
    ffw.corner(0)
    line.step(2, 0)
    cot.step(2, 0)
    for d in (1, 3):
        mix.corner(d)
    mix.sides(2)
    line.step(3, 0)
    cot.step(3, 0)
    mix.corner(2)
    from_z(0, piece_1)
    mix.close(range(TP))
    ffw.close((0,))
    for copy in started:
        copy.wait_send()
    line.close(1)
    cot.close(1)
    for copy in stays:
        copy.wait()


def intake(mix_p, ffw_0, ffw_1, x_p, cot_p, p):
    whole = lambda v: jax.ShapeDtypeStruct((p.fs, 1, TP, 2, 2) + v.shape[-2:], BF)
    mix_w, ffw_w, piece_1, x_all, cot_all = pl.pallas_call(
        intake_kernel,
        in_specs=[ANY] * 5,
        out_specs=[ANY] * 5,
        out_shape=[
            whole(mix_p),
            whole(ffw_0),
            jax.ShapeDtypeStruct(ffw_1.shape, BF),
            jax.ShapeDtypeStruct((TP, 1) + x_p.shape, BF),
            jax.ShapeDtypeStruct((TP, 1) + cot_p.shape, BF),
        ],
        scratch_shapes=[
            *pairs(TP),
            *pairs(TP - 1, 1),
            *pairs(TP - 1, 1),
            *pairs(TP - 1, 1),
            *pairs(TP - 1, 1),
            pltpu.SemaphoreType.DMA((4,)),
            *Spread.scratch(),
            *Spread.scratch(),
        ],
        compiler_params=pltpu.CompilerParams(collective_id=0, has_side_effects=True),
    )(mix_p, ffw_0, ffw_1, x_p, cot_p)
    return mix_w.reshape(-1, mix_p.shape[-1]), ffw_w, piece_1, x_all[:, 0], cot_all


class Stream:
    def __init__(self, pick, count, buffers, sems):
        self.pick, self.count, self.buffers, self.sems = pick, count, buffers, sems

    def load(self, i):
        slot = i % 2
        return pltpu.make_async_copy(self.pick(i), self.buffers.at[slot], self.sems.at[slot])

    def start(self):
        self.load(0).start()

    def run(self, low, high, body):
        def turn(i, _):
            @pl.when(i + 1 < self.count)
            def _():
                self.load(i + 1).start()

            self.load(i).wait()
            body(i, self.buffers.at[i % 2])
            return 0

        lax.fori_loop(low, high, turn, 0)


def flat(block):
    return block.reshape(-1, block.shape[-1])


FFW_CHUNK = 256


def ffw_streams(ffw_w, part, buffers):
    chunks, rest = part // FFW_CHUNK, part % FFW_CHUNK
    col = lambda base, i: pl.ds(pl.multiple_of(base + i * FFW_CHUNK, 128), FFW_CHUNK)
    pick = lambda base: lambda i: ffw_w.at[:, 0, :, :, :, :, col(base, i)]
    half = TP // 2
    rows = lambda cols: lambda i: ffw_w.at[i // 2, 0, pl.ds(i % 2 * half, half), :, :, :, cols]
    gate = Stream(pick(0), chunks, buffers[0], buffers[1])
    up = Stream(pick(part), chunks, buffers[2], buffers[3])
    down = Stream(pick(2 * part), chunks, buffers[0], buffers[1])
    down_rows = Stream(rows(pl.ds(2 * part, part)), 4, buffers[4], buffers[5])
    both_rows = Stream(rows(pl.ds(0, 2 * part)), 4, buffers[6], buffers[7])
    return gate, up, down, down_rows, both_rows


class Feed:
    def __init__(self, x, cot, ffw_w, outs, vals, scratch):
        self.x, self.cot, self.vals = x, cot, vals
        self.hidden, self.grad_pair, self.out_parts, self.in_parts = outs
        self.part = part = self.hidden.shape[1]
        self.chunks, self.rest = part // FFW_CHUNK, part % FFW_CHUNK
        streams = ffw_streams(ffw_w, part, scratch[:8])
        self.gate, self.up, self.down, self.down_rows, self.both_rows = streams
        self.tails, tail_sems = scratch[8:10]
        self.last = last = self.chunks * FFW_CHUNK
        self.loads = [
            pltpu.make_async_copy(
                ffw_w.at[:, 0, :, :, :, :, pl.ds(k * part + last, self.rest)],
                self.tails.at[k],
                tail_sems.at[k],
            )
            for k in range(3)
        ]

    def begin(self):
        self.gate.start()
        self.up.start()
        for load in self.loads:
            load.start()
        self.down_rows.start()
        self.both_rows.start()

    def cols(self, i, base):
        return pl.ds(pl.multiple_of(base + i * FFW_CHUNK, 128), FFW_CHUNK)

    def forward_cols(self, cols, other, gate_w, up_w):
        gate_vals = dot_plain(self.x[...], gate_w)
        up_vals = dot_plain(self.x[...], up_w)
        self.vals[:, cols] = gate_vals
        self.vals[:, other] = up_vals
        self.hidden[:, cols] = (gelu_pair(gate_vals)[0] * up_vals).astype(BF)

    def forward(self, low, high):
        def turn(i, _):
            for stream in (self.gate, self.up):

                @pl.when(i + 1 < self.chunks)
                def _(stream=stream):
                    stream.load(i + 1).start()

                stream.load(i).wait()
            weights = [flat(stream.buffers[i % 2]) for stream in (self.gate, self.up)]
            self.forward_cols(self.cols(i, 0), self.cols(i, self.part), *weights)
            return 0

        lax.fori_loop(low, high, turn, 0)

    def forward_end(self):
        self.down.start()
        for load in self.loads:
            load.wait()
        cols = pl.ds(self.last, self.rest), pl.ds(self.part + self.last, self.rest)
        self.forward_cols(*cols, flat(self.tails[0]), flat(self.tails[1]))

    def by_weight_rows(self, stream, source, out, low=0, high=4):
        def body(i, buffer):
            weights = flat(buffer[...])
            count = weights.shape[0]
            cols = pl.ds(pl.multiple_of(i * count, 128), count)
            out[:, cols] = dot_right_t(source[...], weights).astype(BF)

        stream.run(low, high, body)

    def forward_out(self):
        self.by_weight_rows(self.down_rows, self.hidden, self.out_parts)

    def backward_cols(self, cols, other, weights):
        grad = dot_plain(self.cot[...], weights)
        act, slope = gelu_pair(self.vals[:, cols])
        self.grad_pair[:, cols] = (grad * self.vals[:, other] * slope).astype(BF)
        self.grad_pair[:, other] = (grad * act).astype(BF)

    def backward(self, low, high):
        def body(i, buffer):
            self.backward_cols(self.cols(i, 0), self.cols(i, self.part), flat(buffer[...]))

        self.down.run(low, high, body)

    def backward_end(self):
        cols = pl.ds(self.last, self.rest), pl.ds(self.part + self.last, self.rest)
        self.backward_cols(*cols, flat(self.tails[2]))

    def backward_in(self, low, high):
        self.by_weight_rows(self.both_rows, self.grad_pair, self.in_parts, low, high)


def ffw_scratch(ffw_w, part):
    f, _, z, x, c, rows, _ = ffw_w.shape
    column = lambda width: pltpu.VMEM((2, f, z, x, c, rows, width), BF)
    wide = lambda width: pltpu.VMEM((2, z // 2, x, c, rows, width), BF)
    pair = pltpu.SemaphoreType.DMA((2,))
    return [
        column(FFW_CHUNK), pair, column(FFW_CHUNK), pair, wide(part), pair, wide(2 * part), pair,
        pltpu.VMEM((3, f, z, x, c, rows, part % FFW_CHUNK), BF),
        pltpu.SemaphoreType.DMA((3,)),
    ]


def middle_kernel(with_ffw, *refs):
    parts, x_zero, gain, cot_p, cot_first, piece_1, by_x, by_f, piece_2, piece_3, _ = refs[:11]
    x_one_out, ffw_out, cot_out, ffw_w, *refs = refs[11:]
    if with_ffw:
        hidden_out, pair_out, parts_out, in_out, *refs = refs
    x_one, ffw_all, cot_all, own, local, gu0, gu1, gd0, gd1, cu0, cu1, cd0, cd1 = refs[:13]
    p = Place()
    line = LineSum(p, parts, refs[13:21])
    out = Gather(p, ffw_all, (gu0, gu1), (gd0, gd1))
    cot = Gather(p, cot_all, (cu0, cu1), (cd0, cd1))
    halves, rows = parts.shape[1:3]
    line.clear()
    stays = []

    def stay(src, dst):
        copy = pltpu.make_async_copy(src, dst, local.at[len(stays)])
        copy.start()
        stays.append(copy)

    if with_ffw:
        ffw = Spread(p, ffw_w, refs[21:29])
        outs, vals, buffers = refs[29:33], refs[33], refs[34:44]
        bounce_sems = refs[44]
        greet_line(p, (ffw.to_x, ffw.to_f, ffw.to_c))
    else:
        greet_line(p)
    side = lambda name, *args: getattr(ffw, name)(*args) if with_ffw else None
    for h in range(halves):
        line.step(TP - 1, h)
    stay(cot_first, cot_all.at[:, pl.ds(0, 1)])
    side("given", 1, piece_1, by_x, by_f)
    side("spread", 3, piece_3)
    side("spread", 2, piece_2)
    if with_ffw:
        part = vals.shape[1] // 2
        moves = [(piece_1, 0, 1), (by_x, 1, 1), (by_f, 2, 1), (piece_3, 0, 3), (piece_2, 0, 2)]
        steps = [(src, ffw.slot(kind, d), k) for src, kind, d in moves for k in range(2)]

        def bounce(i, out):
            src, dst, k = steps[i]
            cols = pl.ds(0, 2 * part) if k == 0 else pl.ds(2 * part, part)
            space = buffers[6 - 2 * k].at[i // 2 % 2, 0, 0, 0]
            if out:
                return pltpu.make_async_copy(space, dst.at[:, cols], bounce_sems.at[i % 4])
            return pltpu.make_async_copy(src.at[:, cols], space, bounce_sems.at[4])

        for i in range(len(steps)):
            if i >= 4:
                bounce(i - 4, True).wait()
            bounce(i, False).start()
            bounce(i, False).wait()
            bounce(i, True).start()
        for i in range(len(steps) - 4, len(steps)):
            bounce(i, True).wait()
    for k in range(TP - 2, 0, -1):
        for h in range(halves):
            line.step(k, h)
    for h in range(halves):
        line.arrive(h)

        def finish(at, h=h):
            value = x_zero[h, at].astype(F32) + line.total(h, at)
            x_one[h, at] = value
            own[h, at] = normed(value, gain[...]).astype(BF)

        by_rows(rows, finish)
        out.begin(h, own.at[h])
        stay(own.at[h], ffw_all.at[p.z, h])
    for h in range(halves):
        out.step(1, h)
    for d in (3, 2):
        side("sides", d)
    for h in range(halves):
        out.step(2, h)
    cot.begin(1, cot_p)
    stay(cot_p, cot_all.at[p.z, 1])
    side("corner", 1)
    for d in (3, 2):
        side("corner", d)
    for h in range(halves):
        out.step(3, h)
    cot.step(1, 1)
    side("close", (1, 2, 3))
    if not with_ffw:
        cot.step(2, 1)
        cot.step(3, 1)
    for copy in stays:
        copy.wait()
    done = len(stays)
    stay(x_one, x_one_out)
    stay(ffw_all, ffw_out)
    if not with_ffw:
        stay(cot_all, cot_out)
    else:
        tokens = lambda ref: ref.reshape(TP * halves * rows, parts.shape[3])
        hidden, pair, out_parts, in_parts = outs
        flat_outs = (hidden, pair, tokens(out_parts), in_parts)
        feed = Feed(tokens(ffw_all), tokens(cot_all), ffw_w, flat_outs, vals, buffers)
        feed.begin()
        feed.forward(0, 2)
        cot.step(2, 1)
        feed.forward(2, 6)
        cot.step(3, 1)
        stay(cot_all, cot_out)
        feed.forward(6, feed.chunks)
        feed.forward_end()
        feed.forward_out()
        stay(hidden, hidden_out)
        stay(out_parts, parts_out)
        feed.backward(0, feed.chunks)
        feed.backward_end()
        stay(pair, pair_out)
        feed.backward_in(0, 4)
        stay(in_parts, in_out)
    line.close()
    out.close(halves)
    cot.close((1,))
    for copy in stays[done:]:
        copy.wait()


def middle(parts, x_zero, gain, cot_p, cot_first, pieces, ffw_w):
    shape = parts.shape
    with_ffw = ffw_w is not None
    line = (TP, 2) + cot_p.shape
    outs, extra = [], []
    if with_ffw:
        tokens, part = shape[0] * shape[1] * shape[2], ffw_w.shape[-1] // 3
        assert part // FFW_CHUNK >= 6 and part % FFW_CHUNK
        outs = [(tokens, part), (tokens, 2 * part), shape, (tokens, shape[3])]
        extra = [
            *Spread.scratch(),
            *(pltpu.VMEM(kept, BF) for kept in outs),
            pltpu.VMEM((tokens, 2 * part), F32),
            *ffw_scratch(ffw_w, part),
            pltpu.SemaphoreType.DMA((5,)),
        ]
    else:
        ffw_w = jnp.zeros((16, 128), BF)
        pieces = [ffw_w] * 5
    return pl.pallas_call(
        functools.partial(middle_kernel, with_ffw),
        in_specs=[VMEM] * 3 + [ANY] * 8,
        out_specs=[ANY] * (4 + len(outs)),
        out_shape=[
            jax.ShapeDtypeStruct(shape[1:], F32),
            jax.ShapeDtypeStruct(shape, BF),
            jax.ShapeDtypeStruct(line, BF),
            jax.ShapeDtypeStruct(ffw_w.shape, BF),
            *(jax.ShapeDtypeStruct(out, BF) for out in outs),
        ],
        input_output_aliases={10: 3},
        scratch_shapes=[
            pltpu.VMEM(shape[1:], F32),
            pltpu.VMEM(shape, BF),
            pltpu.VMEM(line, BF),
            pltpu.VMEM(shape[1:], BF),
            pltpu.SemaphoreType.DMA((shape[1] + 10,)),
            *pairs(TP - 1, shape[1]),
            *pairs(TP - 1, shape[1]),
            *pairs(TP - 1, 2),
            *pairs(TP - 1, 2),
            *LineSum.scratch(shape),
            *extra,
        ],
        compiler_params=pltpu.CompilerParams(
            collective_id=1, has_side_effects=True, vmem_limit_bytes=GRANT
        ),
    )(parts, x_zero, gain, cot_p, cot_first, *pieces, ffw_w)


def norm_back(values, gain, grad):
    inv = lax.rsqrt(jnp.mean(values * values, axis=-1, keepdims=True) + EPS)
    unit = values * inv
    through = grad * gain
    inner = jnp.mean(through * unit, axis=-1, keepdims=True)
    return inv * (through - unit * inner), grad * unit


class Fold:
    ORDER = ((0, 1, 1), (1, 1, 1), (0, 0, 1), (1, 1, 0), (0, 1, 0), (1, 0, 1), (0, 0, 0), (1, 0, 0))

    def __init__(self, p, grad, cores, scratch):
        self.p, self.grad, self.cores = p, grad, cores
        self.sums, self.stage, self.got, self.got_late = scratch[:4]
        self.near, self.staged = scratch[4:6]
        self.core_sems, self.early, self.late = scratch[6:8], scratch[8:10], scratch[10:12]
        self.to = (device(p, x=1 - p.x), device(p, f=1 - p.f))
        self.to_c = device(p, c=1 - p.c)

    @staticmethod
    def shapes(grad, staged):
        block = (TP // 2,) + grad.shape[-2:]
        waiting = (2,) if staged else (2, 2, 2)
        return jax.ShapeDtypeStruct((2, 2, 2) + block, BF), [
            pltpu.VMEM((2, 2, 2) + block, BF),
            pltpu.VMEM(waiting + block, BF),
            pltpu.VMEM((2, 2) + block, BF),
            pltpu.VMEM((2,) + block, BF),
            pltpu.SemaphoreType.DMA((8,)),
            pltpu.SemaphoreType.DMA((2,)),
            *pairs(8),
            *pairs(2, 2),
            *pairs(2),
        ]

    def block(self, way, f_rel, x_rel, c):
        p, half = self.p, TP // 2
        f, x = (p.f + f_rel) % 2, (p.x + x_rel) % 2
        return self.grad.at[f, 0, pl.ds(way * half, half), x, c]

    def cross(self, i):
        name = self.ORDER[i]
        src = self.block(*name, 1 - self.p.c)
        dst = self.stage if self.cores is None else self.cores
        return copy_to(src, dst.at[name], self.core_sems, (i,), self.to_c)

    def load(self, i):
        name = self.ORDER[i]
        return pltpu.make_async_copy(
            self.block(*name, self.p.c), self.sums.at[name], self.near.at[i]
        )

    def fetch(self, i):
        src = self.cores.at[self.ORDER[i]]
        return pltpu.make_async_copy(src, self.stage.at[i % 2], self.staged.at[i % 2])

    def first(self, way, block):
        src = self.sums.at[(0, block, 1) if way == 0 else (1, 1, block)]
        return copy_to(src, self.got.at[way, block], self.early, (way, block), self.to[way])

    def second(self, way):
        src = self.sums.at[(0, 1, 0) if way == 0 else (1, 0, 1)]
        return copy_to(src, self.got_late.at[way], self.late, (way,), self.to[1 - way])

    def add(self, name, *others):
        rows = self.sums.shape[-2]

        def turn(at):
            for k in range(TP // 2):
                total = self.sums[(*name, k, at)].astype(F32)
                for other in others:
                    total = total + other[k, at].astype(F32)
                self.sums[(*name, k, at)] = total.astype(BF)

        by_rows(rows, turn)

    def begin(self, blocks=range(8)):
        for i in blocks:
            self.cross(i).start()
            self.load(i).start()

    def issue(self, i):
        self.cross(i).wait_recv()
        self.fetch(i).start()

    def join(self, i):
        if self.cores is None:
            self.cross(i).wait_recv()
            self.load(i).wait()
            self.add(self.ORDER[i], self.stage.at[self.ORDER[i]])
        else:
            if i == 0:
                self.issue(0)
            if i + 1 < 8:
                self.issue(i + 1)
            self.fetch(i).wait()
            self.load(i).wait()
            self.add(self.ORDER[i], self.stage.at[i % 2])
        if i < 4:
            way = self.ORDER[i][0]
            self.first(way, self.ORDER[i][1 + way]).start()

    def middle(self):
        for way in range(2):
            self.first(way, 1).wait_recv()
            self.add((0, 1, 0) if way == 0 else (1, 0, 1), self.got.at[way, 1])
            self.second(way).start()

    def finish(self):
        for way in range(2):
            self.first(way, 0).wait_recv()
            self.second(way).wait_recv()
            self.add((way, 0, 0), self.got.at[way, 0], self.got_late.at[way])

    def result(self, z):
        return self.sums.at[z // (TP // 2), 0, 0, z % (TP // 2)]

    def close(self):
        for i in range(8):
            self.cross(i).wait_send()
        for way in range(2):
            self.second(way).wait_send()
            for block in range(2):
                self.first(way, block).wait_send()


def folds_of(p, grads, cores, scratch):
    return [Fold(p, g, c, scratch[12 * i : 12 * i + 12]) for i, (g, c) in enumerate(zip(grads, cores))]


GRAD_CHUNK = 640


class Outer:
    def __init__(self, grad, left, right, turned, buffers, sems):
        self.grad, self.left, self.right, self.turned = grad, left, right, turned
        self.buffers, self.sems = buffers, sems
        self.wide = buffers.shape[-1]
        self.across = grad.shape[-1] // self.wide
        self.count = 4 * self.across

    def place(self, i):
        return (lax.axis_index("fsdp") * 2 + 2 + i // self.across) % 4

    def store(self, i):
        k, half = self.place(i), TP // 2
        cols = pl.ds(pl.multiple_of(i % self.across * self.wide, 128), self.wide)
        dst = self.grad.at[k // 2, 0, pl.ds(k % 2 * half, half), :, :, :, cols]
        return pltpu.make_async_copy(self.buffers.at[i % 2], dst, self.sems.at[i % 2])

    def run(self, low, high):
        rows = self.turned.shape[0]

        def turn(i, _):
            @pl.when(i % self.across == 0)
            def _():
                cols = pl.ds(pl.multiple_of(self.place(i) * rows, 128), rows)
                self.turned[...] = jnp.transpose(self.left[:, cols])

            @pl.when(i >= low + 2)
            def _():
                self.store(i - 2).wait()

            cols = pl.ds(pl.multiple_of(i % self.across * self.wide, 128), self.wide)
            chunk = dot_plain(self.turned[...], self.right[:, cols]).astype(BF)
            self.buffers[i % 2] = chunk.reshape(self.buffers.shape[1:])
            self.store(i).start()
            return 0

        lax.fori_loop(low, high, turn, 0)

    def flush(self, done):
        for i in (done - 2, done - 1):
            self.store(i).wait()


def turn_kernel(count, *refs):
    parts, out_parts, x_one, cot, gain = refs[:5]
    factors, refs = refs[5 : 5 + (4 if count else 0)], refs[5 + (4 if count else 0) :]
    mixed_out, grad_x_one, grad_gain, mix_all = refs[:4]
    pieces, downs, refs = refs[4 : 4 + TP], refs[4 + TP : 4 + 2 * TP], refs[4 + 2 * TP :]
    grads, cores, refs = refs[:count], refs[count : 2 * count], refs[2 * count :]
    own, local, zs, zr, gu0, gu1, gd0, gd1 = refs[:8]
    p = Place()
    line, late = LineSum(p, parts, refs[8:16]), LineSum(p, out_parts, refs[16:24])
    folds = folds_of(p, grads, cores, refs[24 : 24 + 12 * count])
    out = Gather(p, mix_all, (gu0, gu1), (gd0, gd1))
    halves, rows = parts.shape[1:3]
    line.clear()
    late.clear()
    to_z = [device(p, z=(p.z + d) % TP) for d in range(TP)]
    started = []
    if folds:
        greet(to_z[1:] + [*folds[0].to, folds[0].to_c])
    else:
        greet_line(p)
    stays = []

    def stay(src, dst):
        copy = pltpu.make_async_copy(src, dst, local.at[len(stays)])
        copy.start()
        stays.append(copy)

    if folds:
        left, right, turned, buffers, chunk_sems, load_sems = refs[24 + 12 * count :]
        part = factors[1].shape[1]
        outers = [
            Outer(grads[m], left, right.at[:, pl.ds(m // 2 * part, part)], turned, buffers, chunk_sems)
            for m in range(3)
        ]
        down, gate, up = folds
        size = outers[0].count
        half = size // 2

    def load(m):
        cols = right.at[:, pl.ds(0, factors[2 * m + 1].shape[1])]
        copies = [
            pltpu.make_async_copy(factors[2 * m], left, load_sems.at[0]),
            pltpu.make_async_copy(factors[2 * m + 1], cols, load_sems.at[1]),
        ]
        for copy in copies:
            copy.start()
        for copy in copies:
            copy.wait()

    def outer(m, low, high):
        outers[m].run(low, high)
        outers[m].flush(high)
        folds[m].begin((0, 1, 3, 4) if high == half else (2, 5, 6, 7))

    def join(fold, *blocks):
        for i in blocks:
            fold.join(i)

    def line_step(k):
        for h in range(halves):
            line.step(k, h)

    line_step(3)
    for h in range(halves):
        late.step(TP - 1, h)
    if folds:
        load(0)
        outer(0, 0, half)
        outer(0, half, size)
        join(down, 0, 1)
        load(1)
        outer(1, 0, half)
        join(down, 2, 3)
    line_step(2)
    if folds:
        outer(1, half, size)
        join(down, 4, 5)
        outer(2, 0, half)
        join(gate, 0, 1)
        down.middle()
        join(gate, 2, 3)
    line_step(1)
    if folds:
        outer(2, half, size)
        join(gate, 4, 5)
    grad_gain[...] = jnp.zeros(grad_gain.shape, F32)
    for h in range(halves):
        line.arrive(h)

        def finish(at, h=h):
            grad, gains = norm_back(x_one[h, at], gain[...], line.total(h, at))
            grad = grad + cot[h, at].astype(F32)
            grad_x_one[h, at] = grad
            own[h, at] = grad.astype(BF)
            grad_gain[0:1] += jnp.sum(gains, axis=0, keepdims=True)

        by_rows(rows, finish)
        out.begin(h, own.at[h])
        stay(own.at[h], mix_all.at[p.z, h])
    if folds:
        join(up, 0, 1)
        gate.middle()
        join(up, 2, 3)
    for h in range(halves):
        out.step(1, h)
        late.step(2, h)
    if folds:
        join(down, 6, 7)
        down.finish()
        stay(down.result(p.z), downs[0])
        for d in (1, 3, 2):
            copy = copy_to(down.result((p.z + d) % TP), downs[d], (zs, zr), (d,), to_z[d])
            copy.start()
            started.append(copy)
        join(up, 4, 5)
        join(gate, 6, 7)
    for h in range(halves):
        out.step(2, h)
        late.step(1, h)
    if folds:
        join(up, 6, 7)
        up.middle()
    for h in range(halves):
        out.step(3, h)
    for h in range(halves):
        late.arrive(h)

        def store(at, h=h):
            mixed_out[h, at] = (x_one[h, at] + late.total(h, at)).astype(BF)

        by_rows(rows, store)
    for m, fold in enumerate(folds[1:]):
        fold.finish()
        for d in range(TP):
            stay(fold.result((p.z + d) % TP), pieces[d].at[:, pl.ds(m * part, part)])
    if folds:
        for d in range(1, TP):
            copy_to(downs[d], downs[d], (zs, zr), (d,), to_z[1]).wait_recv()
    for copy in started:
        copy.wait_send()
    for fold in folds:
        fold.close()
    line.close()
    late.close()
    out.close(halves)
    for copy in stays:
        copy.wait()


def turn(parts, out_parts, x_one, cot, gain, factors, p):
    shape, count, width = parts.shape, 3 if factors else 0, parts.shape[-1]
    rows = width // (p.fs * TP * 4)
    sizes = [factors[1].shape[1]] * count if factors else []
    grads = [jax.ShapeDtypeStruct((p.fs, 1, TP, 2, 2, rows, size), BF) for size in sizes]
    folded = [Fold.shapes(grad, True) for grad in grads]
    piece = jax.ShapeDtypeStruct((rows, 2 * sizes[0]) if factors else (16, 128), BF)
    down = jax.ShapeDtypeStruct((rows, sizes[0]) if factors else (16, 128), BF)
    extra = []
    if factors:
        assert all(size % GRAD_CHUNK == 0 for size in sizes)
        tokens, deep = factors[0].shape[0], width // 4
        extra = [
            pltpu.VMEM((tokens, width), BF),
            pltpu.VMEM((tokens, 2 * sizes[0]), BF),
            pltpu.VMEM((deep, tokens), BF),
            pltpu.VMEM((2, TP // 2, 2, 2, rows, GRAD_CHUNK), BF),
            pltpu.SemaphoreType.DMA((2,)),
            pltpu.SemaphoreType.DMA((2,)),
        ]
    results = pl.pallas_call(
        functools.partial(turn_kernel, count),
        in_specs=[VMEM] * 5 + [ANY] * len(factors),
        out_specs=[VMEM, VMEM, VMEM, ANY] + [ANY] * (2 * TP + 2 * count),
        out_shape=[
            jax.ShapeDtypeStruct(shape[1:], BF),
            jax.ShapeDtypeStruct(shape[1:], F32),
            jax.ShapeDtypeStruct((8, width), F32),
            jax.ShapeDtypeStruct(shape, BF),
            *[piece] * TP,
            *[down] * TP,
            *grads,
            *(cores for cores, _ in folded),
        ],
        scratch_shapes=[
            pltpu.VMEM(shape[1:], BF),
            pltpu.SemaphoreType.DMA((shape[1] + 2 * TP + 1,)),
            *pairs(TP),
            *pairs(TP - 1, shape[1]),
            *pairs(TP - 1, shape[1]),
            *LineSum.scratch(shape),
            *LineSum.scratch(shape),
            *(item for _, scratch in folded for item in scratch),
            *extra,
        ],
        compiler_params=pltpu.CompilerParams(
            collective_id=2, has_side_effects=True, vmem_limit_bytes=GRANT
        ),
    )(parts, out_parts, x_one, cot, gain, *factors)
    return results[:4], results[4 : 4 + TP], results[4 + TP : 4 + 2 * TP]


def final_kernel(*refs):
    parts, x_zero, gain, grad_x_one, vectors, blocks = refs[:6]
    factors, refs = refs[6:10], refs[10:]
    grad_in, sums = refs[:2]
    outs, grads, refs = refs[2:6], (blocks, *refs[6:9]), refs[9:]
    acc, got, vs, vr, zs, zr, local, left, right, turned, buffers, chunk_sems, load_sems = refs[:13]
    p = Place()
    line = LineSum(p, parts, refs[13:21])
    folds = folds_of(p, grads, [None] * 4, refs[21:])
    halves, rows = parts.shape[1:3]
    line.clear()
    to_z = [device(p, z=(p.z + d) % TP) for d in range(TP)]
    (to_x, to_f), to_c = folds[0].to, folds[0].to_c
    greet(to_z[1:] + [to_x, to_f, to_c])
    partners = [to_c, to_x, to_f] + [
        device(p, z=p.z + bit * (1 - 2 * (p.z // bit % 2))) for bit in (1, 2)
    ]
    part = factors[1].shape[1]
    outers = [
        Outer(grads[m], left, right.at[:, pl.ds(m // 3 * part, part)], turned, buffers, chunk_sems)
        for m in range(1, 4)
    ]

    def load(m):
        cols = right.at[:, pl.ds(0, factors[2 * m + 1].shape[1])]
        copies = [
            pltpu.make_async_copy(factors[2 * m], left, load_sems.at[0]),
            pltpu.make_async_copy(factors[2 * m + 1], cols, load_sems.at[1]),
        ]
        for copy in copies:
            copy.start()
        for copy in copies:
            copy.wait()

    def outer(m):
        outers[m - 1].run(0, outers[m - 1].count)
        outers[m - 1].flush(outers[m - 1].count)
        folds[m].begin()

    def join(m, *blocks):
        for i in blocks:
            folds[m].join(i)

    def line_step(k):
        for h in range(halves):
            line.step(k, h)

    def vector(i):
        return copy_to(acc.at[i], got.at[i], (vs, vr), (i,), partners[i])

    def next_vector(i):
        vector(i).wait_recv()
        if i < 4:
            acc[i + 1] = acc[i] + got[i]
            vector(i + 1).start()
        else:
            sums[...] = acc[i] + got[i]

    started, stays = [], []

    def send_on(m):
        folds[m].finish()
        for d in (1, 3, 2):
            src = folds[m].result((p.z + d) % TP)
            copy = copy_to(src, outs[m].at[p.z], (zs, zr), (m, d - 1), to_z[d])
            copy.start()
            started.append(copy)
        stays.append(pltpu.make_async_copy(folds[m].result(p.z), outs[m].at[p.z], local.at[m]))
        stays[-1].start()

    acc[0] = vectors[...]
    vector(0).start()
    folds[0].begin()
    line_step(3)
    join(0, 0, 1, 2, 3)
    load(0)
    outer(1)
    load(1)
    join(0, 4, 5)
    join(1, 0, 1)
    folds[0].middle()
    join(1, 2, 3)
    outer(2)
    line_step(2)
    next_vector(0)
    join(0, 6, 7)
    join(1, 4, 5)
    join(2, 0, 1)
    folds[1].middle()
    join(2, 2, 3)
    outer(3)
    line_step(1)
    next_vector(1)
    send_on(0)
    join(1, 6, 7)
    join(2, 4, 5)
    join(3, 0, 1)
    folds[2].middle()
    join(3, 2, 3)
    next_vector(2)
    send_on(1)
    join(2, 6, 7)
    join(3, 4, 5)
    folds[3].middle()
    join(3, 6, 7)
    send_on(2)
    next_vector(3)
    for h in range(halves):
        line.arrive(h)

        def finish(at, h=h):
            grad, _ = norm_back(x_zero[h, at].astype(F32), gain[...], line.total(h, at))
            grad_in[h, at] = grad_x_one[h, at] + grad

        by_rows(rows, finish)
    next_vector(4)
    send_on(3)
    for m in range(4):
        for d in range(1, TP):
            ref = outs[m].at[(p.z - d) % TP]
            copy_to(ref, ref, (zs, zr), (m, d - 1), to_z[1]).wait_recv()
    for copy in started:
        copy.wait_send()
    for i in range(5):
        vector(i).wait_send()
    for fold in folds:
        fold.close()
    line.close()
    for copy in stays:
        copy.wait()


def final(parts, x_zero, gain, grad_x_one, vectors, blocks, factors, p):
    shape = parts.shape
    rows, part = blocks.shape[-2], factors[1].shape[1]
    tokens, width = factors[0].shape
    shaped = jax.ShapeDtypeStruct
    grads = [shaped((p.fs, 1, TP, 2, 2, rows, part), BF)] * 3
    widths = [blocks.shape[-1]] + [part] * 3
    folded = [Fold.shapes(grad, False)[1] for grad in (blocks, *grads)]
    results = pl.pallas_call(
        final_kernel,
        in_specs=[VMEM] * 5 + [ANY] * 5,
        out_specs=[VMEM, VMEM] + [ANY] * 7,
        out_shape=[
            shaped(shape[1:], F32),
            shaped(vectors.shape, F32),
            *(shaped((TP, rows, wide), BF) for wide in widths),
            *grads,
        ],
        scratch_shapes=[
            pltpu.VMEM((5,) + vectors.shape, F32),
            pltpu.VMEM((5,) + vectors.shape, F32),
            *pairs(5),
            *pairs(4, TP - 1),
            pltpu.SemaphoreType.DMA((4,)),
            pltpu.VMEM((tokens, width), BF),
            pltpu.VMEM((tokens, 2 * part), BF),
            pltpu.VMEM((width // 4, tokens), BF),
            pltpu.VMEM((2, TP // 2, 2, 2, rows, part), BF),
            pltpu.SemaphoreType.DMA((2,)),
            pltpu.SemaphoreType.DMA((2,)),
            *LineSum.scratch(shape),
            *(item for scratch in folded for item in scratch),
        ],
        cost_estimate=FREE,
        compiler_params=pltpu.CompilerParams(
            collective_id=3, has_side_effects=True, vmem_limit_bytes=GRANT
        ),
    )(parts, x_zero, gain, grad_x_one, vectors, blocks, *factors)
    return results[0], results[1], results[2:6]


def chain_kernel(backward, sums, *refs):
    if backward:
        known, start, spans, send, recv = refs
    else:
        start, spans, send, recv = refs
    p = Place()
    peers = [device_q(p, (p.q + d) % NQ) for d in range(NQ)]
    greet(peers[1:])
    spans[p.q] = sums[...]
    copies = []
    for d in range(1, NQ):
        copies.append(copy_to(spans.at[p.q], spans.at[p.q], (send, recv), (d,), peers[d]))
        copies[-1].start()
    for d in range(1, NQ):
        ref = spans.at[(p.q - d) % NQ]
        copy_to(ref, ref, (send, recv), (d,), peers[d]).wait_recv()
    micro = sums.shape[1] // TP
    carry = jnp.zeros((micro, sums.shape[2]), F32)
    order = [(z, q) for z in range(TP) for q in range(NQ)]
    for z, q in reversed(order) if backward else order:
        here = slice(z * micro, (z + 1) * micro)

        @pl.when(p.q == q)
        def _(carry=carry, here=here):
            start[here] = carry

        decay = known[q, 0, here] if backward else spans[q, 0, here]
        carry = decay * carry + spans[q, 0 if backward else 1, here]
    for copy in copies:
        copy.wait_send()


def device_q(p, q):
    return device(p, x=q // 2, c=q % 2)


def chain(sums, known=None):
    backward = known is not None
    every = (NQ,) + sums.shape
    return pl.pallas_call(
        functools.partial(chain_kernel, backward),
        in_specs=[VMEM] * (2 if backward else 1),
        out_specs=[VMEM, VMEM],
        out_shape=[
            jax.ShapeDtypeStruct(sums.shape[1:], F32),
            jax.ShapeDtypeStruct(every, F32),
        ],
        scratch_shapes=pairs(NQ),
        cost_estimate=FREE,
        compiler_params=pltpu.CompilerParams(
            collective_id=5 if backward else 4, has_side_effects=True
        ),
    )(*((sums, known) if backward else (sums,)))


def unpack_kernel(count, *refs):
    p = Place()
    pieces, outs = refs[: TP * len(count)], refs[TP * len(count) :]
    for d in range(TP):
        first = 0
        for m, parts in enumerate(count):
            piece = pieces[m * TP + d]
            part = piece.shape[1] // parts
            cols = pl.ds(pl.multiple_of((p.z - d) % TP * part, 128), part)
            for i in range(parts):
                outs[first + i][:, cols] = piece[:, i * part : (i + 1) * part].astype(F32)
            first += parts


def unpack(groups, count):
    shapes = []
    for pieces, parts in zip(groups, count):
        rows, cols = pieces[0].shape
        shapes += [jax.ShapeDtypeStruct((rows, cols // parts * TP), F32)] * parts
    return pl.pallas_call(
        functools.partial(unpack_kernel, count),
        in_specs=[VMEM] * (TP * len(groups)),
        out_specs=[VMEM] * len(shapes),
        out_shape=shapes,
        compiler_params=pltpu.CompilerParams(vmem_limit_bytes=GRANT),
    )(*(piece for pieces in groups for piece in pieces))


def unpack_mix_kernel(spans, *refs):
    (blocks, *mix), (blocks_out, *mix_out) = refs[:4], refs[4:]
    total = blocks[0].astype(F32)
    for k in range(1, TP):
        total = total + blocks[k].astype(F32)
    blocks_out[...] = total
    for piece, out in zip(mix, mix_out):
        for k, (start, count) in enumerate(spans):
            out[:, start : start + count] = piece[k, :, :count].astype(F32)


def unpack_mix(mix, spans):
    wide = spans[-1][0] + spans[-1][1]
    shapes = [mix[0].shape[1:]] + [(mix[0].shape[1], wide)] * 3
    return pl.pallas_call(
        functools.partial(unpack_mix_kernel, spans),
        in_specs=[VMEM] * 4,
        out_specs=[VMEM] * 4,
        out_shape=[jax.ShapeDtypeStruct(shape, F32) for shape in shapes],
        compiler_params=pltpu.CompilerParams(vmem_limit_bytes=GRANT),
    )(*mix)


def geglu(gate_vals, up_vals):
    return jax.nn.gelu(gate_vals) * up_vals


def all_spans(value, p):
    by_q = everywhere(value, shift_q, p.q, NQ)
    by_r = everywhere(by_q, shift_r, p.r, p.rests)
    return jnp.swapaxes(by_r, 1, 2).reshape((-1,) + value.shape[1:])


def own_spans(spans, p):
    split = spans.reshape((p.rests, TP, NQ) + spans.shape[1:])
    return lax.dynamic_index_in_dim(at(split, p.r), p.q, 1, keepdims=False)


def on_device(
    inputs,
    cotangent,
    proj_gelu,
    proj_lru,
    gate_blocks,
    proj_out,
    ffw_gate,
    ffw_up,
    ffw_down,
    norm_mix,
    norm_ffw,
    decay_param,
    conv_taps,
):
    p = Place()
    micro, span, width = inputs.shape[0], inputs.shape[2], inputs.shape[3]
    lru_width = proj_gelu.shape[1]
    tap_count = conv_taps.shape[1]
    block_width = gate_blocks.shape[1] // 2
    heads = lru_width // block_width
    ffw_part = ffw_gate.shape[1] // TP
    rows = proj_gelu.shape[0]
    held = -(-heads // TP)
    first = [k * heads // TP for k in range(TP)]
    owned = [range(first[k], first[k + 1] if k + 1 < TP else heads) for k in range(TP)]
    part = held * block_width

    out_t, down_t = proj_out.T, ffw_down.T
    small = jnp.concatenate([norm_mix[None], norm_ffw[None], decay_param[None], conv_taps.T])
    small = jnp.pad(small, ((0, 128 - small.shape[0]), (0, 0))).T
    x_rows, cot = inputs[:, 0], cotangent[:, 0]
    one = 1 if p.rests == 1 else 0
    cot_halves = cot.reshape(2, -1, width)
    edge = lax.ppermute(
        x_rows[:, span - (tap_count - 1) :],
        "seq",
        [(i, i + 1) for i in range(lax.axis_size("seq") - 1)],
    )
    edge = jnp.pad(edge, ((0, 0), (HALO - (tap_count - 1), 0), (0, 0)))
    x_wide = jnp.concatenate([x_rows.reshape(-1, width), edge.reshape(-1, width)])
    if p.rests == 1:
        weights = (proj_gelu, proj_lru, out_t, gate_blocks, small, ffw_gate, ffw_up, down_t)
        mix_pieces, ffw_pieces = pack(weights, block_width)
        mix_w, ffw_w, piece_1, x_all, cot_first = intake(
            mix_pieces, ffw_pieces[0], ffw_pieces[1], x_wide, cot_halves[0], p
        )
        piece_2, piece_3, x_all = lax.optimization_barrier((*ffw_pieces[2:], x_all))
        piece_3, piece_2 = shift_z(piece_3, 3), shift_z(piece_2, 2)
        passed = (piece_1, swap_x(piece_1), swap_f(piece_1), piece_2, piece_3)
    else:
        mix_pieces, ffw_pieces = [], []
        for k in range(TP):
            cols = slice(first[k] * block_width, first[k] * block_width + part)
            pieces = [proj_gelu[:, cols], proj_lru[:, cols], out_t[:, cols], gate_blocks, small]
            mix_pieces.append(jnp.concatenate(pieces, axis=1))
            cols = slice(k * ffw_part, (k + 1) * ffw_part)
            pieces = [ffw_gate[:, cols], ffw_up[:, cols], down_t[:, cols]]
            ffw_pieces.append(jnp.concatenate(pieces, axis=1))
        mix_w = weights_in(jnp.stack(mix_pieces), p)
        whole_ffw = weights_in(jnp.stack(ffw_pieces), p)
        x_all, passed, ffw_w = gather_z(x_wide, p), None, None
        cot_first = gather_z(cot_halves[:1], p)
    dims = (span, micro, heads, held, block_width, tap_count)
    small_w, rows_w, mixed, pre, pre_lru, conv, gate, state, prod, sums = recur(
        x_all.reshape(-1, width), mix_w, dims
    )
    mix_gain, ffw_gain = small_w[0:1], small_w[1:2]
    start = sum(jnp.where(p.z == k, first[k] * block_width, 0) for k in range(TP))

    ends = (TP, micro, part)
    if p.rests == 1:
        state_in, every_sum = chain(sums)
    else:
        sums = all_spans(jnp.stack([sums[0].reshape(ends), sums[1].reshape(ends)], axis=1), p)
        carry, carries = jnp.zeros_like(sums[0, 0]), []
        for k in range(sums.shape[0]):
            carries.append(carry)
            carry = sums[k, 0] * carry + sums[k, 1]
        state_in = own_spans(jnp.stack(carries), p).reshape(-1, part)
    mix_bf, out_parts = recur_mix(pre, rows_w, state, prod, state_in, mix_w, dims)
    blocked = (TP, micro * CUTS, span // CUTS, width)
    x_own, cot_own = x_rows.reshape(blocked[1:]), cot.reshape(blocked[1:])
    out_parts = out_parts.reshape(blocked)
    x_one, ffw_bf, cot_all, _, *fed = middle(
        out_parts, x_own, ffw_gain, cot_halves[1], cot_first, passed, ffw_w
    )
    cot_all = cot_all.reshape(-1, width)

    ffw_bf = ffw_bf.reshape(-1, width)
    if p.rests == 1:
        hidden_bf, grad_gate_up, ffw_parts, grad_in_parts = fed
    else:
        gate_up_w, down_w = whole_ffw[:, : 2 * ffw_part], whole_ffw[:, 2 * ffw_part :]
        gate_up = dot_plain(ffw_bf, gate_up_w)
        gate_vals, up_vals = gate_up[:, :ffw_part], gate_up[:, ffw_part:]
        hidden_bf = geglu(gate_vals, up_vals).astype(BF)
        grad_hidden = dot_plain(cot_all, down_w)
        _, pull_back = jax.vjp(geglu, gate_vals, up_vals)
        grad_gate_up = jnp.concatenate(pull_back(grad_hidden), axis=1).astype(BF)
        ffw_parts = dot_right_t(hidden_bf, down_w).astype(BF)
        grad_in_parts = dot_right_t(grad_gate_up, gate_up_w).astype(BF)
    ffw_parts, grad_in_parts = ffw_parts.reshape(blocked), grad_in_parts.reshape(blocked)
    factors = [cot_all, hidden_bf, ffw_bf, grad_gate_up]
    (mixed_out, grad_x_one, gain_rows, grad_mix), ffw_pieces, down_pieces = turn(
        grad_in_parts, ffw_parts, x_one, cot_own, ffw_gain, factors * one, p
    )
    if p.rests == 1:
        ffw_pieces = [shift_z(piece, d) if d else piece for d, piece in enumerate(ffw_pieces)]
    grad_mix = grad_mix.reshape(-1, width)

    grad_gelu_bf, local_back, prod_back, back_sums = recur_back(
        grad_mix, pre, rows_w, state, prod, state_in, gate, mix_w, dims
    )
    if p.rests == 1:
        carried, _ = chain(back_sums[None], every_sum)
    else:
        back_sums = all_spans(back_sums.reshape(ends), p)
        carry, carries = jnp.zeros_like(sums[0, 0]), []
        for k in range(sums.shape[0] - 1, -1, -1):
            carries.append(carry)
            carry = sums[k, 0] * carry + back_sums[k]
        carried = own_spans(jnp.stack(carries[::-1]), p).reshape(-1, part)
    block_mats = lax.dynamic_slice(mix_w, (start, 3 * part), (part, 2 * block_width))
    grad_blocks, grad_lru, spill, row_grads = recur_grad(
        local_back, prod_back, carried, state, prod, state_in, gate, conv, pre_lru, rows_w,
        block_mats.reshape(held, block_width, 2 * block_width), dims,
    )
    spill = spill.reshape(TP, micro, HALO, part)
    from_next = shift_q(spill, -1)
    last = jnp.zeros_like(spill[:1])
    if p.rests > 1:
        last = move(spill[:1], lambda r, z, q: (r - 1, z, NQ - 1) if q == 0 and r > 0 else None)
    from_next = jnp.where(
        p.q == NQ - 1, jnp.concatenate([from_next[1:], last], axis=0), from_next
    )
    grad_pair, grad_mixed_parts, mix_gain_rows = recur_in(
        grad_gelu_bf, grad_lru, from_next.reshape(-1, part), rows_w, small_w, mixed, mix_w, dims
    )
    grad_mixed_parts = grad_mixed_parts.reshape(blocked)

    blocks_all = lax.dynamic_update_slice_in_dim(
        jnp.zeros((lru_width, 2 * block_width), BF),
        (grad_blocks * rows_w[6][:, None]).astype(BF),
        start,
        0,
    )
    mix_factors = [grad_mix, mix_bf, mixed, grad_pair]
    vectors = lax.dynamic_update_slice_in_dim(
        jnp.zeros((1 + tap_count, lru_width), F32), row_grads[: 1 + tap_count], start, 1
    )
    vectors = jnp.concatenate([mix_gain_rows[:1], gain_rows[:1], vectors], axis=0)
    vectors = jnp.pad(vectors, ((0, -vectors.shape[0] % 8), (0, 0)))
    if p.rests == 1:
        grad_inputs, vectors, mix_grads = final(
            grad_mixed_parts, x_own, mix_gain, grad_x_one, vectors,
            by_owner(blocks_all, p), mix_factors, p,
        )
    else:
        products = [dot_left_t(*mix_factors[:2]), dot_left_t(*mix_factors[2:])]
        products = [blocks_all, products[0], products[1][:, :part], products[1][:, part:]]
        mix_grads = [grads_out(grad.astype(BF), p) for grad in products]
        grad_mixed_own = scatter_z(grad_mixed_parts, p)
        grad_inputs = grad_x_one + norm_back(x_own.astype(F32), mix_gain, grad_mixed_own)[0]
        for exchange in (swap_core, swap_x, swap_f):
            vectors = vectors + exchange(vectors)
        for bit in (1, 2):
            vectors = vectors + move(vectors, lambda r, z, q, bit=bit: (r, z ^ bit, q))
        total = vectors
        for d in range(1, p.rests):
            total = total + shift_r(vectors, d)
        vectors = total
    vectors = lax.dynamic_slice_in_dim(vectors, p.index * rows, rows, 1)

    if p.rests == 1:
        spans = [(first[k] * block_width, len(owned[k]) * block_width) for k in range(TP)]
        share_blocks, share_out, share_gelu, share_lru = unpack_mix(mix_grads, spans)
        share_gate, share_up, share_down = unpack((ffw_pieces, down_pieces), (2, 1))
    else:
        ffw_grads = [dot_left_t(*factors[:2]), dot_left_t(*factors[2:])]
        ffw_grads = [grads_out(grad.astype(BF), p) for grad in ffw_grads]
        beside = lambda v: jnp.swapaxes(v, 0, 1).reshape(rows, -1).astype(F32)
        share_gate = beside(ffw_grads[1][:, :, :ffw_part])
        share_up = beside(ffw_grads[1][:, :, ffw_part:])
        share_down = beside(ffw_grads[0])

        def mix_columns(grad):
            picked = [grad[k][:, : len(owned[k]) * block_width] for k in range(TP)]
            return jnp.concatenate(picked, axis=1).astype(F32)

        share_blocks = jnp.sum(mix_grads[0].astype(F32), axis=0)
        share_out, share_gelu, share_lru = (mix_columns(grad) for grad in mix_grads[1:])
    shape = (micro, 1, span, width)
    return (
        mixed_out.reshape(shape),
        grad_inputs.reshape(shape),
        share_gelu,
        share_lru,
        share_blocks,
        share_out.T,
        share_gate,
        share_up,
        share_down.T,
        vectors[0],
        vectors[1],
        vectors[2],
        vectors[3 : 3 + tap_count].T,
    )


def solution(mesh):
    in_specs = (
        P(None, "fsdp", "seq", None),
        P(None, "fsdp", "seq", None),
        P(("fsdp", "seq"), None),
        P(("fsdp", "seq"), None),
        P(("fsdp", "seq"), None),
        P(None, ("fsdp", "seq")),
        P(("fsdp", "seq"), None),
        P(("fsdp", "seq"), None),
        P(None, ("fsdp", "seq")),
        P(("fsdp", "seq")),
        P(("fsdp", "seq")),
        P(("fsdp", "seq")),
        P(("fsdp", "seq"), None),
    )
    out_specs = (
        P(None, "fsdp", "seq", None),
        P(None, "fsdp", "seq", None),
        P(("fsdp", "seq"), None),
        P(("fsdp", "seq"), None),
        P(("fsdp", "seq"), None),
        P(None, ("fsdp", "seq")),
        P(("fsdp", "seq"), None),
        P(("fsdp", "seq"), None),
        P(None, ("fsdp", "seq")),
        P(("fsdp", "seq")),
        P(("fsdp", "seq")),
        P(("fsdp", "seq")),
        P(("fsdp", "seq"), None),
    )
    return jax.shard_map(
        on_device, mesh=mesh, in_specs=in_specs, out_specs=out_specs, check_vma=False
    )
```

```python
import functools

import jax
import jax.numpy as jnp
from jax import lax
from jax.experimental import pallas as pl
from jax.experimental.pallas import tpu as pltpu
from jax.sharding import PartitionSpec as P

EPS = 1e-06
GUARD = 0.001
RATE = 8.0
TP = 4
NQ = 4
HALO = 8
BF = jnp.bfloat16
F32 = jnp.float32
MESH = pl.DeviceIdType.MESH
ANY = pl.BlockSpec(memory_space=pl.ANY)
VMEM = pl.BlockSpec(memory_space=pltpu.VMEM)
GRANT = 60 * 1024 * 1024
CUTS = 2
FREE = pl.CostEstimate(flops=0, bytes_accessed=0, transcendentals=0)


def move(value, step):
    pairs = []
    for here in range(lax.axis_size("seq")):
        there = step(here // (TP * NQ), here // NQ % TP, here % NQ)
        if there is not None:
            pairs.append((here, (there[0] * TP + there[1]) * NQ + there[2]))
    return lax.ppermute(value, "seq", pairs)


def swap_core(value):
    return move(value, lambda r, z, q: (r, z, q ^ 1))


def swap_x(value):
    return move(value, lambda r, z, q: (r, z, q ^ 2))


def swap_f(value):
    return lax.ppermute(value, "fsdp", [(0, 1), (1, 0)])


def shift_z(value, d):
    return move(value, lambda r, z, q: (r, (z + d) % TP, q))


def shift_q(value, d):
    return move(value, lambda r, z, q: (r, z, (q + d) % NQ))


def shift_r(value, d):
    count = lax.axis_size("seq") // (TP * NQ)
    return move(value, lambda r, z, q: ((r + d) % count, z, q))


def hop(value, d, low, high):
    return move(value, lambda r, z, q: (r, z + d, q) if low <= z <= high else None)


class Place:
    def __init__(self):
        seq = lax.axis_index("seq")
        self.f = lax.axis_index("fsdp")
        self.r, self.z, self.q = seq // (TP * NQ), seq // NQ % TP, seq % NQ
        self.x, self.c = self.q // 2, self.q % 2
        self.rests = lax.axis_size("seq") // (TP * NQ)
        self.fs = lax.axis_size("fsdp")
        self.index = self.f * lax.axis_size("seq") + seq


def at(value, index):
    return lax.dynamic_index_in_dim(value, index, 0, keepdims=False)


def put(base, value, *index):
    starts = [jnp.int32(0) if i is None else jnp.int32(i) for i in index]
    starts += [jnp.int32(0)] * (base.ndim - len(index))
    for dim, i in enumerate(index):
        if i is not None:
            value = jnp.expand_dims(value, dim)
    return lax.dynamic_update_slice(base, value, starts)


def everywhere(value, shifter, mine, count):
    out = put(jnp.zeros((count,) + value.shape, value.dtype), value, mine)
    for d in range(1, count):
        out = put(out, shifter(value, d), (mine - d) % count)
    return out


def gather_z(value, p):
    ups, downs = [], []
    up = down = value
    for k in range(1, TP):
        up = hop(up, 1, k - 1, TP - 2)
        down = hop(down, -1, 1, TP - k)
        ups.append(up)
        downs.append(down)
    out = put(jnp.zeros((TP,) + value.shape, value.dtype), value, p.z)
    for k in range(1, TP):
        out = put(out, downs[k - 1] + ups[TP - 1 - k], (p.z + k) % TP)
    return out


def scatter_z(parts, p):
    right = left = None
    for k in range(TP - 1, 0, -1):
        send = at(parts, (p.z + k) % TP)
        if right is not None:
            send = (send.astype(F32) + right.astype(F32)).astype(BF)
        right = hop(send, 1, 0, TP - 1 - k)
        send = at(parts, (p.z - k) % TP)
        if left is not None:
            send = (send.astype(F32) + left.astype(F32)).astype(BF)
        left = hop(send, -1, k, TP - 1)
    return at(parts, p.z).astype(F32) + right.astype(F32) + left.astype(F32)


def weights_in(pieces, p):
    rows, cols = pieces.shape[1:]
    mine = put(jnp.zeros(pieces.shape, BF), at(pieces, p.z), p.z)
    for d in range(1, TP):
        mine = put(mine, shift_z(at(pieces, (p.z + d) % TP), d), (p.z - d) % TP)
    mine = everywhere(mine, shift_r, p.r, p.rests)
    half = TP // 2
    by_x, by_f = swap_x(mine), swap_f(mine)
    corner = (swap_f(by_x[:, :half]), swap_x(by_f[:, half:]))
    whole = jnp.zeros((p.fs, p.rests, TP, 2, 2, rows, cols), BF)
    for block, f, x, z in (
        (mine, p.f, p.x, 0),
        (by_x, p.f, 1 - p.x, 0),
        (by_f, 1 - p.f, p.x, 0),
        (corner[0], 1 - p.f, 1 - p.x, 0),
        (corner[1], 1 - p.f, 1 - p.x, half),
    ):
        other = swap_core(block)
        for part, c in ((block, p.c), (other, 1 - p.c)):
            part = part[None, :, :, None, None]
            whole = lax.dynamic_update_slice(
                whole, part, [jnp.int32(i) for i in (f, 0, z, x, c, 0, 0)]
            )
    return whole.reshape(-1, cols)


def by_owner(grad, p):
    return grad.reshape(p.fs, p.rests, TP, 2, 2, -1, grad.shape[1])


def to_owner_z(total, p):
    out = put(jnp.zeros(total.shape, BF), at(total, p.z), p.z)
    for d in (1, 3, 2):
        out = put(out, shift_z(at(total, (p.z + d) % TP), d), (p.z - d) % TP)
    return out


def grads_out(grad, p):
    plus = lambda a, b: (a.astype(F32) + b.astype(F32)).astype(BF)
    pick = lambda v, dim, i: lax.dynamic_index_in_dim(v, i, dim, keepdims=False)
    total = by_owner(grad, p)
    total = plus(pick(total, 4, p.c), swap_core(pick(total, 4, 1 - p.c)))
    total = plus(pick(total, 3, p.x), swap_x(pick(total, 3, 1 - p.x)))
    total = plus(at(total, p.f), swap_f(at(total, 1 - p.f)))
    mine = at(total, p.r)
    for d in range(1, p.rests):
        mine = plus(mine, shift_r(at(total, (p.r + d) % p.rests), d))
    return to_owner_z(mine, p)


def dot_left_t(left_mat, right_mat):
    return lax.dot_general(
        left_mat, right_mat, (((0,), (0,)), ((), ())), preferred_element_type=F32
    )


def dot_plain(left_mat, right_mat):
    return jnp.dot(left_mat, right_mat, preferred_element_type=F32)


def dot_right_t(left_mat, right_mat):
    return lax.dot_general(
        left_mat, right_mat, (((1,), (1,)), ((), ())), preferred_element_type=F32
    )


def normed(values, gain_vec):
    return values * lax.rsqrt(jnp.mean(values * values, axis=-1, keepdims=True) + EPS) * gain_vec


def gelu_pair(v):
    scale = 0.7978845608028654
    inner = jnp.tanh(scale * (v + 0.044715 * v * v * v))
    slope = 0.5 * v * (1.0 - inner * inner) * scale * (1.0 + 0.134145 * v * v)
    return 0.5 * v * (1.0 + inner), 0.5 * (1.0 + inner) + slope


def span_scan(decay, drive, backward):
    count = decay.shape[0]
    row = lax.broadcasted_iota(jnp.int32, decay.shape, 0)
    step = 1
    while step < count:
        inside = row < count - step if backward else row >= step
        turn = count - step if backward else step
        drive = drive + jnp.where(inside, decay * pltpu.roll(drive, turn, 0), 0.0)
        decay = decay * jnp.where(inside, pltpu.roll(decay, turn, 0), 1.0)
        step *= 2
    return decay, drive


def gate_values(gate, soft):
    half = gate.shape[1] // 2
    rec_gate = jax.nn.sigmoid(gate[:, :half])
    in_gate = jax.nn.sigmoid(gate[:, half:])
    log_decay = -RATE * rec_gate * soft
    square = jnp.exp(2.0 * log_decay)
    return rec_gate, in_gate, jnp.exp(log_decay), square, jnp.sqrt(1.0 - square + GUARD)


def main_rows(i, span, micro):
    return pl.ds(i // micro * micro * (span + HALO) + i % micro * span, span)


def with_halo(pre, i, span, micro):
    start = i // micro * micro * (span + HALO) + micro * span + i % micro * HALO
    both = [pre[pl.ds(start, HALO)], pre[main_rows(i, span, micro)]]
    return jnp.concatenate(both, axis=0)


def recur_head(span, micro, pre, rows, block, conv, gate, state, prod, sums):
    count = conv.shape[0] // span
    soft, taps = rows[0:1], [rows[k + 2 : k + 3] for k in range(4)]
    for i in range(count):
        vals = with_halo(pre, i, span, micro).astype(BF).astype(F32)
        total = taps[0] * vals
        for k in range(1, 4):
            total = total + taps[k] * pltpu.roll(vals, k, 0)
        conv[pl.ds(i * span, span)] = total[HALO:].astype(BF)
    gate[...] = dot_plain(conv[...], block[...])
    for i in range(count):
        here = pl.ds(i * span, span)
        _, in_gate, decay, _, root = gate_values(gate[here], soft)
        decay, local = span_scan(decay, root * in_gate * conv[here].astype(F32), False)
        state[here] = local
        prod[here] = decay
        sums[0, i : i + 1] = decay[span - 1 :]
        sums[1, i : i + 1] = local[span - 1 :]


def columns(ref, h, width):
    return ref.at[:, pl.ds(pl.multiple_of(h * width, 128), width)]


def by_heads(count, body):
    def turn(h, _):
        body(h)
        return 0

    lax.fori_loop(0, count, turn, 0)


def recur_kernel(
    dims, x_all, gelu_w, lru_w, mix_w, small, rows, mixed, pre_gelu, pre_lru, conv, gate, state,
    prod, sums, small_w, block_w, mixed_all, sems,
):
    span, micro, heads, held, bw, taps = dims
    part, h = held * bw, pl.program_id(0)

    @pl.when(h == 0)
    def _():
        p = Place()
        start = pl.multiple_of(p.z * heads // TP * bw, 128)
        pieces = (
            (mix_w.at[:, pl.ds(3 * part + 2 * bw, 128)], small_w),
            (mix_w.at[pl.ds(start, part), pl.ds(3 * part, 2 * bw)], block_w),
        )
        loads = [pltpu.make_async_copy(src, dst, sems.at[i]) for i, (src, dst) in enumerate(pieces)]
        for load in loads:
            load.start()
        loads[0].wait()
        row = lax.broadcasted_iota(jnp.int32, (8, 128), 0)
        lane = lax.broadcasted_iota(jnp.int32, (8, 128), 1)
        small[...] = dot_right_t(jnp.where(row == lane, 1.0, 0.0).astype(BF), small_w[...])
        own = small[:, pl.ds(start, part)]
        decay = -own[2:3]
        feature = lax.broadcasted_iota(jnp.int32, (1, part), 1)
        count = ((p.z + 1) * heads // TP - p.z * heads // TP) * bw
        rows[0:1] = jnp.maximum(decay, 0.0) + jnp.log1p(jnp.exp(-jnp.abs(decay)))
        rows[1:2] = jax.nn.sigmoid(decay)
        rows[2 : 2 + taps] = own[3 : 3 + taps]
        rows[6:7] = jnp.where(feature < count, 1.0, 0.0)
        rows[7:8] = jnp.zeros((1, part), F32)
        gain, wide, step = small[0:1], micro * (span + HALO), 16

        def norm(z, _):
            for k in range(0, wide, step):
                vals = x_all[pl.ds(pl.multiple_of(z * wide + k, step), step)].astype(F32)
                vals = normed(vals, gain).astype(BF)
                mixed_all[pl.ds(pl.multiple_of(z * wide + k, step), step)] = vals
                if k < micro * span:
                    mixed[pl.ds(pl.multiple_of(z * micro * span + k, step), step)] = vals
            return 0

        lax.fori_loop(0, TP, norm, 0)
        loads[1].wait()

    pre_gelu[...] = dot_plain(mixed_all[...], gelu_w[...])
    pre_lru[...] = dot_plain(mixed_all[...], lru_w[...])
    block = block_w.at[pl.ds(pl.multiple_of(h * bw, 128), bw)]
    recur_head(span, micro, pre_lru, columns(rows, h, bw), block, conv, gate, state, prod, sums)


def recur(x_all, mix_w, dims):
    span, micro, _, held, bw, _ = dims
    part, width, wide = held * bw, x_all.shape[1], x_all.shape[0]
    tokens = wide // (span + HALO) * span
    whole = lambda shape: pl.BlockSpec(shape, lambda h: (0, 0))
    column = lambda rows, cols: pl.BlockSpec((rows, cols), lambda h: (0, h))
    shapes = [((8, width), F32), ((8, part), F32), ((tokens, width), BF)]
    shapes += [((wide, part), F32), ((wide, part), F32), ((tokens, part), BF)]
    shapes += [((tokens, 2 * part), F32), ((tokens, part), F32), ((tokens, part), F32)]
    shapes += [((2, tokens // span, part), F32)]
    return pl.pallas_call(
        functools.partial(recur_kernel, dims),
        grid=(held,),
        in_specs=[
            whole(x_all.shape),
            column(width, bw),
            pl.BlockSpec((width, bw), lambda h: (0, held + h)),
            ANY,
        ],
        out_specs=[
            whole((8, width)),
            whole((8, part)),
            whole((tokens, width)),
            column(wide, bw),
            column(wide, bw),
            column(tokens, bw),
            column(tokens, 2 * bw),
            column(tokens, bw),
            column(tokens, bw),
            pl.BlockSpec((2, tokens // span, bw), lambda h: (0, 0, h)),
        ],
        out_shape=[jax.ShapeDtypeStruct(*shape) for shape in shapes],
        scratch_shapes=[
            pltpu.VMEM((width, 128), BF),
            pltpu.VMEM((part, 2 * bw), BF),
            pltpu.VMEM(x_all.shape, BF),
            pltpu.SemaphoreType.DMA((2,)),
        ],
        cost_estimate=FREE,
        compiler_params=pltpu.CompilerParams(vmem_limit_bytes=GRANT),
    )(x_all, mix_w, mix_w, mix_w)


def recur_mix_kernel(dims, pre, rows, state, prod, start, mix_w, mix, parts, out_w, sem):
    span, micro, _, held, bw, _ = dims
    part = held * bw
    load = pltpu.make_async_copy(mix_w.at[:, pl.ds(2 * part, part)], out_w, sem.at[0])
    load.start()

    def one_head(h):
        pre_h, state_h, prod_h = columns(pre, h, bw), columns(state, h, bw), columns(prod, h, bw)
        rows_h, start_h, mix_h = columns(rows, h, bw), columns(start, h, bw), columns(mix, h, bw)
        for i in range(state.shape[0] // span):
            here = pl.ds(i * span, span)
            act, _ = gelu_pair(pre_h[main_rows(i, span, micro)])
            states = state_h[here] + prod_h[here] * start_h[i : i + 1]
            mix_h[here] = (states * act * rows_h[6:7]).astype(BF)

    by_heads(held, one_head)
    load.wait()

    def project(j):
        cols = pl.ds(pl.multiple_of(j * 256, 256), 256)
        parts[:, cols] = dot_right_t(mix[...], out_w[cols]).astype(BF)

    by_heads(out_w.shape[0] // 256, project)


def recur_mix(pre, rows, state, prod, start, mix_w, dims):
    tokens, part = state.shape
    width = mix_w.shape[0]
    return pl.pallas_call(
        functools.partial(recur_mix_kernel, dims),
        in_specs=[VMEM] * 5 + [ANY],
        out_specs=[VMEM, VMEM],
        out_shape=[
            jax.ShapeDtypeStruct((tokens, part), BF),
            jax.ShapeDtypeStruct((tokens, width), BF),
        ],
        scratch_shapes=[pltpu.VMEM((width, part), BF), pltpu.SemaphoreType.DMA((1,))],
        cost_estimate=FREE,
        compiler_params=pltpu.CompilerParams(vmem_limit_bytes=GRANT),
    )(pre, rows, state, prod, start, mix_w)


def recur_back_kernel(
    dims, grad, pre, rows, state, prod, start, gate, out_w, gelu, local, prods, sums, back
):
    span, micro = dims[:2]
    soft = rows[0:1]
    back[...] = dot_plain(grad[...], out_w[...])
    for i in range(back.shape[0] // span):
        here = pl.ds(i * span, span)
        act, slope = gelu_pair(pre[main_rows(i, span, micro)])
        states = state[here] + prod[here] * start[i : i + 1]
        gelu[here] = (back[here] * states * slope * rows[6:7]).astype(BF)
        _, _, decay, _, _ = gate_values(gate[here], soft)
        row = lax.broadcasted_iota(jnp.int32, decay.shape, 0)
        later = jnp.where(row < span - 1, pltpu.roll(decay, span - 1, 0), 1.0)
        later, adjoint = span_scan(later, back[here] * act, True)
        local[here] = adjoint
        prods[here] = later
        sums[i : i + 1] = decay[:1] * adjoint[:1]


def recur_back(grad, pre, rows, state, prod, start, gate, mix_w, dims):
    tokens, part = state.shape
    held, bw = dims[3:5]
    column = lambda h: (0, h)
    whole = pl.BlockSpec((tokens, bw), column)
    ends = pl.BlockSpec((start.shape[0], bw), column)
    shapes = [((tokens, part), BF), ((tokens, part), F32), ((tokens, part), F32), (start.shape, F32)]
    return pl.pallas_call(
        functools.partial(recur_back_kernel, dims),
        grid=(held,),
        in_specs=[
            pl.BlockSpec(grad.shape, lambda h: (0, 0)),
            pl.BlockSpec((pre.shape[0], bw), column),
            pl.BlockSpec((8, bw), column),
            whole,
            whole,
            ends,
            pl.BlockSpec((tokens, 2 * bw), column),
            pl.BlockSpec((mix_w.shape[0], bw), lambda h: (0, 2 * held + h)),
        ],
        out_specs=[whole, whole, whole, ends],
        out_shape=[jax.ShapeDtypeStruct(*shape) for shape in shapes],
        scratch_shapes=[pltpu.VMEM((tokens, bw), F32)],
        cost_estimate=FREE,
        compiler_params=pltpu.CompilerParams(vmem_limit_bytes=GRANT),
    )(grad, pre, rows, state, prod, start, gate, mix_w)


def recur_grad_kernel(
    span, micro, local, prods, carried, state, prod, start, gate, conv, pre, rows, block,
    blocks_out, lru_out, spill_out, rows_out, gate_grad, conv_grad,
):
    count = local.shape[0] // span
    soft, sig, own = rows[0:1], rows[1:2], rows[6:7]
    taps = [rows[k + 2 : k + 3] for k in range(4)]
    width = local.shape[1]
    add_up = lambda v: jnp.sum(v, axis=0, keepdims=True)
    decay_sum = jnp.zeros((1, width), F32)
    for i in range(count):
        here = pl.ds(i * span, span)
        adjoint = local[here] + prods[here] * carried[i : i + 1]
        states = state[here] + prod[here] * start[i : i + 1]
        row = lax.broadcasted_iota(jnp.int32, states.shape, 0)
        earlier = jnp.where(row >= 1, pltpu.roll(states, 1, 0), start[i : i + 1])
        rec_gate, in_gate, decay, square, root = gate_values(gate[here], soft)
        conv_vals = conv[here].astype(F32)
        drive = adjoint * conv_vals
        grad_log = adjoint * earlier * decay - drive * in_gate * square / root
        decay_sum = decay_sum + add_up(grad_log * rec_gate)
        gate_grad[here, :width] = (-RATE * soft * grad_log * rec_gate * (1.0 - rec_gate)).astype(BF)
        gate_grad[here, width:] = (drive * root * in_gate * (1.0 - in_gate)).astype(BF)
        conv_grad[here] = adjoint * root * in_gate
    blocks_out[...] = lax.dot_general(
        conv[...], gate_grad[...], (((0,), (0,)), ((), ())), preferred_element_type=F32
    )
    conv_grad[...] += dot_right_t(gate_grad[...], block[0])
    tap_sums = [jnp.zeros((1, width), F32) for _ in range(4)]
    for i in range(count):
        here = pl.ds(i * span, span)
        grad = conv_grad[here]
        vals = with_halo(pre, i, span, micro).astype(BF).astype(F32)
        wide = jnp.concatenate([jnp.zeros((HALO, width), F32), grad], axis=0)
        total = taps[0] * wide
        tap_sums[0] = tap_sums[0] + add_up(grad * vals[HALO:])
        for k in range(1, 4):
            total = total + taps[k] * pltpu.roll(wide, span + HALO - k, 0)
            tap_sums[k] = tap_sums[k] + add_up(grad * pltpu.roll(vals, k, 0)[HALO:])
        lru_out[here] = total[HALO:]
        spill_out[pl.ds(i * HALO, HALO)] = total[:HALO]
    rows_out[...] = jnp.zeros(rows_out.shape, F32)
    rows_out[0:1] = decay_sum * sig * own * RATE
    for k in range(4):
        rows_out[k + 1 : k + 2] = tap_sums[k] * own


def recur_grad(local, prods, carried, state, prod, start, gate, conv, pre, rows, blocks, dims):
    tokens, part = state.shape
    span, micro, _, held, bw, _ = dims
    column = lambda h: (0, h)
    whole = pl.BlockSpec((tokens, bw), column)
    ends = pl.BlockSpec((start.shape[0], bw), column)
    return pl.pallas_call(
        functools.partial(recur_grad_kernel, span, micro),
        grid=(held,),
        in_specs=[
            whole,
            whole,
            ends,
            whole,
            whole,
            ends,
            pl.BlockSpec((tokens, 2 * bw), column),
            whole,
            pl.BlockSpec((pre.shape[0], bw), column),
            pl.BlockSpec((8, bw), column),
            pl.BlockSpec((1, bw, 2 * bw), lambda h: (h, 0, 0)),
        ],
        out_specs=[
            pl.BlockSpec((bw, 2 * bw), lambda h: (h, 0)),
            whole,
            pl.BlockSpec((start.shape[0] * HALO, bw), column),
            pl.BlockSpec((8, bw), column),
        ],
        out_shape=[
            jax.ShapeDtypeStruct((part, 2 * bw), F32),
            jax.ShapeDtypeStruct((tokens, part), F32),
            jax.ShapeDtypeStruct((start.shape[0] * HALO, part), F32),
            jax.ShapeDtypeStruct((8, part), F32),
        ],
        scratch_shapes=[pltpu.VMEM((tokens, 2 * bw), BF), pltpu.VMEM((tokens, bw), F32)],
        cost_estimate=FREE,
        compiler_params=pltpu.CompilerParams(vmem_limit_bytes=GRANT),
    )(local, prods, carried, state, prod, start, gate, conv, pre, rows, blocks)


def recur_in_kernel(dims, gelu, lru, spill, rows, small, mixed, mix_w, pair, parts, gains):
    span, _, _, held, bw, _ = dims
    part = held * bw

    @pl.when(pl.program_id(0) == 0)
    def _():
        pair[:, :part] = gelu[...]

        def one_head(h):
            lru_h, spill_h, own = columns(lru, h, bw), columns(spill, h, bw), columns(rows, h, bw)[6:7]
            cols = pl.ds(pl.multiple_of((held + h) * bw, 128), bw)
            for i in range(lru.shape[0] // span):
                vals = lru_h[pl.ds(i * span, span)]
                late = vals[span - HALO :] + spill_h[pl.ds(i * HALO, HALO)]
                vals = jnp.concatenate([vals[: span - HALO], late], axis=0) * own
                pair[pl.ds(i * span, span), cols] = vals.astype(BF)

        by_heads(held, one_head)

    grad = dot_right_t(pair[...], mix_w[...])
    parts[...] = grad.astype(BF)
    gain = jnp.sum(grad * mixed[...].astype(F32), axis=0, keepdims=True)
    gains[0:1] = gain / small[0:1]


def recur_in(gelu, lru, spill, rows, small, mixed, mix_w, dims):
    tokens, part = gelu.shape
    width, chunk = mix_w.shape[0], 256
    whole = lambda v: pl.BlockSpec(v.shape, lambda j: (0, 0))
    column = lambda j: (0, j)
    return pl.pallas_call(
        functools.partial(recur_in_kernel, dims),
        grid=(width // chunk,),
        in_specs=[
            whole(gelu),
            whole(lru),
            whole(spill),
            whole(rows),
            pl.BlockSpec((8, chunk), column),
            pl.BlockSpec((tokens, chunk), column),
            pl.BlockSpec((chunk, 2 * part), lambda j: (j, 0)),
        ],
        out_specs=[
            pl.BlockSpec((tokens, 2 * part), lambda j: (0, 0)),
            pl.BlockSpec((tokens, chunk), column),
            pl.BlockSpec((8, chunk), column),
        ],
        out_shape=[
            jax.ShapeDtypeStruct((tokens, 2 * part), BF),
            jax.ShapeDtypeStruct((tokens, width), BF),
            jax.ShapeDtypeStruct((8, width), F32),
        ],
        cost_estimate=FREE,
        compiler_params=pltpu.CompilerParams(vmem_limit_bytes=GRANT),
    )(gelu, lru, spill, rows, small, mixed, mix_w)


def device(p, f=None, z=None, x=None, c=None):
    f, z = p.f if f is None else f, p.z if z is None else z
    x, c = p.x if x is None else x, p.c if c is None else c
    return (f, ((p.r * TP + z) * 2 + x) * 2 + c)


def copy_to(src, dst, sems, index, dev):
    return pltpu.make_async_remote_copy(
        src_ref=src,
        dst_ref=dst,
        send_sem=sems[0].at[index],
        recv_sem=sems[1].at[index],
        device_id=dev,
        device_id_type=MESH,
    )


def pairs(*shape):
    return [pltpu.SemaphoreType.DMA(shape), pltpu.SemaphoreType.DMA(shape)]


def greet(devices):
    barrier = pltpu.get_barrier_semaphore()
    for dev in devices:
        pl.semaphore_signal(barrier, inc=1, device_id=dev, device_id_type=MESH)
    pl.semaphore_wait(barrier, len(devices))


def by_rows(count, body, step=16):
    def turn(i, _):
        body(pl.ds(pl.multiple_of(i * step, step), step))
        return 0

    assert count % step == 0
    lax.fori_loop(0, count // step, turn, 0)


class Gather:
    def __init__(self, p, out, ups, downs):
        self.p, self.out, self.ups, self.downs = p, out, ups, downs
        self.up = device(p, z=jnp.minimum(p.z + 1, TP - 1))
        self.down = device(p, z=jnp.maximum(p.z - 1, 0))

    def begin(self, h, src):
        z = self.p.z

        @pl.when(z < TP - 1)
        def _():
            copy_to(src, self.out.at[z, h], self.ups, (0, h), self.up).start()

        @pl.when(z > 0)
        def _():
            copy_to(src, self.out.at[z, h], self.downs, (0, h), self.down).start()

    def step(self, k, h):
        z, out = self.p.z, self.out

        @pl.when(z >= k)
        def _():
            block = out.at[z - k, h]
            copy_to(block, block, self.ups, (k - 1, h), self.up).wait_recv()
            if k < TP - 1:

                @pl.when(z < TP - 1)
                def _():
                    copy_to(block, block, self.ups, (k, h), self.up).start()

        @pl.when(z <= TP - 1 - k)
        def _():
            block = out.at[z + k, h]
            copy_to(block, block, self.downs, (k - 1, h), self.down).wait_recv()
            if k < TP - 1:

                @pl.when(z > 0)
                def _():
                    copy_to(block, block, self.downs, (k, h), self.down).start()

    def close(self, halves):
        z, block = self.p.z, self.out.at[0, 0]
        for h in range(halves) if isinstance(halves, int) else halves:
            for k in range(TP - 1):

                @pl.when((z >= k) & (z < TP - 1))
                def _():
                    copy_to(block, block, self.ups, (k, h), self.up).wait_send()

                @pl.when((z <= TP - 1 - k) & (z > 0))
                def _():
                    copy_to(block, block, self.downs, (k, h), self.down).wait_send()


class LineSum:
    def __init__(self, p, parts, scratch):
        self.p, self.parts = p, parts
        self.got_up, self.got_down, self.out_up, self.out_down = scratch[:4]
        self.ups, self.downs = scratch[4:6], scratch[6:8]
        self.halves, self.rows = parts.shape[1:3]
        self.up = device(p, z=jnp.minimum(p.z + 1, TP - 1))
        self.down = device(p, z=jnp.maximum(p.z - 1, 0))

    @staticmethod
    def scratch(parts):
        block = parts[1:]
        return [
            pltpu.VMEM((TP - 1,) + block, BF),
            pltpu.VMEM((TP - 1,) + block, BF),
            pltpu.VMEM((TP - 2,) + block, BF),
            pltpu.VMEM((TP - 2,) + block, BF),
            *pairs(TP - 1, parts[1]),
            *pairs(TP - 1, parts[1]),
        ]

    def clear(self):
        z = self.p.z

        @pl.when(z == 0)
        def _():
            for h in range(self.halves):
                by_rows(self.rows, lambda at: self.fill(self.got_up, h, at))

        @pl.when(z == TP - 1)
        def _():
            for h in range(self.halves):
                by_rows(self.rows, lambda at: self.fill(self.got_down, h, at))

    def fill(self, ref, h, at):
        ref[0, h, at] = jnp.zeros((at.size, ref.shape[-1]), BF)

    def one_way(self, k, h, place, block, got, out, sems, dev):
        @pl.when(place == 0)
        def _():
            copy_to(self.parts.at[block, h], got.at[k - 1, h], sems, (k - 1, h), dev).start()

        if k < TP - 1:

            @pl.when((place >= 1) & (place + k <= TP - 1))
            def _():
                copy_to(got.at[k, h], got.at[k, h], sems, (k, h), dev).wait_recv()

                def add(at):
                    total = self.parts[block, h, at].astype(F32) + got[k, h, at].astype(F32)
                    out[k - 1, h, at] = total.astype(BF)

                by_rows(self.rows, add)
                copy_to(out.at[k - 1, h], got.at[k - 1, h], sems, (k - 1, h), dev).start()

    def step(self, k, h):
        z = self.p.z
        block = jnp.minimum(z + k, TP - 1)
        self.one_way(k, h, z, block, self.got_up, self.out_up, self.ups, self.up)
        block = jnp.maximum(z - k, 0)
        self.one_way(k, h, TP - 1 - z, block, self.got_down, self.out_down, self.downs, self.down)

    def arrive(self, h):
        z = self.p.z

        @pl.when(z >= 1)
        def _():
            got = self.got_up.at[0, h]
            copy_to(got, got, self.ups, (0, h), self.up).wait_recv()

        @pl.when(z <= TP - 2)
        def _():
            got = self.got_down.at[0, h]
            copy_to(got, got, self.downs, (0, h), self.down).wait_recv()

    def total(self, h, at):
        total = self.parts[self.p.z, h, at].astype(F32) + self.got_up[0, h, at].astype(F32)
        return total + self.got_down[0, h, at].astype(F32)

    def close(self):
        z, got = self.p.z, self.got_up.at[0, 0]
        for h in range(self.halves):
            for k in range(1, TP):

                @pl.when(z + k <= TP - 1)
                def _():
                    copy_to(got, got, self.ups, (k - 1, h), self.up).wait_send()

                @pl.when(z - k >= 0)
                def _():
                    copy_to(got, got, self.downs, (k - 1, h), self.down).wait_send()


def greet_line(p, others=()):
    barrier = pltpu.get_barrier_semaphore()
    for dev in others:
        pl.semaphore_signal(barrier, inc=1, device_id=dev, device_id_type=MESH)

    @pl.when(p.z > 0)
    def _():
        pl.semaphore_signal(barrier, inc=1, device_id=device(p, z=p.z - 1), device_id_type=MESH)

    @pl.when(p.z < TP - 1)
    def _():
        pl.semaphore_signal(barrier, inc=1, device_id=device(p, z=p.z + 1), device_id_type=MESH)

    inner = (p.z > 0) & (p.z < TP - 1)

    @pl.when(inner)
    def _():
        pl.semaphore_wait(barrier, len(others) + 2)

    @pl.when(jnp.logical_not(inner))
    def _():
        pl.semaphore_wait(barrier, len(others) + 1)


class Spread:
    KINDS = ((0, 0), (0, 1), (1, 0), (1, 1))

    def __init__(self, p, whole, sems):
        self.p, self.whole, self.started = p, whole, []
        self.xs, self.fs, self.gs, self.cs = sems[0:2], sems[2:4], sems[4:6], sems[6:8]
        self.to_x, self.to_f = device(p, x=1 - p.x), device(p, f=1 - p.f)
        self.to_c = device(p, c=1 - p.c)

    @staticmethod
    def scratch():
        return [*pairs(TP), *pairs(TP), *pairs(TP), *pairs(4, TP)]

    def slot(self, kind, d, other_core=False):
        p, (f, x) = self.p, self.KINDS[kind]
        c = 1 - p.c if other_core else p.c
        return self.whole.at[(p.f + f) % 2, 0, (p.z - d) % TP, (p.x + x) % 2, c]

    def send(self, src, dst, sems, index, dev):
        copy = copy_to(src, dst, sems, index, dev)
        copy.start()
        self.started.append(copy)

    def wait(self, ref, sems, index):
        copy_to(ref, ref, sems, index, self.to_x).wait_recv()

    def spread(self, d, src=None):
        dst = self.slot(0, d)
        src = dst if src is None else src
        self.send(src, dst, self.xs, (d,), self.to_x)
        self.send(src, dst, self.fs, (d,), self.to_f)
        self.send(src, dst, self.cs, (0, d), self.to_c)

    def given(self, d, own, by_x, by_f):
        self.send(own, self.slot(0, d), self.cs, (0, d), self.to_c)
        self.send(by_x, self.slot(1, d), self.cs, (1, d), self.to_c)
        self.send(by_f, self.slot(2, d), self.cs, (2, d), self.to_c)
        if d % 2 == 0:
            self.send(by_x, self.slot(1, d), self.gs, (d,), self.to_f)
        else:
            self.send(by_f, self.slot(2, d), self.gs, (d,), self.to_x)

    def sides(self, d):
        ref = self.slot(1, d)
        self.wait(ref, self.xs, (d,))
        if d % 2 == 0:
            self.send(ref, ref, self.gs, (d,), self.to_f)
        self.send(ref, ref, self.cs, (1, d), self.to_c)
        ref = self.slot(2, d)
        self.wait(ref, self.fs, (d,))
        if d % 2 == 1:
            self.send(ref, ref, self.gs, (d,), self.to_x)
        self.send(ref, ref, self.cs, (2, d), self.to_c)

    def corner(self, d):
        ref = self.slot(3, d)
        self.wait(ref, self.gs, (d,))
        self.send(ref, ref, self.cs, (3, d), self.to_c)

    def close(self, pieces):
        for kind in range(4):
            for d in pieces:
                self.wait(self.slot(kind, d, True), self.cs, (kind, d))
        for copy in self.started:
            copy.wait_send()


def pack_kernel(bw, gelu, lru, out_t, blocks, small, gate, up, down_t, mix, *ffw):
    p = Place()
    heads = gelu.shape[1] // bw
    part, ffw_part = -(-heads // TP) * bw, gate.shape[1] // TP
    for d in range(TP):
        z = (p.z + d) % TP
        cols = pl.ds(pl.multiple_of(z * heads // TP * bw, 128), part)
        sources = [gelu[:, cols], lru[:, cols], out_t[:, cols], blocks[...], small[...]]
        offset = 0
        for source in sources:
            mix[d, :, offset : offset + source.shape[1]] = source
            offset += source.shape[1]
        cols = pl.ds(pl.multiple_of(z * ffw_part, 128), ffw_part)
        for i, source in enumerate((gate, up, down_t)):
            ffw[d][:, i * ffw_part : (i + 1) * ffw_part] = source[:, cols]


def pack(weights, bw):
    rows, lru_width = weights[0].shape
    part = -(-lru_width // bw // TP) * bw
    mix_cols = 3 * part + weights[3].shape[1] + weights[4].shape[1]
    piece = jax.ShapeDtypeStruct((rows, 3 * weights[5].shape[1] // TP), BF)
    mix, *ffw = pl.pallas_call(
        functools.partial(pack_kernel, bw),
        in_specs=[VMEM] * 8,
        out_specs=[VMEM] * (1 + TP),
        out_shape=[jax.ShapeDtypeStruct((TP, rows, mix_cols), BF), *[piece] * TP],
        compiler_params=pltpu.CompilerParams(vmem_limit_bytes=GRANT),
    )(*weights)
    return mix, ffw


def intake_kernel(
    mix_p, ffw_0, ffw_1, x_p, cot_p, mix_w, ffw_w, piece_1, x_all, cot_all,
    zs, zr, us, ur, vs, vr, cus, cur, cvs, cvr, local, *sems
):
    p = Place()
    mix, ffw = Spread(p, mix_w, sems[:8]), Spread(p, ffw_w, sems[8:])
    to_z = [device(p, z=(p.z + d) % TP) for d in range(TP)]
    greet(to_z[1:] + [mix.to_x, mix.to_f, mix.to_c])
    started = []

    def along_z(i, src, dst, d):
        copy = copy_to(src, dst, (zs, zr), (i,), to_z[d])
        copy.start()
        started.append(copy)

    def from_z(i, ref):
        copy_to(ref, ref, (zs, zr), (i,), to_z[1]).wait_recv()

    for d in (1, 3, 2):
        along_z(d, mix_p.at[d], mix.slot(0, 0), d)
    mix.spread(0, mix_p.at[0])
    ffw.spread(0, ffw_0)
    stays = [
        pltpu.make_async_copy(mix_p.at[0], mix.slot(0, 0), local.at[0]),
        pltpu.make_async_copy(ffw_0, ffw.slot(0, 0), local.at[1]),
        pltpu.make_async_copy(x_p, x_all.at[p.z], local.at[2]),
        pltpu.make_async_copy(cot_p, cot_all.at[p.z, 0], local.at[3]),
    ]
    for copy in stays:
        copy.start()
    line = Gather(p, x_all, (us, ur), (vs, vr))
    cot = Gather(p, cot_all, (cus, cur), (cvs, cvr))
    for d in (1, 3):
        from_z(d, mix.slot(0, d))
        mix.spread(d)
    for h in range(x_p.shape[0]):
        line.begin(h, x_p.at[h])
    cot.begin(0, cot_p)
    from_z(2, mix.slot(0, 2))
    mix.spread(2)
    along_z(0, ffw_1, piece_1, 1)
    mix.sides(0)
    ffw.sides(0)
    mix.corner(0)
    for h in range(x_p.shape[0]):
        line.step(1, h)
    cot.step(1, 0)
    for d in (1, 3):
        mix.sides(d)
    ffw.corner(0)
    for h in range(x_p.shape[0]):
        line.step(2, h)
    cot.step(2, 0)
    for d in (1, 3):
        mix.corner(d)
    mix.sides(2)
    for h in range(x_p.shape[0]):
        line.step(3, h)
    cot.step(3, 0)
    mix.corner(2)
    from_z(0, piece_1)
    mix.close(range(TP))
    ffw.close((0,))
    for copy in started:
        copy.wait_send()
    line.close(x_p.shape[0])
    cot.close(1)
    for copy in stays:
        copy.wait()


def intake(mix_p, ffw_0, ffw_1, x_p, cot_p, p):
    whole = lambda v: jax.ShapeDtypeStruct((p.fs, 1, TP, 2, 2) + v.shape[-2:], BF)
    mix_w, ffw_w, piece_1, x_all, cot_all = pl.pallas_call(
        intake_kernel,
        in_specs=[ANY] * 5,
        out_specs=[ANY] * 5,
        out_shape=[
            whole(mix_p),
            whole(ffw_0),
            jax.ShapeDtypeStruct(ffw_1.shape, BF),
            jax.ShapeDtypeStruct((TP,) + x_p.shape, BF),
            jax.ShapeDtypeStruct((TP, 1) + cot_p.shape, BF),
        ],
        scratch_shapes=[
            *pairs(TP),
            *pairs(TP - 1, x_p.shape[0]),
            *pairs(TP - 1, x_p.shape[0]),
            *pairs(TP - 1, 1),
            *pairs(TP - 1, 1),
            pltpu.SemaphoreType.DMA((4,)),
            *Spread.scratch(),
            *Spread.scratch(),
        ],
        compiler_params=pltpu.CompilerParams(collective_id=0, has_side_effects=True),
    )(mix_p, ffw_0, ffw_1, x_p, cot_p)
    return mix_w.reshape(-1, mix_p.shape[-1]), ffw_w, piece_1, x_all, cot_all


class Stream:
    def __init__(self, pick, count, buffers, sems):
        self.pick, self.count, self.buffers, self.sems = pick, count, buffers, sems

    def load(self, i):
        slot = i % 2
        return pltpu.make_async_copy(self.pick(i), self.buffers.at[slot], self.sems.at[slot])

    def start(self):
        self.load(0).start()

    def run(self, low, high, body):
        def turn(i, _):
            @pl.when(i + 1 < self.count)
            def _():
                self.load(i + 1).start()

            self.load(i).wait()
            body(i, self.buffers.at[i % 2])
            return 0

        lax.fori_loop(low, high, turn, 0)


def flat(block):
    return block.reshape(-1, block.shape[-1])


FFW_CHUNK = 256


def ffw_streams(ffw_w, part, buffers):
    chunks, rest = part // FFW_CHUNK, part % FFW_CHUNK
    col = lambda base, i: pl.ds(pl.multiple_of(base + i * FFW_CHUNK, 128), FFW_CHUNK)
    pick = lambda base: lambda i: ffw_w.at[:, 0, :, :, :, :, col(base, i)]
    half = TP // 2
    rows = lambda cols: lambda i: ffw_w.at[i // 2, 0, pl.ds(i % 2 * half, half), :, :, :, cols]
    gate = Stream(pick(0), chunks, buffers[0], buffers[1])
    up = Stream(pick(part), chunks, buffers[2], buffers[3])
    down = Stream(pick(2 * part), chunks, buffers[0], buffers[1])
    down_rows = Stream(rows(pl.ds(2 * part, part)), 4, buffers[4], buffers[5])
    both_rows = Stream(rows(pl.ds(0, 2 * part)), 4, buffers[6], buffers[7])
    return gate, up, down, down_rows, both_rows


class Feed:
    def __init__(self, x, cot, ffw_w, outs, vals, scratch):
        self.x, self.cot, self.vals = x, cot, vals
        self.hidden, self.grad_pair, self.out_parts, self.in_parts = outs
        self.part = part = self.hidden.shape[1]
        self.chunks, self.rest = part // FFW_CHUNK, part % FFW_CHUNK
        streams = ffw_streams(ffw_w, part, scratch[:8])
        self.gate, self.up, self.down, self.down_rows, self.both_rows = streams
        self.tails, tail_sems = scratch[8:10]
        self.last = last = self.chunks * FFW_CHUNK
        self.loads = [
            pltpu.make_async_copy(
                ffw_w.at[:, 0, :, :, :, :, pl.ds(k * part + last, self.rest)],
                self.tails.at[k],
                tail_sems.at[k],
            )
            for k in range(3)
        ]

    def begin(self):
        self.gate.start()
        self.up.start()
        for load in self.loads:
            load.start()
        self.down_rows.start()
        self.both_rows.start()

    def cols(self, i, base):
        return pl.ds(pl.multiple_of(base + i * FFW_CHUNK, 128), FFW_CHUNK)

    def forward_cols(self, cols, other, gate_w, up_w):
        gate_vals = dot_plain(self.x[...], gate_w)
        up_vals = dot_plain(self.x[...], up_w)
        self.vals[:, cols] = gate_vals
        self.vals[:, other] = up_vals
        self.hidden[:, cols] = (gelu_pair(gate_vals)[0] * up_vals).astype(BF)

    def forward(self, low, high):
        def turn(i, _):
            for stream in (self.gate, self.up):

                @pl.when(i + 1 < self.chunks)
                def _(stream=stream):
                    stream.load(i + 1).start()

                stream.load(i).wait()
            weights = [flat(stream.buffers[i % 2]) for stream in (self.gate, self.up)]
            self.forward_cols(self.cols(i, 0), self.cols(i, self.part), *weights)
            return 0

        lax.fori_loop(low, high, turn, 0)

    def forward_end(self):
        self.down.start()
        for load in self.loads:
            load.wait()
        cols = pl.ds(self.last, self.rest), pl.ds(self.part + self.last, self.rest)
        self.forward_cols(*cols, flat(self.tails[0]), flat(self.tails[1]))

    def by_weight_rows(self, stream, source, out, low=0, high=4):
        def body(i, buffer):
            weights = flat(buffer[...])
            count = weights.shape[0]
            cols = pl.ds(pl.multiple_of(i * count, 128), count)
            out[:, cols] = dot_right_t(source[...], weights).astype(BF)

        stream.run(low, high, body)

    def forward_out(self):
        self.by_weight_rows(self.down_rows, self.hidden, self.out_parts)

    def backward_cols(self, cols, other, weights):
        grad = dot_plain(self.cot[...], weights)
        act, slope = gelu_pair(self.vals[:, cols])
        self.grad_pair[:, cols] = (grad * self.vals[:, other] * slope).astype(BF)
        self.grad_pair[:, other] = (grad * act).astype(BF)

    def backward(self, low, high):
        def body(i, buffer):
            self.backward_cols(self.cols(i, 0), self.cols(i, self.part), flat(buffer[...]))

        self.down.run(low, high, body)

    def backward_end(self):
        cols = pl.ds(self.last, self.rest), pl.ds(self.part + self.last, self.rest)
        self.backward_cols(*cols, flat(self.tails[2]))

    def backward_in(self, low, high):
        self.by_weight_rows(self.both_rows, self.grad_pair, self.in_parts, low, high)


def ffw_scratch(ffw_w, part):
    f, _, z, x, c, rows, _ = ffw_w.shape
    column = lambda width: pltpu.VMEM((2, f, z, x, c, rows, width), BF)
    wide = lambda width: pltpu.VMEM((2, z // 2, x, c, rows, width), BF)
    pair = pltpu.SemaphoreType.DMA((2,))
    return [
        column(FFW_CHUNK), pair, column(FFW_CHUNK), pair, wide(part), pair, wide(2 * part), pair,
        pltpu.VMEM((3, f, z, x, c, rows, part % FFW_CHUNK), BF),
        pltpu.SemaphoreType.DMA((3,)),
    ]


def middle_kernel(with_ffw, *refs):
    parts, x_zero, gain, cot_p, cot_first, piece_1, by_x, by_f, piece_2, piece_3, _ = refs[:11]
    x_one_out, ffw_out, cot_out, ffw_w, *refs = refs[11:]
    if with_ffw:
        hidden_out, pair_out, parts_out, in_out, *refs = refs
    x_one, ffw_all, cot_all, own, local, gu0, gu1, gd0, gd1, cu0, cu1, cd0, cd1 = refs[:13]
    p = Place()
    line = LineSum(p, parts, refs[13:21])
    out = Gather(p, ffw_all, (gu0, gu1), (gd0, gd1))
    cot = Gather(p, cot_all, (cu0, cu1), (cd0, cd1))
    halves, rows = parts.shape[1:3]
    line.clear()
    stays = []

    def stay(src, dst):
        copy = pltpu.make_async_copy(src, dst, local.at[len(stays)])
        copy.start()
        stays.append(copy)

    if with_ffw:
        ffw = Spread(p, ffw_w, refs[21:29])
        outs, vals, buffers = refs[29:33], refs[33], refs[34:44]
        bounce_sems = refs[44]
        greet_line(p, (ffw.to_x, ffw.to_f, ffw.to_c))
    else:
        greet_line(p)
    side = lambda name, *args: getattr(ffw, name)(*args) if with_ffw else None
    for h in range(halves):
        line.step(TP - 1, h)
    stay(cot_first, cot_all.at[:, pl.ds(0, 1)])
    side("given", 1, piece_1, by_x, by_f)
    side("spread", 3, piece_3)
    side("spread", 2, piece_2)
    if with_ffw:
        part = vals.shape[1] // 2
        moves = [(piece_1, 0, 1), (by_x, 1, 1), (by_f, 2, 1), (piece_3, 0, 3), (piece_2, 0, 2)]
        steps = [(src, ffw.slot(kind, d), k) for src, kind, d in moves for k in range(2)]

        def bounce(i, out):
            src, dst, k = steps[i]
            cols = pl.ds(0, 2 * part) if k == 0 else pl.ds(2 * part, part)
            space = buffers[6 - 2 * k].at[i // 2 % 2, 0, 0, 0]
            if out:
                return pltpu.make_async_copy(space, dst.at[:, cols], bounce_sems.at[i % 4])
            return pltpu.make_async_copy(src.at[:, cols], space, bounce_sems.at[4])

        for i in range(len(steps)):
            if i >= 4:
                bounce(i - 4, True).wait()
            bounce(i, False).start()
            bounce(i, False).wait()
            bounce(i, True).start()
        for i in range(len(steps) - 4, len(steps)):
            bounce(i, True).wait()
    for k in range(TP - 2, 0, -1):
        for h in range(halves):
            line.step(k, h)
    for h in range(halves):
        line.arrive(h)

        def finish(at, h=h):
            value = x_zero[h, at].astype(F32) + line.total(h, at)
            x_one[h, at] = value
            own[h, at] = normed(value, gain[...]).astype(BF)

        by_rows(rows, finish)
        out.begin(h, own.at[h])
        stay(own.at[h], ffw_all.at[p.z, h])
    for h in range(halves):
        out.step(1, h)
    for d in (3, 2):
        side("sides", d)
    for h in range(halves):
        out.step(2, h)
    cot.begin(1, cot_p)
    stay(cot_p, cot_all.at[p.z, 1])
    side("corner", 1)
    for d in (3, 2):
        side("corner", d)
    for h in range(halves):
        out.step(3, h)
    cot.step(1, 1)
    side("close", (1, 2, 3))
    if not with_ffw:
        cot.step(2, 1)
        cot.step(3, 1)
    for copy in stays:
        copy.wait()
    done = len(stays)
    stay(x_one, x_one_out)
    stay(ffw_all, ffw_out)
    if not with_ffw:
        stay(cot_all, cot_out)
    else:
        tokens = lambda ref: ref.reshape(TP * halves * rows, parts.shape[3])
        hidden, pair, out_parts, in_parts = outs
        flat_outs = (hidden, pair, tokens(out_parts), in_parts)
        feed = Feed(tokens(ffw_all), tokens(cot_all), ffw_w, flat_outs, vals, buffers)
        feed.begin()
        feed.forward(0, 2)
        cot.step(2, 1)
        feed.forward(2, 6)
        cot.step(3, 1)
        stay(cot_all, cot_out)
        feed.forward(6, feed.chunks)
        feed.forward_end()
        feed.forward_out()
        stay(hidden, hidden_out)
        stay(out_parts, parts_out)
        feed.backward(0, feed.chunks)
        feed.backward_end()
        stay(pair, pair_out)
        feed.backward_in(0, 4)
        stay(in_parts, in_out)
    line.close()
    out.close(halves)
    cot.close((1,))
    for copy in stays[done:]:
        copy.wait()


def middle(parts, x_zero, gain, cot_p, cot_first, pieces, ffw_w):
    shape = parts.shape
    with_ffw = ffw_w is not None
    line = (TP, 2) + cot_p.shape
    outs, extra = [], []
    if with_ffw:
        tokens, part = shape[0] * shape[1] * shape[2], ffw_w.shape[-1] // 3
        assert part // FFW_CHUNK >= 6 and part % FFW_CHUNK
        outs = [(tokens, part), (tokens, 2 * part), shape, (tokens, shape[3])]
        extra = [
            *Spread.scratch(),
            *(pltpu.VMEM(kept, BF) for kept in outs),
            pltpu.VMEM((tokens, 2 * part), F32),
            *ffw_scratch(ffw_w, part),
            pltpu.SemaphoreType.DMA((5,)),
        ]
    else:
        ffw_w = jnp.zeros((16, 128), BF)
        pieces = [ffw_w] * 5
    return pl.pallas_call(
        functools.partial(middle_kernel, with_ffw),
        in_specs=[VMEM] * 3 + [ANY] * 8,
        out_specs=[ANY] * (4 + len(outs)),
        out_shape=[
            jax.ShapeDtypeStruct(shape[1:], F32),
            jax.ShapeDtypeStruct(shape, BF),
            jax.ShapeDtypeStruct(line, BF),
            jax.ShapeDtypeStruct(ffw_w.shape, BF),
            *(jax.ShapeDtypeStruct(out, BF) for out in outs),
        ],
        input_output_aliases={10: 3},
        scratch_shapes=[
            pltpu.VMEM(shape[1:], F32),
            pltpu.VMEM(shape, BF),
            pltpu.VMEM(line, BF),
            pltpu.VMEM(shape[1:], BF),
            pltpu.SemaphoreType.DMA((shape[1] + 10,)),
            *pairs(TP - 1, shape[1]),
            *pairs(TP - 1, shape[1]),
            *pairs(TP - 1, 2),
            *pairs(TP - 1, 2),
            *LineSum.scratch(shape),
            *extra,
        ],
        compiler_params=pltpu.CompilerParams(
            collective_id=1, has_side_effects=True, vmem_limit_bytes=GRANT
        ),
    )(parts, x_zero, gain, cot_p, cot_first, *pieces, ffw_w)


def norm_back(values, gain, grad):
    inv = lax.rsqrt(jnp.mean(values * values, axis=-1, keepdims=True) + EPS)
    unit = values * inv
    through = grad * gain
    inner = jnp.mean(through * unit, axis=-1, keepdims=True)
    return inv * (through - unit * inner), grad * unit


class Fold:
    ORDER = ((0, 1, 1), (1, 1, 1), (0, 0, 1), (1, 1, 0), (0, 1, 0), (1, 0, 1), (0, 0, 0), (1, 0, 0))

    def __init__(self, p, grad, cores, scratch):
        self.p, self.grad, self.cores = p, grad, cores
        self.sums, self.stage, self.got, self.got_late = scratch[:4]
        self.near, self.staged = scratch[4:6]
        self.core_sems, self.early, self.late = scratch[6:8], scratch[8:10], scratch[10:12]
        self.to = (device(p, x=1 - p.x), device(p, f=1 - p.f))
        self.to_c = device(p, c=1 - p.c)

    @staticmethod
    def shapes(grad, staged):
        block = (TP // 2,) + grad.shape[-2:]
        waiting = (2,) if staged else (2, 2, 2)
        return jax.ShapeDtypeStruct((2, 2, 2) + block, BF), [
            pltpu.VMEM((2, 2, 2) + block, BF),
            pltpu.VMEM(waiting + block, BF),
            pltpu.VMEM((2, 2) + block, BF),
            pltpu.VMEM((2,) + block, BF),
            pltpu.SemaphoreType.DMA((8,)),
            pltpu.SemaphoreType.DMA((2,)),
            *pairs(8),
            *pairs(2, 2),
            *pairs(2),
        ]

    def block(self, way, f_rel, x_rel, c):
        p, half = self.p, TP // 2
        f, x = (p.f + f_rel) % 2, (p.x + x_rel) % 2
        return self.grad.at[f, 0, pl.ds(way * half, half), x, c]

    def cross(self, i):
        name = self.ORDER[i]
        src = self.block(*name, 1 - self.p.c)
        dst = self.stage if self.cores is None else self.cores
        return copy_to(src, dst.at[name], self.core_sems, (i,), self.to_c)

    def load(self, i):
        name = self.ORDER[i]
        return pltpu.make_async_copy(
            self.block(*name, self.p.c), self.sums.at[name], self.near.at[i]
        )

    def fetch(self, i):
        src = self.cores.at[self.ORDER[i]]
        return pltpu.make_async_copy(src, self.stage.at[i % 2], self.staged.at[i % 2])

    def first(self, way, block):
        src = self.sums.at[(0, block, 1) if way == 0 else (1, 1, block)]
        return copy_to(src, self.got.at[way, block], self.early, (way, block), self.to[way])

    def second(self, way):
        src = self.sums.at[(0, 1, 0) if way == 0 else (1, 0, 1)]
        return copy_to(src, self.got_late.at[way], self.late, (way,), self.to[1 - way])

    def add(self, name, *others):
        rows = self.sums.shape[-2]

        def turn(at):
            for k in range(TP // 2):
                total = self.sums[(*name, k, at)].astype(F32)
                for other in others:
                    total = total + other[k, at].astype(F32)
                self.sums[(*name, k, at)] = total.astype(BF)

        by_rows(rows, turn)

    def begin(self, blocks=range(8)):
        for i in blocks:
            self.cross(i).start()
            self.load(i).start()

    def issue(self, i):
        self.cross(i).wait_recv()
        self.fetch(i).start()

    def join(self, i):
        if self.cores is None:
            self.cross(i).wait_recv()
            self.load(i).wait()
            self.add(self.ORDER[i], self.stage.at[self.ORDER[i]])
        else:
            if i == 0:
                self.issue(0)
            if i + 1 < 8:
                self.issue(i + 1)
            self.fetch(i).wait()
            self.load(i).wait()
            self.add(self.ORDER[i], self.stage.at[i % 2])
        if i < 4:
            way = self.ORDER[i][0]
            self.first(way, self.ORDER[i][1 + way]).start()

    def middle(self):
        for way in range(2):
            self.first(way, 1).wait_recv()
            self.add((0, 1, 0) if way == 0 else (1, 0, 1), self.got.at[way, 1])
            self.second(way).start()

    def finish(self):
        for way in range(2):
            self.first(way, 0).wait_recv()
            self.second(way).wait_recv()
            self.add((way, 0, 0), self.got.at[way, 0], self.got_late.at[way])

    def result(self, z):
        return self.sums.at[z // (TP // 2), 0, 0, z % (TP // 2)]

    def close(self):
        for i in range(8):
            self.cross(i).wait_send()
        for way in range(2):
            self.second(way).wait_send()
            for block in range(2):
                self.first(way, block).wait_send()


def folds_of(p, grads, cores, scratch):
    return [Fold(p, g, c, scratch[12 * i : 12 * i + 12]) for i, (g, c) in enumerate(zip(grads, cores))]


GRAD_CHUNK = 640


class Outer:
    def __init__(self, grad, left, right, turned, buffers, sems):
        self.grad, self.left, self.right, self.turned = grad, left, right, turned
        self.buffers, self.sems = buffers, sems
        self.wide = buffers.shape[-1]
        self.across = grad.shape[-1] // self.wide
        self.count = 4 * self.across

    def place(self, i):
        return (lax.axis_index("fsdp") * 2 + 2 + i // self.across) % 4

    def store(self, i):
        k, half = self.place(i), TP // 2
        cols = pl.ds(pl.multiple_of(i % self.across * self.wide, 128), self.wide)
        dst = self.grad.at[k // 2, 0, pl.ds(k % 2 * half, half), :, :, :, cols]
        return pltpu.make_async_copy(self.buffers.at[i % 2], dst, self.sems.at[i % 2])

    def run(self, low, high):
        rows = self.turned.shape[0]

        def turn(i, _):
            @pl.when(i % self.across == 0)
            def _():
                cols = pl.ds(pl.multiple_of(self.place(i) * rows, 128), rows)
                self.turned[...] = jnp.transpose(self.left[:, cols])

            @pl.when(i >= low + 2)
            def _():
                self.store(i - 2).wait()

            cols = pl.ds(pl.multiple_of(i % self.across * self.wide, 128), self.wide)
            chunk = dot_plain(self.turned[...], self.right[:, cols]).astype(BF)
            self.buffers[i % 2] = chunk.reshape(self.buffers.shape[1:])
            self.store(i).start()
            return 0

        lax.fori_loop(low, high, turn, 0)

    def flush(self, done):
        for i in (done - 2, done - 1):
            self.store(i).wait()


def turn_kernel(count, *refs):
    parts, out_parts, x_one, cot, gain = refs[:5]
    factors, refs = refs[5 : 5 + (4 if count else 0)], refs[5 + (4 if count else 0) :]
    mixed_out, grad_x_one, grad_gain, mix_all = refs[:4]
    pieces, downs, refs = refs[4 : 4 + TP], refs[4 + TP : 4 + 2 * TP], refs[4 + 2 * TP :]
    grads, cores, refs = refs[:count], refs[count : 2 * count], refs[2 * count :]
    own, local, zs, zr, gu0, gu1, gd0, gd1 = refs[:8]
    p = Place()
    line, late = LineSum(p, parts, refs[8:16]), LineSum(p, out_parts, refs[16:24])
    folds = folds_of(p, grads, cores, refs[24 : 24 + 12 * count])
    out = Gather(p, mix_all, (gu0, gu1), (gd0, gd1))
    halves, rows = parts.shape[1:3]
    line.clear()
    late.clear()
    to_z = [device(p, z=(p.z + d) % TP) for d in range(TP)]
    started = []
    if folds:
        greet(to_z[1:] + [*folds[0].to, folds[0].to_c])
    else:
        greet_line(p)
    stays = []

    def stay(src, dst):
        copy = pltpu.make_async_copy(src, dst, local.at[len(stays)])
        copy.start()
        stays.append(copy)

    if folds:
        left, right, turned, buffers, chunk_sems, load_sems = refs[24 + 12 * count :]
        part = factors[1].shape[1]
        outers = [
            Outer(grads[m], left, right.at[:, pl.ds(m // 2 * part, part)], turned, buffers, chunk_sems)
            for m in range(3)
        ]
        down, gate, up = folds
        size = outers[0].count
        half = size // 2

    def load(m):
        cols = right.at[:, pl.ds(0, factors[2 * m + 1].shape[1])]
        copies = [
            pltpu.make_async_copy(factors[2 * m], left, load_sems.at[0]),
            pltpu.make_async_copy(factors[2 * m + 1], cols, load_sems.at[1]),
        ]
        for copy in copies:
            copy.start()
        for copy in copies:
            copy.wait()

    def outer(m, low, high):
        outers[m].run(low, high)
        outers[m].flush(high)
        folds[m].begin((0, 1, 3, 4) if high == half else (2, 5, 6, 7))

    def join(fold, *blocks):
        for i in blocks:
            fold.join(i)

    def line_step(k):
        for h in range(halves):
            line.step(k, h)

    line_step(3)
    for h in range(halves):
        late.step(TP - 1, h)
    if folds:
        load(0)
        outer(0, 0, half)
        outer(0, half, size)
        join(down, 0, 1)
        load(1)
        outer(1, 0, half)
        join(down, 2, 3)
    line_step(2)
    if folds:
        outer(1, half, size)
        join(down, 4, 5)
        outer(2, 0, half)
        join(gate, 0, 1)
        down.middle()
        join(gate, 2, 3)
    line_step(1)
    if folds:
        outer(2, half, size)
        join(gate, 4, 5)
    grad_gain[...] = jnp.zeros(grad_gain.shape, F32)
    for h in range(halves):
        line.arrive(h)

        def finish(at, h=h):
            grad, gains = norm_back(x_one[h, at], gain[...], line.total(h, at))
            grad = grad + cot[h, at].astype(F32)
            grad_x_one[h, at] = grad
            own[h, at] = grad.astype(BF)
            grad_gain[0:1] += jnp.sum(gains, axis=0, keepdims=True)

        by_rows(rows, finish)
        out.begin(h, own.at[h])
        stay(own.at[h], mix_all.at[p.z, h])
    if folds:
        join(up, 0, 1)
        gate.middle()
        join(up, 2, 3)
    for h in range(halves):
        out.step(1, h)
        late.step(2, h)
    if folds:
        join(down, 6, 7)
        down.finish()
        stay(down.result(p.z), downs[0])
        for d in (1, 3, 2):
            copy = copy_to(down.result((p.z + d) % TP), downs[d], (zs, zr), (d,), to_z[d])
            copy.start()
            started.append(copy)
        join(up, 4, 5)
        join(gate, 6, 7)
    for h in range(halves):
        out.step(2, h)
        late.step(1, h)
    if folds:
        join(up, 6, 7)
        up.middle()
    for h in range(halves):
        out.step(3, h)
    for h in range(halves):
        late.arrive(h)

        def store(at, h=h):
            mixed_out[h, at] = (x_one[h, at] + late.total(h, at)).astype(BF)

        by_rows(rows, store)
    for m, fold in enumerate(folds[1:]):
        fold.finish()
        for d in range(TP):
            stay(fold.result((p.z + d) % TP), pieces[d].at[:, pl.ds(m * part, part)])
    if folds:
        for d in range(1, TP):
            copy_to(downs[d], downs[d], (zs, zr), (d,), to_z[1]).wait_recv()
    for copy in started:
        copy.wait_send()
    for fold in folds:
        fold.close()
    line.close()
    late.close()
    out.close(halves)
    for copy in stays:
        copy.wait()


def turn(parts, out_parts, x_one, cot, gain, factors, p):
    shape, count, width = parts.shape, 3 if factors else 0, parts.shape[-1]
    rows = width // (p.fs * TP * 4)
    sizes = [factors[1].shape[1]] * count if factors else []
    grads = [jax.ShapeDtypeStruct((p.fs, 1, TP, 2, 2, rows, size), BF) for size in sizes]
    folded = [Fold.shapes(grad, True) for grad in grads]
    piece = jax.ShapeDtypeStruct((rows, 2 * sizes[0]) if factors else (16, 128), BF)
    down = jax.ShapeDtypeStruct((rows, sizes[0]) if factors else (16, 128), BF)
    extra = []
    if factors:
        assert all(size % GRAD_CHUNK == 0 for size in sizes)
        tokens, deep = factors[0].shape[0], width // 4
        extra = [
            pltpu.VMEM((tokens, width), BF),
            pltpu.VMEM((tokens, 2 * sizes[0]), BF),
            pltpu.VMEM((deep, tokens), BF),
            pltpu.VMEM((2, TP // 2, 2, 2, rows, GRAD_CHUNK), BF),
            pltpu.SemaphoreType.DMA((2,)),
            pltpu.SemaphoreType.DMA((2,)),
        ]
    results = pl.pallas_call(
        functools.partial(turn_kernel, count),
        in_specs=[VMEM] * 5 + [ANY] * len(factors),
        out_specs=[VMEM, VMEM, VMEM, ANY] + [ANY] * (2 * TP + 2 * count),
        out_shape=[
            jax.ShapeDtypeStruct(shape[1:], BF),
            jax.ShapeDtypeStruct(shape[1:], F32),
            jax.ShapeDtypeStruct((8, width), F32),
            jax.ShapeDtypeStruct(shape, BF),
            *[piece] * TP,
            *[down] * TP,
            *grads,
            *(cores for cores, _ in folded),
        ],
        scratch_shapes=[
            pltpu.VMEM(shape[1:], BF),
            pltpu.SemaphoreType.DMA((shape[1] + 2 * TP + 1,)),
            *pairs(TP),
            *pairs(TP - 1, shape[1]),
            *pairs(TP - 1, shape[1]),
            *LineSum.scratch(shape),
            *LineSum.scratch(shape),
            *(item for _, scratch in folded for item in scratch),
            *extra,
        ],
        compiler_params=pltpu.CompilerParams(
            collective_id=2, has_side_effects=True, vmem_limit_bytes=GRANT
        ),
    )(parts, out_parts, x_one, cot, gain, *factors)
    return results[:4], results[4 : 4 + TP], results[4 + TP : 4 + 2 * TP]


def final_kernel(*refs):
    parts, x_zero, gain, grad_x_one, vectors, blocks = refs[:6]
    factors, refs = refs[6:10], refs[10:]
    grad_in, sums = refs[:2]
    outs, grads, refs = refs[2:6], (blocks, *refs[6:9]), refs[9:]
    acc, got, vs, vr, zs, zr, local, left, right, turned, buffers, chunk_sems, load_sems = refs[:13]
    p = Place()
    line = LineSum(p, parts, refs[13:21])
    folds = folds_of(p, grads, [None] * 4, refs[21:])
    halves, rows = parts.shape[1:3]
    line.clear()
    to_z = [device(p, z=(p.z + d) % TP) for d in range(TP)]
    (to_x, to_f), to_c = folds[0].to, folds[0].to_c
    greet(to_z[1:] + [to_x, to_f, to_c])
    partners = [to_c, to_x, to_f] + [
        device(p, z=p.z + bit * (1 - 2 * (p.z // bit % 2))) for bit in (1, 2)
    ]
    part = factors[1].shape[1]
    outers = [
        Outer(grads[m], left, right.at[:, pl.ds(m // 3 * part, part)], turned, buffers, chunk_sems)
        for m in range(1, 4)
    ]

    def load(m):
        cols = right.at[:, pl.ds(0, factors[2 * m + 1].shape[1])]
        copies = [
            pltpu.make_async_copy(factors[2 * m], left, load_sems.at[0]),
            pltpu.make_async_copy(factors[2 * m + 1], cols, load_sems.at[1]),
        ]
        for copy in copies:
            copy.start()
        for copy in copies:
            copy.wait()

    def outer(m):
        outers[m - 1].run(0, outers[m - 1].count)
        outers[m - 1].flush(outers[m - 1].count)
        folds[m].begin()

    def join(m, *blocks):
        for i in blocks:
            folds[m].join(i)

    def line_step(k):
        for h in range(halves):
            line.step(k, h)

    def vector(i):
        return copy_to(acc.at[i], got.at[i], (vs, vr), (i,), partners[i])

    def next_vector(i):
        vector(i).wait_recv()
        if i < 4:
            acc[i + 1] = acc[i] + got[i]
            vector(i + 1).start()
        else:
            sums[...] = acc[i] + got[i]

    started, stays = [], []

    def send_on(m):
        folds[m].finish()
        for d in (1, 3, 2):
            src = folds[m].result((p.z + d) % TP)
            copy = copy_to(src, outs[m].at[p.z], (zs, zr), (m, d - 1), to_z[d])
            copy.start()
            started.append(copy)
        stays.append(pltpu.make_async_copy(folds[m].result(p.z), outs[m].at[p.z], local.at[m]))
        stays[-1].start()

    acc[0] = vectors[...]
    vector(0).start()
    folds[0].begin()
    line_step(3)
    join(0, 0, 1, 2, 3)
    load(0)
    outer(1)
    load(1)
    join(0, 4, 5)
    join(1, 0, 1)
    folds[0].middle()
    join(1, 2, 3)
    outer(2)
    line_step(2)
    next_vector(0)
    join(0, 6, 7)
    join(1, 4, 5)
    join(2, 0, 1)
    folds[1].middle()
    join(2, 2, 3)
    outer(3)
    line_step(1)
    next_vector(1)
    send_on(0)
    join(1, 6, 7)
    join(2, 4, 5)
    join(3, 0, 1)
    folds[2].middle()
    join(3, 2, 3)
    next_vector(2)
    send_on(1)
    join(2, 6, 7)
    join(3, 4, 5)
    folds[3].middle()
    join(3, 6, 7)
    send_on(2)
    next_vector(3)
    for h in range(halves):
        line.arrive(h)

        def finish(at, h=h):
            grad, _ = norm_back(x_zero[h, at].astype(F32), gain[...], line.total(h, at))
            grad_in[h, at] = grad_x_one[h, at] + grad

        by_rows(rows, finish)
    next_vector(4)
    send_on(3)
    for m in range(4):
        for d in range(1, TP):
            ref = outs[m].at[(p.z - d) % TP]
            copy_to(ref, ref, (zs, zr), (m, d - 1), to_z[1]).wait_recv()
    for copy in started:
        copy.wait_send()
    for i in range(5):
        vector(i).wait_send()
    for fold in folds:
        fold.close()
    line.close()
    for copy in stays:
        copy.wait()


def final(parts, x_zero, gain, grad_x_one, vectors, blocks, factors, p):
    shape = parts.shape
    rows, part = blocks.shape[-2], factors[1].shape[1]
    tokens, width = factors[0].shape
    shaped = jax.ShapeDtypeStruct
    grads = [shaped((p.fs, 1, TP, 2, 2, rows, part), BF)] * 3
    widths = [blocks.shape[-1]] + [part] * 3
    folded = [Fold.shapes(grad, False)[1] for grad in (blocks, *grads)]
    results = pl.pallas_call(
        final_kernel,
        in_specs=[VMEM] * 5 + [ANY] * 5,
        out_specs=[VMEM, VMEM] + [ANY] * 7,
        out_shape=[
            shaped(shape[1:], F32),
            shaped(vectors.shape, F32),
            *(shaped((TP, rows, wide), BF) for wide in widths),
            *grads,
        ],
        scratch_shapes=[
            pltpu.VMEM((5,) + vectors.shape, F32),
            pltpu.VMEM((5,) + vectors.shape, F32),
            *pairs(5),
            *pairs(4, TP - 1),
            pltpu.SemaphoreType.DMA((4,)),
            pltpu.VMEM((tokens, width), BF),
            pltpu.VMEM((tokens, 2 * part), BF),
            pltpu.VMEM((width // 4, tokens), BF),
            pltpu.VMEM((2, TP // 2, 2, 2, rows, part), BF),
            pltpu.SemaphoreType.DMA((2,)),
            pltpu.SemaphoreType.DMA((2,)),
            *LineSum.scratch(shape),
            *(item for scratch in folded for item in scratch),
        ],
        cost_estimate=FREE,
        compiler_params=pltpu.CompilerParams(
            collective_id=3, has_side_effects=True, vmem_limit_bytes=GRANT
        ),
    )(parts, x_zero, gain, grad_x_one, vectors, blocks, *factors)
    return results[0], results[1], results[2:6]


def chain_kernel(backward, sums, *refs):
    if backward:
        known, start, spans, send, recv = refs
    else:
        start, spans, send, recv = refs
    p = Place()
    peers = [device_q(p, (p.q + d) % NQ) for d in range(NQ)]
    greet(peers[1:])
    spans[p.q] = sums[...]
    copies = []
    for d in range(1, NQ):
        copies.append(copy_to(spans.at[p.q], spans.at[p.q], (send, recv), (d,), peers[d]))
        copies[-1].start()
    for d in range(1, NQ):
        ref = spans.at[(p.q - d) % NQ]
        copy_to(ref, ref, (send, recv), (d,), peers[d]).wait_recv()
    micro = sums.shape[1] // TP
    carry = jnp.zeros((micro, sums.shape[2]), F32)
    order = [(z, q) for z in range(TP) for q in range(NQ)]
    for z, q in reversed(order) if backward else order:
        here = slice(z * micro, (z + 1) * micro)

        @pl.when(p.q == q)
        def _(carry=carry, here=here):
            start[here] = carry

        decay = known[q, 0, here] if backward else spans[q, 0, here]
        carry = decay * carry + spans[q, 0 if backward else 1, here]
    for copy in copies:
        copy.wait_send()


def device_q(p, q):
    return device(p, x=q // 2, c=q % 2)


def chain(sums, known=None):
    backward = known is not None
    every = (NQ,) + sums.shape
    return pl.pallas_call(
        functools.partial(chain_kernel, backward),
        in_specs=[VMEM] * (2 if backward else 1),
        out_specs=[VMEM, VMEM],
        out_shape=[
            jax.ShapeDtypeStruct(sums.shape[1:], F32),
            jax.ShapeDtypeStruct(every, F32),
        ],
        scratch_shapes=pairs(NQ),
        cost_estimate=FREE,
        compiler_params=pltpu.CompilerParams(
            collective_id=5 if backward else 4, has_side_effects=True
        ),
    )(*((sums, known) if backward else (sums,)))


def unpack_kernel(count, *refs):
    p = Place()
    pieces, outs = refs[: TP * len(count)], refs[TP * len(count) :]
    for d in range(TP):
        first = 0
        for m, parts in enumerate(count):
            piece = pieces[m * TP + d]
            part = piece.shape[1] // parts
            cols = pl.ds(pl.multiple_of((p.z - d) % TP * part, 128), part)
            for i in range(parts):
                outs[first + i][:, cols] = piece[:, i * part : (i + 1) * part].astype(F32)
            first += parts


def unpack(groups, count):
    shapes = []
    for pieces, parts in zip(groups, count):
        rows, cols = pieces[0].shape
        shapes += [jax.ShapeDtypeStruct((rows, cols // parts * TP), F32)] * parts
    return pl.pallas_call(
        functools.partial(unpack_kernel, count),
        in_specs=[VMEM] * (TP * len(groups)),
        out_specs=[VMEM] * len(shapes),
        out_shape=shapes,
        compiler_params=pltpu.CompilerParams(vmem_limit_bytes=GRANT),
    )(*(piece for pieces in groups for piece in pieces))


def unpack_mix_kernel(spans, *refs):
    (blocks, *mix), (blocks_out, *mix_out) = refs[:4], refs[4:]
    total = blocks[0].astype(F32)
    for k in range(1, TP):
        total = total + blocks[k].astype(F32)
    blocks_out[...] = total
    for piece, out in zip(mix, mix_out):
        for k, (start, count) in enumerate(spans):
            out[:, start : start + count] = piece[k, :, :count].astype(F32)


def unpack_mix(mix, spans):
    wide = spans[-1][0] + spans[-1][1]
    shapes = [mix[0].shape[1:]] + [(mix[0].shape[1], wide)] * 3
    return pl.pallas_call(
        functools.partial(unpack_mix_kernel, spans),
        in_specs=[VMEM] * 4,
        out_specs=[VMEM] * 4,
        out_shape=[jax.ShapeDtypeStruct(shape, F32) for shape in shapes],
        compiler_params=pltpu.CompilerParams(vmem_limit_bytes=GRANT),
    )(*mix)


def geglu(gate_vals, up_vals):
    return jax.nn.gelu(gate_vals) * up_vals


def all_spans(value, p):
    by_q = everywhere(value, shift_q, p.q, NQ)
    by_r = everywhere(by_q, shift_r, p.r, p.rests)
    return jnp.swapaxes(by_r, 1, 2).reshape((-1,) + value.shape[1:])


def own_spans(spans, p):
    split = spans.reshape((p.rests, TP, NQ) + spans.shape[1:])
    return lax.dynamic_index_in_dim(at(split, p.r), p.q, 1, keepdims=False)


def on_device(
    inputs,
    cotangent,
    proj_gelu,
    proj_lru,
    gate_blocks,
    proj_out,
    ffw_gate,
    ffw_up,
    ffw_down,
    norm_mix,
    norm_ffw,
    decay_param,
    conv_taps,
):
    p = Place()
    micro, span, width = inputs.shape[0], inputs.shape[2], inputs.shape[3]
    lru_width = proj_gelu.shape[1]
    tap_count = conv_taps.shape[1]
    block_width = gate_blocks.shape[1] // 2
    heads = lru_width // block_width
    ffw_part = ffw_gate.shape[1] // TP
    rows = proj_gelu.shape[0]
    held = -(-heads // TP)
    first = [k * heads // TP for k in range(TP)]
    owned = [range(first[k], first[k + 1] if k + 1 < TP else heads) for k in range(TP)]
    part = held * block_width

    out_t, down_t = proj_out.T, ffw_down.T
    small = jnp.concatenate([norm_mix[None], norm_ffw[None], decay_param[None], conv_taps.T])
    small = jnp.pad(small, ((0, 128 - small.shape[0]), (0, 0))).T
    x_rows, cot = inputs[:, 0], cotangent[:, 0]
    one = 1 if p.rests == 1 else 0
    cot_halves = cot.reshape(2, -1, width)
    edge = lax.ppermute(
        x_rows[:, span - (tap_count - 1) :],
        "seq",
        [(i, i + 1) for i in range(lax.axis_size("seq") - 1)],
    )
    edge = jnp.pad(edge, ((0, 0), (HALO - (tap_count - 1), 0), (0, 0)))
    x_wide = jnp.concatenate([x_rows.reshape(-1, width), edge.reshape(-1, width)])
    if p.rests == 1:
        weights = (proj_gelu, proj_lru, out_t, gate_blocks, small, ffw_gate, ffw_up, down_t)
        mix_pieces, ffw_pieces = pack(weights, block_width)
        mix_w, ffw_w, piece_1, x_all, cot_first = intake(
            mix_pieces, ffw_pieces[0], ffw_pieces[1], x_wide.reshape(3, -1, width), cot_halves[0], p
        )
        piece_2, piece_3, x_all = lax.optimization_barrier((*ffw_pieces[2:], x_all))
        piece_3, piece_2 = shift_z(piece_3, 3), shift_z(piece_2, 2)
        passed = (piece_1, swap_x(piece_1), swap_f(piece_1), piece_2, piece_3)
    else:
        mix_pieces, ffw_pieces = [], []
        for k in range(TP):
            cols = slice(first[k] * block_width, first[k] * block_width + part)
            pieces = [proj_gelu[:, cols], proj_lru[:, cols], out_t[:, cols], gate_blocks, small]
            mix_pieces.append(jnp.concatenate(pieces, axis=1))
            cols = slice(k * ffw_part, (k + 1) * ffw_part)
            pieces = [ffw_gate[:, cols], ffw_up[:, cols], down_t[:, cols]]
            ffw_pieces.append(jnp.concatenate(pieces, axis=1))
        mix_w = weights_in(jnp.stack(mix_pieces), p)
        whole_ffw = weights_in(jnp.stack(ffw_pieces), p)
        x_all, passed, ffw_w = gather_z(x_wide, p), None, None
        cot_first = gather_z(cot_halves[:1], p)
    dims = (span, micro, heads, held, block_width, tap_count)
    small_w, rows_w, mixed, pre, pre_lru, conv, gate, state, prod, sums = recur(
        x_all.reshape(-1, width), mix_w, dims
    )
    mix_gain, ffw_gain = small_w[0:1], small_w[1:2]
    start = sum(jnp.where(p.z == k, first[k] * block_width, 0) for k in range(TP))

    ends = (TP, micro, part)
    if p.rests == 1:
        state_in, every_sum = chain(sums)
    else:
        sums = all_spans(jnp.stack([sums[0].reshape(ends), sums[1].reshape(ends)], axis=1), p)
        carry, carries = jnp.zeros_like(sums[0, 0]), []
        for k in range(sums.shape[0]):
            carries.append(carry)
            carry = sums[k, 0] * carry + sums[k, 1]
        state_in = own_spans(jnp.stack(carries), p).reshape(-1, part)
    mix_bf, out_parts = recur_mix(pre, rows_w, state, prod, state_in, mix_w, dims)
    blocked = (TP, micro * CUTS, span // CUTS, width)
    x_own, cot_own = x_rows.reshape(blocked[1:]), cot.reshape(blocked[1:])
    out_parts = out_parts.reshape(blocked)
    x_one, ffw_bf, cot_all, _, *fed = middle(
        out_parts, x_own, ffw_gain, cot_halves[1], cot_first, passed, ffw_w
    )
    cot_all = cot_all.reshape(-1, width)

    ffw_bf = ffw_bf.reshape(-1, width)
    if p.rests == 1:
        hidden_bf, grad_gate_up, ffw_parts, grad_in_parts = fed
    else:
        gate_up_w, down_w = whole_ffw[:, : 2 * ffw_part], whole_ffw[:, 2 * ffw_part :]
        gate_up = dot_plain(ffw_bf, gate_up_w)
        gate_vals, up_vals = gate_up[:, :ffw_part], gate_up[:, ffw_part:]
        hidden_bf = geglu(gate_vals, up_vals).astype(BF)
        grad_hidden = dot_plain(cot_all, down_w)
        _, pull_back = jax.vjp(geglu, gate_vals, up_vals)
        grad_gate_up = jnp.concatenate(pull_back(grad_hidden), axis=1).astype(BF)
        ffw_parts = dot_right_t(hidden_bf, down_w).astype(BF)
        grad_in_parts = dot_right_t(grad_gate_up, gate_up_w).astype(BF)
    ffw_parts, grad_in_parts = ffw_parts.reshape(blocked), grad_in_parts.reshape(blocked)
    factors = [cot_all, hidden_bf, ffw_bf, grad_gate_up]
    (mixed_out, grad_x_one, gain_rows, grad_mix), ffw_pieces, down_pieces = turn(
        grad_in_parts, ffw_parts, x_one, cot_own, ffw_gain, factors * one, p
    )
    if p.rests == 1:
        ffw_pieces = [shift_z(piece, d) if d else piece for d, piece in enumerate(ffw_pieces)]
    grad_mix = grad_mix.reshape(-1, width)

    grad_gelu_bf, local_back, prod_back, back_sums = recur_back(
        grad_mix, pre, rows_w, state, prod, state_in, gate, mix_w, dims
    )
    if p.rests == 1:
        carried, _ = chain(back_sums[None], every_sum)
    else:
        back_sums = all_spans(back_sums.reshape(ends), p)
        carry, carries = jnp.zeros_like(sums[0, 0]), []
        for k in range(sums.shape[0] - 1, -1, -1):
            carries.append(carry)
            carry = sums[k, 0] * carry + back_sums[k]
        carried = own_spans(jnp.stack(carries[::-1]), p).reshape(-1, part)
    block_mats = lax.dynamic_slice(mix_w, (start, 3 * part), (part, 2 * block_width))
    grad_blocks, grad_lru, spill, row_grads = recur_grad(
        local_back, prod_back, carried, state, prod, state_in, gate, conv, pre_lru, rows_w,
        block_mats.reshape(held, block_width, 2 * block_width), dims,
    )
    spill = spill.reshape(TP, micro, HALO, part)
    from_next = shift_q(spill, -1)
    last = jnp.zeros_like(spill[:1])
    if p.rests > 1:
        last = move(spill[:1], lambda r, z, q: (r - 1, z, NQ - 1) if q == 0 and r > 0 else None)
    from_next = jnp.where(
        p.q == NQ - 1, jnp.concatenate([from_next[1:], last], axis=0), from_next
    )
    grad_pair, grad_mixed_parts, mix_gain_rows = recur_in(
        grad_gelu_bf, grad_lru, from_next.reshape(-1, part), rows_w, small_w, mixed, mix_w, dims
    )
    grad_mixed_parts = grad_mixed_parts.reshape(blocked)

    blocks_all = lax.dynamic_update_slice_in_dim(
        jnp.zeros((lru_width, 2 * block_width), BF),
        (grad_blocks * rows_w[6][:, None]).astype(BF),
        start,
        0,
    )
    mix_factors = [grad_mix, mix_bf, mixed, grad_pair]
    vectors = lax.dynamic_update_slice_in_dim(
        jnp.zeros((1 + tap_count, lru_width), F32), row_grads[: 1 + tap_count], start, 1
    )
    vectors = jnp.concatenate([mix_gain_rows[:1], gain_rows[:1], vectors], axis=0)
    vectors = jnp.pad(vectors, ((0, -vectors.shape[0] % 8), (0, 0)))
    if p.rests == 1:
        grad_inputs, vectors, mix_grads = final(
            grad_mixed_parts, x_own, mix_gain, grad_x_one, vectors,
            by_owner(blocks_all, p), mix_factors, p,
        )
    else:
        products = [dot_left_t(*mix_factors[:2]), dot_left_t(*mix_factors[2:])]
        products = [blocks_all, products[0], products[1][:, :part], products[1][:, part:]]
        mix_grads = [grads_out(grad.astype(BF), p) for grad in products]
        grad_mixed_own = scatter_z(grad_mixed_parts, p)
        grad_inputs = grad_x_one + norm_back(x_own.astype(F32), mix_gain, grad_mixed_own)[0]
        for exchange in (swap_core, swap_x, swap_f):
            vectors = vectors + exchange(vectors)
        for bit in (1, 2):
            vectors = vectors + move(vectors, lambda r, z, q, bit=bit: (r, z ^ bit, q))
        total = vectors
        for d in range(1, p.rests):
            total = total + shift_r(vectors, d)
        vectors = total
    vectors = lax.dynamic_slice_in_dim(vectors, p.index * rows, rows, 1)

    if p.rests == 1:
        spans = [(first[k] * block_width, len(owned[k]) * block_width) for k in range(TP)]
        share_blocks, share_out, share_gelu, share_lru = unpack_mix(mix_grads, spans)
        share_gate, share_up, share_down = unpack((ffw_pieces, down_pieces), (2, 1))
    else:
        ffw_grads = [dot_left_t(*factors[:2]), dot_left_t(*factors[2:])]
        ffw_grads = [grads_out(grad.astype(BF), p) for grad in ffw_grads]
        beside = lambda v: jnp.swapaxes(v, 0, 1).reshape(rows, -1).astype(F32)
        share_gate = beside(ffw_grads[1][:, :, :ffw_part])
        share_up = beside(ffw_grads[1][:, :, ffw_part:])
        share_down = beside(ffw_grads[0])

        def mix_columns(grad):
            picked = [grad[k][:, : len(owned[k]) * block_width] for k in range(TP)]
            return jnp.concatenate(picked, axis=1).astype(F32)

        share_blocks = jnp.sum(mix_grads[0].astype(F32), axis=0)
        share_out, share_gelu, share_lru = (mix_columns(grad) for grad in mix_grads[1:])
    shape = (micro, 1, span, width)
    return (
        mixed_out.reshape(shape),
        grad_inputs.reshape(shape),
        share_gelu,
        share_lru,
        share_blocks,
        share_out.T,
        share_gate,
        share_up,
        share_down.T,
        vectors[0],
        vectors[1],
        vectors[2],
        vectors[3 : 3 + tap_count].T,
    )


def solution(mesh):
    in_specs = (
        P(None, "fsdp", "seq", None),
        P(None, "fsdp", "seq", None),
        P(("fsdp", "seq"), None),
        P(("fsdp", "seq"), None),
        P(("fsdp", "seq"), None),
        P(None, ("fsdp", "seq")),
        P(("fsdp", "seq"), None),
        P(("fsdp", "seq"), None),
        P(None, ("fsdp", "seq")),
        P(("fsdp", "seq")),
        P(("fsdp", "seq")),
        P(("fsdp", "seq")),
        P(("fsdp", "seq"), None),
    )
    out_specs = (
        P(None, "fsdp", "seq", None),
        P(None, "fsdp", "seq", None),
        P(("fsdp", "seq"), None),
        P(("fsdp", "seq"), None),
        P(("fsdp", "seq"), None),
        P(None, ("fsdp", "seq")),
        P(("fsdp", "seq"), None),
        P(("fsdp", "seq"), None),
        P(None, ("fsdp", "seq")),
        P(("fsdp", "seq")),
        P(("fsdp", "seq")),
        P(("fsdp", "seq")),
        P(("fsdp", "seq"), None),
    )
    return jax.shard_map(
        on_device, mesh=mesh, in_specs=in_specs, out_specs=out_specs, check_vma=False
    )
```

```python
import functools

import jax
import jax.numpy as jnp
from jax import lax
from jax.experimental import pallas as pl
from jax.experimental.pallas import tpu as pltpu
from jax.sharding import PartitionSpec as P

EPS = 1e-06
GUARD = 0.001
RATE = 8.0
TP = 4
NQ = 4
HALO = 8
BF = jnp.bfloat16
F32 = jnp.float32
MESH = pl.DeviceIdType.MESH
ANY = pl.BlockSpec(memory_space=pl.ANY)
VMEM = pl.BlockSpec(memory_space=pltpu.VMEM)
GRANT = 60 * 1024 * 1024
CUTS = 2
FREE = pl.CostEstimate(flops=0, bytes_accessed=0, transcendentals=0)


def move(value, step):
    pairs = []
    for here in range(lax.axis_size("seq")):
        there = step(here // (TP * NQ), here // NQ % TP, here % NQ)
        if there is not None:
            pairs.append((here, (there[0] * TP + there[1]) * NQ + there[2]))
    return lax.ppermute(value, "seq", pairs)


def swap_core(value):
    return move(value, lambda r, z, q: (r, z, q ^ 1))


def swap_x(value):
    return move(value, lambda r, z, q: (r, z, q ^ 2))


def swap_f(value):
    return lax.ppermute(value, "fsdp", [(0, 1), (1, 0)])


def shift_z(value, d):
    return move(value, lambda r, z, q: (r, (z + d) % TP, q))


def shift_q(value, d):
    return move(value, lambda r, z, q: (r, z, (q + d) % NQ))


def shift_r(value, d):
    count = lax.axis_size("seq") // (TP * NQ)
    return move(value, lambda r, z, q: ((r + d) % count, z, q))


def hop(value, d, low, high):
    return move(value, lambda r, z, q: (r, z + d, q) if low <= z <= high else None)


class Place:
    def __init__(self):
        seq = lax.axis_index("seq")
        self.f = lax.axis_index("fsdp")
        self.r, self.z, self.q = seq // (TP * NQ), seq // NQ % TP, seq % NQ
        self.x, self.c = self.q // 2, self.q % 2
        self.rests = lax.axis_size("seq") // (TP * NQ)
        self.fs = lax.axis_size("fsdp")
        self.index = self.f * lax.axis_size("seq") + seq


def at(value, index):
    return lax.dynamic_index_in_dim(value, index, 0, keepdims=False)


def put(base, value, *index):
    starts = [jnp.int32(0) if i is None else jnp.int32(i) for i in index]
    starts += [jnp.int32(0)] * (base.ndim - len(index))
    for dim, i in enumerate(index):
        if i is not None:
            value = jnp.expand_dims(value, dim)
    return lax.dynamic_update_slice(base, value, starts)


def everywhere(value, shifter, mine, count):
    out = put(jnp.zeros((count,) + value.shape, value.dtype), value, mine)
    for d in range(1, count):
        out = put(out, shifter(value, d), (mine - d) % count)
    return out


def gather_z(value, p):
    ups, downs = [], []
    up = down = value
    for k in range(1, TP):
        up = hop(up, 1, k - 1, TP - 2)
        down = hop(down, -1, 1, TP - k)
        ups.append(up)
        downs.append(down)
    out = put(jnp.zeros((TP,) + value.shape, value.dtype), value, p.z)
    for k in range(1, TP):
        out = put(out, downs[k - 1] + ups[TP - 1 - k], (p.z + k) % TP)
    return out


def scatter_z(parts, p):
    right = left = None
    for k in range(TP - 1, 0, -1):
        send = at(parts, (p.z + k) % TP)
        if right is not None:
            send = (send.astype(F32) + right.astype(F32)).astype(BF)
        right = hop(send, 1, 0, TP - 1 - k)
        send = at(parts, (p.z - k) % TP)
        if left is not None:
            send = (send.astype(F32) + left.astype(F32)).astype(BF)
        left = hop(send, -1, k, TP - 1)
    return at(parts, p.z).astype(F32) + right.astype(F32) + left.astype(F32)


def weights_in(pieces, p):
    rows, cols = pieces.shape[1:]
    mine = put(jnp.zeros(pieces.shape, BF), at(pieces, p.z), p.z)
    for d in range(1, TP):
        mine = put(mine, shift_z(at(pieces, (p.z + d) % TP), d), (p.z - d) % TP)
    mine = everywhere(mine, shift_r, p.r, p.rests)
    half = TP // 2
    by_x, by_f = swap_x(mine), swap_f(mine)
    corner = (swap_f(by_x[:, :half]), swap_x(by_f[:, half:]))
    whole = jnp.zeros((p.fs, p.rests, TP, 2, 2, rows, cols), BF)
    for block, f, x, z in (
        (mine, p.f, p.x, 0),
        (by_x, p.f, 1 - p.x, 0),
        (by_f, 1 - p.f, p.x, 0),
        (corner[0], 1 - p.f, 1 - p.x, 0),
        (corner[1], 1 - p.f, 1 - p.x, half),
    ):
        other = swap_core(block)
        for part, c in ((block, p.c), (other, 1 - p.c)):
            part = part[None, :, :, None, None]
            whole = lax.dynamic_update_slice(
                whole, part, [jnp.int32(i) for i in (f, 0, z, x, c, 0, 0)]
            )
    return whole.reshape(-1, cols)


def by_owner(grad, p):
    return grad.reshape(p.fs, p.rests, TP, 2, 2, -1, grad.shape[1])


def to_owner_z(total, p):
    out = put(jnp.zeros(total.shape, BF), at(total, p.z), p.z)
    for d in (1, 3, 2):
        out = put(out, shift_z(at(total, (p.z + d) % TP), d), (p.z - d) % TP)
    return out


def grads_out(grad, p):
    plus = lambda a, b: (a.astype(F32) + b.astype(F32)).astype(BF)
    pick = lambda v, dim, i: lax.dynamic_index_in_dim(v, i, dim, keepdims=False)
    total = by_owner(grad, p)
    total = plus(pick(total, 4, p.c), swap_core(pick(total, 4, 1 - p.c)))
    total = plus(pick(total, 3, p.x), swap_x(pick(total, 3, 1 - p.x)))
    total = plus(at(total, p.f), swap_f(at(total, 1 - p.f)))
    mine = at(total, p.r)
    for d in range(1, p.rests):
        mine = plus(mine, shift_r(at(total, (p.r + d) % p.rests), d))
    return to_owner_z(mine, p)


def dot_left_t(left_mat, right_mat):
    return lax.dot_general(
        left_mat, right_mat, (((0,), (0,)), ((), ())), preferred_element_type=F32
    )


def dot_plain(left_mat, right_mat):
    return jnp.dot(left_mat, right_mat, preferred_element_type=F32)


def dot_right_t(left_mat, right_mat):
    return lax.dot_general(
        left_mat, right_mat, (((1,), (1,)), ((), ())), preferred_element_type=F32
    )


def normed(values, gain_vec):
    return values * lax.rsqrt(jnp.mean(values * values, axis=-1, keepdims=True) + EPS) * gain_vec


def gelu_pair(v):
    scale = 0.7978845608028654
    inner = jnp.tanh(scale * (v + 0.044715 * v * v * v))
    slope = 0.5 * v * (1.0 - inner * inner) * scale * (1.0 + 0.134145 * v * v)
    return 0.5 * v * (1.0 + inner), 0.5 * (1.0 + inner) + slope


def span_scan(decay, drive, backward):
    count = decay.shape[0]
    row = lax.broadcasted_iota(jnp.int32, decay.shape, 0)
    step = 1
    while step < count:
        inside = row < count - step if backward else row >= step
        turn = count - step if backward else step
        drive = drive + jnp.where(inside, decay * pltpu.roll(drive, turn, 0), 0.0)
        decay = decay * jnp.where(inside, pltpu.roll(decay, turn, 0), 1.0)
        step *= 2
    return decay, drive


def gate_values(gate, soft):
    half = gate.shape[1] // 2
    rec_gate = jax.nn.sigmoid(gate[:, :half])
    in_gate = jax.nn.sigmoid(gate[:, half:])
    log_decay = -RATE * rec_gate * soft
    square = jnp.exp(2.0 * log_decay)
    return rec_gate, in_gate, jnp.exp(log_decay), square, jnp.sqrt(1.0 - square + GUARD)


def main_rows(i, span, micro):
    return pl.ds(i // micro * micro * (span + HALO) + i % micro * span, span)


def with_halo(pre, i, span, micro):
    start = i // micro * micro * (span + HALO) + micro * span + i % micro * HALO
    both = [pre[pl.ds(start, HALO)], pre[main_rows(i, span, micro)]]
    return jnp.concatenate(both, axis=0)


def recur_head(span, micro, pre, rows, block, conv, gate, state, prod, sums):
    count = conv.shape[0] // span
    soft, taps = rows[0:1], [rows[k + 2 : k + 3] for k in range(4)]
    for i in range(count):
        vals = with_halo(pre, i, span, micro).astype(BF).astype(F32)
        total = taps[0] * vals
        for k in range(1, 4):
            total = total + taps[k] * pltpu.roll(vals, k, 0)
        conv[pl.ds(i * span, span)] = total[HALO:].astype(BF)
    gate[...] = dot_plain(conv[...], block[...])
    for i in range(count):
        here = pl.ds(i * span, span)
        _, in_gate, decay, _, root = gate_values(gate[here], soft)
        decay, local = span_scan(decay, root * in_gate * conv[here].astype(F32), False)
        state[here] = local
        prod[here] = decay
        sums[0, i : i + 1] = decay[span - 1 :]
        sums[1, i : i + 1] = local[span - 1 :]


def columns(ref, h, width):
    return ref.at[:, pl.ds(pl.multiple_of(h * width, 128), width)]


def by_heads(count, body):
    def turn(h, _):
        body(h)
        return 0

    lax.fori_loop(0, count, turn, 0)


def recur_kernel(
    dims, x_all, gelu_w, lru_w, mix_w, small, rows, mixed, pre_gelu, pre_lru, conv, gate, state,
    prod, sums, small_w, block_w, mixed_all, sems,
):
    span, micro, heads, held, bw, taps = dims
    part, h = held * bw, pl.program_id(0)

    @pl.when(h == 0)
    def _():
        p = Place()
        start = pl.multiple_of(p.z * heads // TP * bw, 128)
        pieces = (
            (mix_w.at[:, pl.ds(3 * part + 2 * bw, 128)], small_w),
            (mix_w.at[pl.ds(start, part), pl.ds(3 * part, 2 * bw)], block_w),
        )
        loads = [pltpu.make_async_copy(src, dst, sems.at[i]) for i, (src, dst) in enumerate(pieces)]
        for load in loads:
            load.start()
        loads[0].wait()
        row = lax.broadcasted_iota(jnp.int32, (8, 128), 0)
        lane = lax.broadcasted_iota(jnp.int32, (8, 128), 1)
        small[...] = dot_right_t(jnp.where(row == lane, 1.0, 0.0).astype(BF), small_w[...])
        own = small[:, pl.ds(start, part)]
        decay = -own[2:3]
        feature = lax.broadcasted_iota(jnp.int32, (1, part), 1)
        count = ((p.z + 1) * heads // TP - p.z * heads // TP) * bw
        rows[0:1] = jnp.maximum(decay, 0.0) + jnp.log1p(jnp.exp(-jnp.abs(decay)))
        rows[1:2] = jax.nn.sigmoid(decay)
        rows[2 : 2 + taps] = own[3 : 3 + taps]
        rows[6:7] = jnp.where(feature < count, 1.0, 0.0)
        rows[7:8] = jnp.zeros((1, part), F32)
        gain, wide, step = small[0:1], micro * (span + HALO), 16

        def norm(z, _):
            for k in range(0, wide, step):
                vals = x_all[pl.ds(pl.multiple_of(z * wide + k, step), step)].astype(F32)
                vals = normed(vals, gain).astype(BF)
                mixed_all[pl.ds(pl.multiple_of(z * wide + k, step), step)] = vals
                if k < micro * span:
                    mixed[pl.ds(pl.multiple_of(z * micro * span + k, step), step)] = vals
            return 0

        lax.fori_loop(0, TP, norm, 0)
        loads[1].wait()

    pre_gelu[...] = dot_plain(mixed_all[...], gelu_w[...])
    pre_lru[...] = dot_plain(mixed_all[...], lru_w[...])
    block = block_w.at[pl.ds(pl.multiple_of(h * bw, 128), bw)]
    recur_head(span, micro, pre_lru, columns(rows, h, bw), block, conv, gate, state, prod, sums)


def recur(x_all, mix_w, dims):
    span, micro, _, held, bw, _ = dims
    part, width, wide = held * bw, x_all.shape[1], x_all.shape[0]
    tokens = wide // (span + HALO) * span
    whole = lambda shape: pl.BlockSpec(shape, lambda h: (0, 0))
    column = lambda rows, cols: pl.BlockSpec((rows, cols), lambda h: (0, h))
    shapes = [((8, width), F32), ((8, part), F32), ((tokens, width), BF)]
    shapes += [((wide, part), F32), ((wide, part), F32), ((tokens, part), BF)]
    shapes += [((tokens, 2 * part), F32), ((tokens, part), F32), ((tokens, part), F32)]
    shapes += [((2, tokens // span, part), F32)]
    return pl.pallas_call(
        functools.partial(recur_kernel, dims),
        grid=(held,),
        in_specs=[
            whole(x_all.shape),
            column(width, bw),
            pl.BlockSpec((width, bw), lambda h: (0, held + h)),
            ANY,
        ],
        out_specs=[
            whole((8, width)),
            whole((8, part)),
            whole((tokens, width)),
            column(wide, bw),
            column(wide, bw),
            column(tokens, bw),
            column(tokens, 2 * bw),
            column(tokens, bw),
            column(tokens, bw),
            pl.BlockSpec((2, tokens // span, bw), lambda h: (0, 0, h)),
        ],
        out_shape=[jax.ShapeDtypeStruct(*shape) for shape in shapes],
        scratch_shapes=[
            pltpu.VMEM((width, 128), BF),
            pltpu.VMEM((part, 2 * bw), BF),
            pltpu.VMEM(x_all.shape, BF),
            pltpu.SemaphoreType.DMA((2,)),
        ],
        cost_estimate=FREE,
        compiler_params=pltpu.CompilerParams(vmem_limit_bytes=GRANT),
    )(x_all, mix_w, mix_w, mix_w)


def recur_mix_kernel(dims, pre, rows, state, prod, start, mix_w, mix, parts, out_w, sem):
    span, micro, _, held, bw, _ = dims
    part = held * bw
    load = pltpu.make_async_copy(mix_w.at[:, pl.ds(2 * part, part)], out_w, sem.at[0])
    load.start()

    def one_head(h):
        pre_h, state_h, prod_h = columns(pre, h, bw), columns(state, h, bw), columns(prod, h, bw)
        rows_h, start_h, mix_h = columns(rows, h, bw), columns(start, h, bw), columns(mix, h, bw)
        for i in range(state.shape[0] // span):
            here = pl.ds(i * span, span)
            act, _ = gelu_pair(pre_h[main_rows(i, span, micro)])
            states = state_h[here] + prod_h[here] * start_h[i : i + 1]
            mix_h[here] = (states * act * rows_h[6:7]).astype(BF)

    by_heads(held, one_head)
    load.wait()

    def project(j):
        cols = pl.ds(pl.multiple_of(j * 256, 256), 256)
        parts[:, cols] = dot_right_t(mix[...], out_w[cols]).astype(BF)

    by_heads(out_w.shape[0] // 256, project)


def recur_mix(pre, rows, state, prod, start, mix_w, dims):
    tokens, part = state.shape
    width = mix_w.shape[0]
    return pl.pallas_call(
        functools.partial(recur_mix_kernel, dims),
        in_specs=[VMEM] * 5 + [ANY],
        out_specs=[VMEM, VMEM],
        out_shape=[
            jax.ShapeDtypeStruct((tokens, part), BF),
            jax.ShapeDtypeStruct((tokens, width), BF),
        ],
        scratch_shapes=[pltpu.VMEM((width, part), BF), pltpu.SemaphoreType.DMA((1,))],
        cost_estimate=FREE,
        compiler_params=pltpu.CompilerParams(vmem_limit_bytes=GRANT),
    )(pre, rows, state, prod, start, mix_w)


def recur_back_kernel(
    dims, grad, pre, rows, state, prod, start, gate, out_w, gelu, local, prods, sums, back
):
    span, micro = dims[:2]
    soft = rows[0:1]
    back[...] = dot_plain(grad[...], out_w[...])
    for i in range(back.shape[0] // span):
        here = pl.ds(i * span, span)
        act, slope = gelu_pair(pre[main_rows(i, span, micro)])
        states = state[here] + prod[here] * start[i : i + 1]
        gelu[here] = (back[here] * states * slope * rows[6:7]).astype(BF)
        _, _, decay, _, _ = gate_values(gate[here], soft)
        row = lax.broadcasted_iota(jnp.int32, decay.shape, 0)
        later = jnp.where(row < span - 1, pltpu.roll(decay, span - 1, 0), 1.0)
        later, adjoint = span_scan(later, back[here] * act, True)
        local[here] = adjoint
        prods[here] = later
        sums[i : i + 1] = decay[:1] * adjoint[:1]


def recur_back(grad, pre, rows, state, prod, start, gate, mix_w, dims):
    tokens, part = state.shape
    held, bw = dims[3:5]
    column = lambda h: (0, h)
    whole = pl.BlockSpec((tokens, bw), column)
    ends = pl.BlockSpec((start.shape[0], bw), column)
    shapes = [((tokens, part), BF), ((tokens, part), F32), ((tokens, part), F32), (start.shape, F32)]
    return pl.pallas_call(
        functools.partial(recur_back_kernel, dims),
        grid=(held,),
        in_specs=[
            pl.BlockSpec(grad.shape, lambda h: (0, 0)),
            pl.BlockSpec((pre.shape[0], bw), column),
            pl.BlockSpec((8, bw), column),
            whole,
            whole,
            ends,
            pl.BlockSpec((tokens, 2 * bw), column),
            pl.BlockSpec((mix_w.shape[0], bw), lambda h: (0, 2 * held + h)),
        ],
        out_specs=[whole, whole, whole, ends],
        out_shape=[jax.ShapeDtypeStruct(*shape) for shape in shapes],
        scratch_shapes=[pltpu.VMEM((tokens, bw), F32)],
        cost_estimate=FREE,
        compiler_params=pltpu.CompilerParams(vmem_limit_bytes=GRANT),
    )(grad, pre, rows, state, prod, start, gate, mix_w)


def recur_grad_kernel(
    span, micro, local, prods, carried, state, prod, start, gate, conv, pre, rows, block,
    blocks_out, lru_out, spill_out, rows_out, gate_grad, conv_grad,
):
    count = local.shape[0] // span
    soft, sig, own = rows[0:1], rows[1:2], rows[6:7]
    taps = [rows[k + 2 : k + 3] for k in range(4)]
    width = local.shape[1]
    add_up = lambda v: jnp.sum(v, axis=0, keepdims=True)
    decay_sum = jnp.zeros((1, width), F32)
    for i in range(count):
        here = pl.ds(i * span, span)
        adjoint = local[here] + prods[here] * carried[i : i + 1]
        states = state[here] + prod[here] * start[i : i + 1]
        row = lax.broadcasted_iota(jnp.int32, states.shape, 0)
        earlier = jnp.where(row >= 1, pltpu.roll(states, 1, 0), start[i : i + 1])
        rec_gate, in_gate, decay, square, root = gate_values(gate[here], soft)
        conv_vals = conv[here].astype(F32)
        drive = adjoint * conv_vals
        grad_log = adjoint * earlier * decay - drive * in_gate * square / root
        decay_sum = decay_sum + add_up(grad_log * rec_gate)
        gate_grad[here, :width] = (-RATE * soft * grad_log * rec_gate * (1.0 - rec_gate)).astype(BF)
        gate_grad[here, width:] = (drive * root * in_gate * (1.0 - in_gate)).astype(BF)
        conv_grad[here] = adjoint * root * in_gate
    blocks_out[...] = lax.dot_general(
        conv[...], gate_grad[...], (((0,), (0,)), ((), ())), preferred_element_type=F32
    )
    conv_grad[...] += dot_right_t(gate_grad[...], block[0])
    tap_sums = [jnp.zeros((1, width), F32) for _ in range(4)]
    for i in range(count):
        here = pl.ds(i * span, span)
        grad = conv_grad[here]
        vals = with_halo(pre, i, span, micro).astype(BF).astype(F32)
        wide = jnp.concatenate([jnp.zeros((HALO, width), F32), grad], axis=0)
        total = taps[0] * wide
        tap_sums[0] = tap_sums[0] + add_up(grad * vals[HALO:])
        for k in range(1, 4):
            total = total + taps[k] * pltpu.roll(wide, span + HALO - k, 0)
            tap_sums[k] = tap_sums[k] + add_up(grad * pltpu.roll(vals, k, 0)[HALO:])
        lru_out[here] = total[HALO:]
        spill_out[pl.ds(i * HALO, HALO)] = total[:HALO]
    rows_out[...] = jnp.zeros(rows_out.shape, F32)
    rows_out[0:1] = decay_sum * sig * own * RATE
    for k in range(4):
        rows_out[k + 1 : k + 2] = tap_sums[k] * own


def recur_grad(local, prods, carried, state, prod, start, gate, conv, pre, rows, blocks, dims):
    tokens, part = state.shape
    span, micro, _, held, bw, _ = dims
    column = lambda h: (0, h)
    whole = pl.BlockSpec((tokens, bw), column)
    ends = pl.BlockSpec((start.shape[0], bw), column)
    return pl.pallas_call(
        functools.partial(recur_grad_kernel, span, micro),
        grid=(held,),
        in_specs=[
            whole,
            whole,
            ends,
            whole,
            whole,
            ends,
            pl.BlockSpec((tokens, 2 * bw), column),
            whole,
            pl.BlockSpec((pre.shape[0], bw), column),
            pl.BlockSpec((8, bw), column),
            pl.BlockSpec((1, bw, 2 * bw), lambda h: (h, 0, 0)),
        ],
        out_specs=[
            pl.BlockSpec((bw, 2 * bw), lambda h: (h, 0)),
            whole,
            pl.BlockSpec((start.shape[0] * HALO, bw), column),
            pl.BlockSpec((8, bw), column),
        ],
        out_shape=[
            jax.ShapeDtypeStruct((part, 2 * bw), F32),
            jax.ShapeDtypeStruct((tokens, part), F32),
            jax.ShapeDtypeStruct((start.shape[0] * HALO, part), F32),
            jax.ShapeDtypeStruct((8, part), F32),
        ],
        scratch_shapes=[pltpu.VMEM((tokens, 2 * bw), BF), pltpu.VMEM((tokens, bw), F32)],
        cost_estimate=FREE,
        compiler_params=pltpu.CompilerParams(vmem_limit_bytes=GRANT),
    )(local, prods, carried, state, prod, start, gate, conv, pre, rows, blocks)


def recur_in_kernel(dims, gelu, lru, spill, rows, small, mixed, mix_w, pair, parts, gains):
    span, _, _, held, bw, _ = dims
    part = held * bw

    @pl.when(pl.program_id(0) == 0)
    def _():
        pair[:, :part] = gelu[...]

        def one_head(h):
            lru_h, spill_h, own = columns(lru, h, bw), columns(spill, h, bw), columns(rows, h, bw)[6:7]
            cols = pl.ds(pl.multiple_of((held + h) * bw, 128), bw)
            for i in range(lru.shape[0] // span):
                vals = lru_h[pl.ds(i * span, span)]
                late = vals[span - HALO :] + spill_h[pl.ds(i * HALO, HALO)]
                vals = jnp.concatenate([vals[: span - HALO], late], axis=0) * own
                pair[pl.ds(i * span, span), cols] = vals.astype(BF)

        by_heads(held, one_head)

    grad = dot_right_t(pair[...], mix_w[...])
    parts[...] = grad.astype(BF)
    gain = jnp.sum(grad * mixed[...].astype(F32), axis=0, keepdims=True)
    gains[0:1] = gain / small[0:1]


def recur_in(gelu, lru, spill, rows, small, mixed, mix_w, dims):
    tokens, part = gelu.shape
    width, chunk = mix_w.shape[0], 256
    whole = lambda v: pl.BlockSpec(v.shape, lambda j: (0, 0))
    column = lambda j: (0, j)
    return pl.pallas_call(
        functools.partial(recur_in_kernel, dims),
        grid=(width // chunk,),
        in_specs=[
            whole(gelu),
            whole(lru),
            whole(spill),
            whole(rows),
            pl.BlockSpec((8, chunk), column),
            pl.BlockSpec((tokens, chunk), column),
            pl.BlockSpec((chunk, 2 * part), lambda j: (j, 0)),
        ],
        out_specs=[
            pl.BlockSpec((tokens, 2 * part), lambda j: (0, 0)),
            pl.BlockSpec((tokens, chunk), column),
            pl.BlockSpec((8, chunk), column),
        ],
        out_shape=[
            jax.ShapeDtypeStruct((tokens, 2 * part), BF),
            jax.ShapeDtypeStruct((tokens, width), BF),
            jax.ShapeDtypeStruct((8, width), F32),
        ],
        cost_estimate=FREE,
        compiler_params=pltpu.CompilerParams(vmem_limit_bytes=GRANT),
    )(gelu, lru, spill, rows, small, mixed, mix_w)


def device(p, f=None, z=None, x=None, c=None):
    f, z = p.f if f is None else f, p.z if z is None else z
    x, c = p.x if x is None else x, p.c if c is None else c
    return (f, ((p.r * TP + z) * 2 + x) * 2 + c)


def copy_to(src, dst, sems, index, dev):
    return pltpu.make_async_remote_copy(
        src_ref=src,
        dst_ref=dst,
        send_sem=sems[0].at[index],
        recv_sem=sems[1].at[index],
        device_id=dev,
        device_id_type=MESH,
    )


def pairs(*shape):
    return [pltpu.SemaphoreType.DMA(shape), pltpu.SemaphoreType.DMA(shape)]


def greet(devices):
    barrier = pltpu.get_barrier_semaphore()
    for dev in devices:
        pl.semaphore_signal(barrier, inc=1, device_id=dev, device_id_type=MESH)
    pl.semaphore_wait(barrier, len(devices))


def by_rows(count, body, step=16):
    def turn(i, _):
        body(pl.ds(pl.multiple_of(i * step, step), step))
        return 0

    assert count % step == 0
    lax.fori_loop(0, count // step, turn, 0)


class Gather:
    def __init__(self, p, out, ups, downs):
        self.p, self.out, self.ups, self.downs = p, out, ups, downs
        self.up = device(p, z=jnp.minimum(p.z + 1, TP - 1))
        self.down = device(p, z=jnp.maximum(p.z - 1, 0))

    def begin(self, h, src):
        z = self.p.z

        @pl.when(z < TP - 1)
        def _():
            copy_to(src, self.out.at[z, h], self.ups, (0, h), self.up).start()

        @pl.when(z > 0)
        def _():
            copy_to(src, self.out.at[z, h], self.downs, (0, h), self.down).start()

    def step(self, k, h):
        z, out = self.p.z, self.out

        @pl.when(z >= k)
        def _():
            block = out.at[z - k, h]
            copy_to(block, block, self.ups, (k - 1, h), self.up).wait_recv()
            if k < TP - 1:

                @pl.when(z < TP - 1)
                def _():
                    copy_to(block, block, self.ups, (k, h), self.up).start()

        @pl.when(z <= TP - 1 - k)
        def _():
            block = out.at[z + k, h]
            copy_to(block, block, self.downs, (k - 1, h), self.down).wait_recv()
            if k < TP - 1:

                @pl.when(z > 0)
                def _():
                    copy_to(block, block, self.downs, (k, h), self.down).start()

    def close(self, halves):
        z, block = self.p.z, self.out.at[0, 0]
        for h in range(halves) if isinstance(halves, int) else halves:
            for k in range(TP - 1):

                @pl.when((z >= k) & (z < TP - 1))
                def _():
                    copy_to(block, block, self.ups, (k, h), self.up).wait_send()

                @pl.when((z <= TP - 1 - k) & (z > 0))
                def _():
                    copy_to(block, block, self.downs, (k, h), self.down).wait_send()


class LineSum:
    def __init__(self, p, parts, scratch):
        self.p, self.parts = p, parts
        self.got_up, self.got_down, self.out_up, self.out_down = scratch[:4]
        self.ups, self.downs = scratch[4:6], scratch[6:8]
        self.halves, self.rows = parts.shape[1:3]
        self.up = device(p, z=jnp.minimum(p.z + 1, TP - 1))
        self.down = device(p, z=jnp.maximum(p.z - 1, 0))

    @staticmethod
    def scratch(parts):
        block = parts[1:]
        return [
            pltpu.VMEM((TP - 1,) + block, BF),
            pltpu.VMEM((TP - 1,) + block, BF),
            pltpu.VMEM((TP - 2,) + block, BF),
            pltpu.VMEM((TP - 2,) + block, BF),
            *pairs(TP - 1, parts[1]),
            *pairs(TP - 1, parts[1]),
        ]

    def clear(self):
        z = self.p.z

        @pl.when(z == 0)
        def _():
            for h in range(self.halves):
                by_rows(self.rows, lambda at: self.fill(self.got_up, h, at))

        @pl.when(z == TP - 1)
        def _():
            for h in range(self.halves):
                by_rows(self.rows, lambda at: self.fill(self.got_down, h, at))

    def fill(self, ref, h, at):
        ref[0, h, at] = jnp.zeros((at.size, ref.shape[-1]), BF)

    def one_way(self, k, h, place, block, got, out, sems, dev):
        @pl.when(place == 0)
        def _():
            copy_to(self.parts.at[block, h], got.at[k - 1, h], sems, (k - 1, h), dev).start()

        if k < TP - 1:

            @pl.when((place >= 1) & (place + k <= TP - 1))
            def _():
                copy_to(got.at[k, h], got.at[k, h], sems, (k, h), dev).wait_recv()

                def add(at):
                    total = self.parts[block, h, at].astype(F32) + got[k, h, at].astype(F32)
                    out[k - 1, h, at] = total.astype(BF)

                by_rows(self.rows, add)
                copy_to(out.at[k - 1, h], got.at[k - 1, h], sems, (k - 1, h), dev).start()

    def step(self, k, h):
        z = self.p.z
        block = jnp.minimum(z + k, TP - 1)
        self.one_way(k, h, z, block, self.got_up, self.out_up, self.ups, self.up)
        block = jnp.maximum(z - k, 0)
        self.one_way(k, h, TP - 1 - z, block, self.got_down, self.out_down, self.downs, self.down)

    def arrive(self, h):
        z = self.p.z

        @pl.when(z >= 1)
        def _():
            got = self.got_up.at[0, h]
            copy_to(got, got, self.ups, (0, h), self.up).wait_recv()

        @pl.when(z <= TP - 2)
        def _():
            got = self.got_down.at[0, h]
            copy_to(got, got, self.downs, (0, h), self.down).wait_recv()

    def total(self, h, at):
        total = self.parts[self.p.z, h, at].astype(F32) + self.got_up[0, h, at].astype(F32)
        return total + self.got_down[0, h, at].astype(F32)

    def close(self):
        z, got = self.p.z, self.got_up.at[0, 0]
        for h in range(self.halves):
            for k in range(1, TP):

                @pl.when(z + k <= TP - 1)
                def _():
                    copy_to(got, got, self.ups, (k - 1, h), self.up).wait_send()

                @pl.when(z - k >= 0)
                def _():
                    copy_to(got, got, self.downs, (k - 1, h), self.down).wait_send()


def greet_line(p, others=()):
    barrier = pltpu.get_barrier_semaphore()
    for dev in others:
        pl.semaphore_signal(barrier, inc=1, device_id=dev, device_id_type=MESH)

    @pl.when(p.z > 0)
    def _():
        pl.semaphore_signal(barrier, inc=1, device_id=device(p, z=p.z - 1), device_id_type=MESH)

    @pl.when(p.z < TP - 1)
    def _():
        pl.semaphore_signal(barrier, inc=1, device_id=device(p, z=p.z + 1), device_id_type=MESH)

    inner = (p.z > 0) & (p.z < TP - 1)

    @pl.when(inner)
    def _():
        pl.semaphore_wait(barrier, len(others) + 2)

    @pl.when(jnp.logical_not(inner))
    def _():
        pl.semaphore_wait(barrier, len(others) + 1)


class Spread:
    KINDS = ((0, 0), (0, 1), (1, 0), (1, 1))

    def __init__(self, p, whole, sems):
        self.p, self.whole, self.started = p, whole, []
        self.xs, self.fs, self.gs, self.cs = sems[0:2], sems[2:4], sems[4:6], sems[6:8]
        self.to_x, self.to_f = device(p, x=1 - p.x), device(p, f=1 - p.f)
        self.to_c = device(p, c=1 - p.c)

    @staticmethod
    def scratch():
        return [*pairs(TP), *pairs(TP), *pairs(TP), *pairs(4, TP)]

    def slot(self, kind, d, other_core=False):
        p, (f, x) = self.p, self.KINDS[kind]
        c = 1 - p.c if other_core else p.c
        return self.whole.at[(p.f + f) % 2, 0, (p.z - d) % TP, (p.x + x) % 2, c]

    def send(self, src, dst, sems, index, dev):
        copy = copy_to(src, dst, sems, index, dev)
        copy.start()
        self.started.append(copy)

    def wait(self, ref, sems, index):
        copy_to(ref, ref, sems, index, self.to_x).wait_recv()

    def spread(self, d, src=None):
        dst = self.slot(0, d)
        src = dst if src is None else src
        self.send(src, dst, self.xs, (d,), self.to_x)
        self.send(src, dst, self.fs, (d,), self.to_f)
        self.send(src, dst, self.cs, (0, d), self.to_c)

    def given(self, d, own, by_x, by_f):
        self.send(own, self.slot(0, d), self.cs, (0, d), self.to_c)
        self.send(by_x, self.slot(1, d), self.cs, (1, d), self.to_c)
        self.send(by_f, self.slot(2, d), self.cs, (2, d), self.to_c)
        if d % 2 == 0:
            self.send(by_x, self.slot(1, d), self.gs, (d,), self.to_f)
        else:
            self.send(by_f, self.slot(2, d), self.gs, (d,), self.to_x)

    def sides(self, d):
        ref = self.slot(1, d)
        self.wait(ref, self.xs, (d,))
        if d % 2 == 0:
            self.send(ref, ref, self.gs, (d,), self.to_f)
        self.send(ref, ref, self.cs, (1, d), self.to_c)
        ref = self.slot(2, d)
        self.wait(ref, self.fs, (d,))
        if d % 2 == 1:
            self.send(ref, ref, self.gs, (d,), self.to_x)
        self.send(ref, ref, self.cs, (2, d), self.to_c)

    def corner(self, d):
        ref = self.slot(3, d)
        self.wait(ref, self.gs, (d,))
        self.send(ref, ref, self.cs, (3, d), self.to_c)

    def close(self, pieces):
        for kind in range(4):
            for d in pieces:
                self.wait(self.slot(kind, d, True), self.cs, (kind, d))
        for copy in self.started:
            copy.wait_send()


def pack_kernel(bw, gelu, lru, out_t, blocks, small, gate, up, down_t, mix, *ffw):
    p = Place()
    heads = gelu.shape[1] // bw
    part, ffw_part = -(-heads // TP) * bw, gate.shape[1] // TP
    for d in range(TP):
        z = (p.z + d) % TP
        cols = pl.ds(pl.multiple_of(z * heads // TP * bw, 128), part)
        sources = [gelu[:, cols], lru[:, cols], out_t[:, cols], blocks[...], small[...]]
        offset = 0
        for source in sources:
            mix[d, :, offset : offset + source.shape[1]] = source
            offset += source.shape[1]
        cols = pl.ds(pl.multiple_of(z * ffw_part, 128), ffw_part)
        for i, source in enumerate((gate, up, down_t)):
            ffw[d][:, i * ffw_part : (i + 1) * ffw_part] = source[:, cols]


def pack(weights, bw):
    rows, lru_width = weights[0].shape
    part = -(-lru_width // bw // TP) * bw
    mix_cols = 3 * part + weights[3].shape[1] + weights[4].shape[1]
    piece = jax.ShapeDtypeStruct((rows, 3 * weights[5].shape[1] // TP), BF)
    mix, *ffw = pl.pallas_call(
        functools.partial(pack_kernel, bw),
        in_specs=[VMEM] * 8,
        out_specs=[VMEM] * (1 + TP),
        out_shape=[jax.ShapeDtypeStruct((TP, rows, mix_cols), BF), *[piece] * TP],
        compiler_params=pltpu.CompilerParams(vmem_limit_bytes=GRANT),
    )(*weights)
    return mix, ffw


def intake_kernel(
    mix_p, ffw_0, ffw_1, x_p, cot_p, mix_w, ffw_w, piece_1, x_all, cot_all,
    zs, zr, us, ur, vs, vr, cus, cur, cvs, cvr, local, *sems
):
    p = Place()
    mix, ffw = Spread(p, mix_w, sems[:8]), Spread(p, ffw_w, sems[8:])
    to_z = [device(p, z=(p.z + d) % TP) for d in range(TP)]
    greet(to_z[1:] + [mix.to_x, mix.to_f, mix.to_c])
    started = []

    def along_z(i, src, dst, d):
        copy = copy_to(src, dst, (zs, zr), (i,), to_z[d])
        copy.start()
        started.append(copy)

    def from_z(i, ref):
        copy_to(ref, ref, (zs, zr), (i,), to_z[1]).wait_recv()

    for d in (1, 3, 2):
        along_z(d, mix_p.at[d], mix.slot(0, 0), d)
    mix.spread(0, mix_p.at[0])
    ffw.spread(0, ffw_0)
    stays = [
        pltpu.make_async_copy(mix_p.at[0], mix.slot(0, 0), local.at[0]),
        pltpu.make_async_copy(ffw_0, ffw.slot(0, 0), local.at[1]),
        pltpu.make_async_copy(x_p, x_all.at[p.z], local.at[2]),
        pltpu.make_async_copy(cot_p, cot_all.at[p.z], local.at[3]),
    ]
    for copy in stays:
        copy.start()
    line = Gather(p, x_all, (us, ur), (vs, vr))
    cot = Gather(p, cot_all, (cus, cur), (cvs, cvr))
    for d in (1, 3):
        from_z(d, mix.slot(0, d))
        mix.spread(d)
    for h in range(x_p.shape[0]):
        line.begin(h, x_p.at[h])
    for h in range(cot_p.shape[0]):
        cot.begin(h, cot_p.at[h])
    from_z(2, mix.slot(0, 2))
    mix.spread(2)
    along_z(0, ffw_1, piece_1, 1)
    mix.sides(0)
    ffw.sides(0)
    mix.corner(0)
    for h in range(x_p.shape[0]):
        line.step(1, h)
    for h in range(cot_p.shape[0]):
        cot.step(1, h)
    for d in (1, 3):
        mix.sides(d)
    ffw.corner(0)
    for h in range(x_p.shape[0]):
        line.step(2, h)
    for h in range(cot_p.shape[0]):
        cot.step(2, h)
    for d in (1, 3):
        mix.corner(d)
    mix.sides(2)
    for h in range(x_p.shape[0]):
        line.step(3, h)
    for h in range(cot_p.shape[0]):
        cot.step(3, h)
    mix.corner(2)
    from_z(0, piece_1)
    mix.close(range(TP))
    ffw.close((0,))
    for copy in started:
        copy.wait_send()
    line.close(x_p.shape[0])
    cot.close(cot_p.shape[0])
    for copy in stays:
        copy.wait()


def intake(mix_p, ffw_0, ffw_1, x_p, cot_p, p):
    whole = lambda v: jax.ShapeDtypeStruct((p.fs, 1, TP, 2, 2) + v.shape[-2:], BF)
    mix_w, ffw_w, piece_1, x_all, cot_all = pl.pallas_call(
        intake_kernel,
        in_specs=[ANY] * 5,
        out_specs=[ANY] * 5,
        out_shape=[
            whole(mix_p),
            whole(ffw_0),
            jax.ShapeDtypeStruct(ffw_1.shape, BF),
            jax.ShapeDtypeStruct((TP,) + x_p.shape, BF),
            jax.ShapeDtypeStruct((TP,) + cot_p.shape, BF),
        ],
        scratch_shapes=[
            *pairs(TP),
            *pairs(TP - 1, x_p.shape[0]),
            *pairs(TP - 1, x_p.shape[0]),
            *pairs(TP - 1, cot_p.shape[0]),
            *pairs(TP - 1, cot_p.shape[0]),
            pltpu.SemaphoreType.DMA((4,)),
            *Spread.scratch(),
            *Spread.scratch(),
        ],
        compiler_params=pltpu.CompilerParams(collective_id=0, has_side_effects=True),
    )(mix_p, ffw_0, ffw_1, x_p, cot_p)
    return mix_w.reshape(-1, mix_p.shape[-1]), ffw_w, piece_1, x_all, cot_all.reshape(TP, 1, -1, cot_p.shape[-1])


class Stream:
    def __init__(self, pick, count, buffers, sems):
        self.pick, self.count, self.buffers, self.sems = pick, count, buffers, sems

    def load(self, i):
        slot = i % 2
        return pltpu.make_async_copy(self.pick(i), self.buffers.at[slot], self.sems.at[slot])

    def start(self):
        self.load(0).start()

    def run(self, low, high, body):
        def turn(i, _):
            @pl.when(i + 1 < self.count)
            def _():
                self.load(i + 1).start()

            self.load(i).wait()
            body(i, self.buffers.at[i % 2])
            return 0

        lax.fori_loop(low, high, turn, 0)


def flat(block):
    return block.reshape(-1, block.shape[-1])


FFW_CHUNK = 256


def ffw_streams(ffw_w, part, buffers):
    chunks, rest = part // FFW_CHUNK, part % FFW_CHUNK
    col = lambda base, i: pl.ds(pl.multiple_of(base + i * FFW_CHUNK, 128), FFW_CHUNK)
    pick = lambda base: lambda i: ffw_w.at[:, 0, :, :, :, :, col(base, i)]
    half = TP // 2
    rows = lambda cols: lambda i: ffw_w.at[i // 2, 0, pl.ds(i % 2 * half, half), :, :, :, cols]
    gate = Stream(pick(0), chunks, buffers[0], buffers[1])
    up = Stream(pick(part), chunks, buffers[2], buffers[3])
    down = Stream(pick(2 * part), chunks, buffers[0], buffers[1])
    down_rows = Stream(rows(pl.ds(2 * part, part)), 4, buffers[4], buffers[5])
    both_rows = Stream(rows(pl.ds(0, 2 * part)), 4, buffers[6], buffers[7])
    return gate, up, down, down_rows, both_rows


class Feed:
    def __init__(self, x, cot, ffw_w, outs, vals, scratch):
        self.x, self.cot, self.vals = x, cot, vals
        self.hidden, self.grad_pair, self.out_parts, self.in_parts = outs
        self.part = part = self.hidden.shape[1]
        self.chunks, self.rest = part // FFW_CHUNK, part % FFW_CHUNK
        streams = ffw_streams(ffw_w, part, scratch[:8])
        self.gate, self.up, self.down, self.down_rows, self.both_rows = streams
        self.tails, tail_sems = scratch[8:10]
        self.last = last = self.chunks * FFW_CHUNK
        self.loads = [
            pltpu.make_async_copy(
                ffw_w.at[:, 0, :, :, :, :, pl.ds(k * part + last, self.rest)],
                self.tails.at[k],
                tail_sems.at[k],
            )
            for k in range(3)
        ]

    def begin(self):
        self.gate.start()
        self.up.start()
        for load in self.loads:
            load.start()
        self.down_rows.start()
        self.both_rows.start()

    def cols(self, i, base):
        return pl.ds(pl.multiple_of(base + i * FFW_CHUNK, 128), FFW_CHUNK)

    def forward_cols(self, cols, other, gate_w, up_w):
        gate_vals = dot_plain(self.x[...], gate_w)
        up_vals = dot_plain(self.x[...], up_w)
        self.vals[:, cols] = gate_vals
        self.vals[:, other] = up_vals
        self.hidden[:, cols] = (gelu_pair(gate_vals)[0] * up_vals).astype(BF)

    def forward(self, low, high):
        def turn(i, _):
            for stream in (self.gate, self.up):

                @pl.when(i + 1 < self.chunks)
                def _(stream=stream):
                    stream.load(i + 1).start()

                stream.load(i).wait()
            weights = [flat(stream.buffers[i % 2]) for stream in (self.gate, self.up)]
            self.forward_cols(self.cols(i, 0), self.cols(i, self.part), *weights)
            return 0

        lax.fori_loop(low, high, turn, 0)

    def forward_end(self):
        self.down.start()
        for load in self.loads:
            load.wait()
        cols = pl.ds(self.last, self.rest), pl.ds(self.part + self.last, self.rest)
        self.forward_cols(*cols, flat(self.tails[0]), flat(self.tails[1]))

    def by_weight_rows(self, stream, source, out, low=0, high=4):
        def body(i, buffer):
            weights = flat(buffer[...])
            count = weights.shape[0]
            cols = pl.ds(pl.multiple_of(i * count, 128), count)
            out[:, cols] = dot_right_t(source[...], weights).astype(BF)

        stream.run(low, high, body)

    def forward_out(self):
        self.by_weight_rows(self.down_rows, self.hidden, self.out_parts)

    def backward_cols(self, cols, other, weights):
        grad = dot_plain(self.cot[...], weights)
        act, slope = gelu_pair(self.vals[:, cols])
        self.grad_pair[:, cols] = (grad * self.vals[:, other] * slope).astype(BF)
        self.grad_pair[:, other] = (grad * act).astype(BF)

    def backward(self, low, high):
        def body(i, buffer):
            self.backward_cols(self.cols(i, 0), self.cols(i, self.part), flat(buffer[...]))

        self.down.run(low, high, body)

    def backward_end(self):
        cols = pl.ds(self.last, self.rest), pl.ds(self.part + self.last, self.rest)
        self.backward_cols(*cols, flat(self.tails[2]))

    def backward_in(self, low, high):
        self.by_weight_rows(self.both_rows, self.grad_pair, self.in_parts, low, high)


def ffw_scratch(ffw_w, part):
    f, _, z, x, c, rows, _ = ffw_w.shape
    column = lambda width: pltpu.VMEM((2, f, z, x, c, rows, width), BF)
    wide = lambda width: pltpu.VMEM((2, z // 2, x, c, rows, width), BF)
    pair = pltpu.SemaphoreType.DMA((2,))
    return [
        column(FFW_CHUNK), pair, column(FFW_CHUNK), pair, wide(part), pair, wide(2 * part), pair,
        pltpu.VMEM((3, f, z, x, c, rows, part % FFW_CHUNK), BF),
        pltpu.SemaphoreType.DMA((3,)),
    ]


def middle_kernel(with_ffw, *refs):
    parts, x_zero, gain, cot_p, cot_first, piece_1, by_x, by_f, piece_2, piece_3, _ = refs[:11]
    x_one_out, ffw_out, cot_out, ffw_w, *refs = refs[11:]
    if with_ffw:
        hidden_out, pair_out, parts_out, in_out, *refs = refs
    x_one, ffw_all, cot_all, own, local, gu0, gu1, gd0, gd1, cu0, cu1, cd0, cd1 = refs[:13]
    p = Place()
    line = LineSum(p, parts, refs[13:21])
    out = Gather(p, ffw_all, (gu0, gu1), (gd0, gd1))
    cot = Gather(p, cot_all, (cu0, cu1), (cd0, cd1))
    halves, rows = parts.shape[1:3]
    line.clear()
    stays = []

    def stay(src, dst):
        copy = pltpu.make_async_copy(src, dst, local.at[len(stays)])
        copy.start()
        stays.append(copy)

    if with_ffw:
        ffw = Spread(p, ffw_w, refs[21:29])
        outs, vals, buffers = refs[29:33], refs[33], refs[34:44]
        bounce_sems = refs[44]
        greet_line(p, (ffw.to_x, ffw.to_f, ffw.to_c))
    else:
        greet_line(p)
    side = lambda name, *args: getattr(ffw, name)(*args) if with_ffw else None
    for h in range(halves):
        line.step(TP - 1, h)
    stay(cot_first, cot_all.at[:, pl.ds(0, 1)])
    side("given", 1, piece_1, by_x, by_f)
    side("spread", 3, piece_3)
    side("spread", 2, piece_2)
    if with_ffw:
        part = vals.shape[1] // 2
        moves = [(piece_1, 0, 1), (by_x, 1, 1), (by_f, 2, 1), (piece_3, 0, 3), (piece_2, 0, 2)]
        steps = [(src, ffw.slot(kind, d), k) for src, kind, d in moves for k in range(2)]

        def bounce(i, out):
            src, dst, k = steps[i]
            cols = pl.ds(0, 2 * part) if k == 0 else pl.ds(2 * part, part)
            space = buffers[6 - 2 * k].at[i // 2 % 2, 0, 0, 0]
            if out:
                return pltpu.make_async_copy(space, dst.at[:, cols], bounce_sems.at[i % 4])
            return pltpu.make_async_copy(src.at[:, cols], space, bounce_sems.at[4])

        for i in range(len(steps)):
            if i >= 4:
                bounce(i - 4, True).wait()
            bounce(i, False).start()
            bounce(i, False).wait()
            bounce(i, True).start()
        for i in range(len(steps) - 4, len(steps)):
            bounce(i, True).wait()
    for k in range(TP - 2, 0, -1):
        for h in range(halves):
            line.step(k, h)
    for h in range(halves):
        line.arrive(h)

        def finish(at, h=h):
            value = x_zero[h, at].astype(F32) + line.total(h, at)
            x_one[h, at] = value
            own[h, at] = normed(value, gain[...]).astype(BF)

        by_rows(rows, finish)
        out.begin(h, own.at[h])
        stay(own.at[h], ffw_all.at[p.z, h])
    for h in range(halves):
        out.step(1, h)
    for d in (3, 2):
        side("sides", d)
    for h in range(halves):
        out.step(2, h)
    cot.begin(1, cot_p)
    stay(cot_p, cot_all.at[p.z, 1])
    side("corner", 1)
    for d in (3, 2):
        side("corner", d)
    for h in range(halves):
        out.step(3, h)
    cot.step(1, 1)
    side("close", (1, 2, 3))
    if not with_ffw:
        cot.step(2, 1)
        cot.step(3, 1)
    for copy in stays:
        copy.wait()
    done = len(stays)
    stay(x_one, x_one_out)
    stay(ffw_all, ffw_out)
    if not with_ffw:
        stay(cot_all, cot_out)
    else:
        tokens = lambda ref: ref.reshape(TP * halves * rows, parts.shape[3])
        hidden, pair, out_parts, in_parts = outs
        flat_outs = (hidden, pair, tokens(out_parts), in_parts)
        feed = Feed(tokens(ffw_all), tokens(cot_all), ffw_w, flat_outs, vals, buffers)
        feed.begin()
        feed.forward(0, 2)
        cot.step(2, 1)
        feed.forward(2, 6)
        cot.step(3, 1)
        stay(cot_all, cot_out)
        feed.forward(6, feed.chunks)
        feed.forward_end()
        feed.forward_out()
        stay(hidden, hidden_out)
        stay(out_parts, parts_out)
        feed.backward(0, feed.chunks)
        feed.backward_end()
        stay(pair, pair_out)
        feed.backward_in(0, 4)
        stay(in_parts, in_out)
    line.close()
    out.close(halves)
    cot.close((1,))
    for copy in stays[done:]:
        copy.wait()


def middle(parts, x_zero, gain, cot_p, cot_first, pieces, ffw_w):
    shape = parts.shape
    with_ffw = ffw_w is not None
    line = (TP, 2) + cot_p.shape
    outs, extra = [], []
    if with_ffw:
        tokens, part = shape[0] * shape[1] * shape[2], ffw_w.shape[-1] // 3
        assert part // FFW_CHUNK >= 6 and part % FFW_CHUNK
        outs = [(tokens, part), (tokens, 2 * part), shape, (tokens, shape[3])]
        extra = [
            *Spread.scratch(),
            *(pltpu.VMEM(kept, BF) for kept in outs),
            pltpu.VMEM((tokens, 2 * part), F32),
            *ffw_scratch(ffw_w, part),
            pltpu.SemaphoreType.DMA((5,)),
        ]
    else:
        ffw_w = jnp.zeros((16, 128), BF)
        pieces = [ffw_w] * 5
    return pl.pallas_call(
        functools.partial(middle_kernel, with_ffw),
        in_specs=[VMEM] * 3 + [ANY] * 8,
        out_specs=[ANY] * (4 + len(outs)),
        out_shape=[
            jax.ShapeDtypeStruct(shape[1:], F32),
            jax.ShapeDtypeStruct(shape, BF),
            jax.ShapeDtypeStruct(line, BF),
            jax.ShapeDtypeStruct(ffw_w.shape, BF),
            *(jax.ShapeDtypeStruct(out, BF) for out in outs),
        ],
        input_output_aliases={10: 3},
        scratch_shapes=[
            pltpu.VMEM(shape[1:], F32),
            pltpu.VMEM(shape, BF),
            pltpu.VMEM(line, BF),
            pltpu.VMEM(shape[1:], BF),
            pltpu.SemaphoreType.DMA((shape[1] + 10,)),
            *pairs(TP - 1, shape[1]),
            *pairs(TP - 1, shape[1]),
            *pairs(TP - 1, 2),
            *pairs(TP - 1, 2),
            *LineSum.scratch(shape),
            *extra,
        ],
        compiler_params=pltpu.CompilerParams(
            collective_id=1, has_side_effects=True, vmem_limit_bytes=GRANT
        ),
    )(parts, x_zero, gain, cot_p, cot_first, *pieces, ffw_w)


def norm_back(values, gain, grad):
    inv = lax.rsqrt(jnp.mean(values * values, axis=-1, keepdims=True) + EPS)
    unit = values * inv
    through = grad * gain
    inner = jnp.mean(through * unit, axis=-1, keepdims=True)
    return inv * (through - unit * inner), grad * unit


class Fold:
    ORDER = ((0, 1, 1), (1, 1, 1), (0, 0, 1), (1, 1, 0), (0, 1, 0), (1, 0, 1), (0, 0, 0), (1, 0, 0))

    def __init__(self, p, grad, cores, scratch):
        self.p, self.grad, self.cores = p, grad, cores
        self.sums, self.stage, self.got, self.got_late = scratch[:4]
        self.near, self.staged = scratch[4:6]
        self.core_sems, self.early, self.late = scratch[6:8], scratch[8:10], scratch[10:12]
        self.to = (device(p, x=1 - p.x), device(p, f=1 - p.f))
        self.to_c = device(p, c=1 - p.c)

    @staticmethod
    def shapes(grad, staged):
        block = (TP // 2,) + grad.shape[-2:]
        waiting = (2,) if staged else (2, 2, 2)
        return jax.ShapeDtypeStruct((2, 2, 2) + block, BF), [
            pltpu.VMEM((2, 2, 2) + block, BF),
            pltpu.VMEM(waiting + block, BF),
            pltpu.VMEM((2, 2) + block, BF),
            pltpu.VMEM((2,) + block, BF),
            pltpu.SemaphoreType.DMA((8,)),
            pltpu.SemaphoreType.DMA((2,)),
            *pairs(8),
            *pairs(2, 2),
            *pairs(2),
        ]

    def block(self, way, f_rel, x_rel, c):
        p, half = self.p, TP // 2
        f, x = (p.f + f_rel) % 2, (p.x + x_rel) % 2
        return self.grad.at[f, 0, pl.ds(way * half, half), x, c]

    def cross(self, i):
        name = self.ORDER[i]
        src = self.block(*name, 1 - self.p.c)
        dst = self.stage if self.cores is None else self.cores
        return copy_to(src, dst.at[name], self.core_sems, (i,), self.to_c)

    def load(self, i):
        name = self.ORDER[i]
        return pltpu.make_async_copy(
            self.block(*name, self.p.c), self.sums.at[name], self.near.at[i]
        )

    def fetch(self, i):
        src = self.cores.at[self.ORDER[i]]
        return pltpu.make_async_copy(src, self.stage.at[i % 2], self.staged.at[i % 2])

    def first(self, way, block):
        src = self.sums.at[(0, block, 1) if way == 0 else (1, 1, block)]
        return copy_to(src, self.got.at[way, block], self.early, (way, block), self.to[way])

    def second(self, way):
        src = self.sums.at[(0, 1, 0) if way == 0 else (1, 0, 1)]
        return copy_to(src, self.got_late.at[way], self.late, (way,), self.to[1 - way])

    def add(self, name, *others):
        rows = self.sums.shape[-2]

        def turn(at):
            for k in range(TP // 2):
                total = self.sums[(*name, k, at)].astype(F32)
                for other in others:
                    total = total + other[k, at].astype(F32)
                self.sums[(*name, k, at)] = total.astype(BF)

        by_rows(rows, turn)

    def begin(self, blocks=range(8)):
        for i in blocks:
            self.cross(i).start()
            self.load(i).start()

    def issue(self, i):
        self.cross(i).wait_recv()
        self.fetch(i).start()

    def join(self, i):
        if self.cores is None:
            self.cross(i).wait_recv()
            self.load(i).wait()
            self.add(self.ORDER[i], self.stage.at[self.ORDER[i]])
        else:
            if i == 0:
                self.issue(0)
            if i + 1 < 8:
                self.issue(i + 1)
            self.fetch(i).wait()
            self.load(i).wait()
            self.add(self.ORDER[i], self.stage.at[i % 2])
        if i < 4:
            way = self.ORDER[i][0]
            self.first(way, self.ORDER[i][1 + way]).start()

    def middle(self):
        for way in range(2):
            self.first(way, 1).wait_recv()
            self.add((0, 1, 0) if way == 0 else (1, 0, 1), self.got.at[way, 1])
            self.second(way).start()

    def finish(self):
        for way in range(2):
            self.first(way, 0).wait_recv()
            self.second(way).wait_recv()
            self.add((way, 0, 0), self.got.at[way, 0], self.got_late.at[way])

    def result(self, z):
        return self.sums.at[z // (TP // 2), 0, 0, z % (TP // 2)]

    def close(self):
        for i in range(8):
            self.cross(i).wait_send()
        for way in range(2):
            self.second(way).wait_send()
            for block in range(2):
                self.first(way, block).wait_send()


def folds_of(p, grads, cores, scratch):
    return [Fold(p, g, c, scratch[12 * i : 12 * i + 12]) for i, (g, c) in enumerate(zip(grads, cores))]


GRAD_CHUNK = 640


class Outer:
    def __init__(self, grad, left, right, turned, buffers, sems):
        self.grad, self.left, self.right, self.turned = grad, left, right, turned
        self.buffers, self.sems = buffers, sems
        self.wide = buffers.shape[-1]
        self.across = grad.shape[-1] // self.wide
        self.count = 4 * self.across

    def place(self, i):
        return (lax.axis_index("fsdp") * 2 + 2 + i // self.across) % 4

    def store(self, i):
        k, half = self.place(i), TP // 2
        cols = pl.ds(pl.multiple_of(i % self.across * self.wide, 128), self.wide)
        dst = self.grad.at[k // 2, 0, pl.ds(k % 2 * half, half), :, :, :, cols]
        return pltpu.make_async_copy(self.buffers.at[i % 2], dst, self.sems.at[i % 2])

    def run(self, low, high):
        rows = self.turned.shape[0]

        def turn(i, _):
            @pl.when(i % self.across == 0)
            def _():
                cols = pl.ds(pl.multiple_of(self.place(i) * rows, 128), rows)
                self.turned[...] = jnp.transpose(self.left[:, cols])

            @pl.when(i >= low + 2)
            def _():
                self.store(i - 2).wait()

            cols = pl.ds(pl.multiple_of(i % self.across * self.wide, 128), self.wide)
            chunk = dot_plain(self.turned[...], self.right[:, cols]).astype(BF)
            self.buffers[i % 2] = chunk.reshape(self.buffers.shape[1:])
            self.store(i).start()
            return 0

        lax.fori_loop(low, high, turn, 0)

    def flush(self, done):
        for i in (done - 2, done - 1):
            self.store(i).wait()


def turn_kernel(count, *refs):
    parts, out_parts, x_one, cot, gain = refs[:5]
    factors, refs = refs[5 : 5 + (4 if count else 0)], refs[5 + (4 if count else 0) :]
    mixed_out, grad_x_one, grad_gain, mix_all = refs[:4]
    pieces, downs, refs = refs[4 : 4 + TP], refs[4 + TP : 4 + 2 * TP], refs[4 + 2 * TP :]
    grads, cores, refs = refs[:count], refs[count : 2 * count], refs[2 * count :]
    own, local, zs, zr, gu0, gu1, gd0, gd1 = refs[:8]
    p = Place()
    line, late = LineSum(p, parts, refs[8:16]), LineSum(p, out_parts, refs[16:24])
    folds = folds_of(p, grads, cores, refs[24 : 24 + 12 * count])
    out = Gather(p, mix_all, (gu0, gu1), (gd0, gd1))
    halves, rows = parts.shape[1:3]
    line.clear()
    late.clear()
    to_z = [device(p, z=(p.z + d) % TP) for d in range(TP)]
    started = []
    if folds:
        greet(to_z[1:] + [*folds[0].to, folds[0].to_c])
    else:
        greet_line(p)
    stays = []

    def stay(src, dst):
        copy = pltpu.make_async_copy(src, dst, local.at[len(stays)])
        copy.start()
        stays.append(copy)

    if folds:
        left, right, turned, buffers, chunk_sems, load_sems = refs[24 + 12 * count :]
        part = factors[1].shape[1]
        outers = [
            Outer(grads[m], left, right.at[:, pl.ds(m // 2 * part, part)], turned, buffers, chunk_sems)
            for m in range(3)
        ]
        down, gate, up = folds
        size = outers[0].count
        half = size // 2

    def load(m):
        cols = right.at[:, pl.ds(0, factors[2 * m + 1].shape[1])]
        copies = [
            pltpu.make_async_copy(factors[2 * m], left, load_sems.at[0]),
            pltpu.make_async_copy(factors[2 * m + 1], cols, load_sems.at[1]),
        ]
        for copy in copies:
            copy.start()
        for copy in copies:
            copy.wait()

    def outer(m, low, high):
        outers[m].run(low, high)
        outers[m].flush(high)
        folds[m].begin((0, 1, 3, 4) if high == half else (2, 5, 6, 7))

    def join(fold, *blocks):
        for i in blocks:
            fold.join(i)

    def line_step(k):
        for h in range(halves):
            line.step(k, h)

    line_step(3)
    for h in range(halves):
        late.step(TP - 1, h)
    if folds:
        load(0)
        outer(0, 0, half)
        outer(0, half, size)
        join(down, 0, 1)
        load(1)
        outer(1, 0, half)
        join(down, 2, 3)
    line_step(2)
    if folds:
        outer(1, half, size)
        join(down, 4, 5)
        outer(2, 0, half)
        join(gate, 0, 1)
        down.middle()
        join(gate, 2, 3)
    line_step(1)
    if folds:
        outer(2, half, size)
        join(gate, 4, 5)
    grad_gain[...] = jnp.zeros(grad_gain.shape, F32)
    for h in range(halves):
        line.arrive(h)

        def finish(at, h=h):
            grad, gains = norm_back(x_one[h, at], gain[...], line.total(h, at))
            grad = grad + cot[h, at].astype(F32)
            grad_x_one[h, at] = grad
            own[h, at] = grad.astype(BF)
            grad_gain[0:1] += jnp.sum(gains, axis=0, keepdims=True)

        by_rows(rows, finish)
        out.begin(h, own.at[h])
        stay(own.at[h], mix_all.at[p.z, h])
    if folds:
        join(up, 0, 1)
        gate.middle()
        join(up, 2, 3)
    for h in range(halves):
        out.step(1, h)
        late.step(2, h)
    if folds:
        join(down, 6, 7)
        down.finish()
        stay(down.result(p.z), downs[0])
        for d in (1, 3, 2):
            copy = copy_to(down.result((p.z + d) % TP), downs[d], (zs, zr), (d,), to_z[d])
            copy.start()
            started.append(copy)
        join(up, 4, 5)
        join(gate, 6, 7)
    for h in range(halves):
        out.step(2, h)
        late.step(1, h)
    if folds:
        join(up, 6, 7)
        up.middle()
    for h in range(halves):
        out.step(3, h)
    for h in range(halves):
        late.arrive(h)

        def store(at, h=h):
            mixed_out[h, at] = (x_one[h, at] + late.total(h, at)).astype(BF)

        by_rows(rows, store)
    for m, fold in enumerate(folds[1:]):
        fold.finish()
        for d in range(TP):
            stay(fold.result((p.z + d) % TP), pieces[d].at[:, pl.ds(m * part, part)])
    if folds:
        for d in range(1, TP):
            copy_to(downs[d], downs[d], (zs, zr), (d,), to_z[1]).wait_recv()
    for copy in started:
        copy.wait_send()
    for fold in folds:
        fold.close()
    line.close()
    late.close()
    out.close(halves)
    for copy in stays:
        copy.wait()


def turn(parts, out_parts, x_one, cot, gain, factors, p):
    shape, count, width = parts.shape, 3 if factors else 0, parts.shape[-1]
    rows = width // (p.fs * TP * 4)
    sizes = [factors[1].shape[1]] * count if factors else []
    grads = [jax.ShapeDtypeStruct((p.fs, 1, TP, 2, 2, rows, size), BF) for size in sizes]
    folded = [Fold.shapes(grad, True) for grad in grads]
    piece = jax.ShapeDtypeStruct((rows, 2 * sizes[0]) if factors else (16, 128), BF)
    down = jax.ShapeDtypeStruct((rows, sizes[0]) if factors else (16, 128), BF)
    extra = []
    if factors:
        assert all(size % GRAD_CHUNK == 0 for size in sizes)
        tokens, deep = factors[0].shape[0], width // 4
        extra = [
            pltpu.VMEM((tokens, width), BF),
            pltpu.VMEM((tokens, 2 * sizes[0]), BF),
            pltpu.VMEM((deep, tokens), BF),
            pltpu.VMEM((2, TP // 2, 2, 2, rows, GRAD_CHUNK), BF),
            pltpu.SemaphoreType.DMA((2,)),
            pltpu.SemaphoreType.DMA((2,)),
        ]
    results = pl.pallas_call(
        functools.partial(turn_kernel, count),
        in_specs=[VMEM] * 5 + [ANY] * len(factors),
        out_specs=[VMEM, VMEM, VMEM, ANY] + [ANY] * (2 * TP + 2 * count),
        out_shape=[
            jax.ShapeDtypeStruct(shape[1:], BF),
            jax.ShapeDtypeStruct(shape[1:], F32),
            jax.ShapeDtypeStruct((8, width), F32),
            jax.ShapeDtypeStruct(shape, BF),
            *[piece] * TP,
            *[down] * TP,
            *grads,
            *(cores for cores, _ in folded),
        ],
        scratch_shapes=[
            pltpu.VMEM(shape[1:], BF),
            pltpu.SemaphoreType.DMA((shape[1] + 2 * TP + 1,)),
            *pairs(TP),
            *pairs(TP - 1, shape[1]),
            *pairs(TP - 1, shape[1]),
            *LineSum.scratch(shape),
            *LineSum.scratch(shape),
            *(item for _, scratch in folded for item in scratch),
            *extra,
        ],
        compiler_params=pltpu.CompilerParams(
            collective_id=2, has_side_effects=True, vmem_limit_bytes=GRANT
        ),
    )(parts, out_parts, x_one, cot, gain, *factors)
    return results[:4], results[4 : 4 + TP], results[4 + TP : 4 + 2 * TP]


def final_kernel(*refs):
    parts, x_zero, gain, grad_x_one, vectors, blocks = refs[:6]
    factors, refs = refs[6:10], refs[10:]
    grad_in, sums = refs[:2]
    outs, grads, refs = refs[2:6], (blocks, *refs[6:9]), refs[9:]
    acc, got, vs, vr, zs, zr, local, left, right, turned, buffers, chunk_sems, load_sems = refs[:13]
    p = Place()
    line = LineSum(p, parts, refs[13:21])
    folds = folds_of(p, grads, [None] * 4, refs[21:])
    halves, rows = parts.shape[1:3]
    line.clear()
    to_z = [device(p, z=(p.z + d) % TP) for d in range(TP)]
    (to_x, to_f), to_c = folds[0].to, folds[0].to_c
    greet(to_z[1:] + [to_x, to_f, to_c])
    partners = [to_c, to_x, to_f] + [
        device(p, z=p.z + bit * (1 - 2 * (p.z // bit % 2))) for bit in (1, 2)
    ]
    part = factors[1].shape[1]
    outers = [
        Outer(grads[m], left, right.at[:, pl.ds(m // 3 * part, part)], turned, buffers, chunk_sems)
        for m in range(1, 4)
    ]

    def load(m):
        cols = right.at[:, pl.ds(0, factors[2 * m + 1].shape[1])]
        copies = [
            pltpu.make_async_copy(factors[2 * m], left, load_sems.at[0]),
            pltpu.make_async_copy(factors[2 * m + 1], cols, load_sems.at[1]),
        ]
        for copy in copies:
            copy.start()
        for copy in copies:
            copy.wait()

    def outer(m):
        outers[m - 1].run(0, outers[m - 1].count)
        outers[m - 1].flush(outers[m - 1].count)
        folds[m].begin()

    def join(m, *blocks):
        for i in blocks:
            folds[m].join(i)

    def line_step(k):
        for h in range(halves):
            line.step(k, h)

    def vector(i):
        return copy_to(acc.at[i], got.at[i], (vs, vr), (i,), partners[i])

    def next_vector(i):
        vector(i).wait_recv()
        if i < 4:
            acc[i + 1] = acc[i] + got[i]
            vector(i + 1).start()
        else:
            sums[...] = acc[i] + got[i]

    started, stays = [], []

    def send_on(m):
        folds[m].finish()
        for d in (1, 3, 2):
            src = folds[m].result((p.z + d) % TP)
            copy = copy_to(src, outs[m].at[p.z], (zs, zr), (m, d - 1), to_z[d])
            copy.start()
            started.append(copy)
        stays.append(pltpu.make_async_copy(folds[m].result(p.z), outs[m].at[p.z], local.at[m]))
        stays[-1].start()

    acc[0] = vectors[...]
    vector(0).start()
    folds[0].begin()
    line_step(3)
    join(0, 0, 1, 2, 3)
    load(0)
    outer(1)
    load(1)
    join(0, 4, 5)
    join(1, 0, 1)
    folds[0].middle()
    join(1, 2, 3)
    outer(2)
    line_step(2)
    next_vector(0)
    join(0, 6, 7)
    join(1, 4, 5)
    join(2, 0, 1)
    folds[1].middle()
    join(2, 2, 3)
    outer(3)
    line_step(1)
    next_vector(1)
    send_on(0)
    join(1, 6, 7)
    join(2, 4, 5)
    join(3, 0, 1)
    folds[2].middle()
    join(3, 2, 3)
    next_vector(2)
    send_on(1)
    join(2, 6, 7)
    join(3, 4, 5)
    folds[3].middle()
    join(3, 6, 7)
    send_on(2)
    next_vector(3)
    for h in range(halves):
        line.arrive(h)

        def finish(at, h=h):
            grad, _ = norm_back(x_zero[h, at].astype(F32), gain[...], line.total(h, at))
            grad_in[h, at] = grad_x_one[h, at] + grad

        by_rows(rows, finish)
    next_vector(4)
    send_on(3)
    for m in range(4):
        for d in range(1, TP):
            ref = outs[m].at[(p.z - d) % TP]
            copy_to(ref, ref, (zs, zr), (m, d - 1), to_z[1]).wait_recv()
    for copy in started:
        copy.wait_send()
    for i in range(5):
        vector(i).wait_send()
    for fold in folds:
        fold.close()
    line.close()
    for copy in stays:
        copy.wait()


def final(parts, x_zero, gain, grad_x_one, vectors, blocks, factors, p):
    shape = parts.shape
    rows, part = blocks.shape[-2], factors[1].shape[1]
    tokens, width = factors[0].shape
    shaped = jax.ShapeDtypeStruct
    grads = [shaped((p.fs, 1, TP, 2, 2, rows, part), BF)] * 3
    widths = [blocks.shape[-1]] + [part] * 3
    folded = [Fold.shapes(grad, False)[1] for grad in (blocks, *grads)]
    results = pl.pallas_call(
        final_kernel,
        in_specs=[VMEM] * 5 + [ANY] * 5,
        out_specs=[VMEM, VMEM] + [ANY] * 7,
        out_shape=[
            shaped(shape[1:], F32),
            shaped(vectors.shape, F32),
            *(shaped((TP, rows, wide), BF) for wide in widths),
            *grads,
        ],
        scratch_shapes=[
            pltpu.VMEM((5,) + vectors.shape, F32),
            pltpu.VMEM((5,) + vectors.shape, F32),
            *pairs(5),
            *pairs(4, TP - 1),
            pltpu.SemaphoreType.DMA((4,)),
            pltpu.VMEM((tokens, width), BF),
            pltpu.VMEM((tokens, 2 * part), BF),
            pltpu.VMEM((width // 4, tokens), BF),
            pltpu.VMEM((2, TP // 2, 2, 2, rows, part), BF),
            pltpu.SemaphoreType.DMA((2,)),
            pltpu.SemaphoreType.DMA((2,)),
            *LineSum.scratch(shape),
            *(item for scratch in folded for item in scratch),
        ],
        cost_estimate=FREE,
        compiler_params=pltpu.CompilerParams(
            collective_id=3, has_side_effects=True, vmem_limit_bytes=GRANT
        ),
    )(parts, x_zero, gain, grad_x_one, vectors, blocks, *factors)
    return results[0], results[1], results[2:6]


def chain_kernel(backward, sums, *refs):
    if backward:
        known, start, spans, send, recv = refs
    else:
        start, spans, send, recv = refs
    p = Place()
    peers = [device_q(p, (p.q + d) % NQ) for d in range(NQ)]
    greet(peers[1:])
    spans[p.q] = sums[...]
    copies = []
    for d in range(1, NQ):
        copies.append(copy_to(spans.at[p.q], spans.at[p.q], (send, recv), (d,), peers[d]))
        copies[-1].start()
    for d in range(1, NQ):
        ref = spans.at[(p.q - d) % NQ]
        copy_to(ref, ref, (send, recv), (d,), peers[d]).wait_recv()
    micro = sums.shape[1] // TP
    carry = jnp.zeros((micro, sums.shape[2]), F32)
    order = [(z, q) for z in range(TP) for q in range(NQ)]
    for z, q in reversed(order) if backward else order:
        here = slice(z * micro, (z + 1) * micro)

        @pl.when(p.q == q)
        def _(carry=carry, here=here):
            start[here] = carry

        decay = known[q, 0, here] if backward else spans[q, 0, here]
        carry = decay * carry + spans[q, 0 if backward else 1, here]
    for copy in copies:
        copy.wait_send()


def device_q(p, q):
    return device(p, x=q // 2, c=q % 2)


def chain(sums, known=None):
    backward = known is not None
    every = (NQ,) + sums.shape
    return pl.pallas_call(
        functools.partial(chain_kernel, backward),
        in_specs=[VMEM] * (2 if backward else 1),
        out_specs=[VMEM, VMEM],
        out_shape=[
            jax.ShapeDtypeStruct(sums.shape[1:], F32),
            jax.ShapeDtypeStruct(every, F32),
        ],
        scratch_shapes=pairs(NQ),
        cost_estimate=FREE,
        compiler_params=pltpu.CompilerParams(
            collective_id=5 if backward else 4, has_side_effects=True
        ),
    )(*((sums, known) if backward else (sums,)))


def unpack_kernel(count, *refs):
    p = Place()
    pieces, outs = refs[: TP * len(count)], refs[TP * len(count) :]
    for d in range(TP):
        first = 0
        for m, parts in enumerate(count):
            piece = pieces[m * TP + d]
            part = piece.shape[1] // parts
            cols = pl.ds(pl.multiple_of((p.z - d) % TP * part, 128), part)
            for i in range(parts):
                outs[first + i][:, cols] = piece[:, i * part : (i + 1) * part].astype(F32)
            first += parts


def unpack(groups, count):
    shapes = []
    for pieces, parts in zip(groups, count):
        rows, cols = pieces[0].shape
        shapes += [jax.ShapeDtypeStruct((rows, cols // parts * TP), F32)] * parts
    return pl.pallas_call(
        functools.partial(unpack_kernel, count),
        in_specs=[VMEM] * (TP * len(groups)),
        out_specs=[VMEM] * len(shapes),
        out_shape=shapes,
        compiler_params=pltpu.CompilerParams(vmem_limit_bytes=GRANT),
    )(*(piece for pieces in groups for piece in pieces))


def unpack_mix_kernel(spans, *refs):
    (blocks, *mix), (blocks_out, *mix_out) = refs[:4], refs[4:]
    total = blocks[0].astype(F32)
    for k in range(1, TP):
        total = total + blocks[k].astype(F32)
    blocks_out[...] = total
    for piece, out in zip(mix, mix_out):
        for k, (start, count) in enumerate(spans):
            out[:, start : start + count] = piece[k, :, :count].astype(F32)


def unpack_mix(mix, spans):
    wide = spans[-1][0] + spans[-1][1]
    shapes = [mix[0].shape[1:]] + [(mix[0].shape[1], wide)] * 3
    return pl.pallas_call(
        functools.partial(unpack_mix_kernel, spans),
        in_specs=[VMEM] * 4,
        out_specs=[VMEM] * 4,
        out_shape=[jax.ShapeDtypeStruct(shape, F32) for shape in shapes],
        compiler_params=pltpu.CompilerParams(vmem_limit_bytes=GRANT),
    )(*mix)


def geglu(gate_vals, up_vals):
    return jax.nn.gelu(gate_vals) * up_vals


def all_spans(value, p):
    by_q = everywhere(value, shift_q, p.q, NQ)
    by_r = everywhere(by_q, shift_r, p.r, p.rests)
    return jnp.swapaxes(by_r, 1, 2).reshape((-1,) + value.shape[1:])


def own_spans(spans, p):
    split = spans.reshape((p.rests, TP, NQ) + spans.shape[1:])
    return lax.dynamic_index_in_dim(at(split, p.r), p.q, 1, keepdims=False)


def on_device(
    inputs,
    cotangent,
    proj_gelu,
    proj_lru,
    gate_blocks,
    proj_out,
    ffw_gate,
    ffw_up,
    ffw_down,
    norm_mix,
    norm_ffw,
    decay_param,
    conv_taps,
):
    p = Place()
    micro, span, width = inputs.shape[0], inputs.shape[2], inputs.shape[3]
    lru_width = proj_gelu.shape[1]
    tap_count = conv_taps.shape[1]
    block_width = gate_blocks.shape[1] // 2
    heads = lru_width // block_width
    ffw_part = ffw_gate.shape[1] // TP
    rows = proj_gelu.shape[0]
    held = -(-heads // TP)
    first = [k * heads // TP for k in range(TP)]
    owned = [range(first[k], first[k + 1] if k + 1 < TP else heads) for k in range(TP)]
    part = held * block_width

    out_t, down_t = proj_out.T, ffw_down.T
    small = jnp.concatenate([norm_mix[None], norm_ffw[None], decay_param[None], conv_taps.T])
    small = jnp.pad(small, ((0, 128 - small.shape[0]), (0, 0))).T
    x_rows, cot = inputs[:, 0], cotangent[:, 0]
    one = 1 if p.rests == 1 else 0
    cot_halves = cot.reshape(2, -1, width)
    edge = lax.ppermute(
        x_rows[:, span - (tap_count - 1) :],
        "seq",
        [(i, i + 1) for i in range(lax.axis_size("seq") - 1)],
    )
    edge = jnp.pad(edge, ((0, 0), (HALO - (tap_count - 1), 0), (0, 0)))
    x_wide = jnp.concatenate([x_rows.reshape(-1, width), edge.reshape(-1, width)])
    if p.rests == 1:
        weights = (proj_gelu, proj_lru, out_t, gate_blocks, small, ffw_gate, ffw_up, down_t)
        mix_pieces, ffw_pieces = pack(weights, block_width)
        mix_w, ffw_w, piece_1, x_all, cot_first = intake(
            mix_pieces, ffw_pieces[0], ffw_pieces[1], x_wide.reshape(3, -1, width), cot_halves[0].reshape(2, -1, width), p
        )
        piece_2, piece_3, x_all = lax.optimization_barrier((*ffw_pieces[2:], x_all))
        piece_3, piece_2 = shift_z(piece_3, 3), shift_z(piece_2, 2)
        passed = (piece_1, swap_x(piece_1), swap_f(piece_1), piece_2, piece_3)
    else:
        mix_pieces, ffw_pieces = [], []
        for k in range(TP):
            cols = slice(first[k] * block_width, first[k] * block_width + part)
            pieces = [proj_gelu[:, cols], proj_lru[:, cols], out_t[:, cols], gate_blocks, small]
            mix_pieces.append(jnp.concatenate(pieces, axis=1))
            cols = slice(k * ffw_part, (k + 1) * ffw_part)
            pieces = [ffw_gate[:, cols], ffw_up[:, cols], down_t[:, cols]]
            ffw_pieces.append(jnp.concatenate(pieces, axis=1))
        mix_w = weights_in(jnp.stack(mix_pieces), p)
        whole_ffw = weights_in(jnp.stack(ffw_pieces), p)
        x_all, passed, ffw_w = gather_z(x_wide, p), None, None
        cot_first = gather_z(cot_halves[:1], p)
    dims = (span, micro, heads, held, block_width, tap_count)
    small_w, rows_w, mixed, pre, pre_lru, conv, gate, state, prod, sums = recur(
        x_all.reshape(-1, width), mix_w, dims
    )
    mix_gain, ffw_gain = small_w[0:1], small_w[1:2]
    start = sum(jnp.where(p.z == k, first[k] * block_width, 0) for k in range(TP))

    ends = (TP, micro, part)
    if p.rests == 1:
        state_in, every_sum = chain(sums)
    else:
        sums = all_spans(jnp.stack([sums[0].reshape(ends), sums[1].reshape(ends)], axis=1), p)
        carry, carries = jnp.zeros_like(sums[0, 0]), []
        for k in range(sums.shape[0]):
            carries.append(carry)
            carry = sums[k, 0] * carry + sums[k, 1]
        state_in = own_spans(jnp.stack(carries), p).reshape(-1, part)
    mix_bf, out_parts = recur_mix(pre, rows_w, state, prod, state_in, mix_w, dims)
    blocked = (TP, micro * CUTS, span // CUTS, width)
    x_own, cot_own = x_rows.reshape(blocked[1:]), cot.reshape(blocked[1:])
    out_parts = out_parts.reshape(blocked)
    x_one, ffw_bf, cot_all, _, *fed = middle(
        out_parts, x_own, ffw_gain, cot_halves[1], cot_first, passed, ffw_w
    )
    cot_all = cot_all.reshape(-1, width)

    ffw_bf = ffw_bf.reshape(-1, width)
    if p.rests == 1:
        hidden_bf, grad_gate_up, ffw_parts, grad_in_parts = fed
    else:
        gate_up_w, down_w = whole_ffw[:, : 2 * ffw_part], whole_ffw[:, 2 * ffw_part :]
        gate_up = dot_plain(ffw_bf, gate_up_w)
        gate_vals, up_vals = gate_up[:, :ffw_part], gate_up[:, ffw_part:]
        hidden_bf = geglu(gate_vals, up_vals).astype(BF)
        grad_hidden = dot_plain(cot_all, down_w)
        _, pull_back = jax.vjp(geglu, gate_vals, up_vals)
        grad_gate_up = jnp.concatenate(pull_back(grad_hidden), axis=1).astype(BF)
        ffw_parts = dot_right_t(hidden_bf, down_w).astype(BF)
        grad_in_parts = dot_right_t(grad_gate_up, gate_up_w).astype(BF)
    ffw_parts, grad_in_parts = ffw_parts.reshape(blocked), grad_in_parts.reshape(blocked)
    factors = [cot_all, hidden_bf, ffw_bf, grad_gate_up]
    (mixed_out, grad_x_one, gain_rows, grad_mix), ffw_pieces, down_pieces = turn(
        grad_in_parts, ffw_parts, x_one, cot_own, ffw_gain, factors * one, p
    )
    if p.rests == 1:
        ffw_pieces = [shift_z(piece, d) if d else piece for d, piece in enumerate(ffw_pieces)]
    grad_mix = grad_mix.reshape(-1, width)

    grad_gelu_bf, local_back, prod_back, back_sums = recur_back(
        grad_mix, pre, rows_w, state, prod, state_in, gate, mix_w, dims
    )
    if p.rests == 1:
        carried, _ = chain(back_sums[None], every_sum)
    else:
        back_sums = all_spans(back_sums.reshape(ends), p)
        carry, carries = jnp.zeros_like(sums[0, 0]), []
        for k in range(sums.shape[0] - 1, -1, -1):
            carries.append(carry)
            carry = sums[k, 0] * carry + back_sums[k]
        carried = own_spans(jnp.stack(carries[::-1]), p).reshape(-1, part)
    block_mats = lax.dynamic_slice(mix_w, (start, 3 * part), (part, 2 * block_width))
    grad_blocks, grad_lru, spill, row_grads = recur_grad(
        local_back, prod_back, carried, state, prod, state_in, gate, conv, pre_lru, rows_w,
        block_mats.reshape(held, block_width, 2 * block_width), dims,
    )
    spill = spill.reshape(TP, micro, HALO, part)
    from_next = shift_q(spill, -1)
    last = jnp.zeros_like(spill[:1])
    if p.rests > 1:
        last = move(spill[:1], lambda r, z, q: (r - 1, z, NQ - 1) if q == 0 and r > 0 else None)
    from_next = jnp.where(
        p.q == NQ - 1, jnp.concatenate([from_next[1:], last], axis=0), from_next
    )
    grad_pair, grad_mixed_parts, mix_gain_rows = recur_in(
        grad_gelu_bf, grad_lru, from_next.reshape(-1, part), rows_w, small_w, mixed, mix_w, dims
    )
    grad_mixed_parts = grad_mixed_parts.reshape(blocked)

    blocks_all = lax.dynamic_update_slice_in_dim(
        jnp.zeros((lru_width, 2 * block_width), BF),
        (grad_blocks * rows_w[6][:, None]).astype(BF),
        start,
        0,
    )
    mix_factors = [grad_mix, mix_bf, mixed, grad_pair]
    vectors = lax.dynamic_update_slice_in_dim(
        jnp.zeros((1 + tap_count, lru_width), F32), row_grads[: 1 + tap_count], start, 1
    )
    vectors = jnp.concatenate([mix_gain_rows[:1], gain_rows[:1], vectors], axis=0)
    vectors = jnp.pad(vectors, ((0, -vectors.shape[0] % 8), (0, 0)))
    if p.rests == 1:
        grad_inputs, vectors, mix_grads = final(
            grad_mixed_parts, x_own, mix_gain, grad_x_one, vectors,
            by_owner(blocks_all, p), mix_factors, p,
        )
    else:
        products = [dot_left_t(*mix_factors[:2]), dot_left_t(*mix_factors[2:])]
        products = [blocks_all, products[0], products[1][:, :part], products[1][:, part:]]
        mix_grads = [grads_out(grad.astype(BF), p) for grad in products]
        grad_mixed_own = scatter_z(grad_mixed_parts, p)
        grad_inputs = grad_x_one + norm_back(x_own.astype(F32), mix_gain, grad_mixed_own)[0]
        for exchange in (swap_core, swap_x, swap_f):
            vectors = vectors + exchange(vectors)
        for bit in (1, 2):
            vectors = vectors + move(vectors, lambda r, z, q, bit=bit: (r, z ^ bit, q))
        total = vectors
        for d in range(1, p.rests):
            total = total + shift_r(vectors, d)
        vectors = total
    vectors = lax.dynamic_slice_in_dim(vectors, p.index * rows, rows, 1)

    if p.rests == 1:
        spans = [(first[k] * block_width, len(owned[k]) * block_width) for k in range(TP)]
        share_blocks, share_out, share_gelu, share_lru = unpack_mix(mix_grads, spans)
        share_gate, share_up, share_down = unpack((ffw_pieces, down_pieces), (2, 1))
    else:
        ffw_grads = [dot_left_t(*factors[:2]), dot_left_t(*factors[2:])]
        ffw_grads = [grads_out(grad.astype(BF), p) for grad in ffw_grads]
        beside = lambda v: jnp.swapaxes(v, 0, 1).reshape(rows, -1).astype(F32)
        share_gate = beside(ffw_grads[1][:, :, :ffw_part])
        share_up = beside(ffw_grads[1][:, :, ffw_part:])
        share_down = beside(ffw_grads[0])

        def mix_columns(grad):
            picked = [grad[k][:, : len(owned[k]) * block_width] for k in range(TP)]
            return jnp.concatenate(picked, axis=1).astype(F32)

        share_blocks = jnp.sum(mix_grads[0].astype(F32), axis=0)
        share_out, share_gelu, share_lru = (mix_columns(grad) for grad in mix_grads[1:])
    shape = (micro, 1, span, width)
    return (
        mixed_out.reshape(shape),
        grad_inputs.reshape(shape),
        share_gelu,
        share_lru,
        share_blocks,
        share_out.T,
        share_gate,
        share_up,
        share_down.T,
        vectors[0],
        vectors[1],
        vectors[2],
        vectors[3 : 3 + tap_count].T,
    )


def solution(mesh):
    in_specs = (
        P(None, "fsdp", "seq", None),
        P(None, "fsdp", "seq", None),
        P(("fsdp", "seq"), None),
        P(("fsdp", "seq"), None),
        P(("fsdp", "seq"), None),
        P(None, ("fsdp", "seq")),
        P(("fsdp", "seq"), None),
        P(("fsdp", "seq"), None),
        P(None, ("fsdp", "seq")),
        P(("fsdp", "seq")),
        P(("fsdp", "seq")),
        P(("fsdp", "seq")),
        P(("fsdp", "seq"), None),
    )
    out_specs = (
        P(None, "fsdp", "seq", None),
        P(None, "fsdp", "seq", None),
        P(("fsdp", "seq"), None),
        P(("fsdp", "seq"), None),
        P(("fsdp", "seq"), None),
        P(None, ("fsdp", "seq")),
        P(("fsdp", "seq"), None),
        P(("fsdp", "seq"), None),
        P(None, ("fsdp", "seq")),
        P(("fsdp", "seq")),
        P(("fsdp", "seq")),
        P(("fsdp", "seq")),
        P(("fsdp", "seq"), None),
    )
    return jax.shard_map(
        on_device, mesh=mesh, in_specs=in_specs, out_specs=out_specs, check_vma=False
    )
```
